32 devices in a mesh: groups: 2 (over x), seq: 4 (over y, core), head: 4 (over z).
Axes of the slice: x: 2, y: 2, z: 4, core: 2. Of those that a mesh axis runs over, the one named last changes fastest.
Arguments:
- latent_cache: bfloat16 [32768, 576], P(('groups', 'seq')), parts along dimension 0, may hold values from -6 to 6
- lengths: int32 [8, 16], P('groups'), parts along dimension 0, may hold values from 1 to 512, 4096 in all within a row
- decode_rows: int32 [128], P('groups'), parts along dimension 0, may hold values from 0 to 63, as said below
- q_nope: bfloat16 [4, 128, 128, 128], P(None, ('groups', 'seq'), 'head'), parts along dimension 1, may hold values from -6 to 6
- q_rope: bfloat16 [4, 128, 128, 64], P(None, ('groups', 'seq'), 'head'), parts along dimension 1, may hold values from -90 to 90
- new_latent: bfloat16 [4, 128, 576], P(None, ('groups', 'seq')), parts along dimension 1, may hold values from -13 to 13
- key_up: bfloat16 [128, 128, 512], P('head'), may hold values from -0.5 to 0.5
- value_up: bfloat16 [128, 512, 128], P('head'), may hold values from -0.25 to 0.25
- out_proj: bfloat16 [16384, 7168], P('head', 'seq'), may hold values from -0.046875 to 0.046875
Outputs:
- mixed: bfloat16 [4, 128, 7168], P(None, 'groups', 'seq'), parts along dimension 1
The draws below stay inside these ranges and needn't reach their ends.
There are 2 independent parts, one for each index of `groups`. The reference program is written for one: setup_inputs(seed, part) draws one part's arguments, and reference() takes and returns one part's arrays. A program takes and returns all parts, laid end to end along the dimension named above; an argument that names none is the same for every part. Nothing has to cross between parts.
Inputs may be any that keep to these rules, and one draw needn't show every extreme that they name: `decode_rows`: a permutation of the rows; the rows of decode owner o are o * 16 to o * 16 + 15, and every prefill device hands exactly 4 of its requests to every owner. Each prefill device's lengths sum to 4096.
All inputs are finite; a program needn't handle non-finite values.
Results may differ from the reference program's by a relative error of at most 0.0077.
Values may be sent and summed in bfloat16 or wider, within the bound.
No kernel may reach another device: no remote copies, remote signals or barrier semaphores. Data moves between devices by JAX's collectives and lax.ppermute only.
A program may use at most 128 MiB of HBM per device.

```python
import math
import jax
import jax.numpy as jnp
import numpy as np
from jax import lax

D = 7168
HEADS = 128
NOPE = 128
ROPE = 64
LATENT = 512
VDIM = 128
REQ_SRC = 16
MOST = 512
STEPS = 4
SRC_TOK = 4096
ROWS = 64
N_SEQ = 4


def shuffle_one(subkey):
    return jax.random.permutation(subkey, REQ_SRC)


def draw_decode_rows(key, part):
    key = jax.random.fold_in(key, 11)
    source_key, owner_key = jax.random.split(key)
    source_count = ROWS // REQ_SRC
    pair_count = REQ_SRC // source_count
    places = jax.vmap(shuffle_one)(jax.random.split(source_key, source_count))
    owner_index = places % source_count
    within = places // source_count
    arrange = jax.vmap(shuffle_one)(jax.random.split(owner_key, source_count))
    sources = jnp.arange(source_count)[:, None]
    row_ids = owner_index * REQ_SRC + arrange[owner_index, sources * pair_count + within]
    return row_ids.reshape(ROWS).astype(jnp.int32)


def draw_q_rope(key, part):
    key = jax.random.fold_in(key, 21)
    full_shape = (STEPS, ROWS, HEADS, ROPE)
    return jnp.clip(jax.random.normal(key, full_shape, jnp.float32), -6.0, 6.0).astype(jnp.bfloat16)


def draw_new_latent(key, part):
    key = jax.random.fold_in(key, 31)
    full_shape = (STEPS, ROWS, LATENT + ROPE)
    return jnp.clip(jax.random.normal(key, full_shape, jnp.float32), -6.0, 6.0).astype(jnp.bfloat16)


def steps_of(own_key, dims, shards, smallest, largest):
    def one(dim, parts):
        draws = jax.random.uniform(jax.random.fold_in(jax.random.fold_in(own_key, 6), dim), (parts,), jnp.float32, smallest / len(shards), largest / len(shards))
        return jnp.repeat(jnp.exp(draws), dims[dim] // parts).reshape((-1,) + (1,) * (len(dims) - dim - 1))

    factor_of = one(*shards[0])
    for cut in shards[1:]:
        factor_of = factor_of * one(*cut)
    return factor_of


def profile(amount, total, limit, slope):
    weights = [(1 << 20) // math.isqrt(rank ** slope) + 1 for rank in range(2, amount + 1)]
    surplus, counts = total - limit - (amount - 1), [1] * (amount - 1)
    while surplus > 0:
        candidates = [i for i in range(amount - 1) if counts[i] < limit]
        whole, remaining = sum([weights[i] for i in candidates]), surplus
        for i in candidates:
            extra = min(limit - counts[i], max(1, remaining * weights[i] // whole), surplus)
            counts[i] = counts[i] + extra
            surplus = surplus - extra
    return np.array([limit] + counts)


def ragged_sizes(key, number_of, total, bound, lean):
    if number_of == 2:
        one = jax.random.randint(key, (), max(1, total - bound), min(bound, total - 1) + 1)
        return jnp.stack([one, total - one])
    tallies = jnp.asarray(profile(number_of, total, bound, lean), jnp.int32)
    couples = (number_of - 1) // 2
    donor, receiver = tallies[1:1 + 2 * couples:2], tallies[2:2 + 2 * couples:2]
    margin = jnp.minimum(donor - 1, bound - receiver)
    passed = jax.random.randint(jax.random.fold_in(key, 1), (couples,), 0, 1 << 20) % (margin + 1)
    tallies = tallies.at[1:1 + 2 * couples:2].set(donor - passed).at[2:2 + 2 * couples:2].set(receiver + passed)
    return tallies[jax.random.permutation(jax.random.fold_in(key, 2), number_of)]


def scatter_about(stream_key, extent, deviation, reach, cuts=(), kind=jnp.bfloat16):
    factor_of = steps_of(stream_key, extent, cuts, -0.22, 0.18) if cuts else 1.0
    result = jax.random.normal(stream_key, extent, jnp.float32) * deviation * factor_of
    return jnp.minimum(jnp.maximum(result, -reach), reach).astype(kind)


def setup_inputs(seed: int = 0, part: int = 0) -> dict:
    splits = jax.random.split(jax.random.key(seed), 10)
    part_keys = jax.random.split(jax.random.fold_in(splits[9], part), 10)
    return {
        "latent_cache": scatter_about(part_keys[0], (N_SEQ * SRC_TOK, LATENT + ROPE), 1.0, 6.0, ((0, 4),)),
        "lengths": jax.vmap(lambda own: ragged_sizes(own, REQ_SRC, SRC_TOK, MOST, 2))(jax.random.split(part_keys[1], N_SEQ)).reshape((N_SEQ, REQ_SRC)).astype(jnp.int32),
        "decode_rows": draw_decode_rows(jax.random.fold_in(jax.random.fold_in(splits[9], part), 71), part),
        "q_nope": scatter_about(part_keys[3], (STEPS, ROWS, HEADS, NOPE), 1.0, 6.0, ((1, 4), (2, 4))),
        "q_rope": draw_q_rope(jax.random.fold_in(jax.random.fold_in(splits[9], part), 71), part),
        "new_latent": draw_new_latent(jax.random.fold_in(jax.random.fold_in(splits[9], part), 71), part),
        "key_up": scatter_about(splits[6], (HEADS, NOPE, LATENT), NOPE ** -0.5, 0.5, ((0, 4),)),
        "value_up": scatter_about(splits[7], (HEADS, LATENT, VDIM), LATENT ** -0.5, 0.25, ((0, 4),)),
        "out_proj": scatter_about(splits[8], (HEADS * VDIM, D), (HEADS * VDIM) ** -0.5, 0.046875, ((0, 4), (1, 4))),
    }


def reference(latent_cache, lengths, decode_rows, q_nope, q_rope, new_latent, key_up, value_up, out_proj):
    offsets = jnp.cumsum(lengths, axis=1) - lengths
    row_count = decode_rows.shape[0]
    request_of = jnp.zeros((row_count,), jnp.int32).at[decode_rows].set(jnp.arange(row_count, dtype=jnp.int32))
    scale = (NOPE + ROPE) ** -0.5
    positions = jnp.arange(MOST, dtype=jnp.int32)
    causal = jnp.arange(STEPS)[None, :] <= jnp.arange(STEPS)[:, None]
    key_wide = key_up.astype(jnp.float32)
    value_wide = value_up.astype(jnp.float32)

    def one_row(row_index):
        request = request_of[row_index]
        source = request // REQ_SRC
        within = request % REQ_SRC
        length = lengths[source, within]
        tokens = source * SRC_TOK + jnp.minimum(offsets[source, within] + positions, SRC_TOK - 1)
        cache_rows = jnp.take(latent_cache, tokens.astype(jnp.int32), axis=0)
        fresh = lax.dynamic_index_in_dim(new_latent, row_index, 1, keepdims=False)
        nope_part = lax.dynamic_index_in_dim(q_nope, row_index, 1, keepdims=False)
        rope_part = lax.dynamic_index_in_dim(q_rope, row_index, 1, keepdims=False)
        q_abs = jnp.einsum("thn,hnc->thc", nope_part.astype(jnp.float32), key_wide).astype(jnp.bfloat16)
        queries = jnp.concatenate([q_abs, rope_part], axis=2).astype(jnp.float32)
        cache_scores = jnp.einsum("thc,jc->thj", queries, cache_rows.astype(jnp.float32)) * scale
        new_scores = jnp.einsum("thc,uc->thu", queries, fresh.astype(jnp.float32)) * scale
        cache_scores = jnp.where((positions < length)[None, None, :], cache_scores, -jnp.inf)
        new_scores = jnp.where(causal[:, None, :], new_scores, -jnp.inf)
        weights = jax.nn.softmax(jnp.concatenate([cache_scores, new_scores], axis=2), axis=2).astype(jnp.bfloat16)
        values = jnp.concatenate([cache_rows[:, :LATENT], fresh[:, :LATENT]], axis=0)
        latent_out = jnp.einsum("thj,jc->thc", weights.astype(jnp.float32), values.astype(jnp.float32)).astype(jnp.bfloat16)
        head_out = jnp.einsum("thc,hcv->thv", latent_out.astype(jnp.float32), value_wide).astype(jnp.bfloat16)
        return head_out.reshape(STEPS, HEADS * VDIM)

    per_row = lax.map(one_row, jnp.arange(row_count, dtype=jnp.int32))
    head_rows = jnp.transpose(per_row, (1, 0, 2)).reshape(STEPS * row_count, HEADS * VDIM)
    mixed = jnp.dot(head_rows, out_proj, preferred_element_type=jnp.float32)
    return mixed.reshape(STEPS, row_count, D).astype(jnp.bfloat16)
```

```python
import functools

import jax
import jax.numpy as jnp
from jax import lax
from jax.experimental import pallas as pl
from jax.experimental.pallas import tpu as pltpu
from jax.sharding import PartitionSpec as P

LATENT = 512
BLOCK = 256
LANES = 128
LOG2E = 1.4426950408889634
NEG = -1e30
VMEM_LIMIT = 56 * 1024 * 1024


def own_slots(decode_ref, slot_ref, me, sources, requests, per_pair):
    def one_source(s, carry):
        count = jnp.int32(0)
        for r in range(requests):
            row = decode_ref[s * requests + r]
            slot_ref[s * (per_pair + 1) + jnp.minimum(count, per_pair)] = row - me * requests
            count = count + jnp.where(row // requests == me, 1, 0).astype(jnp.int32)
        return carry

    lax.fori_loop(0, sources, one_source, jnp.int32(0))


def pack_kernel(sizes, me_ref, decode_ref, nope_ref, rope_ref, fresh_ref, out_ref, slots, nope_wide, rope_wide):
    sources, per_pair, steps, heads, requests, fresh_rows = sizes
    me = me_ref[0]
    pair_rows = per_pair * steps
    rope_base = heads * pair_rows
    half = heads * steps // 2
    fresh_base = rope_base + per_pair * half
    own_slots(decode_ref, slots, me, sources, requests, per_pair)

    def one_dest(s, carry):
        for j in range(per_pair):
            row = slots[s * (per_pair + 1) + j]
            for t in range(steps):
                nope_wide[pl.ds(j * steps + t, heads, stride=pair_rows), :] = nope_ref[t, row].astype(jnp.float32)
                rope_wide[pl.ds(t, heads, stride=steps), :] = jnp.concatenate(
                    [rope_ref[t, row].astype(jnp.float32)] * 2, axis=1
                )
            low = lax.broadcasted_iota(jnp.int32, (half, LANES), 1) < LANES // 2
            packed = jnp.where(low, rope_wide[0:half, :], rope_wide[half : 2 * half, :])
            out_ref[s, rope_base + j * half : rope_base + (j + 1) * half, :] = packed.astype(jnp.bfloat16)
        out_ref[s, 0:rope_base, :] = nope_wide[...].astype(jnp.bfloat16)
        return carry

    lax.fori_loop(0, sources, one_dest, jnp.int32(0))
    shape = (sources * fresh_rows, steps * requests)
    row_id = lax.broadcasted_iota(jnp.int32, shape, 0)
    col_id = lax.broadcasted_iota(jnp.int32, shape, 1)
    wanted = jnp.full(shape, -1, jnp.int32)
    for s in range(sources):
        for j in range(per_pair):
            first = s * fresh_rows + j * steps
            here = (row_id >= first) & (row_id < first + steps)
            wanted = jnp.where(here, (row_id - first) * requests + slots[s * (per_pair + 1) + j], wanted)
    pick = jnp.where(col_id == wanted, 1.0, 0.0).astype(jnp.bfloat16)
    width = fresh_ref.shape[2]
    source_rows = jnp.concatenate([fresh_ref[t] for t in range(steps)], axis=0)
    picked = jnp.dot(pick, source_rows, preferred_element_type=jnp.float32).astype(jnp.bfloat16)
    for s in range(sources):
        for c in range(-(-width // LANES)):
            piece = picked[s * fresh_rows : (s + 1) * fresh_rows, c * LANES : min((c + 1) * LANES, width)]
            if piece.shape[1] < LANES:
                piece = jnp.concatenate([piece] * (LANES // piece.shape[1]), axis=1)
            first = fresh_base + c * fresh_rows
            out_ref[s, first : first + fresh_rows, :] = piece


def attend_kernel(
    sizes, scale, me_ref, decode_ref, length_ref, recv_ref, cache_hbm, key_hbm, value_hbm, out_ref,
    slot_offset, slot_length, owner_count, pair_slot, pair_block, first_pair,
    cache, key_up, value_up, queries, fresh, part_out, part_max, part_sum, latent, sems,
):
    sources, per_pair, steps, heads, requests, fresh_rows = sizes
    width = cache.shape[0]
    pair_rows = per_pair * steps
    rope_base = heads * pair_rows
    rows = heads * steps
    half = rows // 2
    fresh_base = rope_base + per_pair * half
    group = 16 // steps
    copies = [
        pltpu.make_async_copy(key_hbm, key_up, sems.at[0]),
        pltpu.make_async_copy(cache_hbm, cache, sems.at[1]),
        pltpu.make_async_copy(value_hbm, value_up, sems.at[2]),
    ]
    for copy in copies:
        copy.start()

    me = me_ref[0]
    for o in range(sources):
        owner_count[o] = jnp.int32(0)
    total = jnp.int32(0)
    for r in range(requests):
        owner = decode_ref[me * requests + r] // requests
        at = owner_count[owner]
        owner_count[owner] = at + 1
        slot = owner * per_pair + at
        slot_offset[slot] = total
        slot_length[slot] = length_ref[me, r]
        total = total + length_ref[me, r]
    count = jnp.int32(0)
    spans = 512 // BLOCK + 1
    for slot in range(requests):
        first_block = slot_offset[slot] // BLOCK
        last_block = (slot_offset[slot] + slot_length[slot] - 1) // BLOCK
        first_pair[slot] = count
        for k in range(spans):
            pair_slot[count] = jnp.int32(slot)
            pair_block[count] = first_block + k
            count = count + jnp.where(first_block + k <= last_block, 1, 0).astype(jnp.int32)
    first_pair[requests] = count

    for o in range(sources):
        for c in range(-(-width // LANES)):
            lanes = min(LANES, width - c * LANES)
            first = fresh_base + c * fresh_rows
            fresh[o * fresh_rows : (o + 1) * fresh_rows, c * LANES : c * LANES + lanes] = recv_ref[
                o, first : first + fresh_rows, 0:lanes
            ]
        for j in range(per_pair):
            slot = o * per_pair + j
            first = rope_base + j * half
            piece = recv_ref[o, first : first + half, :]
            queries[slot * rows : slot * rows + half, LATENT:width] = piece[:, 0 : width - LATENT]
            queries[slot * rows + half : (slot + 1) * rows, LATENT:width] = piece[:, LANES - (width - LATENT) :]

    copies[0].wait()

    def absorb(i, carry):
        results = []
        for u in range(group):
            head = i * group + u
            if pair_rows % 16 == 0:
                first = pl.multiple_of(head * pair_rows, 16)
                left = jnp.concatenate([recv_ref[o, pl.ds(first, pair_rows), :] for o in range(sources)], axis=0)
            else:
                first = pl.multiple_of(i * group * pair_rows, 16)
                left = jnp.concatenate(
                    [
                        recv_ref[o, pl.ds(first, group * pair_rows), :].astype(jnp.float32)[
                            u * pair_rows : (u + 1) * pair_rows
                        ]
                        for o in range(sources)
                    ],
                    axis=0,
                ).astype(jnp.bfloat16)
            results.append(jnp.dot(left, key_up[head], preferred_element_type=jnp.float32))
        for slot in range(requests):
            tile = jnp.concatenate([res[slot * steps : (slot + 1) * steps] for res in results], axis=0)
            queries[pl.ds(pl.multiple_of(slot * rows + i * 16, 16), 16), 0:LATENT] = tile.astype(jnp.bfloat16)
        return carry

    lax.fori_loop(0, heads // group, absorb, jnp.int32(0))
    copies[1].wait()

    unroll = 2
    factor = scale * LOG2E

    def some_pairs(i, carry):
        for u in range(unroll):
            p = jnp.minimum(i * unroll + u, count - 1)
            slot = pair_slot[p]
            start = pair_block[p] * BLOCK
            low = slot_offset[slot] - start
            high = low + slot_length[slot]
            q = queries[pl.ds(pl.multiple_of(slot * rows, 16), rows), :]
            keys = cache[:, pl.ds(pl.multiple_of(start, BLOCK), BLOCK)]
            scores = jnp.dot(q, keys, preferred_element_type=jnp.float32) * factor
            token = lax.broadcasted_iota(jnp.int32, scores.shape, 1)
            scores = jnp.where((token >= low) & (token < high), scores, NEG)
            top = jnp.max(scores, axis=1, keepdims=True)
            weights = jnp.exp2(scores - top)
            part_max[p] = jnp.broadcast_to(top, (rows, LANES))
            part_sum[p] = jnp.broadcast_to(jnp.sum(weights, axis=1, keepdims=True), (rows, LANES))
            part_out[p] = lax.dot_general(
                weights.astype(jnp.bfloat16),
                keys[0:LATENT],
                (((1,), (1,)), ((), ())),
                preferred_element_type=jnp.float32,
            )
        return carry

    lax.fori_loop(0, (count + unroll - 1) // unroll, some_pairs, jnp.int32(0))

    def merge(slot, carry):
        q = queries[pl.ds(pl.multiple_of(slot * rows, 16), rows), :]
        scores = (
            lax.dot_general(q, fresh[...], (((1,), (1,)), ((), ())), preferred_element_type=jnp.float32) * factor
        )
        row_id = lax.broadcasted_iota(jnp.int32, scores.shape, 0)
        col_id = lax.broadcasted_iota(jnp.int32, scores.shape, 1)
        base = (slot // per_pair) * fresh_rows + (slot % per_pair) * steps
        scores = jnp.where((col_id >= base) & (col_id <= base + (row_id & (steps - 1))), scores, NEG)
        top = jnp.max(scores, axis=1, keepdims=True)
        first = first_pair[slot]
        last = first_pair[slot + 1] - 1
        tops = []
        for k in range(spans):
            own = part_max[jnp.minimum(first + k, last)][:, 0:1]
            own = jnp.where(first + k <= last, own, 2 * NEG)
            tops.append(own)
        highest = functools.reduce(jnp.maximum, tops, top)
        weights = jnp.exp2(scores - highest)
        norm = jnp.sum(weights, axis=1, keepdims=True)
        out = jnp.dot(weights.astype(jnp.bfloat16), fresh[:, 0:LATENT], preferred_element_type=jnp.float32)
        for k in range(spans):
            at = jnp.minimum(first + k, last)
            share = jnp.exp2(tops[k] - highest)
            norm = norm + share * part_sum[at][:, 0:1]
            out = out + share * part_out[at]
        latent[pl.ds(pl.multiple_of(slot * rows, 16), rows), :] = (out / norm).astype(jnp.bfloat16)
        return carry

    lax.fori_loop(0, requests, merge, jnp.int32(0))
    copies[2].wait()

    def project(i, carry):
        tiles = [
            latent[pl.ds(pl.multiple_of(slot * rows + i * 16, 16), 16), :].astype(jnp.float32)
            for slot in range(requests)
        ]
        for u in range(group):
            head = i * group + u
            left = jnp.concatenate([tile[u * steps : (u + 1) * steps] for tile in tiles], axis=0)
            res = jnp.dot(left.astype(jnp.bfloat16), value_up[head], preferred_element_type=jnp.float32)
            vdim = res.shape[1]
            out_ref[:, pl.ds(pl.multiple_of(head * vdim, vdim), vdim)] = res.astype(jnp.bfloat16)
        return carry

    lax.fori_loop(0, heads // group, project, jnp.int32(0))


def order_kernel(sizes, relative, me_ref, decode_ref, x_ref, out_ref, owner_count, place):
    sources, per_pair, steps, requests = sizes
    me = me_ref[0]
    rows = sources * requests

    def one_source(q, carry):
        s = me ^ q if relative else q
        for o in range(sources):
            owner_count[o] = jnp.int32(0)
        for r in range(requests):
            row = decode_ref[s * requests + r]
            owner = row // requests
            at = owner_count[owner]
            owner_count[owner] = at + 1
            place[row] = (q * requests + owner * per_pair + at) * steps
        return carry

    lax.fori_loop(0, sources, one_source, jnp.int32(0))
    narrow = (rows, LANES)
    row_id = lax.broadcasted_iota(jnp.int32, narrow, 0)

    def put(b, wanted):
        return jnp.where(row_id == b, place[b], wanted)

    wanted = lax.fori_loop(0, rows, put, jnp.zeros(narrow, jnp.int32), unroll=8)[:, 0:1]
    col_id = lax.broadcasted_iota(jnp.int32, (rows, rows * steps), 1)
    for t in range(steps):
        pick = jnp.where(col_id == wanted + t, 1.0, 0.0).astype(jnp.bfloat16)
        out_ref[t] = jnp.dot(pick, x_ref[...], preferred_element_type=jnp.float32).astype(jnp.bfloat16)


def smem():
    return pl.BlockSpec(memory_space=pltpu.SMEM)


def vmem():
    return pl.BlockSpec(memory_space=pltpu.VMEM)


def hbm():
    return pl.BlockSpec(memory_space=pl.ANY)


def local(latent_cache, lengths, decode_rows, q_nope, q_rope, new_latent, key_up, value_up, out_proj):
    sources = lax.axis_size("seq")
    groups_of_heads = lax.axis_size("head")
    me = lax.axis_index("seq")
    requests = lengths.shape[1]
    per_pair = requests // sources
    tokens, width = latent_cache.shape
    steps, _, heads, nope = q_nope.shape
    rope = q_rope.shape[3]
    scale = (nope + rope) ** (-0.5)
    fresh_rows = -(-per_pair * steps // 16) * 16
    pair_rows = per_pair * steps
    rows = heads * steps
    packed_rows = heads * pair_rows + per_pair * rows // 2 + -(-width // LANES) * fresh_rows
    sizes = (sources, per_pair, steps, heads, requests, fresh_rows)
    params = pltpu.CompilerParams(vmem_limit_bytes=VMEM_LIMIT)
    me_array = me.astype(jnp.int32).reshape(1)

    packed = pl.pallas_call(
        functools.partial(pack_kernel, sizes),
        out_shape=jax.ShapeDtypeStruct((sources, packed_rows, LANES), jnp.bfloat16),
        in_specs=[smem(), smem(), vmem(), vmem(), vmem()],
        out_specs=vmem(),
        scratch_shapes=[
            pltpu.SMEM((sources * (per_pair + 1),), jnp.int32),
            pltpu.VMEM((heads * pair_rows, LANES), jnp.float32),
            pltpu.VMEM((rows, LANES), jnp.float32),
        ],
        compiler_params=params,
        name="pack_queries",
    )(me_array, decode_rows, q_nope, q_rope, new_latent)
    received = lax.all_to_all(packed, "seq", split_axis=0, concat_axis=0, tiled=True)

    pairs = tokens // BLOCK + requests + 2
    head_rows = pl.pallas_call(
        functools.partial(attend_kernel, sizes, scale),
        out_shape=jax.ShapeDtypeStruct((requests * steps, heads * value_up.shape[2]), jnp.bfloat16),
        in_specs=[smem(), smem(), smem(), vmem(), hbm(), hbm(), hbm()],
        out_specs=vmem(),
        scratch_shapes=[
            pltpu.SMEM((requests,), jnp.int32),
            pltpu.SMEM((requests,), jnp.int32),
            pltpu.SMEM((sources,), jnp.int32),
            pltpu.SMEM((pairs,), jnp.int32),
            pltpu.SMEM((pairs,), jnp.int32),
            pltpu.SMEM((requests + 1,), jnp.int32),
            pltpu.VMEM((width, tokens), jnp.bfloat16),
            pltpu.VMEM(key_up.shape, jnp.bfloat16),
            pltpu.VMEM(value_up.shape, jnp.bfloat16),
            pltpu.VMEM((requests * rows, width), jnp.bfloat16),
            pltpu.VMEM((sources * fresh_rows, width), jnp.bfloat16),
            pltpu.VMEM((pairs, rows, LATENT), jnp.float32),
            pltpu.VMEM((pairs, rows, LANES), jnp.float32),
            pltpu.VMEM((pairs, rows, LANES), jnp.float32),
            pltpu.VMEM((requests * rows, LATENT), jnp.bfloat16),
            pltpu.SemaphoreType.DMA((3,)),
        ],
        compiler_params=params,
        name="attend",
    )(me_array, decode_rows, lengths, received, latent_cache.T, key_up, value_up)

    relative = sources == 4
    if relative:
        across = lax.ppermute(head_rows, "seq", [(i, i ^ 2) for i in range(4)])
        beside = lax.ppermute(head_rows, "seq", [(i, i ^ 1) for i in range(4)])
        beyond = lax.ppermute(across, "seq", [(i, i ^ 1) for i in range(4)])
        every_row = jnp.concatenate([head_rows, beside, across, beyond], axis=0)
    else:
        every_row = lax.all_gather(head_rows, "seq", axis=0, tiled=True)
    partial_value = jnp.dot(every_row, out_proj, preferred_element_type=jnp.float32).astype(jnp.bfloat16)
    shares = lax.all_to_all(partial_value, "head", split_axis=0, concat_axis=0, tiled=True)
    shares = shares.reshape(groups_of_heads, -1, shares.shape[1])
    summed = jnp.sum(shares.astype(jnp.float32), axis=0).astype(jnp.bfloat16)
    mixed = lax.all_gather(summed, "head", axis=0, tiled=True)
    return pl.pallas_call(
        functools.partial(order_kernel, (sources, per_pair, steps, requests), relative),
        out_shape=jax.ShapeDtypeStruct((steps, sources * requests, out_proj.shape[1]), jnp.bfloat16),
        in_specs=[smem(), smem(), vmem()],
        out_specs=vmem(),
        scratch_shapes=[pltpu.SMEM((sources,), jnp.int32), pltpu.SMEM((sources * requests,), jnp.int32)],
        compiler_params=params,
        name="order_rows",
    )(me_array, decode_rows, mixed)


def solution(mesh):
    return jax.shard_map(
        local,
        mesh=mesh,
        in_specs=(
            P(("groups", "seq"), None),
            P("groups", None),
            P("groups"),
            P(None, ("groups", "seq"), "head", None),
            P(None, ("groups", "seq"), "head", None),
            P(None, ("groups", "seq"), None),
            P("head", None, None),
            P("head", None, None),
            P("head", "seq"),
        ),
        out_specs=P(None, "groups", "seq"),
        check_vma=False,
    )
```

```python
import functools

import jax
import jax.numpy as jnp
from jax import lax
from jax.experimental import pallas as pl
from jax.experimental.pallas import tpu as pltpu
from jax.sharding import PartitionSpec as P

LATENT = 512
BLOCK = 256
LANES = 128
LOG2E = 1.4426950408889634
NEG = -1e30


def own_slots(decode_ref, slot_ref, me, sources, requests, per_pair):
    shift = requests.bit_length() - 1

    def one_source(s, carry):
        count = jnp.int32(0)
        for r in range(requests):
            row = decode_ref[s * requests + r]
            slot_ref[s * (per_pair + 1) + jnp.minimum(count, per_pair)] = row & (requests - 1)
            count = count + jnp.where((row >> shift) == me, 1, 0).astype(jnp.int32)
        return carry

    lax.fori_loop(0, sources, one_source, jnp.int32(0))


def pack_kernel(sizes, relative, me_ref, decode_ref, nope_ref, rope_ref, fresh_ref, *rest):
    sources, per_pair, steps, heads, requests, fresh_rows = sizes
    out_refs, (slots, nope_wide, rope_wide) = rest[:-3], rest[-3:]
    me = me_ref[0]
    pair_rows = per_pair * steps
    rope_base = heads * pair_rows
    half = heads * steps // 2
    fresh_base = rope_base + per_pair * half
    own_slots(decode_ref, slots, me, sources, requests, per_pair)

    def one_dest(s, out_ref, e):
        for j in range(per_pair):
            row = slots[s * (per_pair + 1) + j]
            for t in range(steps):
                nope_wide[pl.ds(j * steps + t, heads, stride=pair_rows), :] = nope_ref[t, row].astype(jnp.float32)
                rope_wide[pl.ds(t, heads, stride=steps), :] = jnp.concatenate(
                    [rope_ref[t, row].astype(jnp.float32)] * 2, axis=1
                )
            low = lax.broadcasted_iota(jnp.int32, (half, LANES), 1) < LANES // 2
            packed = jnp.where(low, rope_wide[0:half, :], rope_wide[half : 2 * half, :])
            out_ref[e, rope_base + j * half : rope_base + (j + 1) * half, :] = packed.astype(jnp.bfloat16)
        out_ref[e, 0:rope_base, :] = nope_wide[...].astype(jnp.bfloat16)

    if relative:
        dests = [me ^ k for k in range(sources)]
        for k in range(sources):
            one_dest(dests[k], out_refs[k], 0)
    else:
        dests = list(range(sources))

        def step(s, carry):
            one_dest(s, out_refs[0], s)
            return carry

        lax.fori_loop(0, sources, step, jnp.int32(0))
    shape = (sources * fresh_rows, steps * requests)
    row_id = lax.broadcasted_iota(jnp.int32, shape, 0)
    col_id = lax.broadcasted_iota(jnp.int32, shape, 1)
    wanted = jnp.full(shape, -1, jnp.int32)
    for k in range(sources):
        for j in range(per_pair):
            first = k * fresh_rows + j * steps
            here = (row_id >= first) & (row_id < first + steps)
            wanted = jnp.where(here, (row_id - first) * requests + slots[dests[k] * (per_pair + 1) + j], wanted)
    pick = jnp.where(col_id == wanted, 1.0, 0.0).astype(jnp.bfloat16)
    width = fresh_ref.shape[2]
    source_rows = jnp.concatenate([fresh_ref[t] for t in range(steps)], axis=0)
    picked = jnp.dot(pick, source_rows, preferred_element_type=jnp.float32).astype(jnp.bfloat16)
    for k in range(sources):
        for c in range(-(-width // LANES)):
            piece = picked[k * fresh_rows : (k + 1) * fresh_rows, c * LANES : min((c + 1) * LANES, width)]
            if piece.shape[1] < LANES:
                piece = jnp.concatenate([piece] * (LANES // piece.shape[1]), axis=1)
            first = fresh_base + c * fresh_rows
            if relative:
                out_refs[k][0, first : first + fresh_rows, :] = piece
            else:
                out_refs[0][k, first : first + fresh_rows, :] = piece


def attend_kernel(sizes, scale, relative, base, recv_count, me_ref, decode_ref, length_ref, *rest):
    sources, per_pair, steps, heads, requests, fresh_rows = sizes
    recv_refs = rest[:recv_count]
    (
        cache, key_up, value_up, out_ref,
        slot_offset, slot_length, owner_count, pair_slot, pair_start, first_pair,
        queries, fresh, part_out, part_max, part_sum, latent,
    ) = rest[recv_count:]
    owners = [(ref, e) for ref in recv_refs for e in range(ref.shape[0])]
    here = len(owners)
    slots = here * per_pair
    width, tokens = cache.shape
    pair_rows = per_pair * steps
    rope_base = heads * pair_rows
    rows = heads * steps
    half = rows // 2
    fresh_base = rope_base + per_pair * half
    group = 16 // steps
    shift = requests.bit_length() - 1

    me = me_ref[0]
    for o in range(sources):
        owner_count[o] = jnp.int32(0)
    total = jnp.int32(0)
    for r in range(requests):
        owner = decode_ref[me * requests + r] >> shift
        at = owner_count[owner]
        owner_count[owner] = at + 1
        e = (owner ^ me) - base if relative else owner
        slot = jnp.where((e >= 0) & (e < here), e * per_pair + at, slots)
        length = length_ref[me, r]
        slot_offset[slot] = total
        slot_length[slot] = length
        total = total + length
    count = jnp.int32(0)
    spans = 512 // BLOCK + 1
    for slot in range(slots):
        start = slot_offset[slot] & ~(LANES - 1)
        end = slot_offset[slot] + slot_length[slot]
        first_pair[slot] = count
        for k in range(spans):
            pair_slot[count] = jnp.int32(slot)
            pair_start[count] = start + k * BLOCK
            count = count + jnp.where(start + k * BLOCK < end, 1, 0).astype(jnp.int32)
    first_pair[slots] = count

    for e in range(here):
        ref, at = owners[e]
        for c in range(-(-width // LANES)):
            lanes = min(LANES, width - c * LANES)
            first = fresh_base + c * fresh_rows
            fresh[e * fresh_rows : (e + 1) * fresh_rows, c * LANES : c * LANES + lanes] = ref[
                at, first : first + fresh_rows, 0:lanes
            ]
        for j in range(per_pair):
            slot = e * per_pair + j
            first = rope_base + j * half
            piece = ref[at, first : first + half, :]
            queries[slot * rows : slot * rows + half, LATENT:width] = piece[:, 0 : width - LATENT]
            queries[slot * rows + half : (slot + 1) * rows, LATENT:width] = piece[:, LANES - (width - LATENT) :]

    def absorb(i, carry):
        results = []
        for u in range(group):
            head = i * group + u
            if pair_rows % 16 == 0:
                first = pl.multiple_of(head * pair_rows, 16)
                left = jnp.concatenate([ref[at, pl.ds(first, pair_rows), :] for ref, at in owners], axis=0)
            else:
                first = pl.multiple_of(i * group * pair_rows, 16)
                left = jnp.concatenate(
                    [
                        ref[at, pl.ds(first, group * pair_rows), :].astype(jnp.float32)[
                            u * pair_rows : (u + 1) * pair_rows
                        ]
                        for ref, at in owners
                    ],
                    axis=0,
                ).astype(jnp.bfloat16)
            results.append(jnp.dot(left, key_up[head], preferred_element_type=jnp.float32))
        for slot in range(slots):
            tile = jnp.concatenate([res[slot * steps : (slot + 1) * steps] for res in results], axis=0)
            queries[pl.ds(pl.multiple_of(slot * rows + i * 16, 16), 16), 0:LATENT] = tile.astype(jnp.bfloat16)
        return carry

    lax.fori_loop(0, heads // group, absorb, jnp.int32(0))

    unroll = 2
    factor = scale * LOG2E

    def some_pairs(i, carry):
        for u in range(unroll):
            p = jnp.minimum(i * unroll + u, count - 1)
            slot = pair_slot[p]
            start = pair_start[p]
            read = jnp.minimum(start, tokens - BLOCK)
            low = jnp.maximum(slot_offset[slot], start) - read
            high = jnp.minimum(slot_offset[slot] + slot_length[slot], start + BLOCK) - read
            q = queries[pl.ds(pl.multiple_of(slot * rows, 16), rows), :]
            keys = cache[:, pl.ds(pl.multiple_of(read, LANES), BLOCK)]
            scores = jnp.dot(q, keys, preferred_element_type=jnp.float32) * factor
            token = lax.broadcasted_iota(jnp.int32, scores.shape, 1)
            scores = jnp.where((token >= low) & (token < high), scores, NEG)
            top = jnp.max(scores, axis=1, keepdims=True)
            weights = jnp.exp2(scores - top)
            part_max[p] = jnp.broadcast_to(top, (rows, LANES))
            part_sum[p] = jnp.broadcast_to(jnp.sum(weights, axis=1, keepdims=True), (rows, LANES))
            part_out[p] = lax.dot_general(
                weights.astype(jnp.bfloat16),
                keys[0:LATENT],
                (((1,), (1,)), ((), ())),
                preferred_element_type=jnp.float32,
            )
        return carry

    lax.fori_loop(0, (count + unroll - 1) // unroll, some_pairs, jnp.int32(0))

    def merge(slot, carry):
        q = queries[pl.ds(pl.multiple_of(slot * rows, 16), rows), :]
        scores = (
            lax.dot_general(q, fresh[...], (((1,), (1,)), ((), ())), preferred_element_type=jnp.float32) * factor
        )
        row_id = lax.broadcasted_iota(jnp.int32, scores.shape, 0)
        col_id = lax.broadcasted_iota(jnp.int32, scores.shape, 1)
        first_col = (slot // per_pair) * fresh_rows + (slot % per_pair) * steps
        scores = jnp.where(
            (col_id >= first_col) & (col_id <= first_col + (row_id & (steps - 1))), scores, NEG
        )
        top = jnp.max(scores, axis=1, keepdims=True)
        first = first_pair[slot]
        last = first_pair[slot + 1] - 1
        tops = []
        for k in range(spans):
            own = part_max[jnp.minimum(first + k, last)][:, 0:1]
            own = jnp.where(first + k <= last, own, 2 * NEG)
            tops.append(own)
        highest = functools.reduce(jnp.maximum, tops, top)
        weights = jnp.exp2(scores - highest)
        norm = jnp.sum(weights, axis=1, keepdims=True)
        out = jnp.dot(weights.astype(jnp.bfloat16), fresh[:, 0:LATENT], preferred_element_type=jnp.float32)
        for k in range(spans):
            at = jnp.minimum(first + k, last)
            share = jnp.exp2(tops[k] - highest)
            norm = norm + share * part_sum[at][:, 0:1]
            out = out + share * part_out[at]
        latent[pl.ds(pl.multiple_of(slot * rows, 16), rows), :] = (out / norm).astype(jnp.bfloat16)
        return carry

    lax.fori_loop(0, slots, merge, jnp.int32(0))

    def project(i, carry):
        tiles = [
            latent[pl.ds(pl.multiple_of(slot * rows + i * 16, 16), 16), :].astype(jnp.float32)
            for slot in range(slots)
        ]
        count_rows = slots * steps
        vdim = value_up.shape[2]
        for u in range(0, group, 2):
            head = i * group + u
            left = jnp.concatenate(
                [tile[v * steps : (v + 1) * steps] for v in (u, u + 1) for tile in tiles], axis=0
            ).astype(jnp.bfloat16)
            right = jnp.concatenate([value_up[head], value_up[head + 1]], axis=1)
            res = jnp.dot(left, right, preferred_element_type=jnp.float32)
            both = jnp.concatenate([res[:count_rows, :vdim], res[count_rows:, vdim:]], axis=1)
            out_ref[:, pl.ds(pl.multiple_of(head * vdim, vdim), 2 * vdim)] = both.astype(jnp.bfloat16)
        return carry

    lax.fori_loop(0, heads // group, project, jnp.int32(0))


def place_kernel(sizes, relative, me_ref, decode_ref, out_ref, owner_count, place):
    sources, per_pair, steps, requests = sizes
    me = me_ref[0]
    rows = sources * requests
    shift = requests.bit_length() - 1

    def one_source(s, carry):
        for o in range(sources):
            owner_count[o] = jnp.int32(0)
        for r in range(requests):
            row = decode_ref[s * requests + r]
            owner = row >> shift
            at = owner_count[owner]
            owner_count[owner] = at + 1
            if relative:
                e = owner ^ s
                at_row = (e >> 1) * (2 * sources * per_pair) + (me ^ s) * (2 * per_pair) + (e & 1) * per_pair + at
            else:
                at_row = s * requests + owner * per_pair + at
            place[row] = at_row * steps
        return carry

    lax.fori_loop(0, sources, one_source, jnp.int32(0))
    narrow = (rows, LANES)
    row_id = lax.broadcasted_iota(jnp.int32, narrow, 0)

    def put(b, wanted):
        return jnp.where(row_id == b, place[b], wanted)

    wanted = lax.fori_loop(0, rows, put, jnp.zeros(narrow, jnp.int32), unroll=8)[:, 0:1]
    col_id = lax.broadcasted_iota(jnp.int32, (rows, rows * steps), 1)
    for t in range(steps):
        out_ref[t] = jnp.where(col_id == wanted + t, 1.0, 0.0).astype(jnp.bfloat16)


def order_kernel(pieces, z_ref, pick_ref, *rest):
    out_ref, x = rest[2 * pieces], rest[2 * pieces + 1]
    if pieces == 0:
        x_ref, out_ref = rest
        for t in range(pick_ref.shape[0]):
            out_ref[t] = jnp.dot(pick_ref[t], x_ref[...], preferred_element_type=jnp.float32).astype(jnp.bfloat16)
        return
    inner = (z_ref[0] == 1) | (z_ref[0] == 2)
    rows = x.shape[0] // pieces

    @pl.when(inner)
    def _():
        for i in range(pieces):
            x[i * rows : (i + 1) * rows, :] = rest[2 * i][...]

    @pl.when(jnp.logical_not(inner))
    def _():
        for i in range(pieces):
            x[i * rows : (i + 1) * rows, :] = rest[2 * i + 1][...]

    for t in range(pick_ref.shape[0]):
        out_ref[t] = jnp.dot(pick_ref[t], x[...], preferred_element_type=jnp.float32).astype(jnp.bfloat16)


def project_kernel(pieces, *rest):
    parts, weight, outs, x = rest[:4], rest[4], rest[5 : 5 + pieces], rest[5 + pieces]
    rows = parts[0].shape[0]
    for q in range(4):
        x[q * rows : (q + 1) * rows, :] = parts[q][...]
    out_rows = outs[0].shape[0]

    def tile(n, carry):
        cols = pl.ds(pl.multiple_of(n * BLOCK, BLOCK), BLOCK)
        res = jnp.dot(x[...], weight[:, cols], preferred_element_type=jnp.float32).astype(jnp.bfloat16)
        for i in range(pieces):
            outs[i][:, cols] = res[i * out_rows : (i + 1) * out_rows]
        return carry

    lax.fori_loop(0, weight.shape[1] // BLOCK, tile, jnp.int32(0))


def smem():
    return pl.BlockSpec(memory_space=pltpu.SMEM)


def vmem():
    return pl.BlockSpec(memory_space=pltpu.VMEM)


def limit(mib):
    return pltpu.CompilerParams(vmem_limit_bytes=mib * 1024 * 1024)


def cost(microseconds):
    return pl.CostEstimate(
        flops=int(microseconds * 1.0e9), bytes_accessed=int(microseconds * 3.0e6), transcendentals=0
    )


def flip(x, axis, distance):
    size = lax.axis_size(axis)
    return lax.ppermute(x, axis, [(i, i ^ distance) for i in range(size)])


def line_sum(piece):
    inward = lax.ppermute(piece, "head", [(0, 1), (3, 2)])
    pair = (piece.astype(jnp.float32) + inward.astype(jnp.float32)).astype(jnp.bfloat16)
    crossed = lax.ppermute(pair, "head", [(1, 2), (2, 1)])
    whole = (pair.astype(jnp.float32) + crossed.astype(jnp.float32)).astype(jnp.bfloat16)
    outward = lax.ppermute(whole, "head", [(1, 0), (2, 3)])
    return whole, outward


def local(latent_cache, lengths, decode_rows, q_nope, q_rope, new_latent, key_up, value_up, out_proj):
    sources = lax.axis_size("seq")
    head_devices = lax.axis_size("head")
    relative = sources == 4 and head_devices == 4
    requests = lengths.shape[1]
    per_pair = requests // sources
    tokens, width = latent_cache.shape
    steps, _, heads, nope = q_nope.shape
    scale = (nope + q_rope.shape[3]) ** (-0.5)
    fresh_rows = -(-per_pair * steps // 16) * 16
    pair_rows = per_pair * steps
    rows = heads * steps
    columns = out_proj.shape[1]
    packed_rows = heads * pair_rows + per_pair * rows // 2 + -(-width // LANES) * fresh_rows
    sizes = (sources, per_pair, steps, heads, requests, fresh_rows)
    me = lax.axis_index("seq").astype(jnp.int32).reshape(1)
    z = lax.axis_index("head").astype(jnp.int32).reshape(1)
    cache = latent_cache.T

    outs, each = (sources, 1) if relative else (1, sources)
    packed = pl.pallas_call(
        functools.partial(pack_kernel, sizes, relative),
        out_shape=[jax.ShapeDtypeStruct((each, packed_rows, LANES), jnp.bfloat16)] * outs,
        in_specs=[smem(), smem(), vmem(), vmem(), vmem()],
        out_specs=[vmem()] * outs,
        scratch_shapes=[
            pltpu.SMEM((sources * (per_pair + 1),), jnp.int32),
            pltpu.VMEM((heads * pair_rows, LANES), jnp.float32),
            pltpu.VMEM((rows, LANES), jnp.float32),
        ],
        compiler_params=limit(12),
        cost_estimate=cost(3),
        name="pack_queries",
    )(me, decode_rows, q_nope, q_rope, new_latent)

    def attend(received, base):
        here = sum(part.shape[0] for part in received)
        slots = here * per_pair
        pairs = slots * (512 // BLOCK + 1) + 1
        return pl.pallas_call(
            functools.partial(attend_kernel, sizes, scale, relative, base, len(received)),
            out_shape=jax.ShapeDtypeStruct((slots * steps, heads * value_up.shape[2]), jnp.bfloat16),
            in_specs=[smem(), smem(), smem()] + [vmem()] * (len(received) + 3),
            out_specs=vmem(),
            scratch_shapes=[
                pltpu.SMEM((slots + 1,), jnp.int32),
                pltpu.SMEM((slots + 1,), jnp.int32),
                pltpu.SMEM((sources,), jnp.int32),
                pltpu.SMEM((pairs,), jnp.int32),
                pltpu.SMEM((pairs,), jnp.int32),
                pltpu.SMEM((slots + 1,), jnp.int32),
                pltpu.VMEM((slots * rows, width), jnp.bfloat16),
                pltpu.VMEM((here * fresh_rows, width), jnp.bfloat16),
                pltpu.VMEM((pairs, rows, LATENT), jnp.float32),
                pltpu.VMEM((pairs, rows, LANES), jnp.float32),
                pltpu.VMEM((pairs, rows, LANES), jnp.float32),
                pltpu.VMEM((slots * rows, LATENT), jnp.bfloat16),
            ],
            compiler_params=limit(32),
            cost_estimate=cost(14),
            name="attend",
        )(me, decode_rows, lengths, *received, cache, key_up, value_up)

    pick = pl.pallas_call(
        functools.partial(place_kernel, (sources, per_pair, steps, requests), relative),
        out_shape=jax.ShapeDtypeStruct((steps, sources * requests, steps * sources * requests), jnp.bfloat16),
        in_specs=[smem(), smem()],
        out_specs=vmem(),
        scratch_shapes=[pltpu.SMEM((sources,), jnp.int32), pltpu.SMEM((sources * requests,), jnp.int32)],
        compiler_params=limit(12),
        cost_estimate=cost(2),
        name="place_rows",
    )(me, decode_rows)

    def order(pieces, arrays, scratch):
        return pl.pallas_call(
            functools.partial(order_kernel, pieces),
            out_shape=jax.ShapeDtypeStruct((steps, sources * requests, columns), jnp.bfloat16),
            in_specs=[smem()] + [vmem()] * (1 + len(arrays)),
            out_specs=vmem(),
            scratch_shapes=scratch,
            compiler_params=limit(16),
            cost_estimate=cost(2),
            name="order_rows",
        )(z, pick, *arrays)

    if not relative:
        received = lax.all_to_all(packed[0], "seq", split_axis=0, concat_axis=0, tiled=True)
        every_row = lax.all_gather(attend([received], 0), "seq", axis=0, tiled=True)
        partial_value = jnp.dot(every_row, out_proj, preferred_element_type=jnp.float32).astype(jnp.bfloat16)
        shares = lax.all_to_all(partial_value, "head", split_axis=0, concat_axis=0, tiled=True)
        shares = shares.reshape(head_devices, -1, columns)
        summed = jnp.sum(shares.astype(jnp.float32), axis=0).astype(jnp.bfloat16)
        return order(0, [lax.all_gather(summed, "head", axis=0, tiled=True)], [])

    pieces = 2

    def project(parts):
        part_rows = parts[0].shape[0]
        return pl.pallas_call(
            functools.partial(project_kernel, pieces),
            out_shape=[jax.ShapeDtypeStruct((4 * part_rows // pieces, columns), jnp.bfloat16)] * pieces,
            in_specs=[vmem()] * 5,
            out_specs=[vmem()] * pieces,
            scratch_shapes=[pltpu.VMEM((4 * part_rows, out_proj.shape[0]), jnp.bfloat16)],
            compiler_params=limit(24),
            cost_estimate=cost(6),
            name="project_out",
        )(*parts, out_proj)

    received = [packed[0]] + [flip(packed[k], "seq", k) for k in range(1, 4)]
    near = attend(received[:2], 0)
    near_parts = [near] + [flip(near, "seq", k) for k in range(1, 4)]
    far = attend(received[2:], 2)
    far_across = flip(far, "seq", 2)
    far_parts = [far, flip(far, "seq", 1), far_across, flip(far_across, "seq", 1)]
    sums = [line_sum(piece) for piece in project(near_parts)]
    sums += [line_sum(piece) for piece in project(far_parts)]
    arrays = [array for pair in sums for array in pair]
    return order(len(sums), arrays, [pltpu.VMEM((steps * sources * requests, columns), jnp.bfloat16)])


def solution(mesh):
    return jax.shard_map(
        local,
        mesh=mesh,
        in_specs=(
            P(("groups", "seq"), None),
            P("groups", None),
            P("groups"),
            P(None, ("groups", "seq"), "head", None),
            P(None, ("groups", "seq"), "head", None),
            P(None, ("groups", "seq"), None),
            P("head", None, None),
            P("head", None, None),
            P("head", "seq"),
        ),
        out_specs=P(None, "groups", "seq"),
        check_vma=False,
    )
```

```python
import functools

import jax
import jax.numpy as jnp
from jax import lax
from jax.experimental import pallas as pl
from jax.experimental.pallas import tpu as pltpu
from jax.sharding import PartitionSpec as P

LATENT = 512
BLOCK = 256
LANES = 128
LOG2E = 1.4426950408889634
NEG = -1e30


def own_slots(decode_ref, slot_ref, me, sources, requests, per_pair):
    shift = requests.bit_length() - 1

    def one_source(s, carry):
        count = jnp.int32(0)
        for r in range(requests):
            row = decode_ref[s * requests + r]
            slot_ref[s * (per_pair + 1) + jnp.minimum(count, per_pair)] = row & (requests - 1)
            count = count + jnp.where((row >> shift) == me, 1, 0).astype(jnp.int32)
        return carry

    lax.fori_loop(0, sources, one_source, jnp.int32(0))


def pack_kernel(sizes, relative, me_ref, decode_ref, nope_ref, rope_ref, fresh_ref, after_ref, *rest):
    sources, per_pair, steps, heads, requests, fresh_rows = sizes
    out_refs, (slots, wide) = rest[:-2], rest[-2:]
    me = me_ref[0]
    rows = heads * steps
    half = rows // 2
    rope_base = per_pair * rows
    fresh_base = rope_base + per_pair * half
    own_slots(decode_ref, slots, me, sources, requests, per_pair)

    def one_dest(s, out_ref, e):
        for j in range(per_pair):
            row = slots[s * (per_pair + 1) + j]
            for t in range(steps):
                wide[2 * j, pl.ds(t, heads, stride=steps), :] = nope_ref[t, row].astype(jnp.float32)
                wide[2 * j + 1, pl.ds(t, heads, stride=steps), :] = jnp.concatenate(
                    [rope_ref[t, row].astype(jnp.float32)] * 2, axis=1
                )
        for j in range(per_pair):
            out_ref[e, j * rows : (j + 1) * rows, :] = wide[2 * j].astype(jnp.bfloat16)
            low = lax.broadcasted_iota(jnp.int32, (half, LANES), 1) < LANES // 2
            packed = jnp.where(low, wide[2 * j + 1, 0:half, :], wide[2 * j + 1, half : 2 * half, :])
            out_ref[e, rope_base + j * half : rope_base + (j + 1) * half, :] = packed.astype(jnp.bfloat16)

    if relative:
        dests = [me ^ k for k in range(sources)]
        for k in range(sources):
            one_dest(dests[k], out_refs[k], 0)
    else:
        dests = list(range(sources))

        def step(s, carry):
            one_dest(s, out_refs[0], s)
            return carry

        lax.fori_loop(0, sources, step, jnp.int32(0))
    shape = (sources * fresh_rows, steps * requests)
    row_id = lax.broadcasted_iota(jnp.int32, shape, 0)
    col_id = lax.broadcasted_iota(jnp.int32, shape, 1)
    wanted = jnp.full(shape, -1, jnp.int32)
    for k in range(sources):
        for j in range(per_pair):
            first = k * fresh_rows + j * steps
            here = (row_id >= first) & (row_id < first + steps)
            wanted = jnp.where(here, (row_id - first) * requests + slots[dests[k] * (per_pair + 1) + j], wanted)
    pick = jnp.where(col_id == wanted, 1.0, 0.0).astype(jnp.bfloat16)
    width = fresh_ref.shape[2]
    source_rows = jnp.concatenate([fresh_ref[t] for t in range(steps)], axis=0)
    picked = jnp.dot(pick, source_rows, preferred_element_type=jnp.float32).astype(jnp.bfloat16)
    for k in range(sources):
        for c in range(-(-width // LANES)):
            piece = picked[k * fresh_rows : (k + 1) * fresh_rows, c * LANES : min((c + 1) * LANES, width)]
            if piece.shape[1] < LANES:
                piece = jnp.concatenate([piece] * (LANES // piece.shape[1]), axis=1)
            first = fresh_base + c * fresh_rows
            if relative:
                out_refs[k][0, first : first + fresh_rows, :] = piece
            else:
                out_refs[0][k, first : first + fresh_rows, :] = piece


def attend_kernel(sizes, scale, relative, base, recv_count, me_ref, decode_ref, length_ref, *rest):
    sources, per_pair, steps, heads, requests, fresh_rows = sizes
    recv_refs = rest[:recv_count]
    (
        cache, key_up, value_up, out_ref,
        slot_offset, slot_length, owner_count, pair_slot, pair_start,
        queries, fresh, acc, run_max, run_sum, latent,
    ) = rest[recv_count:]
    owners = [(ref, e) for ref in recv_refs for e in range(ref.shape[0])]
    here = len(owners)
    slots = here * per_pair
    width, tokens = cache.shape
    rows = heads * steps
    half = rows // 2
    rope_base = per_pair * rows
    fresh_base = rope_base + per_pair * half
    group = 16 // steps
    shift = requests.bit_length() - 1
    factor = scale * LOG2E

    for e in range(here):
        ref, at = owners[e]
        for c in range(-(-width // LANES)):
            lanes = min(LANES, width - c * LANES)
            first = fresh_base + c * fresh_rows
            fresh[e * fresh_rows : (e + 1) * fresh_rows, c * LANES : c * LANES + lanes] = ref[
                at, first : first + fresh_rows, 0:lanes
            ]
        for j in range(per_pair):
            slot = e * per_pair + j
            first = rope_base + j * half
            piece = ref[at, first : first + half, :]
            queries[slot * rows : slot * rows + half, LATENT:width] = piece[:, 0 : width - LATENT]
            queries[slot * rows + half : (slot + 1) * rows, LATENT:width] = piece[:, LANES - (width - LATENT) :]

    inner_head = lax.broadcasted_iota(jnp.int32, (slots * 16, LANES), 0) // steps % group
    own_head = [jnp.where(inner_head == u, 1.0, 0.0).astype(jnp.bfloat16) for u in range(group)]
    for i in range(heads // group):
        tall = jnp.concatenate(
            [ref[at, j * rows + i * 16 : j * rows + (i + 1) * 16, :] for ref, at in owners for j in range(per_pair)],
            axis=0,
        )
        left = jnp.concatenate([tall * own_head[u] for u in range(group)], axis=1)
        right = jnp.concatenate([key_up[i * group + u] for u in range(group)], axis=0)
        res = jnp.dot(left, right, preferred_element_type=jnp.float32).astype(jnp.bfloat16)
        for slot in range(slots):
            queries[slot * rows + i * 16 : slot * rows + (i + 1) * 16, 0:LATENT] = res[slot * 16 : (slot + 1) * 16]

    me = me_ref[0]
    for o in range(sources):
        owner_count[o] = jnp.int32(0)
    total = jnp.int32(0)
    for r in range(requests):
        owner = decode_ref[me * requests + r] >> shift
        at = owner_count[owner]
        owner_count[owner] = at + 1
        e = (owner ^ me) - base if relative else owner
        slot = jnp.where((e >= 0) & (e < here), e * per_pair + at, slots)
        length = length_ref[me, r]
        slot_offset[slot] = total
        slot_length[slot] = length
        total = total + length
    count = jnp.int32(0)
    for slot in range(slots):
        start = slot_offset[slot] & ~(LANES - 1)
        end = slot_offset[slot] + slot_length[slot]
        for k in range(512 // BLOCK + 1):
            pair_slot[count] = jnp.int32(slot)
            pair_start[count] = start + k * BLOCK
            count = count + jnp.where(start + k * BLOCK < end, 1, 0).astype(jnp.int32)

    fresh_scores = (
        lax.dot_general(queries[...], fresh[...], (((1,), (1,)), ((), ())), preferred_element_type=jnp.float32) * factor
    )
    row_id = lax.broadcasted_iota(jnp.int32, (rows, here * fresh_rows), 0)
    col_id = lax.broadcasted_iota(jnp.int32, (rows, here * fresh_rows), 1)
    behind = row_id & (steps - 1)
    fresh_weights = []
    for slot in range(slots):
        first = (slot // per_pair) * fresh_rows + (slot % per_pair) * steps
        seen = (col_id >= first) & (col_id <= first + behind)
        scores = jnp.where(seen, fresh_scores[slot * rows : (slot + 1) * rows], NEG)
        top = jnp.max(scores, axis=1, keepdims=True)
        weights = jnp.exp2(scores - top)
        run_max[slot] = jnp.broadcast_to(top, (rows, LANES))
        run_sum[slot] = jnp.broadcast_to(jnp.sum(weights, axis=1, keepdims=True), (rows, LANES))
        fresh_weights.append(weights.astype(jnp.bfloat16))
    for slot in range(slots):
        acc[slot] = jnp.dot(fresh_weights[slot], fresh[:, 0:LATENT], preferred_element_type=jnp.float32)

    unroll = 4

    def some_pairs(i, carry):
        for u in range(unroll):
            p = i * unroll + u
            slot = pair_slot[jnp.minimum(p, count - 1)]
            start = pair_start[jnp.minimum(p, count - 1)]
            read = jnp.minimum(start, tokens - BLOCK)
            low = jnp.maximum(slot_offset[slot], start) - read
            high = jnp.minimum(slot_offset[slot] + slot_length[slot], start + BLOCK) - read
            high = jnp.where(p < count, high, low)
            q = queries[pl.ds(pl.multiple_of(slot * rows, 16), rows), :]
            keys = cache[:, pl.ds(pl.multiple_of(read, LANES), BLOCK)]
            scores = jnp.dot(q, keys, preferred_element_type=jnp.float32) * factor
            token = lax.broadcasted_iota(jnp.int32, scores.shape, 1)
            scores = jnp.where((token >= low) & (token < high), scores, NEG)
            top = jnp.max(scores, axis=1, keepdims=True)
            weights = jnp.exp2(scores - top)
            part_sum = jnp.broadcast_to(jnp.sum(weights, axis=1, keepdims=True), (rows, LANES))
            part = lax.dot_general(
                weights.astype(jnp.bfloat16),
                keys[0:LATENT],
                (((1,), (1,)), ((), ())),
                preferred_element_type=jnp.float32,
            )
            part_max = jnp.broadcast_to(top, (rows, LANES))
            old_max = run_max[slot]
            new_max = jnp.maximum(old_max, part_max)
            keep = jnp.exp2(old_max - new_max)
            add = jnp.exp2(part_max - new_max)
            run_max[slot] = new_max
            run_sum[slot] = run_sum[slot] * keep + part_sum * add
            for c in range(LATENT // LANES):
                cols = slice(c * LANES, (c + 1) * LANES)
                acc[slot, :, cols] = acc[slot, :, cols] * keep + part[:, cols] * add
        return carry

    lax.fori_loop(0, (count + unroll - 1) // unroll, some_pairs, jnp.int32(0))

    for slot in range(slots):
        inverse = 1.0 / run_sum[slot]
        for c in range(LATENT // LANES):
            cols = slice(c * LANES, (c + 1) * LANES)
            latent[slot * rows : (slot + 1) * rows, cols] = (acc[slot, :, cols] * inverse).astype(jnp.bfloat16)
    vdim = value_up.shape[2]
    for i in range(heads // group):
        left = jnp.concatenate(
            [latent[slot * rows + i * 16 : slot * rows + (i + 1) * 16, :] for slot in range(slots)], axis=0
        )
        right = jnp.concatenate([value_up[i * group + u] for u in range(group)], axis=1)
        res = jnp.dot(left, right, preferred_element_type=jnp.float32)
        for u in range(group):
            own = jnp.concatenate(
                [
                    res[slot * 16 + u * steps : slot * 16 + (u + 1) * steps, u * vdim : (u + 1) * vdim]
                    for slot in range(slots)
                ],
                axis=0,
            )
            head = i * group + u
            out_ref[:, head * vdim : (head + 1) * vdim] = own.astype(jnp.bfloat16)


def place_kernel(sizes, relative, me_ref, decode_ref, out_ref, owner_count, place):
    sources, per_pair, steps, requests = sizes
    me = me_ref[0]
    rows = sources * requests
    shift = requests.bit_length() - 1

    def one_source(s, carry):
        for o in range(sources):
            owner_count[o] = jnp.int32(0)
        for r in range(requests):
            row = decode_ref[s * requests + r]
            owner = row >> shift
            at = owner_count[owner]
            owner_count[owner] = at + 1
            if relative:
                e = owner ^ s
                at_row = (e >> 1) * (2 * sources * per_pair) + (me ^ s) * (2 * per_pair) + (e & 1) * per_pair + at
            else:
                at_row = s * requests + owner * per_pair + at
            place[row] = at_row * steps
        return carry

    lax.fori_loop(0, sources, one_source, jnp.int32(0))
    narrow = (rows, LANES)
    row_id = lax.broadcasted_iota(jnp.int32, narrow, 0)

    def put(b, wanted):
        return jnp.where(row_id == b, place[b], wanted)

    wanted = lax.fori_loop(0, rows, put, jnp.zeros(narrow, jnp.int32), unroll=8)[:, 0:1]
    col_id = lax.broadcasted_iota(jnp.int32, (rows, rows * steps), 1)
    for t in range(steps):
        out_ref[t] = jnp.where(col_id == wanted + t, 1.0, 0.0).astype(jnp.bfloat16)


def order_kernel(pieces, z_ref, pick_ref, *rest):
    out_ref, x = rest[2 * pieces], rest[2 * pieces + 1]
    if pieces == 0:
        x_ref, out_ref = rest
        for t in range(pick_ref.shape[0]):
            out_ref[t] = jnp.dot(pick_ref[t], x_ref[...], preferred_element_type=jnp.float32).astype(jnp.bfloat16)
        return
    inner = (z_ref[0] == 1) | (z_ref[0] == 2)
    rows = x.shape[0] // pieces

    @pl.when(inner)
    def _():
        for i in range(pieces):
            x[i * rows : (i + 1) * rows, :] = rest[2 * i][...]

    @pl.when(jnp.logical_not(inner))
    def _():
        for i in range(pieces):
            x[i * rows : (i + 1) * rows, :] = rest[2 * i + 1][...]

    for t in range(pick_ref.shape[0]):
        out_ref[t] = jnp.dot(pick_ref[t], x[...], preferred_element_type=jnp.float32).astype(jnp.bfloat16)


def project_kernel(pieces, *rest):
    parts, weight, outs, x = rest[:4], rest[4], rest[5 : 5 + pieces], rest[5 + pieces]
    rows = parts[0].shape[0]
    for q in range(4):
        x[q * rows : (q + 1) * rows, :] = parts[q][...]
    out_rows = outs[0].shape[0]

    def tile(n, carry):
        cols = pl.ds(pl.multiple_of(n * BLOCK, BLOCK), BLOCK)
        res = jnp.dot(x[...], weight[:, cols], preferred_element_type=jnp.float32).astype(jnp.bfloat16)
        for i in range(pieces):
            outs[i][:, cols] = res[i * out_rows : (i + 1) * out_rows]
        return carry

    lax.fori_loop(0, weight.shape[1] // BLOCK, tile, jnp.int32(0))


def smem():
    return pl.BlockSpec(memory_space=pltpu.SMEM)


def vmem():
    return pl.BlockSpec(memory_space=pltpu.VMEM)


def anywhere():
    return pl.BlockSpec(memory_space=pl.ANY)


def limit(mib):
    return pltpu.CompilerParams(vmem_limit_bytes=mib * 1024 * 1024)


def cost(microseconds):
    return pl.CostEstimate(
        flops=int(microseconds * 1.0e9), bytes_accessed=int(microseconds * 3.0e6), transcendentals=0
    )


def flip(x, axis, distance):
    size = lax.axis_size(axis)
    return lax.ppermute(x, axis, [(i, i ^ distance) for i in range(size)])


def add(x, y):
    return (x.astype(jnp.float32) + y.astype(jnp.float32)).astype(jnp.bfloat16)


def inwards(piece):
    return lax.ppermute(piece, "head", [(0, 1), (3, 2)])


def across_middle(pair):
    return lax.ppermute(pair, "head", [(1, 2), (2, 1)])


def outwards(whole):
    return lax.ppermute(whole, "head", [(1, 0), (2, 3)])


def local(latent_cache, lengths, decode_rows, q_nope, q_rope, new_latent, key_up, value_up, out_proj):
    sources = lax.axis_size("seq")
    head_devices = lax.axis_size("head")
    relative = sources == 4 and head_devices == 4
    requests = lengths.shape[1]
    per_pair = requests // sources
    tokens, width = latent_cache.shape
    steps, _, heads, nope = q_nope.shape
    scale = (nope + q_rope.shape[3]) ** (-0.5)
    fresh_rows = -(-per_pair * steps // 16) * 16
    rows = heads * steps
    columns = out_proj.shape[1]
    packed_rows = per_pair * rows + per_pair * rows // 2 + -(-width // LANES) * fresh_rows
    sizes = (sources, per_pair, steps, heads, requests, fresh_rows)
    me = lax.axis_index("seq").astype(jnp.int32).reshape(1)
    z = lax.axis_index("head").astype(jnp.int32).reshape(1)
    cache = latent_cache.T

    pick = pl.pallas_call(
        functools.partial(place_kernel, (sources, per_pair, steps, requests), relative),
        out_shape=jax.ShapeDtypeStruct((steps, sources * requests, steps * sources * requests), jnp.bfloat16),
        in_specs=[smem(), smem()],
        out_specs=vmem(),
        scratch_shapes=[pltpu.SMEM((sources,), jnp.int32), pltpu.SMEM((sources * requests,), jnp.int32)],
        compiler_params=limit(12),
        cost_estimate=cost(2),
        name="place_rows",
    )(me, decode_rows)

    outs, each = (sources, 1) if relative else (1, sources)
    packed = pl.pallas_call(
        functools.partial(pack_kernel, sizes, relative),
        out_shape=[jax.ShapeDtypeStruct((each, packed_rows, LANES), jnp.bfloat16)] * outs,
        in_specs=[smem(), smem(), vmem(), vmem(), vmem(), anywhere()],
        out_specs=[vmem()] * outs,
        scratch_shapes=[
            pltpu.SMEM((sources * (per_pair + 1),), jnp.int32),
            pltpu.VMEM((2 * per_pair, rows, LANES), jnp.float32),
        ],
        compiler_params=limit(8),
        cost_estimate=cost(6),
        name="pack_queries",
    )(me, decode_rows, q_nope, q_rope, new_latent, pick)

    def attend(received, base):
        here = sum(part.shape[0] for part in received)
        slots = here * per_pair
        pairs = slots * (512 // BLOCK + 1) + 1
        return pl.pallas_call(
            functools.partial(attend_kernel, sizes, scale, relative, base, len(received)),
            out_shape=jax.ShapeDtypeStruct((slots * steps, heads * value_up.shape[2]), jnp.bfloat16),
            in_specs=[smem(), smem(), smem()] + [vmem()] * (len(received) + 3),
            out_specs=vmem(),
            scratch_shapes=[
                pltpu.SMEM((slots + 1,), jnp.int32),
                pltpu.SMEM((slots + 1,), jnp.int32),
                pltpu.SMEM((sources,), jnp.int32),
                pltpu.SMEM((pairs,), jnp.int32),
                pltpu.SMEM((pairs,), jnp.int32),
                pltpu.VMEM((slots * rows, width), jnp.bfloat16),
                pltpu.VMEM((here * fresh_rows, width), jnp.bfloat16),
                pltpu.VMEM((slots, rows, LATENT), jnp.float32),
                pltpu.VMEM((slots, rows, LANES), jnp.float32),
                pltpu.VMEM((slots, rows, LANES), jnp.float32),
                pltpu.VMEM((slots * rows, LATENT), jnp.bfloat16),
            ],
            compiler_params=limit(18),
            cost_estimate=cost(8),
            name="attend",
        )(me, decode_rows, lengths, *received, cache, key_up, value_up)

    def order(pieces, arrays, scratch):
        return pl.pallas_call(
            functools.partial(order_kernel, pieces),
            out_shape=jax.ShapeDtypeStruct((steps, sources * requests, columns), jnp.bfloat16),
            in_specs=[smem()] + [vmem()] * (1 + len(arrays)),
            out_specs=vmem(),
            scratch_shapes=scratch,
            compiler_params=limit(16),
            cost_estimate=cost(2),
            name="order_rows",
        )(z, pick, *arrays)

    if not relative:
        received = lax.all_to_all(packed[0], "seq", split_axis=0, concat_axis=0, tiled=True)
        every_row = lax.all_gather(attend([received], 0), "seq", axis=0, tiled=True)
        partial_value = jnp.dot(every_row, out_proj, preferred_element_type=jnp.float32).astype(jnp.bfloat16)
        shares = lax.all_to_all(partial_value, "head", split_axis=0, concat_axis=0, tiled=True)
        shares = shares.reshape(head_devices, -1, columns)
        summed = jnp.sum(shares.astype(jnp.float32), axis=0).astype(jnp.bfloat16)
        return order(0, [lax.all_gather(summed, "head", axis=0, tiled=True)], [])

    pieces = 2

    def project(parts):
        part_rows = parts[0].shape[0]
        return pl.pallas_call(
            functools.partial(project_kernel, pieces),
            out_shape=[jax.ShapeDtypeStruct((4 * part_rows // pieces, columns), jnp.bfloat16)] * pieces,
            in_specs=[vmem()] * 5,
            out_specs=[vmem()] * pieces,
            scratch_shapes=[pltpu.VMEM((4 * part_rows, out_proj.shape[0]), jnp.bfloat16)],
            compiler_params=limit(24),
            cost_estimate=cost(6),
            name="project_out",
        )(*parts, out_proj)

    received = [packed[0]] + [flip(packed[k], "seq", k) for k in range(1, 4)]
    near_rows = attend(received[:2], 0)
    near_across = flip(near_rows, "seq", 2)
    far_rows = attend(received[2:], 2)
    near_across, far_rows = lax.optimization_barrier((near_across, far_rows))
    near = [near_rows, flip(near_rows, "seq", 1), near_across, flip(near_across, "seq", 1)]
    far_across = flip(far_rows, "seq", 2)
    far = [far_rows, flip(far_rows, "seq", 1), far_across, flip(far_across, "seq", 1)]
    first, second = project(near)
    first_in, second_in = inwards(first), inwards(second)
    first_pair = add(first, first_in)
    first_cross = across_middle(first_pair)
    third, fourth = project(far)
    second_in, first_cross, third, fourth = lax.optimization_barrier((second_in, first_cross, third, fourth))
    second_pair = add(second, second_in)
    second_cross = across_middle(second_pair)
    third_in, fourth_in = inwards(third), inwards(fourth)
    first_whole = add(first_pair, first_cross)
    second_whole = add(second_pair, second_cross)
    third_pair, fourth_pair = add(third, third_in), add(fourth, fourth_in)
    third_whole = add(third_pair, across_middle(third_pair))
    fourth_whole = add(fourth_pair, across_middle(fourth_pair))
    sums = [(whole, outwards(whole)) for whole in (first_whole, second_whole, third_whole, fourth_whole)]
    arrays = [array for both in sums for array in both]
    return order(len(sums), arrays, [pltpu.VMEM((steps * sources * requests, columns), jnp.bfloat16)])


def solution(mesh):
    return jax.shard_map(
        local,
        mesh=mesh,
        in_specs=(
            P(("groups", "seq"), None),
            P("groups", None),
            P("groups"),
            P(None, ("groups", "seq"), "head", None),
            P(None, ("groups", "seq"), "head", None),
            P(None, ("groups", "seq"), None),
            P("head", None, None),
            P("head", None, None),
            P("head", "seq"),
        ),
        out_specs=P(None, "groups", "seq"),
        check_vma=False,
    )
```

```python
import functools

import jax
import jax.numpy as jnp
from jax import lax
from jax.experimental import pallas as pl
from jax.experimental.pallas import tpu as pltpu
from jax.sharding import PartitionSpec as P

LATENT = 512
BLOCK = 256
LANES = 128
LOG2E = 1.4426950408889634
NEG = -1e30


def own_slots(decode_ref, slot_ref, me, sources, requests, per_pair):
    shift = requests.bit_length() - 1

    def one_source(s, carry):
        count = jnp.int32(0)
        for r in range(requests):
            row = decode_ref[s * requests + r]
            slot_ref[s * (per_pair + 1) + jnp.minimum(count, per_pair)] = row & (requests - 1)
            count = count + jnp.where((row >> shift) == me, 1, 0).astype(jnp.int32)
        return carry

    lax.fori_loop(0, sources, one_source, jnp.int32(0))


def pack_kernel(sizes, relative, me_ref, decode_ref, nope_ref, rope_ref, fresh_ref, after_ref, *rest):
    sources, per_pair, steps, heads, requests, fresh_rows = sizes
    out_refs, (slots, wide) = rest[:-2], rest[-2:]
    me = me_ref[0]
    rows = heads * steps
    half = rows // 2
    rope_base = per_pair * rows
    fresh_base = rope_base + per_pair * half
    own_slots(decode_ref, slots, me, sources, requests, per_pair)

    def one_dest(s, out_ref, e):
        for j in range(per_pair):
            row = slots[s * (per_pair + 1) + j]
            for t in range(steps):
                wide[2 * j, pl.ds(t, heads, stride=steps), :] = nope_ref[t, row].astype(jnp.float32)
                wide[2 * j + 1, pl.ds(t, heads, stride=steps), :] = jnp.concatenate(
                    [rope_ref[t, row].astype(jnp.float32)] * 2, axis=1
                )
        for j in range(per_pair):
            out_ref[e, j * rows : (j + 1) * rows, :] = wide[2 * j].astype(jnp.bfloat16)
            low = lax.broadcasted_iota(jnp.int32, (half, LANES), 1) < LANES // 2
            packed = jnp.where(low, wide[2 * j + 1, 0:half, :], wide[2 * j + 1, half : 2 * half, :])
            out_ref[e, rope_base + j * half : rope_base + (j + 1) * half, :] = packed.astype(jnp.bfloat16)

    if relative:
        dests = [me ^ k for k in range(sources)]
        for k in range(sources):
            one_dest(dests[k], out_refs[k], 0)
    else:
        dests = list(range(sources))

        def step(s, carry):
            one_dest(s, out_refs[0], s)
            return carry

        lax.fori_loop(0, sources, step, jnp.int32(0))
    shape = (sources * fresh_rows, steps * requests)
    row_id = lax.broadcasted_iota(jnp.int32, shape, 0)
    col_id = lax.broadcasted_iota(jnp.int32, shape, 1)
    wanted = jnp.full(shape, -1, jnp.int32)
    for k in range(sources):
        for j in range(per_pair):
            first = k * fresh_rows + j * steps
            here = (row_id >= first) & (row_id < first + steps)
            wanted = jnp.where(here, (row_id - first) * requests + slots[dests[k] * (per_pair + 1) + j], wanted)
    pick = jnp.where(col_id == wanted, 1.0, 0.0).astype(jnp.bfloat16)
    width = fresh_ref.shape[2]
    source_rows = jnp.concatenate([fresh_ref[t] for t in range(steps)], axis=0)
    picked = jnp.dot(pick, source_rows, preferred_element_type=jnp.float32).astype(jnp.bfloat16)
    for k in range(sources):
        for c in range(-(-width // LANES)):
            piece = picked[k * fresh_rows : (k + 1) * fresh_rows, c * LANES : min((c + 1) * LANES, width)]
            if piece.shape[1] < LANES:
                piece = jnp.concatenate([piece] * (LANES // piece.shape[1]), axis=1)
            first = fresh_base + c * fresh_rows
            if relative:
                out_refs[k][0, first : first + fresh_rows, :] = piece
            else:
                out_refs[0][k, first : first + fresh_rows, :] = piece


def attend_kernel(sizes, scale, relative, base, recv_count, me_ref, decode_ref, length_ref, *rest):
    sources, per_pair, steps, heads, requests, fresh_rows = sizes
    recv_refs = rest[:recv_count]
    (
        cache, key_up, value_up, out_ref,
        slot_offset, slot_length, owner_count, pair_slot, pair_start,
        queries, fresh, acc, run_max, run_sum, latent,
    ) = rest[recv_count:]
    owners = [(ref, e) for ref in recv_refs for e in range(ref.shape[0])]
    here = len(owners)
    slots = here * per_pair
    width, tokens = cache.shape
    rows = heads * steps
    half = rows // 2
    rope_base = per_pair * rows
    fresh_base = rope_base + per_pair * half
    group = 16 // steps
    shift = requests.bit_length() - 1
    factor = scale * LOG2E

    for e in range(here):
        ref, at = owners[e]
        for c in range(-(-width // LANES)):
            lanes = min(LANES, width - c * LANES)
            first = fresh_base + c * fresh_rows
            fresh[e * fresh_rows : (e + 1) * fresh_rows, c * LANES : c * LANES + lanes] = ref[
                at, first : first + fresh_rows, 0:lanes
            ]
        for j in range(per_pair):
            slot = e * per_pair + j
            first = rope_base + j * half
            piece = ref[at, first : first + half, :]
            queries[slot * rows : slot * rows + half, LATENT:width] = piece[:, 0 : width - LATENT]
            queries[slot * rows + half : (slot + 1) * rows, LATENT:width] = piece[:, LANES - (width - LATENT) :]

    inner_head = lax.broadcasted_iota(jnp.int32, (slots * 16, LANES), 0) // steps % group
    own_head = [jnp.where(inner_head == u, 1.0, 0.0).astype(jnp.bfloat16) for u in range(group)]
    for i in range(heads // group):
        tall = jnp.concatenate(
            [ref[at, j * rows + i * 16 : j * rows + (i + 1) * 16, :] for ref, at in owners for j in range(per_pair)],
            axis=0,
        )
        left = jnp.concatenate([tall * own_head[u] for u in range(group)], axis=1)
        right = jnp.concatenate([key_up[i * group + u] for u in range(group)], axis=0)
        res = jnp.dot(left, right, preferred_element_type=jnp.float32).astype(jnp.bfloat16)
        for slot in range(slots):
            queries[slot * rows + i * 16 : slot * rows + (i + 1) * 16, 0:LATENT] = res[slot * 16 : (slot + 1) * 16]

    me = me_ref[0]
    for o in range(sources):
        owner_count[o] = jnp.int32(0)
    total = jnp.int32(0)
    for r in range(requests):
        owner = decode_ref[me * requests + r] >> shift
        at = owner_count[owner]
        owner_count[owner] = at + 1
        e = (owner ^ me) - base if relative else owner
        slot = jnp.where((e >= 0) & (e < here), e * per_pair + at, slots)
        length = length_ref[me, r]
        slot_offset[slot] = total
        slot_length[slot] = length
        total = total + length
    count = jnp.int32(0)
    for slot in range(slots):
        start = slot_offset[slot] & ~(LANES - 1)
        end = slot_offset[slot] + slot_length[slot]
        for k in range(512 // BLOCK + 1):
            pair_slot[count] = jnp.int32(slot)
            pair_start[count] = start + k * BLOCK
            count = count + jnp.where(start + k * BLOCK < end, 1, 0).astype(jnp.int32)

    fresh_scores = (
        lax.dot_general(queries[...], fresh[...], (((1,), (1,)), ((), ())), preferred_element_type=jnp.float32) * factor
    )
    row_id = lax.broadcasted_iota(jnp.int32, (rows, here * fresh_rows), 0)
    col_id = lax.broadcasted_iota(jnp.int32, (rows, here * fresh_rows), 1)
    behind = row_id & (steps - 1)
    fresh_weights = []
    for slot in range(slots):
        first = (slot // per_pair) * fresh_rows + (slot % per_pair) * steps
        seen = (col_id >= first) & (col_id <= first + behind)
        scores = jnp.where(seen, fresh_scores[slot * rows : (slot + 1) * rows], NEG)
        top = jnp.max(scores, axis=1, keepdims=True)
        weights = jnp.exp2(scores - top)
        run_max[slot] = jnp.broadcast_to(top, (rows, LANES))
        run_sum[slot] = jnp.broadcast_to(jnp.sum(weights, axis=1, keepdims=True), (rows, LANES))
        fresh_weights.append(weights.astype(jnp.bfloat16))
    for slot in range(slots):
        acc[slot] = jnp.dot(fresh_weights[slot], fresh[:, 0:LATENT], preferred_element_type=jnp.float32)

    unroll = 4

    def some_pairs(i, carry):
        for u in range(unroll):
            p = i * unroll + u
            slot = pair_slot[jnp.minimum(p, count - 1)]
            start = pair_start[jnp.minimum(p, count - 1)]
            read = jnp.minimum(start, tokens - BLOCK)
            low = jnp.maximum(slot_offset[slot], start) - read
            high = jnp.minimum(slot_offset[slot] + slot_length[slot], start + BLOCK) - read
            high = jnp.where(p < count, high, low)
            q = queries[pl.ds(pl.multiple_of(slot * rows, 16), rows), :]
            keys = cache[:, pl.ds(pl.multiple_of(read, LANES), BLOCK)]
            scores = jnp.dot(q, keys, preferred_element_type=jnp.float32) * factor
            token = lax.broadcasted_iota(jnp.int32, scores.shape, 1)
            scores = jnp.where((token >= low) & (token < high), scores, NEG)
            top = jnp.max(scores, axis=1, keepdims=True)
            weights = jnp.exp2(scores - top)
            part_sum = jnp.broadcast_to(jnp.sum(weights, axis=1, keepdims=True), (rows, LANES))
            part = lax.dot_general(
                weights.astype(jnp.bfloat16),
                keys[0:LATENT],
                (((1,), (1,)), ((), ())),
                preferred_element_type=jnp.float32,
            )
            part_max = jnp.broadcast_to(top, (rows, LANES))
            old_max = run_max[slot]
            new_max = jnp.maximum(old_max, part_max)
            keep = jnp.exp2(old_max - new_max)
            add = jnp.exp2(part_max - new_max)
            run_max[slot] = new_max
            run_sum[slot] = run_sum[slot] * keep + part_sum * add
            for c in range(LATENT // LANES):
                cols = slice(c * LANES, (c + 1) * LANES)
                acc[slot, :, cols] = acc[slot, :, cols] * keep + part[:, cols] * add
        return carry

    lax.fori_loop(0, (count + unroll - 1) // unroll, some_pairs, jnp.int32(0))

    for slot in range(slots):
        inverse = 1.0 / run_sum[slot]
        for c in range(LATENT // LANES):
            cols = slice(c * LANES, (c + 1) * LANES)
            latent[slot * rows : (slot + 1) * rows, cols] = (acc[slot, :, cols] * inverse).astype(jnp.bfloat16)
    vdim = value_up.shape[2]
    for i in range(heads // group):
        left = jnp.concatenate(
            [latent[slot * rows + i * 16 : slot * rows + (i + 1) * 16, :] for slot in range(slots)], axis=0
        )
        right = jnp.concatenate([value_up[i * group + u] for u in range(group)], axis=1)
        res = jnp.dot(left, right, preferred_element_type=jnp.float32)
        for u in range(group):
            own = jnp.concatenate(
                [
                    res[slot * 16 + u * steps : slot * 16 + (u + 1) * steps, u * vdim : (u + 1) * vdim]
                    for slot in range(slots)
                ],
                axis=0,
            )
            head = i * group + u
            out_ref[:, head * vdim : (head + 1) * vdim] = own.astype(jnp.bfloat16)


def place_kernel(sizes, relative, me_ref, decode_ref, out_ref, owner_count, place):
    sources, per_pair, steps, requests = sizes
    me = me_ref[0]
    rows = sources * requests
    shift = requests.bit_length() - 1

    def one_source(s, carry):
        for o in range(sources):
            owner_count[o] = jnp.int32(0)
        for r in range(requests):
            row = decode_ref[s * requests + r]
            owner = row >> shift
            at = owner_count[owner]
            owner_count[owner] = at + 1
            if relative:
                e = owner ^ s
                at_row = (e >> 1) * (2 * sources * per_pair) + (me ^ s) * (2 * per_pair) + (e & 1) * per_pair + at
            else:
                at_row = s * requests + owner * per_pair + at
            place[row] = at_row * steps
        return carry

    lax.fori_loop(0, sources, one_source, jnp.int32(0))
    narrow = (rows, LANES)
    row_id = lax.broadcasted_iota(jnp.int32, narrow, 0)

    def put(b, wanted):
        return jnp.where(row_id == b, place[b], wanted)

    wanted = lax.fori_loop(0, rows, put, jnp.zeros(narrow, jnp.int32), unroll=8)[:, 0:1]
    col_id = lax.broadcasted_iota(jnp.int32, (rows, rows * steps), 1)
    for t in range(steps):
        out_ref[t] = jnp.where(col_id == wanted + t, 1.0, 0.0).astype(jnp.bfloat16)


def order_kernel(pieces, pick_ref, *rest):
    out_ref = rest[pieces]
    whole = jnp.concatenate([rest[i][...] for i in range(pieces)], axis=0)
    for t in range(pick_ref.shape[0]):
        out_ref[t] = jnp.dot(pick_ref[t], whole, preferred_element_type=jnp.float32).astype(jnp.bfloat16)


def project_kernel(*rest):
    parts, weight, out, x = rest[:4], rest[4], rest[5], rest[6]
    rows = parts[0].shape[0]
    for q in range(4):
        x[q * rows : (q + 1) * rows, :] = parts[q][...]

    def tile(n, carry):
        cols = pl.ds(pl.multiple_of(n * BLOCK, BLOCK), BLOCK)
        out[:, cols] = jnp.dot(x[...], weight[:, cols], preferred_element_type=jnp.float32).astype(jnp.bfloat16)
        return carry

    lax.fori_loop(0, weight.shape[1] // BLOCK, tile, jnp.int32(0))


def smem():
    return pl.BlockSpec(memory_space=pltpu.SMEM)


def vmem():
    return pl.BlockSpec(memory_space=pltpu.VMEM)


def anywhere():
    return pl.BlockSpec(memory_space=pl.ANY)


def limit(mib):
    return pltpu.CompilerParams(vmem_limit_bytes=mib * 1024 * 1024)


def cost(microseconds):
    return pl.CostEstimate(
        flops=int(microseconds * 1.0e9), bytes_accessed=int(microseconds * 3.0e6), transcendentals=0
    )


def flip(x, axis, distance):
    size = lax.axis_size(axis)
    return lax.ppermute(x, axis, [(i, i ^ distance) for i in range(size)])


def local(latent_cache, lengths, decode_rows, q_nope, q_rope, new_latent, key_up, value_up, out_proj):
    sources = lax.axis_size("seq")
    head_devices = lax.axis_size("head")
    relative = sources == 4 and head_devices == 4
    requests = lengths.shape[1]
    per_pair = requests // sources
    tokens, width = latent_cache.shape
    steps, _, heads, nope = q_nope.shape
    scale = (nope + q_rope.shape[3]) ** (-0.5)
    fresh_rows = -(-per_pair * steps // 16) * 16
    rows = heads * steps
    columns = out_proj.shape[1]
    packed_rows = per_pair * rows + per_pair * rows // 2 + -(-width // LANES) * fresh_rows
    sizes = (sources, per_pair, steps, heads, requests, fresh_rows)
    me = lax.axis_index("seq").astype(jnp.int32).reshape(1)
    cache = latent_cache.T

    pick = pl.pallas_call(
        functools.partial(place_kernel, (sources, per_pair, steps, requests), relative),
        out_shape=jax.ShapeDtypeStruct((steps, sources * requests, steps * sources * requests), jnp.bfloat16),
        in_specs=[smem(), smem()],
        out_specs=vmem(),
        scratch_shapes=[pltpu.SMEM((sources,), jnp.int32), pltpu.SMEM((sources * requests,), jnp.int32)],
        compiler_params=limit(12),
        cost_estimate=cost(2),
        name="place_rows",
    )(me, decode_rows)

    outs, each = (sources, 1) if relative else (1, sources)
    packed = pl.pallas_call(
        functools.partial(pack_kernel, sizes, relative),
        out_shape=[jax.ShapeDtypeStruct((each, packed_rows, LANES), jnp.bfloat16)] * outs,
        in_specs=[smem(), smem(), vmem(), vmem(), vmem(), anywhere()],
        out_specs=[vmem()] * outs,
        scratch_shapes=[
            pltpu.SMEM((sources * (per_pair + 1),), jnp.int32),
            pltpu.VMEM((2 * per_pair, rows, LANES), jnp.float32),
        ],
        compiler_params=limit(8),
        cost_estimate=cost(6),
        name="pack_queries",
    )(me, decode_rows, q_nope, q_rope, new_latent, pick)

    def attend(received, base):
        here = sum(part.shape[0] for part in received)
        slots = here * per_pair
        pairs = slots * (512 // BLOCK + 1) + 1
        return pl.pallas_call(
            functools.partial(attend_kernel, sizes, scale, relative, base, len(received)),
            out_shape=jax.ShapeDtypeStruct((slots * steps, heads * value_up.shape[2]), jnp.bfloat16),
            in_specs=[smem(), smem(), smem()] + [vmem()] * (len(received) + 3),
            out_specs=vmem(),
            scratch_shapes=[
                pltpu.SMEM((slots + 1,), jnp.int32),
                pltpu.SMEM((slots + 1,), jnp.int32),
                pltpu.SMEM((sources,), jnp.int32),
                pltpu.SMEM((pairs,), jnp.int32),
                pltpu.SMEM((pairs,), jnp.int32),
                pltpu.VMEM((slots * rows, width), jnp.bfloat16),
                pltpu.VMEM((here * fresh_rows, width), jnp.bfloat16),
                pltpu.VMEM((slots, rows, LATENT), jnp.float32),
                pltpu.VMEM((slots, rows, LANES), jnp.float32),
                pltpu.VMEM((slots, rows, LANES), jnp.float32),
                pltpu.VMEM((slots * rows, LATENT), jnp.bfloat16),
            ],
            compiler_params=limit(18),
            cost_estimate=cost(8),
            name="attend",
        )(me, decode_rows, lengths, *received, cache, key_up, value_up)

    def order(*pieces):
        return pl.pallas_call(
            functools.partial(order_kernel, len(pieces)),
            out_shape=jax.ShapeDtypeStruct((steps, sources * requests, columns), jnp.bfloat16),
            in_specs=[vmem()] * (1 + len(pieces)),
            out_specs=vmem(),
            compiler_params=limit(16),
            cost_estimate=cost(2),
            name="order_rows",
        )(pick, *pieces)

    if not relative:
        received = lax.all_to_all(packed[0], "seq", split_axis=0, concat_axis=0, tiled=True)
        every_row = lax.all_gather(attend([received], 0), "seq", axis=0, tiled=True)
        partial_value = jnp.dot(every_row, out_proj, preferred_element_type=jnp.float32).astype(jnp.bfloat16)
        return order(lax.psum(partial_value, "head"))

    def project(parts):
        part_rows = parts[0].shape[0]
        return pl.pallas_call(
            project_kernel,
            out_shape=jax.ShapeDtypeStruct((4 * part_rows, columns), jnp.bfloat16),
            in_specs=[vmem()] * 5,
            out_specs=vmem(),
            scratch_shapes=[pltpu.VMEM((4 * part_rows, out_proj.shape[0]), jnp.bfloat16)],
            compiler_params=limit(24),
            cost_estimate=cost(6),
            name="project_out",
        )(*parts, out_proj)

    received = [packed[0]] + [flip(packed[k], "seq", k) for k in range(1, 4)]
    near_rows = attend(received[:2], 0)
    near_across = flip(near_rows, "seq", 2)
    far_rows = attend(received[2:], 2)
    near_across, far_rows = lax.optimization_barrier((near_across, far_rows))
    near = [near_rows, flip(near_rows, "seq", 1), near_across, flip(near_across, "seq", 1)]
    far_across = flip(far_rows, "seq", 2)
    far = [far_rows, flip(far_rows, "seq", 1), far_across, flip(far_across, "seq", 1)]
    near_sum = lax.psum(project(near), "head")
    far_share = lax.psum_scatter(project(far), "head", scatter_dimension=0, tiled=True)
    far_sum = lax.all_gather(far_share, "head", axis=0, tiled=True)
    return order(near_sum, far_sum)


def solution(mesh):
    return jax.shard_map(
        local,
        mesh=mesh,
        in_specs=(
            P(("groups", "seq"), None),
            P("groups", None),
            P("groups"),
            P(None, ("groups", "seq"), "head", None),
            P(None, ("groups", "seq"), "head", None),
            P(None, ("groups", "seq"), None),
            P("head", None, None),
            P("head", None, None),
            P("head", "seq"),
        ),
        out_specs=P(None, "groups", "seq"),
        check_vma=False,
    )
```

```python
import functools

import jax
import jax.numpy as jnp
from jax import lax
from jax.experimental import pallas as pl
from jax.experimental.pallas import tpu as pltpu
from jax.sharding import PartitionSpec as P

LATENT = 512
BLOCK = 256
LANES = 128
LOG2E = 1.4426950408889634
NEG = -1e30


def own_slots(decode_ref, slot_ref, me, sources, requests, per_pair):
    shift = requests.bit_length() - 1

    def one_source(s, carry):
        count = jnp.int32(0)
        for r in range(requests):
            row = decode_ref[s * requests + r]
            slot_ref[s * (per_pair + 1) + jnp.minimum(count, per_pair)] = row & (requests - 1)
            count = count + jnp.where((row >> shift) == me, 1, 0).astype(jnp.int32)
        return carry

    lax.fori_loop(0, sources, one_source, jnp.int32(0))


def pack_kernel(sizes, relative, me_ref, decode_ref, nope_ref, rope_ref, fresh_ref, after_ref, *rest):
    sources, per_pair, steps, heads, requests, fresh_rows = sizes
    out_refs, (slots, wide) = rest[:-2], rest[-2:]
    me = me_ref[0]
    rows = heads * steps
    half = rows // 2
    rope_base = per_pair * rows
    fresh_base = rope_base + per_pair * half
    own_slots(decode_ref, slots, me, sources, requests, per_pair)

    def one_dest(s, out_ref, e):
        for j in range(per_pair):
            row = slots[s * (per_pair + 1) + j]
            for t in range(steps):
                wide[2 * j, pl.ds(t, heads, stride=steps), :] = nope_ref[t, row].astype(jnp.float32)
                wide[2 * j + 1, pl.ds(t, heads, stride=steps), :] = jnp.concatenate(
                    [rope_ref[t, row].astype(jnp.float32)] * 2, axis=1
                )
        for j in range(per_pair):
            out_ref[e, j * rows : (j + 1) * rows, :] = wide[2 * j].astype(jnp.bfloat16)
            low = lax.broadcasted_iota(jnp.int32, (half, LANES), 1) < LANES // 2
            packed = jnp.where(low, wide[2 * j + 1, 0:half, :], wide[2 * j + 1, half : 2 * half, :])
            out_ref[e, rope_base + j * half : rope_base + (j + 1) * half, :] = packed.astype(jnp.bfloat16)

    if relative:
        dests = [me ^ k for k in range(sources)]
        for k in range(sources):
            one_dest(dests[k], out_refs[k], 0)
    else:
        dests = list(range(sources))

        def step(s, carry):
            one_dest(s, out_refs[0], s)
            return carry

        lax.fori_loop(0, sources, step, jnp.int32(0))
    shape = (sources * fresh_rows, steps * requests)
    row_id = lax.broadcasted_iota(jnp.int32, shape, 0)
    col_id = lax.broadcasted_iota(jnp.int32, shape, 1)
    wanted = jnp.full(shape, -1, jnp.int32)
    for k in range(sources):
        for j in range(per_pair):
            first = k * fresh_rows + j * steps
            here = (row_id >= first) & (row_id < first + steps)
            wanted = jnp.where(here, (row_id - first) * requests + slots[dests[k] * (per_pair + 1) + j], wanted)
    pick = jnp.where(col_id == wanted, 1.0, 0.0).astype(jnp.bfloat16)
    width = fresh_ref.shape[2]
    source_rows = jnp.concatenate([fresh_ref[t] for t in range(steps)], axis=0)
    picked = jnp.dot(pick, source_rows, preferred_element_type=jnp.float32).astype(jnp.bfloat16)
    for k in range(sources):
        for c in range(-(-width // LANES)):
            piece = picked[k * fresh_rows : (k + 1) * fresh_rows, c * LANES : min((c + 1) * LANES, width)]
            if piece.shape[1] < LANES:
                piece = jnp.concatenate([piece] * (LANES // piece.shape[1]), axis=1)
            first = fresh_base + c * fresh_rows
            if relative:
                out_refs[k][0, first : first + fresh_rows, :] = piece
            else:
                out_refs[0][k, first : first + fresh_rows, :] = piece


def attend_kernel(sizes, scale, relative, base, recv_count, me_ref, decode_ref, length_ref, *rest):
    sources, per_pair, steps, heads, requests, fresh_rows = sizes
    recv_refs = rest[:recv_count]
    (
        cache, key_up, value_up, out_ref,
        slot_offset, slot_length, owner_count, pair_slot, pair_start,
        queries, fresh, acc, run_max, run_sum, latent,
    ) = rest[recv_count:]
    owners = [(ref, e) for ref in recv_refs for e in range(ref.shape[0])]
    here = len(owners)
    slots = here * per_pair
    width, tokens = cache.shape
    rows = heads * steps
    half = rows // 2
    rope_base = per_pair * rows
    fresh_base = rope_base + per_pair * half
    group = 16 // steps
    shift = requests.bit_length() - 1
    factor = scale * LOG2E

    for e in range(here):
        ref, at = owners[e]
        for c in range(-(-width // LANES)):
            lanes = min(LANES, width - c * LANES)
            first = fresh_base + c * fresh_rows
            fresh[e * fresh_rows : (e + 1) * fresh_rows, c * LANES : c * LANES + lanes] = ref[
                at, first : first + fresh_rows, 0:lanes
            ]
        for j in range(per_pair):
            slot = e * per_pair + j
            first = rope_base + j * half
            piece = ref[at, first : first + half, :]
            queries[slot * rows : slot * rows + half, LATENT:width] = piece[:, 0 : width - LATENT]
            queries[slot * rows + half : (slot + 1) * rows, LATENT:width] = piece[:, LANES - (width - LATENT) :]

    inner_head = lax.broadcasted_iota(jnp.int32, (slots * 16, LANES), 0) // steps % group
    own_head = [jnp.where(inner_head == u, 1.0, 0.0).astype(jnp.bfloat16) for u in range(group)]
    for i in range(heads // group):
        tall = jnp.concatenate(
            [ref[at, j * rows + i * 16 : j * rows + (i + 1) * 16, :] for ref, at in owners for j in range(per_pair)],
            axis=0,
        )
        left = jnp.concatenate([tall * own_head[u] for u in range(group)], axis=1)
        right = jnp.concatenate([key_up[i * group + u] for u in range(group)], axis=0)
        res = jnp.dot(left, right, preferred_element_type=jnp.float32).astype(jnp.bfloat16)
        for slot in range(slots):
            queries[slot * rows + i * 16 : slot * rows + (i + 1) * 16, 0:LATENT] = res[slot * 16 : (slot + 1) * 16]

    me = me_ref[0]
    for o in range(sources):
        owner_count[o] = jnp.int32(0)
    total = jnp.int32(0)
    for r in range(requests):
        owner = decode_ref[me * requests + r] >> shift
        at = owner_count[owner]
        owner_count[owner] = at + 1
        e = (owner ^ me) - base if relative else owner
        slot = jnp.where((e >= 0) & (e < here), e * per_pair + at, slots)
        length = length_ref[me, r]
        slot_offset[slot] = total
        slot_length[slot] = length
        total = total + length
    count = jnp.int32(0)
    for slot in range(slots):
        start = slot_offset[slot] & ~(LANES - 1)
        end = slot_offset[slot] + slot_length[slot]
        for k in range(512 // BLOCK + 1):
            pair_slot[count] = jnp.int32(slot)
            pair_start[count] = start + k * BLOCK
            count = count + jnp.where(start + k * BLOCK < end, 1, 0).astype(jnp.int32)

    fresh_scores = (
        lax.dot_general(queries[...], fresh[...], (((1,), (1,)), ((), ())), preferred_element_type=jnp.float32) * factor
    )
    row_id = lax.broadcasted_iota(jnp.int32, (rows, here * fresh_rows), 0)
    col_id = lax.broadcasted_iota(jnp.int32, (rows, here * fresh_rows), 1)
    behind = row_id & (steps - 1)
    fresh_weights = []
    for slot in range(slots):
        first = (slot // per_pair) * fresh_rows + (slot % per_pair) * steps
        seen = (col_id >= first) & (col_id <= first + behind)
        scores = jnp.where(seen, fresh_scores[slot * rows : (slot + 1) * rows], NEG)
        top = jnp.max(scores, axis=1, keepdims=True)
        weights = jnp.exp2(scores - top)
        run_max[slot] = jnp.broadcast_to(top, (rows, LANES))
        run_sum[slot] = jnp.broadcast_to(jnp.sum(weights, axis=1, keepdims=True), (rows, LANES))
        fresh_weights.append(weights.astype(jnp.bfloat16))
    for slot in range(slots):
        acc[slot] = jnp.dot(fresh_weights[slot], fresh[:, 0:LATENT], preferred_element_type=jnp.float32)

    unroll = 4

    def some_pairs(i, carry):
        for u in range(unroll):
            p = i * unroll + u
            slot = pair_slot[jnp.minimum(p, count - 1)]
            start = pair_start[jnp.minimum(p, count - 1)]
            read = jnp.minimum(start, tokens - BLOCK)
            low = jnp.maximum(slot_offset[slot], start) - read
            high = jnp.minimum(slot_offset[slot] + slot_length[slot], start + BLOCK) - read
            high = jnp.where(p < count, high, low)
            q = queries[pl.ds(pl.multiple_of(slot * rows, 16), rows), :]
            keys = cache[:, pl.ds(pl.multiple_of(read, LANES), BLOCK)]
            scores = jnp.dot(q, keys, preferred_element_type=jnp.float32) * factor
            token = lax.broadcasted_iota(jnp.int32, scores.shape, 1)
            scores = jnp.where((token >= low) & (token < high), scores, NEG)
            top = jnp.max(scores, axis=1, keepdims=True)
            weights = jnp.exp2(scores - top)
            part_sum = jnp.broadcast_to(jnp.sum(weights, axis=1, keepdims=True), (rows, LANES))
            part = lax.dot_general(
                weights.astype(jnp.bfloat16),
                keys[0:LATENT],
                (((1,), (1,)), ((), ())),
                preferred_element_type=jnp.float32,
            )
            part_max = jnp.broadcast_to(top, (rows, LANES))
            old_max = run_max[slot]
            new_max = jnp.maximum(old_max, part_max)
            keep = jnp.exp2(old_max - new_max)
            add = jnp.exp2(part_max - new_max)
            run_max[slot] = new_max
            run_sum[slot] = run_sum[slot] * keep + part_sum * add
            for c in range(LATENT // LANES):
                cols = slice(c * LANES, (c + 1) * LANES)
                acc[slot, :, cols] = acc[slot, :, cols] * keep + part[:, cols] * add
        return carry

    lax.fori_loop(0, (count + unroll - 1) // unroll, some_pairs, jnp.int32(0))

    for slot in range(slots):
        inverse = 1.0 / run_sum[slot]
        for c in range(LATENT // LANES):
            cols = slice(c * LANES, (c + 1) * LANES)
            latent[slot * rows : (slot + 1) * rows, cols] = (acc[slot, :, cols] * inverse).astype(jnp.bfloat16)
    vdim = value_up.shape[2]
    for i in range(heads // group):
        left = jnp.concatenate(
            [latent[slot * rows + i * 16 : slot * rows + (i + 1) * 16, :] for slot in range(slots)], axis=0
        )
        right = jnp.concatenate([value_up[i * group + u] for u in range(group)], axis=1)
        res = jnp.dot(left, right, preferred_element_type=jnp.float32)
        for u in range(group):
            own = jnp.concatenate(
                [
                    res[slot * 16 + u * steps : slot * 16 + (u + 1) * steps, u * vdim : (u + 1) * vdim]
                    for slot in range(slots)
                ],
                axis=0,
            )
            head = i * group + u
            out_ref[:, head * vdim : (head + 1) * vdim] = own.astype(jnp.bfloat16)


def place_kernel(sizes, relative, me_ref, decode_ref, out_ref, owner_count, place):
    sources, per_pair, steps, requests = sizes
    me = me_ref[0]
    rows = sources * requests
    shift = requests.bit_length() - 1

    def one_source(s, carry):
        for o in range(sources):
            owner_count[o] = jnp.int32(0)
        for r in range(requests):
            row = decode_ref[s * requests + r]
            owner = row >> shift
            at = owner_count[owner]
            owner_count[owner] = at + 1
            if relative:
                e = owner ^ s
                at_row = (e >> 1) * (2 * sources * per_pair) + (me ^ s) * (2 * per_pair) + (e & 1) * per_pair + at
            else:
                at_row = s * requests + owner * per_pair + at
            place[row] = at_row * steps
        return carry

    lax.fori_loop(0, sources, one_source, jnp.int32(0))
    narrow = (rows, LANES)
    row_id = lax.broadcasted_iota(jnp.int32, narrow, 0)

    def put(b, wanted):
        return jnp.where(row_id == b, place[b], wanted)

    wanted = lax.fori_loop(0, rows, put, jnp.zeros(narrow, jnp.int32), unroll=8)[:, 0:1]
    col_id = lax.broadcasted_iota(jnp.int32, (rows, rows * steps), 1)
    for t in range(steps):
        out_ref[t] = jnp.where(col_id == wanted + t, 1.0, 0.0).astype(jnp.bfloat16)


def order_kernel(halves, z_ref, pick_ref, *rest):
    pieces, out_ref, x = rest[:-2], rest[-2], rest[-1]
    middle = (z_ref[0] == 1) | (z_ref[0] == 2)
    rows = x.shape[0] // halves
    each = len(pieces) // (2 * halves)
    cols = x.shape[1] // each

    def assemble(side):
        for h in range(halves):
            for c in range(each):
                x[h * rows : (h + 1) * rows, c * cols : (c + 1) * cols] = pieces[2 * (h * each + c) + side][...]

    pl.when(middle)(lambda: assemble(0))
    pl.when(jnp.logical_not(middle))(lambda: assemble(1))
    for t in range(pick_ref.shape[0]):
        out_ref[t] = jnp.dot(pick_ref[t], x[...], preferred_element_type=jnp.float32).astype(jnp.bfloat16)


def order_whole_kernel(pick_ref, x_ref, out_ref):
    for t in range(pick_ref.shape[0]):
        out_ref[t] = jnp.dot(pick_ref[t], x_ref[...], preferred_element_type=jnp.float32).astype(jnp.bfloat16)


def project_kernel(first_col, *rest):
    parts, weight, out, x = rest[:4], rest[4], rest[5], rest[6]
    rows = parts[0].shape[0]
    for q in range(4):
        x[q * rows : (q + 1) * rows, :] = parts[q][...]
    cols = out.shape[1]
    for c in range(0, cols, BLOCK):
        n = min(BLOCK, cols - c)
        tile = jnp.dot(x[...], weight[:, first_col + c : first_col + c + n], preferred_element_type=jnp.float32)
        out[:, c : c + n] = tile.astype(jnp.bfloat16)


def smem():
    return pl.BlockSpec(memory_space=pltpu.SMEM)


def vmem():
    return pl.BlockSpec(memory_space=pltpu.VMEM)


def anywhere():
    return pl.BlockSpec(memory_space=pl.ANY)


def limit(mib):
    return pltpu.CompilerParams(vmem_limit_bytes=mib * 1024 * 1024)


def cost(microseconds):
    return pl.CostEstimate(
        flops=int(microseconds * 1.0e9), bytes_accessed=int(microseconds * 3.0e6), transcendentals=0
    )


def flip(x, axis, distance):
    size = lax.axis_size(axis)
    return lax.ppermute(x, axis, [(i, i ^ distance) for i in range(size)])


def add(x, y):
    return (x.astype(jnp.float32) + y.astype(jnp.float32)).astype(jnp.bfloat16)


def inwards(piece):
    return lax.ppermute(piece, "head", [(0, 1), (3, 2)])


def across_middle(pair):
    return lax.ppermute(pair, "head", [(1, 2), (2, 1)])


def outwards(whole):
    return lax.ppermute(whole, "head", [(1, 0), (2, 3)])


def local(latent_cache, lengths, decode_rows, q_nope, q_rope, new_latent, key_up, value_up, out_proj):
    sources = lax.axis_size("seq")
    head_devices = lax.axis_size("head")
    relative = sources == 4 and head_devices == 4
    requests = lengths.shape[1]
    per_pair = requests // sources
    tokens, width = latent_cache.shape
    steps, _, heads, nope = q_nope.shape
    scale = (nope + q_rope.shape[3]) ** (-0.5)
    fresh_rows = -(-per_pair * steps // 16) * 16
    rows = heads * steps
    columns = out_proj.shape[1]
    packed_rows = per_pair * rows + per_pair * rows // 2 + -(-width // LANES) * fresh_rows
    sizes = (sources, per_pair, steps, heads, requests, fresh_rows)
    me = lax.axis_index("seq").astype(jnp.int32).reshape(1)
    z = lax.axis_index("head").astype(jnp.int32).reshape(1)
    cache = latent_cache.T

    pick = pl.pallas_call(
        functools.partial(place_kernel, (sources, per_pair, steps, requests), relative),
        out_shape=jax.ShapeDtypeStruct((steps, sources * requests, steps * sources * requests), jnp.bfloat16),
        in_specs=[smem(), smem()],
        out_specs=vmem(),
        scratch_shapes=[pltpu.SMEM((sources,), jnp.int32), pltpu.SMEM((sources * requests,), jnp.int32)],
        compiler_params=limit(12),
        cost_estimate=cost(2),
        name="place_rows",
    )(me, decode_rows)

    outs, each = (sources, 1) if relative else (1, sources)
    packed = pl.pallas_call(
        functools.partial(pack_kernel, sizes, relative),
        out_shape=[jax.ShapeDtypeStruct((each, packed_rows, LANES), jnp.bfloat16)] * outs,
        in_specs=[smem(), smem(), vmem(), vmem(), vmem(), anywhere()],
        out_specs=[vmem()] * outs,
        scratch_shapes=[
            pltpu.SMEM((sources * (per_pair + 1),), jnp.int32),
            pltpu.VMEM((2 * per_pair, rows, LANES), jnp.float32),
        ],
        compiler_params=limit(8),
        cost_estimate=cost(6),
        name="pack_queries",
    )(me, decode_rows, q_nope, q_rope, new_latent, pick)

    def attend(received, base):
        here = sum(part.shape[0] for part in received)
        slots = here * per_pair
        pairs = slots * (512 // BLOCK + 1) + 1
        return pl.pallas_call(
            functools.partial(attend_kernel, sizes, scale, relative, base, len(received)),
            out_shape=jax.ShapeDtypeStruct((slots * steps, heads * value_up.shape[2]), jnp.bfloat16),
            in_specs=[smem(), smem(), smem()] + [vmem()] * (len(received) + 3),
            out_specs=vmem(),
            scratch_shapes=[
                pltpu.SMEM((slots + 1,), jnp.int32),
                pltpu.SMEM((slots + 1,), jnp.int32),
                pltpu.SMEM((sources,), jnp.int32),
                pltpu.SMEM((pairs,), jnp.int32),
                pltpu.SMEM((pairs,), jnp.int32),
                pltpu.VMEM((slots * rows, width), jnp.bfloat16),
                pltpu.VMEM((here * fresh_rows, width), jnp.bfloat16),
                pltpu.VMEM((slots, rows, LATENT), jnp.float32),
                pltpu.VMEM((slots, rows, LANES), jnp.float32),
                pltpu.VMEM((slots, rows, LANES), jnp.float32),
                pltpu.VMEM((slots * rows, LATENT), jnp.bfloat16),
            ],
            compiler_params=limit(18),
            cost_estimate=cost(8),
            name="attend",
        )(me, decode_rows, lengths, *received, cache, key_up, value_up)

    def order(kernel, in_specs, scratch, arrays):
        return pl.pallas_call(
            kernel,
            out_shape=jax.ShapeDtypeStruct((steps, sources * requests, columns), jnp.bfloat16),
            in_specs=in_specs,
            out_specs=vmem(),
            scratch_shapes=scratch,
            compiler_params=limit(16),
            cost_estimate=cost(2),
            name="order_rows",
        )(*arrays)

    if not relative:
        received = lax.all_to_all(packed[0], "seq", split_axis=0, concat_axis=0, tiled=True)
        every_row = lax.all_gather(attend([received], 0), "seq", axis=0, tiled=True)
        partial_value = jnp.dot(every_row, out_proj, preferred_element_type=jnp.float32).astype(jnp.bfloat16)
        shares = lax.all_to_all(partial_value, "head", split_axis=0, concat_axis=0, tiled=True)
        shares = shares.reshape(head_devices, -1, columns)
        summed = jnp.sum(shares.astype(jnp.float32), axis=0).astype(jnp.bfloat16)
        whole = lax.all_gather(summed, "head", axis=0, tiled=True)
        return order(order_whole_kernel, [vmem()] * 2, [], [pick, whole])

    pieces = 2

    def project(parts, piece):
        part_rows = parts[0].shape[0]
        cols = columns // pieces
        return pl.pallas_call(
            functools.partial(project_kernel, piece * cols),
            out_shape=jax.ShapeDtypeStruct((4 * part_rows, cols), jnp.bfloat16),
            in_specs=[vmem()] * 5,
            out_specs=vmem(),
            scratch_shapes=[pltpu.VMEM((4 * part_rows, out_proj.shape[0]), jnp.bfloat16)],
            compiler_params=limit(24),
            cost_estimate=cost(2),
            name="project_out",
        )(*parts, out_proj)

    received = [packed[0]] + [flip(packed[k], "seq", k) for k in range(1, 4)]
    near_rows = attend(received[:2], 0)
    near_across = flip(near_rows, "seq", 2)
    far_rows = attend(received[2:], 2)
    near_across, far_rows = lax.optimization_barrier((near_across, far_rows))
    near = [near_rows, flip(near_rows, "seq", 1), near_across, flip(near_across, "seq", 1)]
    far_across = flip(far_rows, "seq", 2)
    first, second = project(near, 0), project(near, 1)
    relayed, _ = lax.optimization_barrier((far_across, second))
    far = [far_rows, flip(far_rows, "seq", 1), far_across, flip(relayed, "seq", 1)]
    first_in, second_in = inwards(first), inwards(second)
    first_pair = add(first, first_in)
    first_cross = across_middle(first_pair)
    third, fourth = project(far, 0), project(far, 1)
    third_in, fourth_in = inwards(third), inwards(fourth)
    second_in, _ = lax.optimization_barrier((second_in, third))
    second_pair = add(second, second_in)
    second_cross = across_middle(second_pair)
    first_cross, _ = lax.optimization_barrier((first_cross, fourth))
    first_whole = add(first_pair, first_cross)
    first_out = outwards(first_whole)
    third_pair = add(third, third_in)
    third_cross = across_middle(third_pair)
    second_whole = add(second_pair, second_cross)
    second_out = outwards(second_whole)
    fourth_pair = add(fourth, fourth_in)
    fourth_cross = across_middle(fourth_pair)
    third_whole = add(third_pair, third_cross)
    third_out = outwards(third_whole)
    fourth_whole = add(fourth_pair, fourth_cross)
    fourth_out = outwards(fourth_whole)
    arrays = [first_whole, first_out, second_whole, second_out, third_whole, third_out, fourth_whole, fourth_out]
    scratch = [pltpu.VMEM((steps * sources * requests, columns), jnp.bfloat16)]
    kernel = functools.partial(order_kernel, 2)
    return order(kernel, [smem()] + [vmem()] * (1 + len(arrays)), scratch, [z, pick] + arrays)


def solution(mesh):
    return jax.shard_map(
        local,
        mesh=mesh,
        in_specs=(
            P(("groups", "seq"), None),
            P("groups", None),
            P("groups"),
            P(None, ("groups", "seq"), "head", None),
            P(None, ("groups", "seq"), "head", None),
            P(None, ("groups", "seq"), None),
            P("head", None, None),
            P("head", None, None),
            P("head", "seq"),
        ),
        out_specs=P(None, "groups", "seq"),
        check_vma=False,
    )
```

```python
import functools

import jax
import jax.numpy as jnp
from jax import lax
from jax.experimental import pallas as pl
from jax.experimental.pallas import tpu as pltpu
from jax.sharding import PartitionSpec as P

LATENT = 512
BLOCK = 256
LANES = 128
LOG2E = 1.4426950408889634
NEG = -1e30


def own_slots(decode_ref, slot_ref, me, sources, requests, per_pair):
    shift = requests.bit_length() - 1

    def one_source(s, carry):
        count = jnp.int32(0)
        for r in range(requests):
            row = decode_ref[s * requests + r]
            slot_ref[s * (per_pair + 1) + jnp.minimum(count, per_pair)] = row & (requests - 1)
            count = count + jnp.where((row >> shift) == me, 1, 0).astype(jnp.int32)
        return carry

    lax.fori_loop(0, sources, one_source, jnp.int32(0))


def pack_kernel(sizes, relative, me_ref, decode_ref, nope_ref, rope_ref, fresh_ref, after_ref, *rest):
    sources, per_pair, steps, heads, requests, fresh_rows = sizes
    out_refs, (slots, wide) = rest[:-2], rest[-2:]
    me = me_ref[0]
    rows = heads * steps
    half = rows // 2
    rope_base = per_pair * rows
    fresh_base = rope_base + per_pair * half
    own_slots(decode_ref, slots, me, sources, requests, per_pair)

    def one_dest(s, out_ref, e):
        for j in range(per_pair):
            row = slots[s * (per_pair + 1) + j]
            for t in range(steps):
                wide[2 * j, pl.ds(t, heads, stride=steps), :] = nope_ref[t, row].astype(jnp.float32)
                wide[2 * j + 1, pl.ds(t, heads, stride=steps), :] = jnp.concatenate(
                    [rope_ref[t, row].astype(jnp.float32)] * 2, axis=1
                )
        for j in range(per_pair):
            out_ref[e, j * rows : (j + 1) * rows, :] = wide[2 * j].astype(jnp.bfloat16)
            low = lax.broadcasted_iota(jnp.int32, (half, LANES), 1) < LANES // 2
            packed = jnp.where(low, wide[2 * j + 1, 0:half, :], wide[2 * j + 1, half : 2 * half, :])
            out_ref[e, rope_base + j * half : rope_base + (j + 1) * half, :] = packed.astype(jnp.bfloat16)

    if relative:
        dests = [me ^ k for k in range(sources)]
        for k in range(sources):
            one_dest(dests[k], out_refs[k], 0)
    else:
        dests = list(range(sources))

        def step(s, carry):
            one_dest(s, out_refs[0], s)
            return carry

        lax.fori_loop(0, sources, step, jnp.int32(0))
    shape = (sources * fresh_rows, steps * requests)
    row_id = lax.broadcasted_iota(jnp.int32, shape, 0)
    col_id = lax.broadcasted_iota(jnp.int32, shape, 1)
    wanted = jnp.full(shape, -1, jnp.int32)
    for k in range(sources):
        for j in range(per_pair):
            first = k * fresh_rows + j * steps
            here = (row_id >= first) & (row_id < first + steps)
            wanted = jnp.where(here, (row_id - first) * requests + slots[dests[k] * (per_pair + 1) + j], wanted)
    pick = jnp.where(col_id == wanted, 1.0, 0.0).astype(jnp.bfloat16)
    width = fresh_ref.shape[2]
    source_rows = jnp.concatenate([fresh_ref[t] for t in range(steps)], axis=0)
    picked = jnp.dot(pick, source_rows, preferred_element_type=jnp.float32).astype(jnp.bfloat16)
    for k in range(sources):
        for c in range(-(-width // LANES)):
            piece = picked[k * fresh_rows : (k + 1) * fresh_rows, c * LANES : min((c + 1) * LANES, width)]
            if piece.shape[1] < LANES:
                piece = jnp.concatenate([piece] * (LANES // piece.shape[1]), axis=1)
            first = fresh_base + c * fresh_rows
            if relative:
                out_refs[k][0, first : first + fresh_rows, :] = piece
            else:
                out_refs[0][k, first : first + fresh_rows, :] = piece


def attend_kernel(sizes, scale, relative, base, recv_count, me_ref, decode_ref, length_ref, *rest):
    sources, per_pair, steps, heads, requests, fresh_rows = sizes
    recv_refs = rest[:recv_count]
    (
        cache, key_up, value_up, out_ref,
        slot_offset, slot_length, owner_count, pair_slot, pair_start,
        queries, fresh, acc, run_max, run_sum, latent,
    ) = rest[recv_count:]
    owners = [(ref, e) for ref in recv_refs for e in range(ref.shape[0])]
    here = len(owners)
    slots = here * per_pair
    width, tokens = cache.shape
    rows = heads * steps
    half = rows // 2
    rope_base = per_pair * rows
    fresh_base = rope_base + per_pair * half
    group = 16 // steps
    shift = requests.bit_length() - 1
    factor = scale * LOG2E

    for e in range(here):
        ref, at = owners[e]
        for c in range(-(-width // LANES)):
            lanes = min(LANES, width - c * LANES)
            first = fresh_base + c * fresh_rows
            fresh[e * fresh_rows : (e + 1) * fresh_rows, c * LANES : c * LANES + lanes] = ref[
                at, first : first + fresh_rows, 0:lanes
            ]
        for j in range(per_pair):
            slot = e * per_pair + j
            first = rope_base + j * half
            piece = ref[at, first : first + half, :]
            queries[slot * rows : slot * rows + half, LATENT:width] = piece[:, 0 : width - LATENT]
            queries[slot * rows + half : (slot + 1) * rows, LATENT:width] = piece[:, LANES - (width - LATENT) :]

    inner_head = lax.broadcasted_iota(jnp.int32, (slots * 16, LANES), 0) // steps % group
    own_head = [jnp.where(inner_head == u, 1.0, 0.0).astype(jnp.bfloat16) for u in range(group)]
    for i in range(heads // group):
        tall = jnp.concatenate(
            [ref[at, j * rows + i * 16 : j * rows + (i + 1) * 16, :] for ref, at in owners for j in range(per_pair)],
            axis=0,
        )
        left = jnp.concatenate([tall * own_head[u] for u in range(group)], axis=1)
        right = jnp.concatenate([key_up[i * group + u] for u in range(group)], axis=0)
        res = jnp.dot(left, right, preferred_element_type=jnp.float32).astype(jnp.bfloat16)
        for slot in range(slots):
            queries[slot * rows + i * 16 : slot * rows + (i + 1) * 16, 0:LATENT] = res[slot * 16 : (slot + 1) * 16]

    me = me_ref[0]
    for o in range(sources):
        owner_count[o] = jnp.int32(0)
    total = jnp.int32(0)
    for r in range(requests):
        owner = decode_ref[me * requests + r] >> shift
        at = owner_count[owner]
        owner_count[owner] = at + 1
        e = (owner ^ me) - base if relative else owner
        slot = jnp.where((e >= 0) & (e < here), e * per_pair + at, slots)
        length = length_ref[me, r]
        slot_offset[slot] = total
        slot_length[slot] = length
        total = total + length
    count = jnp.int32(0)
    for slot in range(slots):
        start = slot_offset[slot] & ~(LANES - 1)
        end = slot_offset[slot] + slot_length[slot]
        for k in range(512 // BLOCK + 1):
            pair_slot[count] = jnp.int32(slot)
            pair_start[count] = start + k * BLOCK
            count = count + jnp.where(start + k * BLOCK < end, 1, 0).astype(jnp.int32)

    fresh_scores = (
        lax.dot_general(queries[...], fresh[...], (((1,), (1,)), ((), ())), preferred_element_type=jnp.float32) * factor
    )
    row_id = lax.broadcasted_iota(jnp.int32, (rows, here * fresh_rows), 0)
    col_id = lax.broadcasted_iota(jnp.int32, (rows, here * fresh_rows), 1)
    behind = row_id & (steps - 1)
    fresh_weights = []
    for slot in range(slots):
        first = (slot // per_pair) * fresh_rows + (slot % per_pair) * steps
        seen = (col_id >= first) & (col_id <= first + behind)
        scores = jnp.where(seen, fresh_scores[slot * rows : (slot + 1) * rows], NEG)
        top = jnp.max(scores, axis=1, keepdims=True)
        weights = jnp.exp2(scores - top)
        run_max[slot] = jnp.broadcast_to(top, (rows, LANES))
        run_sum[slot] = jnp.broadcast_to(jnp.sum(weights, axis=1, keepdims=True), (rows, LANES))
        fresh_weights.append(weights.astype(jnp.bfloat16))
    for slot in range(slots):
        acc[slot] = jnp.dot(fresh_weights[slot], fresh[:, 0:LATENT], preferred_element_type=jnp.float32)

    unroll = 4

    def some_pairs(i, carry):
        for u in range(unroll):
            p = i * unroll + u
            slot = pair_slot[jnp.minimum(p, count - 1)]
            start = pair_start[jnp.minimum(p, count - 1)]
            read = jnp.minimum(start, tokens - BLOCK)
            low = jnp.maximum(slot_offset[slot], start) - read
            high = jnp.minimum(slot_offset[slot] + slot_length[slot], start + BLOCK) - read
            high = jnp.where(p < count, high, low)
            q = queries[pl.ds(pl.multiple_of(slot * rows, 16), rows), :]
            keys = cache[:, pl.ds(pl.multiple_of(read, LANES), BLOCK)]
            scores = jnp.dot(q, keys, preferred_element_type=jnp.float32) * factor
            token = lax.broadcasted_iota(jnp.int32, scores.shape, 1)
            scores = jnp.where((token >= low) & (token < high), scores, NEG)
            top = jnp.max(scores, axis=1, keepdims=True)
            weights = jnp.exp2(scores - top)
            part_sum = jnp.broadcast_to(jnp.sum(weights, axis=1, keepdims=True), (rows, LANES))
            part = lax.dot_general(
                weights.astype(jnp.bfloat16),
                keys[0:LATENT],
                (((1,), (1,)), ((), ())),
                preferred_element_type=jnp.float32,
            )
            part_max = jnp.broadcast_to(top, (rows, LANES))
            old_max = run_max[slot]
            new_max = jnp.maximum(old_max, part_max)
            keep = jnp.exp2(old_max - new_max)
            add = jnp.exp2(part_max - new_max)
            run_max[slot] = new_max
            run_sum[slot] = run_sum[slot] * keep + part_sum * add
            for c in range(LATENT // LANES):
                cols = slice(c * LANES, (c + 1) * LANES)
                acc[slot, :, cols] = acc[slot, :, cols] * keep + part[:, cols] * add
        return carry

    lax.fori_loop(0, (count + unroll - 1) // unroll, some_pairs, jnp.int32(0))

    for slot in range(slots):
        inverse = 1.0 / run_sum[slot]
        for c in range(LATENT // LANES):
            cols = slice(c * LANES, (c + 1) * LANES)
            latent[slot * rows : (slot + 1) * rows, cols] = (acc[slot, :, cols] * inverse).astype(jnp.bfloat16)
    vdim = value_up.shape[2]
    for i in range(heads // group):
        left = jnp.concatenate(
            [latent[slot * rows + i * 16 : slot * rows + (i + 1) * 16, :] for slot in range(slots)], axis=0
        )
        right = jnp.concatenate([value_up[i * group + u] for u in range(group)], axis=1)
        res = jnp.dot(left, right, preferred_element_type=jnp.float32)
        for u in range(group):
            own = jnp.concatenate(
                [
                    res[slot * 16 + u * steps : slot * 16 + (u + 1) * steps, u * vdim : (u + 1) * vdim]
                    for slot in range(slots)
                ],
                axis=0,
            )
            head = i * group + u
            out_ref[:, head * vdim : (head + 1) * vdim] = own.astype(jnp.bfloat16)


def place_kernel(sizes, relative, me_ref, decode_ref, out_ref, owner_count, place):
    sources, per_pair, steps, requests = sizes
    me = me_ref[0]
    rows = sources * requests
    shift = requests.bit_length() - 1

    def one_source(s, carry):
        for o in range(sources):
            owner_count[o] = jnp.int32(0)
        for r in range(requests):
            row = decode_ref[s * requests + r]
            owner = row >> shift
            at = owner_count[owner]
            owner_count[owner] = at + 1
            if relative:
                e = owner ^ s
                at_row = (e >> 1) * (2 * sources * per_pair) + (me ^ s) * (2 * per_pair) + (e & 1) * per_pair + at
            else:
                at_row = s * requests + owner * per_pair + at
            place[row] = at_row * steps
        return carry

    lax.fori_loop(0, sources, one_source, jnp.int32(0))
    narrow = (rows, LANES)
    row_id = lax.broadcasted_iota(jnp.int32, narrow, 0)

    def put(b, wanted):
        return jnp.where(row_id == b, place[b], wanted)

    wanted = lax.fori_loop(0, rows, put, jnp.zeros(narrow, jnp.int32), unroll=8)[:, 0:1]
    col_id = lax.broadcasted_iota(jnp.int32, (rows, rows * steps), 1)
    for t in range(steps):
        out_ref[t] = jnp.where(col_id == wanted + t, 1.0, 0.0).astype(jnp.bfloat16)


def keeps_upper(z_ref):
    return (z_ref[0] == 1) | (z_ref[0] == 2)


def order_kernel(halves, z_ref, pick_ref, *rest):
    pieces, out_ref, x = rest[:-2], rest[-2], rest[-1]
    upper = keeps_upper(z_ref)
    rows = x.shape[0] // (2 * halves)
    each = len(pieces) // (2 * halves)
    cols = x.shape[1] // each

    def assemble(first, second):
        for h in range(halves):
            for c in range(each):
                at = slice(c * cols, (c + 1) * cols)
                i = 2 * (h * each + c)
                x[2 * h * rows : (2 * h + 1) * rows, at] = pieces[i + first][...]
                x[(2 * h + 1) * rows : (2 * h + 2) * rows, at] = pieces[i + second][...]

    pl.when(upper)(lambda: assemble(1, 0))
    pl.when(jnp.logical_not(upper))(lambda: assemble(0, 1))
    for t in range(pick_ref.shape[0]):
        out_ref[t] = jnp.dot(pick_ref[t], x[...], preferred_element_type=jnp.float32).astype(jnp.bfloat16)


def order_whole_kernel(pick_ref, x_ref, out_ref):
    for t in range(pick_ref.shape[0]):
        out_ref[t] = jnp.dot(pick_ref[t], x_ref[...], preferred_element_type=jnp.float32).astype(jnp.bfloat16)


def project_kernel(first_col, z_ref, *rest):
    parts, weight, keep, send, x = rest[:4], rest[4], rest[5], rest[6], rest[7]
    rows = parts[0].shape[0]
    upper = keeps_upper(z_ref)

    def assemble(order):
        for place, q in enumerate(order):
            x[place * rows : (place + 1) * rows, :] = parts[q][...]

    pl.when(upper)(lambda: assemble((2, 3, 0, 1)))
    pl.when(jnp.logical_not(upper))(lambda: assemble((0, 1, 2, 3)))
    cols = keep.shape[1]
    for c in range(0, cols, BLOCK):
        n = min(BLOCK, cols - c)
        tile = jnp.dot(x[...], weight[:, first_col + c : first_col + c + n], preferred_element_type=jnp.float32)
        tile = tile.astype(jnp.bfloat16)
        keep[:, c : c + n] = tile[: 2 * rows]
        send[:, c : c + n] = tile[2 * rows :]


def smem():
    return pl.BlockSpec(memory_space=pltpu.SMEM)


def vmem():
    return pl.BlockSpec(memory_space=pltpu.VMEM)


def anywhere():
    return pl.BlockSpec(memory_space=pl.ANY)


def limit(mib):
    return pltpu.CompilerParams(vmem_limit_bytes=mib * 1024 * 1024)


def cost(microseconds):
    return pl.CostEstimate(
        flops=int(microseconds * 1.0e9), bytes_accessed=int(microseconds * 3.0e6), transcendentals=0
    )


def flip(x, axis, distance):
    size = lax.axis_size(axis)
    return lax.ppermute(x, axis, [(i, i ^ distance) for i in range(size)])


def add(x, y):
    return (x.astype(jnp.float32) + y.astype(jnp.float32)).astype(jnp.bfloat16)


def local(latent_cache, lengths, decode_rows, q_nope, q_rope, new_latent, key_up, value_up, out_proj):
    sources = lax.axis_size("seq")
    head_devices = lax.axis_size("head")
    relative = sources == 4 and head_devices == 4
    requests = lengths.shape[1]
    per_pair = requests // sources
    tokens, width = latent_cache.shape
    steps, _, heads, nope = q_nope.shape
    scale = (nope + q_rope.shape[3]) ** (-0.5)
    fresh_rows = -(-per_pair * steps // 16) * 16
    rows = heads * steps
    columns = out_proj.shape[1]
    packed_rows = per_pair * rows + per_pair * rows // 2 + -(-width // LANES) * fresh_rows
    sizes = (sources, per_pair, steps, heads, requests, fresh_rows)
    me = lax.axis_index("seq").astype(jnp.int32).reshape(1)
    z = lax.axis_index("head").astype(jnp.int32).reshape(1)
    cache = latent_cache.T

    pick = pl.pallas_call(
        functools.partial(place_kernel, (sources, per_pair, steps, requests), relative),
        out_shape=jax.ShapeDtypeStruct((steps, sources * requests, steps * sources * requests), jnp.bfloat16),
        in_specs=[smem(), smem()],
        out_specs=vmem(),
        scratch_shapes=[pltpu.SMEM((sources,), jnp.int32), pltpu.SMEM((sources * requests,), jnp.int32)],
        compiler_params=limit(12),
        cost_estimate=cost(2),
        name="place_rows",
    )(me, decode_rows)

    outs, each = (sources, 1) if relative else (1, sources)
    packed = pl.pallas_call(
        functools.partial(pack_kernel, sizes, relative),
        out_shape=[jax.ShapeDtypeStruct((each, packed_rows, LANES), jnp.bfloat16)] * outs,
        in_specs=[smem(), smem(), vmem(), vmem(), vmem(), anywhere()],
        out_specs=[vmem()] * outs,
        scratch_shapes=[
            pltpu.SMEM((sources * (per_pair + 1),), jnp.int32),
            pltpu.VMEM((2 * per_pair, rows, LANES), jnp.float32),
        ],
        compiler_params=limit(8),
        cost_estimate=cost(6),
        name="pack_queries",
    )(me, decode_rows, q_nope, q_rope, new_latent, pick)

    def attend(received, base):
        here = sum(part.shape[0] for part in received)
        slots = here * per_pair
        pairs = slots * (512 // BLOCK + 1) + 1
        return pl.pallas_call(
            functools.partial(attend_kernel, sizes, scale, relative, base, len(received)),
            out_shape=jax.ShapeDtypeStruct((slots * steps, heads * value_up.shape[2]), jnp.bfloat16),
            in_specs=[smem(), smem(), smem()] + [vmem()] * (len(received) + 3),
            out_specs=vmem(),
            scratch_shapes=[
                pltpu.SMEM((slots + 1,), jnp.int32),
                pltpu.SMEM((slots + 1,), jnp.int32),
                pltpu.SMEM((sources,), jnp.int32),
                pltpu.SMEM((pairs,), jnp.int32),
                pltpu.SMEM((pairs,), jnp.int32),
                pltpu.VMEM((slots * rows, width), jnp.bfloat16),
                pltpu.VMEM((here * fresh_rows, width), jnp.bfloat16),
                pltpu.VMEM((slots, rows, LATENT), jnp.float32),
                pltpu.VMEM((slots, rows, LANES), jnp.float32),
                pltpu.VMEM((slots, rows, LANES), jnp.float32),
                pltpu.VMEM((slots * rows, LATENT), jnp.bfloat16),
            ],
            compiler_params=limit(18),
            cost_estimate=cost(8),
            name="attend",
        )(me, decode_rows, lengths, *received, cache, key_up, value_up)

    def order(kernel, in_specs, scratch, arrays):
        return pl.pallas_call(
            kernel,
            out_shape=jax.ShapeDtypeStruct((steps, sources * requests, columns), jnp.bfloat16),
            in_specs=in_specs,
            out_specs=vmem(),
            scratch_shapes=scratch,
            compiler_params=limit(16),
            cost_estimate=cost(2),
            name="order_rows",
        )(*arrays)

    if not relative:
        received = lax.all_to_all(packed[0], "seq", split_axis=0, concat_axis=0, tiled=True)
        every_row = lax.all_gather(attend([received], 0), "seq", axis=0, tiled=True)
        partial_value = jnp.dot(every_row, out_proj, preferred_element_type=jnp.float32).astype(jnp.bfloat16)
        shares = lax.all_to_all(partial_value, "head", split_axis=0, concat_axis=0, tiled=True)
        shares = shares.reshape(head_devices, -1, columns)
        summed = jnp.sum(shares.astype(jnp.float32), axis=0).astype(jnp.bfloat16)
        whole = lax.all_gather(summed, "head", axis=0, tiled=True)
        return order(order_whole_kernel, [vmem()] * 2, [], [pick, whole])

    pieces = 2

    def project(parts, piece):
        part_rows = parts[0].shape[0]
        cols = columns // pieces
        return pl.pallas_call(
            functools.partial(project_kernel, piece * cols),
            out_shape=[jax.ShapeDtypeStruct((2 * part_rows, cols), jnp.bfloat16)] * 2,
            in_specs=[smem()] + [vmem()] * 5,
            out_specs=[vmem()] * 2,
            scratch_shapes=[pltpu.VMEM((4 * part_rows, out_proj.shape[0]), jnp.bfloat16)],
            compiler_params=limit(24),
            cost_estimate=cost(2),
            name="project_out",
        )(z, *parts, out_proj)

    received = [packed[0]] + [flip(packed[k], "seq", k) for k in range(1, 4)]
    near_rows = attend(received[:2], 0)
    near_across = flip(near_rows, "seq", 2)
    far_rows = attend(received[2:], 2)
    near_across, far_rows = lax.optimization_barrier((near_across, far_rows))
    near = [near_rows, flip(near_rows, "seq", 1), near_across, flip(near_across, "seq", 1)]
    far_across = flip(far_rows, "seq", 2)
    first, second = project(near, 0), project(near, 1)
    relayed, _ = lax.optimization_barrier((far_across, second[0]))
    far = [far_rows, flip(far_rows, "seq", 1), far_across, flip(relayed, "seq", 1)]
    third, fourth = project(far, 0), project(far, 1)

    def swap(piece):
        return flip(piece[1], "head", 1)

    first_in, second_in = swap(first), swap(second)
    first_pair = add(first[0], first_in)
    first_cross = flip(first_pair, "head", 3)
    third_in, fourth_in = swap(third), swap(fourth)
    second_in, _ = lax.optimization_barrier((second_in, third[0]))
    second_pair = add(second[0], second_in)
    second_cross = flip(second_pair, "head", 3)
    first_cross, _ = lax.optimization_barrier((first_cross, fourth[0]))
    first_sum = add(first_pair, first_cross)
    first_other = flip(first_sum, "head", 1)
    third_pair = add(third[0], third_in)
    third_cross = flip(third_pair, "head", 3)
    second_sum = add(second_pair, second_cross)
    second_other = flip(second_sum, "head", 1)
    fourth_pair = add(fourth[0], fourth_in)
    fourth_cross = flip(fourth_pair, "head", 3)
    third_sum = add(third_pair, third_cross)
    third_other = flip(third_sum, "head", 1)
    fourth_sum = add(fourth_pair, fourth_cross)
    fourth_other = flip(fourth_sum, "head", 1)
    arrays = [first_sum, first_other, second_sum, second_other, third_sum, third_other, fourth_sum, fourth_other]
    scratch = [pltpu.VMEM((steps * sources * requests, columns), jnp.bfloat16)]
    kernel = functools.partial(order_kernel, 2)
    return order(kernel, [smem()] + [vmem()] * (1 + len(arrays)), scratch, [z, pick] + arrays)


def solution(mesh):
    return jax.shard_map(
        local,
        mesh=mesh,
        in_specs=(
            P(("groups", "seq"), None),
            P("groups", None),
            P("groups"),
            P(None, ("groups", "seq"), "head", None),
            P(None, ("groups", "seq"), "head", None),
            P(None, ("groups", "seq"), None),
            P("head", None, None),
            P("head", None, None),
            P("head", "seq"),
        ),
        out_specs=P(None, "groups", "seq"),
        check_vma=False,
    )
```

```python
import functools

import jax
import jax.numpy as jnp
from jax import lax
from jax.experimental import pallas as pl
from jax.experimental.pallas import tpu as pltpu
from jax.sharding import PartitionSpec as P

LATENT = 512
BLOCK = 256
LANES = 128
LOG2E = 1.4426950408889634
NEG = -1e30


def own_slots(decode_ref, slot_ref, me, sources, requests, per_pair):
    shift = requests.bit_length() - 1

    def one_source(s, carry):
        count = jnp.int32(0)
        for r in range(requests):
            row = decode_ref[s * requests + r]
            slot_ref[s * (per_pair + 1) + jnp.minimum(count, per_pair)] = row & (requests - 1)
            count = count + jnp.where((row >> shift) == me, 1, 0).astype(jnp.int32)
        return carry

    lax.fori_loop(0, sources, one_source, jnp.int32(0))


def pack_kernel(sizes, relative, me_ref, decode_ref, nope_ref, rope_ref, fresh_ref, after_ref, *rest):
    sources, per_pair, steps, heads, requests, fresh_rows = sizes
    out_refs, (slots, wide) = rest[:-2], rest[-2:]
    me = me_ref[0]
    rows = heads * steps
    half = rows // 2
    rope_base = per_pair * rows
    fresh_base = rope_base + per_pair * half
    own_slots(decode_ref, slots, me, sources, requests, per_pair)

    def one_dest(s, out_ref, e):
        for j in range(per_pair):
            row = slots[s * (per_pair + 1) + j]
            for t in range(steps):
                wide[2 * j, pl.ds(t, heads, stride=steps), :] = nope_ref[t, row].astype(jnp.float32)
                wide[2 * j + 1, pl.ds(t, heads, stride=steps), :] = jnp.concatenate(
                    [rope_ref[t, row].astype(jnp.float32)] * 2, axis=1
                )
        for j in range(per_pair):
            out_ref[e, j * rows : (j + 1) * rows, :] = wide[2 * j].astype(jnp.bfloat16)
            low = lax.broadcasted_iota(jnp.int32, (half, LANES), 1) < LANES // 2
            packed = jnp.where(low, wide[2 * j + 1, 0:half, :], wide[2 * j + 1, half : 2 * half, :])
            out_ref[e, rope_base + j * half : rope_base + (j + 1) * half, :] = packed.astype(jnp.bfloat16)

    if relative:
        dests = [me ^ k for k in range(sources)]
        for k in range(sources):
            one_dest(dests[k], out_refs[k], 0)
    else:
        dests = list(range(sources))

        def step(s, carry):
            one_dest(s, out_refs[0], s)
            return carry

        lax.fori_loop(0, sources, step, jnp.int32(0))
    shape = (sources * fresh_rows, steps * requests)
    row_id = lax.broadcasted_iota(jnp.int32, shape, 0)
    col_id = lax.broadcasted_iota(jnp.int32, shape, 1)
    wanted = jnp.full(shape, -1, jnp.int32)
    for k in range(sources):
        for j in range(per_pair):
            first = k * fresh_rows + j * steps
            here = (row_id >= first) & (row_id < first + steps)
            wanted = jnp.where(here, (row_id - first) * requests + slots[dests[k] * (per_pair + 1) + j], wanted)
    pick = jnp.where(col_id == wanted, 1.0, 0.0).astype(jnp.bfloat16)
    width = fresh_ref.shape[2]
    source_rows = jnp.concatenate([fresh_ref[t] for t in range(steps)], axis=0)
    picked = jnp.dot(pick, source_rows, preferred_element_type=jnp.float32).astype(jnp.bfloat16)
    for k in range(sources):
        for c in range(-(-width // LANES)):
            piece = picked[k * fresh_rows : (k + 1) * fresh_rows, c * LANES : min((c + 1) * LANES, width)]
            if piece.shape[1] < LANES:
                piece = jnp.concatenate([piece] * (LANES // piece.shape[1]), axis=1)
            first = fresh_base + c * fresh_rows
            if relative:
                out_refs[k][0, first : first + fresh_rows, :] = piece
            else:
                out_refs[0][k, first : first + fresh_rows, :] = piece


def attend_kernel(sizes, scale, relative, base, recv_count, me_ref, decode_ref, length_ref, *rest):
    sources, per_pair, steps, heads, requests, fresh_rows = sizes
    recv_refs = rest[:recv_count]
    (
        cache, key_up, value_up, out_ref,
        slot_offset, slot_length, owner_count, pair_slot, pair_start,
        queries, fresh, acc, run_max, run_sum, latent,
    ) = rest[recv_count:]
    owners = [(ref, e) for ref in recv_refs for e in range(ref.shape[0])]
    here = len(owners)
    slots = here * per_pair
    width, tokens = cache.shape
    rows = heads * steps
    half = rows // 2
    rope_base = per_pair * rows
    fresh_base = rope_base + per_pair * half
    group = 16 // steps
    shift = requests.bit_length() - 1
    factor = scale * LOG2E

    for e in range(here):
        ref, at = owners[e]
        for c in range(-(-width // LANES)):
            lanes = min(LANES, width - c * LANES)
            first = fresh_base + c * fresh_rows
            fresh[e * fresh_rows : (e + 1) * fresh_rows, c * LANES : c * LANES + lanes] = ref[
                at, first : first + fresh_rows, 0:lanes
            ]
        for j in range(per_pair):
            slot = e * per_pair + j
            first = rope_base + j * half
            piece = ref[at, first : first + half, :]
            queries[slot * rows : slot * rows + half, LATENT:width] = piece[:, 0 : width - LATENT]
            queries[slot * rows + half : (slot + 1) * rows, LATENT:width] = piece[:, LANES - (width - LATENT) :]

    inner_head = lax.broadcasted_iota(jnp.int32, (slots * 16, LANES), 0) // steps % group
    own_head = [jnp.where(inner_head == u, 1.0, 0.0).astype(jnp.bfloat16) for u in range(group)]
    for i in range(heads // group):
        tall = jnp.concatenate(
            [ref[at, j * rows + i * 16 : j * rows + (i + 1) * 16, :] for ref, at in owners for j in range(per_pair)],
            axis=0,
        )
        left = jnp.concatenate([tall * own_head[u] for u in range(group)], axis=1)
        right = jnp.concatenate([key_up[i * group + u] for u in range(group)], axis=0)
        res = jnp.dot(left, right, preferred_element_type=jnp.float32).astype(jnp.bfloat16)
        for slot in range(slots):
            queries[slot * rows + i * 16 : slot * rows + (i + 1) * 16, 0:LATENT] = res[slot * 16 : (slot + 1) * 16]

    me = me_ref[0]
    for o in range(sources):
        owner_count[o] = jnp.int32(0)
    total = jnp.int32(0)
    for r in range(requests):
        owner = decode_ref[me * requests + r] >> shift
        at = owner_count[owner]
        owner_count[owner] = at + 1
        e = (owner ^ me) - base if relative else owner
        slot = jnp.where((e >= 0) & (e < here), e * per_pair + at, slots)
        length = length_ref[me, r]
        slot_offset[slot] = total
        slot_length[slot] = length
        total = total + length
    count = jnp.int32(0)
    for slot in range(slots):
        start = slot_offset[slot] & ~(LANES - 1)
        end = slot_offset[slot] + slot_length[slot]
        for k in range(512 // BLOCK + 1):
            pair_slot[count] = jnp.int32(slot)
            pair_start[count] = start + k * BLOCK
            count = count + jnp.where(start + k * BLOCK < end, 1, 0).astype(jnp.int32)

    fresh_scores = (
        lax.dot_general(queries[...], fresh[...], (((1,), (1,)), ((), ())), preferred_element_type=jnp.float32) * factor
    )
    row_id = lax.broadcasted_iota(jnp.int32, (rows, here * fresh_rows), 0)
    col_id = lax.broadcasted_iota(jnp.int32, (rows, here * fresh_rows), 1)
    behind = row_id & (steps - 1)
    fresh_weights = []
    for slot in range(slots):
        first = (slot // per_pair) * fresh_rows + (slot % per_pair) * steps
        seen = (col_id >= first) & (col_id <= first + behind)
        scores = jnp.where(seen, fresh_scores[slot * rows : (slot + 1) * rows], NEG)
        top = jnp.max(scores, axis=1, keepdims=True)
        weights = jnp.exp2(scores - top)
        run_max[slot] = jnp.broadcast_to(top, (rows, LANES))
        run_sum[slot] = jnp.broadcast_to(jnp.sum(weights, axis=1, keepdims=True), (rows, LANES))
        fresh_weights.append(weights.astype(jnp.bfloat16))
    for slot in range(slots):
        acc[slot] = jnp.dot(fresh_weights[slot], fresh[:, 0:LATENT], preferred_element_type=jnp.float32)

    unroll = 4

    def some_pairs(i, carry):
        for u in range(unroll):
            p = i * unroll + u
            slot = pair_slot[jnp.minimum(p, count - 1)]
            start = pair_start[jnp.minimum(p, count - 1)]
            read = jnp.minimum(start, tokens - BLOCK)
            low = jnp.maximum(slot_offset[slot], start) - read
            high = jnp.minimum(slot_offset[slot] + slot_length[slot], start + BLOCK) - read
            high = jnp.where(p < count, high, low)
            q = queries[pl.ds(pl.multiple_of(slot * rows, 16), rows), :]
            keys = cache[:, pl.ds(pl.multiple_of(read, LANES), BLOCK)]
            scores = jnp.dot(q, keys, preferred_element_type=jnp.float32) * factor
            token = lax.broadcasted_iota(jnp.int32, scores.shape, 1)
            scores = jnp.where((token >= low) & (token < high), scores, NEG)
            top = jnp.max(scores, axis=1, keepdims=True)
            weights = jnp.exp2(scores - top)
            part_sum = jnp.broadcast_to(jnp.sum(weights, axis=1, keepdims=True), (rows, LANES))
            part = lax.dot_general(
                weights.astype(jnp.bfloat16),
                keys[0:LATENT],
                (((1,), (1,)), ((), ())),
                preferred_element_type=jnp.float32,
            )
            part_max = jnp.broadcast_to(top, (rows, LANES))
            old_max = run_max[slot]
            new_max = jnp.maximum(old_max, part_max)
            keep = jnp.exp2(old_max - new_max)
            add = jnp.exp2(part_max - new_max)
            run_max[slot] = new_max
            run_sum[slot] = run_sum[slot] * keep + part_sum * add
            for c in range(LATENT // LANES):
                cols = slice(c * LANES, (c + 1) * LANES)
                acc[slot, :, cols] = acc[slot, :, cols] * keep + part[:, cols] * add
        return carry

    lax.fori_loop(0, (count + unroll - 1) // unroll, some_pairs, jnp.int32(0))

    for slot in range(slots):
        inverse = 1.0 / run_sum[slot]
        for c in range(LATENT // LANES):
            cols = slice(c * LANES, (c + 1) * LANES)
            latent[slot * rows : (slot + 1) * rows, cols] = (acc[slot, :, cols] * inverse).astype(jnp.bfloat16)
    vdim = value_up.shape[2]
    for i in range(heads // group):
        left = jnp.concatenate(
            [latent[slot * rows + i * 16 : slot * rows + (i + 1) * 16, :] for slot in range(slots)], axis=0
        )
        right = jnp.concatenate([value_up[i * group + u] for u in range(group)], axis=1)
        res = jnp.dot(left, right, preferred_element_type=jnp.float32)
        for u in range(group):
            own = jnp.concatenate(
                [
                    res[slot * 16 + u * steps : slot * 16 + (u + 1) * steps, u * vdim : (u + 1) * vdim]
                    for slot in range(slots)
                ],
                axis=0,
            )
            head = i * group + u
            out_ref[:, head * vdim : (head + 1) * vdim] = own.astype(jnp.bfloat16)


def place_kernel(sizes, relative, me_ref, decode_ref, out_ref, owner_count, place):
    sources, per_pair, steps, requests = sizes
    me = me_ref[0]
    rows = sources * requests
    shift = requests.bit_length() - 1

    def one_source(s, carry):
        for o in range(sources):
            owner_count[o] = jnp.int32(0)
        for r in range(requests):
            row = decode_ref[s * requests + r]
            owner = row >> shift
            at = owner_count[owner]
            owner_count[owner] = at + 1
            if relative:
                e = owner ^ s
                at_row = (e >> 1) * (2 * sources * per_pair) + (me ^ s) * (2 * per_pair) + (e & 1) * per_pair + at
            else:
                at_row = s * requests + owner * per_pair + at
            place[row] = at_row * steps
        return carry

    lax.fori_loop(0, sources, one_source, jnp.int32(0))
    narrow = (rows, LANES)
    row_id = lax.broadcasted_iota(jnp.int32, narrow, 0)

    def put(b, wanted):
        return jnp.where(row_id == b, place[b], wanted)

    wanted = lax.fori_loop(0, rows, put, jnp.zeros(narrow, jnp.int32), unroll=8)[:, 0:1]
    col_id = lax.broadcasted_iota(jnp.int32, (rows, rows * steps), 1)
    for t in range(steps):
        out_ref[t] = jnp.where(col_id == wanted + t, 1.0, 0.0).astype(jnp.bfloat16)


def keeps_upper(z_ref):
    return (z_ref[0] == 1) | (z_ref[0] == 2)


def order_kernel(halves, z_ref, pick_ref, *rest):
    pieces, out_ref, x = rest[:-2], rest[-2], rest[-1]
    upper = keeps_upper(z_ref)
    rows = x.shape[0] // (2 * halves)
    each = len(pieces) // (2 * halves)
    cols = x.shape[1] // each

    def assemble(first, second):
        for h in range(halves):
            for c in range(each):
                at = slice(c * cols, (c + 1) * cols)
                i = 2 * (h * each + c)
                x[2 * h * rows : (2 * h + 1) * rows, at] = pieces[i + first][...]
                x[(2 * h + 1) * rows : (2 * h + 2) * rows, at] = pieces[i + second][...]

    pl.when(upper)(lambda: assemble(1, 0))
    pl.when(jnp.logical_not(upper))(lambda: assemble(0, 1))
    for t in range(pick_ref.shape[0]):
        out_ref[t] = jnp.dot(pick_ref[t], x[...], preferred_element_type=jnp.float32).astype(jnp.bfloat16)


def order_whole_kernel(pick_ref, x_ref, out_ref):
    for t in range(pick_ref.shape[0]):
        out_ref[t] = jnp.dot(pick_ref[t], x_ref[...], preferred_element_type=jnp.float32).astype(jnp.bfloat16)


def project_kernel(first_col, z_ref, *rest):
    parts, weight, keep, send, x = rest[:4], rest[4], rest[5], rest[6], rest[7]
    rows = parts[0].shape[0]
    upper = keeps_upper(z_ref)

    def assemble(order):
        for place, q in enumerate(order):
            x[place * rows : (place + 1) * rows, :] = parts[q][...]

    pl.when(upper)(lambda: assemble((2, 3, 0, 1)))
    pl.when(jnp.logical_not(upper))(lambda: assemble((0, 1, 2, 3)))
    cols = keep.shape[1]
    for c in range(0, cols, BLOCK):
        n = min(BLOCK, cols - c)
        tile = jnp.dot(x[...], weight[:, first_col + c : first_col + c + n], preferred_element_type=jnp.float32)
        tile = tile.astype(jnp.bfloat16)
        keep[:, c : c + n] = tile[: 2 * rows]
        send[:, c : c + n] = tile[2 * rows :]


def smem():
    return pl.BlockSpec(memory_space=pltpu.SMEM)


def vmem():
    return pl.BlockSpec(memory_space=pltpu.VMEM)


def anywhere():
    return pl.BlockSpec(memory_space=pl.ANY)


def limit(mib):
    return pltpu.CompilerParams(vmem_limit_bytes=mib * 1024 * 1024)


def cost(microseconds):
    return pl.CostEstimate(
        flops=int(microseconds * 1.0e9), bytes_accessed=int(microseconds * 3.0e6), transcendentals=0
    )


def flip(x, axis, distance):
    size = lax.axis_size(axis)
    return lax.ppermute(x, axis, [(i, i ^ distance) for i in range(size)])


def add(x, y):
    return (x.astype(jnp.float32) + y.astype(jnp.float32)).astype(jnp.bfloat16)


def local(latent_cache, lengths, decode_rows, q_nope, q_rope, new_latent, key_up, value_up, out_proj):
    sources = lax.axis_size("seq")
    head_devices = lax.axis_size("head")
    relative = sources == 4 and head_devices == 4
    requests = lengths.shape[1]
    per_pair = requests // sources
    tokens, width = latent_cache.shape
    steps, _, heads, nope = q_nope.shape
    scale = (nope + q_rope.shape[3]) ** (-0.5)
    fresh_rows = -(-per_pair * steps // 16) * 16
    rows = heads * steps
    columns = out_proj.shape[1]
    packed_rows = per_pair * rows + per_pair * rows // 2 + -(-width // LANES) * fresh_rows
    sizes = (sources, per_pair, steps, heads, requests, fresh_rows)
    me = lax.axis_index("seq").astype(jnp.int32).reshape(1)
    z = lax.axis_index("head").astype(jnp.int32).reshape(1)
    cache = latent_cache.T

    pick = pl.pallas_call(
        functools.partial(place_kernel, (sources, per_pair, steps, requests), relative),
        out_shape=jax.ShapeDtypeStruct((steps, sources * requests, steps * sources * requests), jnp.bfloat16),
        in_specs=[smem(), smem()],
        out_specs=vmem(),
        scratch_shapes=[pltpu.SMEM((sources,), jnp.int32), pltpu.SMEM((sources * requests,), jnp.int32)],
        compiler_params=limit(12),
        cost_estimate=cost(2),
        name="place_rows",
    )(me, decode_rows)

    outs, each = (sources, 1) if relative else (1, sources)
    packed = pl.pallas_call(
        functools.partial(pack_kernel, sizes, relative),
        out_shape=[jax.ShapeDtypeStruct((each, packed_rows, LANES), jnp.bfloat16)] * outs,
        in_specs=[smem(), smem(), vmem(), vmem(), vmem(), anywhere()],
        out_specs=[vmem()] * outs,
        scratch_shapes=[
            pltpu.SMEM((sources * (per_pair + 1),), jnp.int32),
            pltpu.VMEM((2 * per_pair, rows, LANES), jnp.float32),
        ],
        compiler_params=limit(8),
        cost_estimate=cost(6),
        name="pack_queries",
    )(me, decode_rows, q_nope, q_rope, new_latent, pick)

    def attend(received, base):
        here = sum(part.shape[0] for part in received)
        slots = here * per_pair
        pairs = slots * (512 // BLOCK + 1) + 1
        return pl.pallas_call(
            functools.partial(attend_kernel, sizes, scale, relative, base, len(received)),
            out_shape=jax.ShapeDtypeStruct((slots * steps, heads * value_up.shape[2]), jnp.bfloat16),
            in_specs=[smem(), smem(), smem()] + [vmem()] * (len(received) + 3),
            out_specs=vmem(),
            scratch_shapes=[
                pltpu.SMEM((slots + 1,), jnp.int32),
                pltpu.SMEM((slots + 1,), jnp.int32),
                pltpu.SMEM((sources,), jnp.int32),
                pltpu.SMEM((pairs,), jnp.int32),
                pltpu.SMEM((pairs,), jnp.int32),
                pltpu.VMEM((slots * rows, width), jnp.bfloat16),
                pltpu.VMEM((here * fresh_rows, width), jnp.bfloat16),
                pltpu.VMEM((slots, rows, LATENT), jnp.float32),
                pltpu.VMEM((slots, rows, LANES), jnp.float32),
                pltpu.VMEM((slots, rows, LANES), jnp.float32),
                pltpu.VMEM((slots * rows, LATENT), jnp.bfloat16),
            ],
            compiler_params=limit(14),
            cost_estimate=cost(8),
            name="attend",
        )(me, decode_rows, lengths, *received, cache, key_up, value_up)

    def order(kernel, in_specs, scratch, arrays):
        return pl.pallas_call(
            kernel,
            out_shape=jax.ShapeDtypeStruct((steps, sources * requests, columns), jnp.bfloat16),
            in_specs=in_specs,
            out_specs=vmem(),
            scratch_shapes=scratch,
            compiler_params=limit(16),
            cost_estimate=cost(2),
            name="order_rows",
        )(*arrays)

    if not relative:
        received = lax.all_to_all(packed[0], "seq", split_axis=0, concat_axis=0, tiled=True)
        every_row = lax.all_gather(attend([received], 0), "seq", axis=0, tiled=True)
        partial_value = jnp.dot(every_row, out_proj, preferred_element_type=jnp.float32).astype(jnp.bfloat16)
        shares = lax.all_to_all(partial_value, "head", split_axis=0, concat_axis=0, tiled=True)
        shares = shares.reshape(head_devices, -1, columns)
        summed = jnp.sum(shares.astype(jnp.float32), axis=0).astype(jnp.bfloat16)
        whole = lax.all_gather(summed, "head", axis=0, tiled=True)
        return order(order_whole_kernel, [vmem()] * 2, [], [pick, whole])

    pieces = 2

    def project(parts, piece):
        part_rows = parts[0].shape[0]
        cols = columns // pieces
        return pl.pallas_call(
            functools.partial(project_kernel, piece * cols),
            out_shape=[jax.ShapeDtypeStruct((2 * part_rows, cols), jnp.bfloat16)] * 2,
            in_specs=[smem()] + [vmem()] * 5,
            out_specs=[vmem()] * 2,
            scratch_shapes=[pltpu.VMEM((4 * part_rows, out_proj.shape[0]), jnp.bfloat16)],
            compiler_params=limit(10),
            cost_estimate=cost(2),
            name="project_out",
        )(z, *parts, out_proj)

    received = [packed[0]] + [flip(packed[k], "seq", k) for k in range(1, 4)]
    near_rows = attend(received[:2], 0)
    near_across = flip(near_rows, "seq", 2)
    far_rows = attend(received[2:], 2)
    near_across, far_rows = lax.optimization_barrier((near_across, far_rows))
    near = [near_rows, flip(near_rows, "seq", 1), near_across, flip(near_across, "seq", 1)]
    far_across = flip(far_rows, "seq", 2)
    first, second = project(near, 0), project(near, 1)
    far = [far_rows, flip(far_rows, "seq", 1), far_across, flip(far_across, "seq", 1)]

    def swap(piece):
        return flip(piece[1], "head", 1)

    first_in, second_in = swap(first), swap(second)
    first_pair = add(first[0], first_in)
    first_cross = flip(first_pair, "head", 3)
    second_pair = add(second[0], second_in)
    second_cross = flip(second_pair, "head", 3)

    third = project(far, 0)
    third_in = swap(third)
    fourth = project(far, 1)
    fourth_in = swap(fourth)
    first_cross, _ = lax.optimization_barrier((first_cross, fourth[0]))
    first_sum = add(first_pair, first_cross)
    first_other = flip(first_sum, "head", 1)
    third_pair = add(third[0], third_in)
    third_cross = flip(third_pair, "head", 3)
    second_sum = add(second_pair, second_cross)
    second_other = flip(second_sum, "head", 1)
    fourth_pair = add(fourth[0], fourth_in)
    fourth_cross = flip(fourth_pair, "head", 3)
    third_sum = add(third_pair, third_cross)
    third_other = flip(third_sum, "head", 1)
    fourth_sum = add(fourth_pair, fourth_cross)
    fourth_other = flip(fourth_sum, "head", 1)
    arrays = [first_sum, first_other, second_sum, second_other, third_sum, third_other, fourth_sum, fourth_other]
    scratch = [pltpu.VMEM((steps * sources * requests, columns), jnp.bfloat16)]
    kernel = functools.partial(order_kernel, 2)
    return order(kernel, [smem()] + [vmem()] * (1 + len(arrays)), scratch, [z, pick] + arrays)


def solution(mesh):
    return jax.shard_map(
        local,
        mesh=mesh,
        in_specs=(
            P(("groups", "seq"), None),
            P("groups", None),
            P("groups"),
            P(None, ("groups", "seq"), "head", None),
            P(None, ("groups", "seq"), "head", None),
            P(None, ("groups", "seq"), None),
            P("head", None, None),
            P("head", None, None),
            P("head", "seq"),
        ),
        out_specs=P(None, "groups", "seq"),
        check_vma=False,
    )
```

```python
import functools

import jax
import jax.numpy as jnp
from jax import lax
from jax.experimental import pallas as pl
from jax.experimental.pallas import tpu as pltpu
from jax.sharding import PartitionSpec as P

LATENT = 512
BLOCK = 256
LANES = 128
LOG2E = 1.4426950408889634
NEG = -1e30
PLACES = 1024


def own_slots(decode_ref, slot_ref, me, sources, requests, per_pair):
    shift = requests.bit_length() - 1

    def one_source(s, carry):
        count = jnp.int32(0)
        for r in range(requests):
            row = decode_ref[s * requests + r]
            slot_ref[s * (per_pair + 1) + jnp.minimum(count, per_pair)] = row & (requests - 1)
            count = count + jnp.where((row >> shift) == me, 1, 0).astype(jnp.int32)
        return carry

    lax.fori_loop(0, sources, one_source, jnp.int32(0))


def pack_kernel(sizes, relative, ids_ref, decode_ref, nope_ref, rope_ref, fresh_ref, after_ref, *rest):
    sources, per_pair, steps, heads, requests, fresh_rows = sizes
    out_refs, (slots, wide) = rest[:-2], rest[-2:]
    me = ids_ref[0] & (PLACES - 1)
    rows = heads * steps
    half = rows // 2
    rope_base = per_pair * rows
    fresh_base = rope_base + per_pair * half
    own_slots(decode_ref, slots, me, sources, requests, per_pair)

    def one_dest(s, out_ref, e):
        for j in range(per_pair):
            row = slots[s * (per_pair + 1) + j]
            for t in range(steps):
                wide[2 * j, pl.ds(t, heads, stride=steps), :] = nope_ref[t, row].astype(jnp.float32)
                wide[2 * j + 1, pl.ds(t, heads, stride=steps), :] = jnp.concatenate(
                    [rope_ref[t, row].astype(jnp.float32)] * 2, axis=1
                )
        for j in range(per_pair):
            out_ref[e, j * rows : (j + 1) * rows, :] = wide[2 * j].astype(jnp.bfloat16)
            low = lax.broadcasted_iota(jnp.int32, (half, LANES), 1) < LANES // 2
            packed = jnp.where(low, wide[2 * j + 1, 0:half, :], wide[2 * j + 1, half : 2 * half, :])
            out_ref[e, rope_base + j * half : rope_base + (j + 1) * half, :] = packed.astype(jnp.bfloat16)

    if relative:
        dests = [me ^ k for k in range(sources)]
        for k in range(sources):
            one_dest(dests[k], out_refs[k], 0)
    else:
        dests = list(range(sources))

        def step(s, carry):
            one_dest(s, out_refs[0], s)
            return carry

        lax.fori_loop(0, sources, step, jnp.int32(0))
    shape = (sources * fresh_rows, steps * requests)
    row_id = lax.broadcasted_iota(jnp.int32, shape, 0)
    col_id = lax.broadcasted_iota(jnp.int32, shape, 1)
    wanted = jnp.full(shape, -1, jnp.int32)
    for k in range(sources):
        for j in range(per_pair):
            first = k * fresh_rows + j * steps
            here = (row_id >= first) & (row_id < first + steps)
            wanted = jnp.where(here, (row_id - first) * requests + slots[dests[k] * (per_pair + 1) + j], wanted)
    pick = jnp.where(col_id == wanted, 1.0, 0.0).astype(jnp.bfloat16)
    width = fresh_ref.shape[2]
    source_rows = jnp.concatenate([fresh_ref[t] for t in range(steps)], axis=0)
    picked = jnp.dot(pick, source_rows, preferred_element_type=jnp.float32).astype(jnp.bfloat16)
    for k in range(sources):
        for c in range(-(-width // LANES)):
            piece = picked[k * fresh_rows : (k + 1) * fresh_rows, c * LANES : min((c + 1) * LANES, width)]
            if piece.shape[1] < LANES:
                piece = jnp.concatenate([piece] * (LANES // piece.shape[1]), axis=1)
            first = fresh_base + c * fresh_rows
            if relative:
                out_refs[k][0, first : first + fresh_rows, :] = piece
            else:
                out_refs[0][k, first : first + fresh_rows, :] = piece


def attend_kernel(sizes, scale, relative, base, recv_count, ids_ref, decode_ref, length_ref, *rest):
    sources, per_pair, steps, heads, requests, fresh_rows = sizes
    recv_refs = rest[:recv_count]
    (
        cache, key_up, value_up, out_ref,
        slot_offset, slot_length, owner_count, pair_slot, pair_start,
        queries, fresh, acc, run_max, run_sum, latent,
    ) = rest[recv_count:]
    owners = [(ref, e) for ref in recv_refs for e in range(ref.shape[0])]
    here = len(owners)
    slots = here * per_pair
    width, tokens = cache.shape
    rows = heads * steps
    half = rows // 2
    rope_base = per_pair * rows
    fresh_base = rope_base + per_pair * half
    group = 16 // steps
    shift = requests.bit_length() - 1
    factor = scale * LOG2E

    for e in range(here):
        ref, at = owners[e]
        for c in range(-(-width // LANES)):
            lanes = min(LANES, width - c * LANES)
            first = fresh_base + c * fresh_rows
            fresh[e * fresh_rows : (e + 1) * fresh_rows, c * LANES : c * LANES + lanes] = ref[
                at, first : first + fresh_rows, 0:lanes
            ]
        for j in range(per_pair):
            slot = e * per_pair + j
            first = rope_base + j * half
            piece = ref[at, first : first + half, :]
            queries[slot * rows : slot * rows + half, LATENT:width] = piece[:, 0 : width - LATENT]
            queries[slot * rows + half : (slot + 1) * rows, LATENT:width] = piece[:, LANES - (width - LATENT) :]

    inner_head = lax.broadcasted_iota(jnp.int32, (slots * 16, LANES), 0) // steps % group
    own_head = [jnp.where(inner_head == u, 1.0, 0.0).astype(jnp.bfloat16) for u in range(group)]
    for i in range(heads // group):
        tall = jnp.concatenate(
            [ref[at, j * rows + i * 16 : j * rows + (i + 1) * 16, :] for ref, at in owners for j in range(per_pair)],
            axis=0,
        )
        left = jnp.concatenate([tall * own_head[u] for u in range(group)], axis=1)
        right = jnp.concatenate([key_up[i * group + u] for u in range(group)], axis=0)
        res = jnp.dot(left, right, preferred_element_type=jnp.float32).astype(jnp.bfloat16)
        for slot in range(slots):
            queries[slot * rows + i * 16 : slot * rows + (i + 1) * 16, 0:LATENT] = res[slot * 16 : (slot + 1) * 16]

    me = ids_ref[0] & (PLACES - 1)
    for o in range(sources):
        owner_count[o] = jnp.int32(0)
    total = jnp.int32(0)
    for r in range(requests):
        owner = decode_ref[me * requests + r] >> shift
        at = owner_count[owner]
        owner_count[owner] = at + 1
        e = (owner ^ me) - base if relative else owner
        slot = jnp.where((e >= 0) & (e < here), e * per_pair + at, slots)
        length = length_ref[me, r]
        slot_offset[slot] = total
        slot_length[slot] = length
        total = total + length
    count = jnp.int32(0)
    for slot in range(slots):
        start = slot_offset[slot] & ~(LANES - 1)
        end = slot_offset[slot] + slot_length[slot]
        for k in range(512 // BLOCK + 1):
            pair_slot[count] = jnp.int32(slot)
            pair_start[count] = start + k * BLOCK
            count = count + jnp.where(start + k * BLOCK < end, 1, 0).astype(jnp.int32)

    fresh_scores = (
        lax.dot_general(queries[...], fresh[...], (((1,), (1,)), ((), ())), preferred_element_type=jnp.float32) * factor
    )
    row_id = lax.broadcasted_iota(jnp.int32, (rows, here * fresh_rows), 0)
    col_id = lax.broadcasted_iota(jnp.int32, (rows, here * fresh_rows), 1)
    behind = row_id & (steps - 1)
    fresh_weights = []
    for slot in range(slots):
        first = (slot // per_pair) * fresh_rows + (slot % per_pair) * steps
        seen = (col_id >= first) & (col_id <= first + behind)
        scores = jnp.where(seen, fresh_scores[slot * rows : (slot + 1) * rows], NEG)
        top = jnp.max(scores, axis=1, keepdims=True)
        weights = jnp.exp2(scores - top)
        run_max[slot] = jnp.broadcast_to(top, (rows, LANES))
        run_sum[slot] = jnp.broadcast_to(jnp.sum(weights, axis=1, keepdims=True), (rows, LANES))
        fresh_weights.append(weights.astype(jnp.bfloat16))
    for slot in range(slots):
        acc[slot] = jnp.dot(fresh_weights[slot], fresh[:, 0:LATENT], preferred_element_type=jnp.float32)

    unroll = 4

    def some_pairs(i, carry):
        for u in range(unroll):
            p = i * unroll + u
            slot = pair_slot[jnp.minimum(p, count - 1)]
            start = pair_start[jnp.minimum(p, count - 1)]
            read = jnp.minimum(start, tokens - BLOCK)
            low = jnp.maximum(slot_offset[slot], start) - read
            high = jnp.minimum(slot_offset[slot] + slot_length[slot], start + BLOCK) - read
            high = jnp.where(p < count, high, low)
            q = queries[pl.ds(pl.multiple_of(slot * rows, 16), rows), :]
            keys = cache[:, pl.ds(pl.multiple_of(read, LANES), BLOCK)]
            scores = jnp.dot(q, keys, preferred_element_type=jnp.float32) * factor
            token = lax.broadcasted_iota(jnp.int32, scores.shape, 1)
            scores = jnp.where((token >= low) & (token < high), scores, NEG)
            top = jnp.max(scores, axis=1, keepdims=True)
            weights = jnp.exp2(scores - top)
            part_sum = jnp.broadcast_to(jnp.sum(weights, axis=1, keepdims=True), (rows, LANES))
            part = lax.dot_general(
                weights.astype(jnp.bfloat16),
                keys[0:LATENT],
                (((1,), (1,)), ((), ())),
                preferred_element_type=jnp.float32,
            )
            part_max = jnp.broadcast_to(top, (rows, LANES))
            old_max = run_max[slot]
            new_max = jnp.maximum(old_max, part_max)
            keep = jnp.exp2(old_max - new_max)
            add = jnp.exp2(part_max - new_max)
            run_max[slot] = new_max
            run_sum[slot] = run_sum[slot] * keep + part_sum * add
            for c in range(LATENT // LANES):
                cols = slice(c * LANES, (c + 1) * LANES)
                acc[slot, :, cols] = acc[slot, :, cols] * keep + part[:, cols] * add
        return carry

    lax.fori_loop(0, (count + unroll - 1) // unroll, some_pairs, jnp.int32(0))

    for slot in range(slots):
        inverse = 1.0 / run_sum[slot]
        for c in range(LATENT // LANES):
            cols = slice(c * LANES, (c + 1) * LANES)
            latent[slot * rows : (slot + 1) * rows, cols] = (acc[slot, :, cols] * inverse).astype(jnp.bfloat16)
    vdim = value_up.shape[2]
    for i in range(heads // group):
        left = jnp.concatenate(
            [latent[slot * rows + i * 16 : slot * rows + (i + 1) * 16, :] for slot in range(slots)], axis=0
        )
        right = jnp.concatenate([value_up[i * group + u] for u in range(group)], axis=1)
        res = jnp.dot(left, right, preferred_element_type=jnp.float32)
        for u in range(group):
            own = jnp.concatenate(
                [
                    res[slot * 16 + u * steps : slot * 16 + (u + 1) * steps, u * vdim : (u + 1) * vdim]
                    for slot in range(slots)
                ],
                axis=0,
            )
            head = i * group + u
            out_ref[:, head * vdim : (head + 1) * vdim] = own.astype(jnp.bfloat16)


def place_kernel(sizes, relative, ids_ref, decode_ref, out_ref, owner_count, place):
    sources, per_pair, steps, requests = sizes
    me = ids_ref[0] & (PLACES - 1)
    rows = sources * requests
    shift = requests.bit_length() - 1

    def one_source(s, carry):
        for o in range(sources):
            owner_count[o] = jnp.int32(0)
        for r in range(requests):
            row = decode_ref[s * requests + r]
            owner = row >> shift
            at = owner_count[owner]
            owner_count[owner] = at + 1
            if relative:
                e = owner ^ s
                at_row = (e >> 1) * (2 * sources * per_pair) + (me ^ s) * (2 * per_pair) + (e & 1) * per_pair + at
            else:
                at_row = s * requests + owner * per_pair + at
            place[row] = at_row * steps
        return carry

    lax.fori_loop(0, sources, one_source, jnp.int32(0))
    narrow = (rows, LANES)
    row_id = lax.broadcasted_iota(jnp.int32, narrow, 0)

    def put(b, wanted):
        return jnp.where(row_id == b, place[b], wanted)

    wanted = lax.fori_loop(0, rows, put, jnp.zeros(narrow, jnp.int32), unroll=8)[:, 0:1]
    col_id = lax.broadcasted_iota(jnp.int32, (rows, rows * steps), 1)
    for t in range(steps):
        out_ref[t] = jnp.where(col_id == wanted + t, 1.0, 0.0).astype(jnp.bfloat16)


def keeps_upper(ids_ref):
    z = ids_ref[0] // PLACES
    return (z == 1) | (z == 2)


def order_kernel(halves, ids_ref, pick_ref, *rest):
    pieces, out_ref, x = rest[:-2], rest[-2], rest[-1]
    upper = keeps_upper(ids_ref)
    rows = x.shape[0] // (2 * halves)
    each = len(pieces) // (2 * halves)
    cols = x.shape[1] // each

    def assemble(first, second):
        for h in range(halves):
            for c in range(each):
                at = slice(c * cols, (c + 1) * cols)
                i = 2 * (h * each + c)
                x[2 * h * rows : (2 * h + 1) * rows, at] = pieces[i + first][...]
                x[(2 * h + 1) * rows : (2 * h + 2) * rows, at] = pieces[i + second][...]

    pl.when(upper)(lambda: assemble(1, 0))
    pl.when(jnp.logical_not(upper))(lambda: assemble(0, 1))
    for t in range(pick_ref.shape[0]):
        out_ref[t] = jnp.dot(pick_ref[t], x[...], preferred_element_type=jnp.float32).astype(jnp.bfloat16)


def order_whole_kernel(pick_ref, x_ref, out_ref):
    for t in range(pick_ref.shape[0]):
        out_ref[t] = jnp.dot(pick_ref[t], x_ref[...], preferred_element_type=jnp.float32).astype(jnp.bfloat16)


def project_kernel(first_col, ids_ref, *rest):
    parts, weight, keep, send, x = rest[:4], rest[4], rest[5], rest[6], rest[7]
    rows = parts[0].shape[0]
    upper = keeps_upper(ids_ref)

    def assemble(order):
        for place, q in enumerate(order):
            x[place * rows : (place + 1) * rows, :] = parts[q][...]

    pl.when(upper)(lambda: assemble((2, 3, 0, 1)))
    pl.when(jnp.logical_not(upper))(lambda: assemble((0, 1, 2, 3)))
    cols = keep.shape[1]
    for c in range(0, cols, BLOCK):
        n = min(BLOCK, cols - c)
        tile = jnp.dot(x[...], weight[:, first_col + c : first_col + c + n], preferred_element_type=jnp.float32)
        tile = tile.astype(jnp.bfloat16)
        keep[:, c : c + n] = tile[: 2 * rows]
        send[:, c : c + n] = tile[2 * rows :]


def smem():
    return pl.BlockSpec(memory_space=pltpu.SMEM)


def vmem():
    return pl.BlockSpec(memory_space=pltpu.VMEM)


def anywhere():
    return pl.BlockSpec(memory_space=pl.ANY)


def limit(mib):
    return pltpu.CompilerParams(vmem_limit_bytes=mib * 1024 * 1024)


def cost(microseconds):
    return pl.CostEstimate(
        flops=int(microseconds * 1.0e9), bytes_accessed=int(microseconds * 3.0e6), transcendentals=0
    )


def flip(x, axis, distance):
    size = lax.axis_size(axis)
    return lax.ppermute(x, axis, [(i, i ^ distance) for i in range(size)])


def add(x, y):
    return (x.astype(jnp.float32) + y.astype(jnp.float32)).astype(jnp.bfloat16)


def local(latent_cache, lengths, decode_rows, q_nope, q_rope, new_latent, key_up, value_up, out_proj):
    sources = lax.axis_size("seq")
    head_devices = lax.axis_size("head")
    relative = sources == 4 and head_devices == 4
    requests = lengths.shape[1]
    per_pair = requests // sources
    tokens, width = latent_cache.shape
    steps, _, heads, nope = q_nope.shape
    scale = (nope + q_rope.shape[3]) ** (-0.5)
    fresh_rows = -(-per_pair * steps // 16) * 16
    rows = heads * steps
    columns = out_proj.shape[1]
    packed_rows = per_pair * rows + per_pair * rows // 2 + -(-width // LANES) * fresh_rows
    sizes = (sources, per_pair, steps, heads, requests, fresh_rows)
    ids = (lax.axis_index("seq") + PLACES * lax.axis_index("head")).astype(jnp.int32).reshape(1)
    cache = latent_cache.T

    pick = pl.pallas_call(
        functools.partial(place_kernel, (sources, per_pair, steps, requests), relative),
        out_shape=jax.ShapeDtypeStruct((steps, sources * requests, steps * sources * requests), jnp.bfloat16),
        in_specs=[smem(), smem()],
        out_specs=vmem(),
        scratch_shapes=[pltpu.SMEM((sources,), jnp.int32), pltpu.SMEM((sources * requests,), jnp.int32)],
        compiler_params=limit(12),
        cost_estimate=cost(2),
        name="place_rows",
    )(ids, decode_rows)

    outs, each = (sources, 1) if relative else (1, sources)
    packed = pl.pallas_call(
        functools.partial(pack_kernel, sizes, relative),
        out_shape=[jax.ShapeDtypeStruct((each, packed_rows, LANES), jnp.bfloat16)] * outs,
        in_specs=[smem(), smem(), vmem(), vmem(), vmem(), anywhere()],
        out_specs=[vmem()] * outs,
        scratch_shapes=[
            pltpu.SMEM((sources * (per_pair + 1),), jnp.int32),
            pltpu.VMEM((2 * per_pair, rows, LANES), jnp.float32),
        ],
        compiler_params=limit(8),
        cost_estimate=cost(6),
        name="pack_queries",
    )(ids, decode_rows, q_nope, q_rope, new_latent, pick)

    def attend(received, base):
        here = sum(part.shape[0] for part in received)
        slots = here * per_pair
        pairs = slots * (512 // BLOCK + 1) + 1
        return pl.pallas_call(
            functools.partial(attend_kernel, sizes, scale, relative, base, len(received)),
            out_shape=jax.ShapeDtypeStruct((slots * steps, heads * value_up.shape[2]), jnp.bfloat16),
            in_specs=[smem(), smem(), smem()] + [vmem()] * (len(received) + 3),
            out_specs=vmem(),
            scratch_shapes=[
                pltpu.SMEM((slots + 1,), jnp.int32),
                pltpu.SMEM((slots + 1,), jnp.int32),
                pltpu.SMEM((sources,), jnp.int32),
                pltpu.SMEM((pairs,), jnp.int32),
                pltpu.SMEM((pairs,), jnp.int32),
                pltpu.VMEM((slots * rows, width), jnp.bfloat16),
                pltpu.VMEM((here * fresh_rows, width), jnp.bfloat16),
                pltpu.VMEM((slots, rows, LATENT), jnp.float32),
                pltpu.VMEM((slots, rows, LANES), jnp.float32),
                pltpu.VMEM((slots, rows, LANES), jnp.float32),
                pltpu.VMEM((slots * rows, LATENT), jnp.bfloat16),
            ],
            compiler_params=limit(14),
            cost_estimate=cost(8),
            name="attend",
        )(ids, decode_rows, lengths, *received, cache, key_up, value_up)

    def order(kernel, in_specs, scratch, arrays):
        return pl.pallas_call(
            kernel,
            out_shape=jax.ShapeDtypeStruct((steps, sources * requests, columns), jnp.bfloat16),
            in_specs=in_specs,
            out_specs=vmem(),
            scratch_shapes=scratch,
            compiler_params=limit(16),
            cost_estimate=cost(2),
            name="order_rows",
        )(*arrays)

    if not relative:
        received = lax.all_to_all(packed[0], "seq", split_axis=0, concat_axis=0, tiled=True)
        every_row = lax.all_gather(attend([received], 0), "seq", axis=0, tiled=True)
        partial_value = jnp.dot(every_row, out_proj, preferred_element_type=jnp.float32).astype(jnp.bfloat16)
        shares = lax.all_to_all(partial_value, "head", split_axis=0, concat_axis=0, tiled=True)
        shares = shares.reshape(head_devices, -1, columns)
        summed = jnp.sum(shares.astype(jnp.float32), axis=0).astype(jnp.bfloat16)
        whole = lax.all_gather(summed, "head", axis=0, tiled=True)
        return order(order_whole_kernel, [vmem()] * 2, [], [pick, whole])

    pieces = 2

    def project(parts, piece):
        part_rows = parts[0].shape[0]
        cols = columns // pieces
        return pl.pallas_call(
            functools.partial(project_kernel, piece * cols),
            out_shape=[jax.ShapeDtypeStruct((2 * part_rows, cols), jnp.bfloat16)] * 2,
            in_specs=[smem()] + [vmem()] * 5,
            out_specs=[vmem()] * 2,
            scratch_shapes=[pltpu.VMEM((4 * part_rows, out_proj.shape[0]), jnp.bfloat16)],
            compiler_params=limit(10),
            cost_estimate=cost(2),
            name="project_out",
        )(ids, *parts, out_proj)

    received = [packed[0]] + [flip(packed[k], "seq", k) for k in range(1, 4)]
    near_rows = attend(received[:2], 0)
    near_across = flip(near_rows, "seq", 2)
    far_rows = attend(received[2:], 2)
    near_across, far_rows = lax.optimization_barrier((near_across, far_rows))
    near = [near_rows, flip(near_rows, "seq", 1), near_across, flip(near_across, "seq", 1)]
    far_across = flip(far_rows, "seq", 2)
    def after(value, *others):
        return lax.optimization_barrier((value,) + others)[0]

    def swap(piece):
        return flip(piece[1], "head", 1)

    first = project(near, 0)
    first_in = swap(first)
    second = project(near, 1)
    second_in = swap(second)
    far = [far_rows, flip(far_rows, "seq", 1), far_across, flip(far_across, "seq", 1)]
    first_pair = add(first[0], first_in)
    first_cross = flip(first_pair, "head", 3)
    second_pair = add(second[0], second_in)
    second_cross = flip(second_pair, "head", 3)
    third = project(far, 0)
    third_in = swap(third)
    fourth = project(far, 1)
    fourth_in = swap(fourth)
    first_cross = after(first_cross, fourth[0])
    second_cross = after(second_cross, fourth[0])
    third_pair = add(third[0], third_in)
    third_cross = flip(third_pair, "head", 3)
    fourth_pair = add(fourth[0], fourth_in)
    fourth_cross = flip(fourth_pair, "head", 3)
    first_sum = add(first_pair, first_cross)
    first_other = flip(first_sum, "head", 1)
    second_sum = add(second_pair, second_cross)
    second_other = flip(second_sum, "head", 1)
    third_sum = add(third_pair, third_cross)
    third_other = flip(third_sum, "head", 1)
    fourth_sum = add(fourth_pair, fourth_cross)
    fourth_other = flip(fourth_sum, "head", 1)
    arrays = [first_sum, first_other, second_sum, second_other, third_sum, third_other, fourth_sum, fourth_other]
    scratch = [pltpu.VMEM((steps * sources * requests, columns), jnp.bfloat16)]
    kernel = functools.partial(order_kernel, 2)
    return order(kernel, [smem()] + [vmem()] * (1 + len(arrays)), scratch, [ids, pick] + arrays)


def solution(mesh):
    return jax.shard_map(
        local,
        mesh=mesh,
        in_specs=(
            P(("groups", "seq"), None),
            P("groups", None),
            P("groups"),
            P(None, ("groups", "seq"), "head", None),
            P(None, ("groups", "seq"), "head", None),
            P(None, ("groups", "seq"), None),
            P("head", None, None),
            P("head", None, None),
            P("head", "seq"),
        ),
        out_specs=P(None, "groups", "seq"),
        check_vma=False,
    )
```

```python
import functools

import jax
import jax.numpy as jnp
from jax import lax
from jax.experimental import pallas as pl
from jax.experimental.pallas import tpu as pltpu
from jax.sharding import PartitionSpec as P

LATENT = 512
BLOCK = 256
LANES = 128
LOG2E = 1.4426950408889634
NEG = -1e30
PLACES = 1024


def own_slots(decode_ref, slot_ref, me, sources, requests, per_pair):
    shift = requests.bit_length() - 1

    def one_source(s, carry):
        count = jnp.int32(0)
        for r in range(requests):
            row = decode_ref[s * requests + r]
            slot_ref[s * (per_pair + 1) + jnp.minimum(count, per_pair)] = row & (requests - 1)
            count = count + jnp.where((row >> shift) == me, 1, 0).astype(jnp.int32)
        return carry

    lax.fori_loop(0, sources, one_source, jnp.int32(0))


def pack_kernel(sizes, relative, ids_ref, decode_ref, nope_ref, rope_ref, fresh_ref, after_ref, *rest):
    sources, per_pair, steps, heads, requests, fresh_rows = sizes
    out_refs, (slots, wide) = rest[:-2], rest[-2:]
    me = ids_ref[0] & (PLACES - 1)
    rows = heads * steps
    half = rows // 2
    rope_base = per_pair * rows
    fresh_base = rope_base + per_pair * half
    own_slots(decode_ref, slots, me, sources, requests, per_pair)

    def one_dest(s, out_ref, e):
        for j in range(per_pair):
            row = slots[s * (per_pair + 1) + j]
            for t in range(steps):
                wide[2 * j, pl.ds(t, heads, stride=steps), :] = nope_ref[t, row].astype(jnp.float32)
                wide[2 * j + 1, pl.ds(t, heads, stride=steps), :] = jnp.concatenate(
                    [rope_ref[t, row].astype(jnp.float32)] * 2, axis=1
                )
        for j in range(per_pair):
            out_ref[e, j * rows : (j + 1) * rows, :] = wide[2 * j].astype(jnp.bfloat16)
            low = lax.broadcasted_iota(jnp.int32, (half, LANES), 1) < LANES // 2
            packed = jnp.where(low, wide[2 * j + 1, 0:half, :], wide[2 * j + 1, half : 2 * half, :])
            out_ref[e, rope_base + j * half : rope_base + (j + 1) * half, :] = packed.astype(jnp.bfloat16)

    if relative:
        dests = [me ^ k for k in range(sources)]
        for k in range(sources):
            one_dest(dests[k], out_refs[k], 0)
    else:
        dests = list(range(sources))

        def step(s, carry):
            one_dest(s, out_refs[0], s)
            return carry

        lax.fori_loop(0, sources, step, jnp.int32(0))
    shape = (sources * fresh_rows, steps * requests)
    row_id = lax.broadcasted_iota(jnp.int32, shape, 0)
    col_id = lax.broadcasted_iota(jnp.int32, shape, 1)
    wanted = jnp.full(shape, -1, jnp.int32)
    for k in range(sources):
        for j in range(per_pair):
            first = k * fresh_rows + j * steps
            here = (row_id >= first) & (row_id < first + steps)
            wanted = jnp.where(here, (row_id - first) * requests + slots[dests[k] * (per_pair + 1) + j], wanted)
    pick = jnp.where(col_id == wanted, 1.0, 0.0).astype(jnp.bfloat16)
    width = fresh_ref.shape[2]
    source_rows = jnp.concatenate([fresh_ref[t] for t in range(steps)], axis=0)
    picked = jnp.dot(pick, source_rows, preferred_element_type=jnp.float32).astype(jnp.bfloat16)
    for k in range(sources):
        for c in range(-(-width // LANES)):
            piece = picked[k * fresh_rows : (k + 1) * fresh_rows, c * LANES : min((c + 1) * LANES, width)]
            if piece.shape[1] < LANES:
                piece = jnp.concatenate([piece] * (LANES // piece.shape[1]), axis=1)
            first = fresh_base + c * fresh_rows
            if relative:
                out_refs[k][0, first : first + fresh_rows, :] = piece
            else:
                out_refs[0][k, first : first + fresh_rows, :] = piece


def attend_kernel(sizes, scale, relative, base, recv_count, ids_ref, decode_ref, length_ref, *rest):
    sources, per_pair, steps, heads, requests, fresh_rows = sizes
    recv_refs = rest[:recv_count]
    (
        cache, key_up, value_up, out_ref,
        slot_offset, slot_length, owner_count, pair_slot, pair_start,
        queries, fresh, acc, run_max, run_sum, latent, even_scores, odd_scores,
    ) = rest[recv_count:]
    owners = [(ref, e) for ref in recv_refs for e in range(ref.shape[0])]
    here = len(owners)
    slots = here * per_pair
    width, tokens = cache.shape
    rows = heads * steps
    half = rows // 2
    rope_base = per_pair * rows
    fresh_base = rope_base + per_pair * half
    group = 16 // steps
    shift = requests.bit_length() - 1
    factor = scale * LOG2E

    for e in range(here):
        ref, at = owners[e]
        for c in range(-(-width // LANES)):
            lanes = min(LANES, width - c * LANES)
            first = fresh_base + c * fresh_rows
            fresh[e * fresh_rows : (e + 1) * fresh_rows, c * LANES : c * LANES + lanes] = ref[
                at, first : first + fresh_rows, 0:lanes
            ]
        for j in range(per_pair):
            slot = e * per_pair + j
            first = rope_base + j * half
            piece = ref[at, first : first + half, :]
            queries[slot * rows : slot * rows + half, LATENT:width] = piece[:, 0 : width - LATENT]
            queries[slot * rows + half : (slot + 1) * rows, LATENT:width] = piece[:, LANES - (width - LATENT) :]

    inner_head = lax.broadcasted_iota(jnp.int32, (slots * 16, LANES), 0) // steps % group
    own_head = [jnp.where(inner_head == u, 1.0, 0.0).astype(jnp.bfloat16) for u in range(group)]
    for i in range(heads // group):
        tall = jnp.concatenate(
            [ref[at, j * rows + i * 16 : j * rows + (i + 1) * 16, :] for ref, at in owners for j in range(per_pair)],
            axis=0,
        )
        left = jnp.concatenate([tall * own_head[u] for u in range(group)], axis=1)
        right = jnp.concatenate([key_up[i * group + u] for u in range(group)], axis=0)
        res = jnp.dot(left, right, preferred_element_type=jnp.float32).astype(jnp.bfloat16)
        for slot in range(slots):
            queries[slot * rows + i * 16 : slot * rows + (i + 1) * 16, 0:LATENT] = res[slot * 16 : (slot + 1) * 16]

    me = ids_ref[0] & (PLACES - 1)
    for o in range(sources):
        owner_count[o] = jnp.int32(0)
    total = jnp.int32(0)
    for r in range(requests):
        owner = decode_ref[me * requests + r] >> shift
        at = owner_count[owner]
        owner_count[owner] = at + 1
        e = (owner ^ me) - base if relative else owner
        slot = jnp.where((e >= 0) & (e < here), e * per_pair + at, slots)
        length = length_ref[me, r]
        slot_offset[slot] = total
        slot_length[slot] = length
        total = total + length
    count = jnp.int32(0)
    for slot in range(slots):
        start = slot_offset[slot] & ~(LANES - 1)
        end = slot_offset[slot] + slot_length[slot]
        for k in range(512 // BLOCK + 1):
            pair_slot[count] = jnp.int32(slot)
            pair_start[count] = start + k * BLOCK
            count = count + jnp.where(start + k * BLOCK < end, 1, 0).astype(jnp.int32)

    fresh_scores = (
        lax.dot_general(queries[...], fresh[...], (((1,), (1,)), ((), ())), preferred_element_type=jnp.float32) * factor
    )
    row_id = lax.broadcasted_iota(jnp.int32, (rows, here * fresh_rows), 0)
    col_id = lax.broadcasted_iota(jnp.int32, (rows, here * fresh_rows), 1)
    behind = row_id & (steps - 1)
    fresh_weights = []
    for slot in range(slots):
        first = (slot // per_pair) * fresh_rows + (slot % per_pair) * steps
        seen = (col_id >= first) & (col_id <= first + behind)
        scores = jnp.where(seen, fresh_scores[slot * rows : (slot + 1) * rows], NEG)
        top = jnp.max(scores, axis=1, keepdims=True)
        weights = jnp.exp2(scores - top)
        run_max[slot] = jnp.broadcast_to(top, (rows, LANES))
        run_sum[slot] = jnp.broadcast_to(jnp.sum(weights, axis=1, keepdims=True), (rows, LANES))
        fresh_weights.append(weights.astype(jnp.bfloat16))
    for slot in range(slots):
        acc[slot] = jnp.dot(fresh_weights[slot], fresh[:, 0:LATENT], preferred_element_type=jnp.float32)

    def make_scores(buffer, g):
        for u in range(2):
            p = jnp.minimum(g * 2 + u, count - 1)
            q = queries[pl.ds(pl.multiple_of(pair_slot[p] * rows, 16), rows), :]
            read = pl.multiple_of(jnp.minimum(pair_start[p], tokens - BLOCK), LANES)
            buffer[u] = jnp.dot(q, cache[:, pl.ds(read, BLOCK)], preferred_element_type=jnp.float32)

    token = lax.broadcasted_iota(jnp.int32, (1, BLOCK), 1)

    def take_scores(buffer, g):
        for u in range(2):
            p = jnp.minimum(g * 2 + u, count - 1)
            slot = pair_slot[p]
            start = pair_start[p]
            read = jnp.minimum(start, tokens - BLOCK)
            low = jnp.maximum(slot_offset[slot], start) - read
            high = jnp.minimum(slot_offset[slot] + slot_length[slot], start + BLOCK) - read
            high = jnp.where(g * 2 + u < count, high, low)
            bias = jnp.where((token >= low) & (token < high), 0.0, NEG)
            scores = buffer[u] * factor + bias
            top = jnp.max(scores, axis=1, keepdims=True)
            weights = jnp.exp2(scores - top)
            part_sum = jnp.broadcast_to(jnp.sum(weights, axis=1, keepdims=True), (rows, LANES))
            part = lax.dot_general(
                weights.astype(jnp.bfloat16),
                cache[0:LATENT, pl.ds(pl.multiple_of(read, LANES), BLOCK)],
                (((1,), (1,)), ((), ())),
                preferred_element_type=jnp.float32,
            )
            part_max = jnp.broadcast_to(top, (rows, LANES))
            old_max = run_max[slot]
            new_max = jnp.maximum(old_max, part_max)
            keep = jnp.exp2(old_max - new_max)
            add = jnp.exp2(part_max - new_max)
            run_max[slot] = new_max
            run_sum[slot] = run_sum[slot] * keep + part_sum * add
            for c in range(LATENT // LANES):
                cols = slice(c * LANES, (c + 1) * LANES)
                acc[slot, :, cols] = acc[slot, :, cols] * keep + part[:, cols] * add

    make_scores(even_scores, 0)

    def four_pairs(i, carry):
        make_scores(odd_scores, 2 * i + 1)
        take_scores(even_scores, 2 * i)
        make_scores(even_scores, 2 * i + 2)
        take_scores(odd_scores, 2 * i + 1)
        return carry

    lax.fori_loop(0, (count + 3) // 4, four_pairs, jnp.int32(0))

    for slot in range(slots):
        inverse = 1.0 / run_sum[slot]
        for c in range(LATENT // LANES):
            cols = slice(c * LANES, (c + 1) * LANES)
            latent[slot * rows : (slot + 1) * rows, cols] = (acc[slot, :, cols] * inverse).astype(jnp.bfloat16)
    vdim = value_up.shape[2]
    for i in range(heads // group):
        left = jnp.concatenate(
            [latent[slot * rows + i * 16 : slot * rows + (i + 1) * 16, :] for slot in range(slots)], axis=0
        )
        right = jnp.concatenate([value_up[i * group + u] for u in range(group)], axis=1)
        res = jnp.dot(left, right, preferred_element_type=jnp.float32)
        for u in range(group):
            own = jnp.concatenate(
                [
                    res[slot * 16 + u * steps : slot * 16 + (u + 1) * steps, u * vdim : (u + 1) * vdim]
                    for slot in range(slots)
                ],
                axis=0,
            )
            head = i * group + u
            out_ref[:, head * vdim : (head + 1) * vdim] = own.astype(jnp.bfloat16)


def place_kernel(sizes, relative, ids_ref, decode_ref, out_ref, owner_count, place):
    sources, per_pair, steps, requests = sizes
    me = ids_ref[0] & (PLACES - 1)
    rows = sources * requests
    shift = requests.bit_length() - 1

    def one_source(s, carry):
        for o in range(sources):
            owner_count[o] = jnp.int32(0)
        for r in range(requests):
            row = decode_ref[s * requests + r]
            owner = row >> shift
            at = owner_count[owner]
            owner_count[owner] = at + 1
            if relative:
                e = owner ^ s
                at_row = (e >> 1) * (2 * sources * per_pair) + (me ^ s) * (2 * per_pair) + (e & 1) * per_pair + at
            else:
                at_row = s * requests + owner * per_pair + at
            place[row] = at_row * steps
        return carry

    lax.fori_loop(0, sources, one_source, jnp.int32(0))
    narrow = (rows, LANES)
    row_id = lax.broadcasted_iota(jnp.int32, narrow, 0)

    def put(b, wanted):
        return jnp.where(row_id == b, place[b], wanted)

    wanted = lax.fori_loop(0, rows, put, jnp.zeros(narrow, jnp.int32), unroll=8)[:, 0:1]
    col_id = lax.broadcasted_iota(jnp.int32, (rows, rows * steps), 1)
    for t in range(steps):
        out_ref[t] = jnp.where(col_id == wanted + t, 1.0, 0.0).astype(jnp.bfloat16)


def keeps_upper(ids_ref):
    z = ids_ref[0] // PLACES
    return (z == 1) | (z == 2)


def order_kernel(halves, ids_ref, pick_ref, *rest):
    pieces, out_ref, x = rest[:-2], rest[-2], rest[-1]
    upper = keeps_upper(ids_ref)
    rows = x.shape[0] // (2 * halves)
    each = len(pieces) // (2 * halves)
    cols = x.shape[1] // each

    def assemble(first, second):
        for h in range(halves):
            for c in range(each):
                at = slice(c * cols, (c + 1) * cols)
                i = 2 * (h * each + c)
                x[2 * h * rows : (2 * h + 1) * rows, at] = pieces[i + first][...]
                x[(2 * h + 1) * rows : (2 * h + 2) * rows, at] = pieces[i + second][...]

    pl.when(upper)(lambda: assemble(1, 0))
    pl.when(jnp.logical_not(upper))(lambda: assemble(0, 1))
    for t in range(pick_ref.shape[0]):
        out_ref[t] = jnp.dot(pick_ref[t], x[...], preferred_element_type=jnp.float32).astype(jnp.bfloat16)


def order_whole_kernel(pick_ref, x_ref, out_ref):
    for t in range(pick_ref.shape[0]):
        out_ref[t] = jnp.dot(pick_ref[t], x_ref[...], preferred_element_type=jnp.float32).astype(jnp.bfloat16)


def project_kernel(first_col, ids_ref, *rest):
    parts, weight, keep, send, x = rest[:4], rest[4], rest[5], rest[6], rest[7]
    rows = parts[0].shape[0]
    upper = keeps_upper(ids_ref)

    def assemble(order):
        for place, q in enumerate(order):
            x[place * rows : (place + 1) * rows, :] = parts[q][...]

    pl.when(upper)(lambda: assemble((2, 3, 0, 1)))
    pl.when(jnp.logical_not(upper))(lambda: assemble((0, 1, 2, 3)))
    cols = keep.shape[1]
    for c in range(0, cols, BLOCK):
        n = min(BLOCK, cols - c)
        tile = jnp.dot(x[...], weight[:, first_col + c : first_col + c + n], preferred_element_type=jnp.float32)
        tile = tile.astype(jnp.bfloat16)
        keep[:, c : c + n] = tile[: 2 * rows]
        send[:, c : c + n] = tile[2 * rows :]


def smem():
    return pl.BlockSpec(memory_space=pltpu.SMEM)


def vmem():
    return pl.BlockSpec(memory_space=pltpu.VMEM)


def anywhere():
    return pl.BlockSpec(memory_space=pl.ANY)


def limit(mib):
    return pltpu.CompilerParams(vmem_limit_bytes=mib * 1024 * 1024)


def cost(microseconds):
    return pl.CostEstimate(
        flops=int(microseconds * 1.0e9), bytes_accessed=int(microseconds * 3.0e6), transcendentals=0
    )


def flip(x, axis, distance):
    size = lax.axis_size(axis)
    return lax.ppermute(x, axis, [(i, i ^ distance) for i in range(size)])


def add(x, y):
    return (x.astype(jnp.float32) + y.astype(jnp.float32)).astype(jnp.bfloat16)


def local(latent_cache, lengths, decode_rows, q_nope, q_rope, new_latent, key_up, value_up, out_proj):
    sources = lax.axis_size("seq")
    head_devices = lax.axis_size("head")
    relative = sources == 4 and head_devices == 4
    requests = lengths.shape[1]
    per_pair = requests // sources
    tokens, width = latent_cache.shape
    steps, _, heads, nope = q_nope.shape
    scale = (nope + q_rope.shape[3]) ** (-0.5)
    fresh_rows = -(-per_pair * steps // 16) * 16
    rows = heads * steps
    columns = out_proj.shape[1]
    packed_rows = per_pair * rows + per_pair * rows // 2 + -(-width // LANES) * fresh_rows
    sizes = (sources, per_pair, steps, heads, requests, fresh_rows)
    ids = (lax.axis_index("seq") + PLACES * lax.axis_index("head")).astype(jnp.int32).reshape(1)
    cache = latent_cache.T

    pick = pl.pallas_call(
        functools.partial(place_kernel, (sources, per_pair, steps, requests), relative),
        out_shape=jax.ShapeDtypeStruct((steps, sources * requests, steps * sources * requests), jnp.bfloat16),
        in_specs=[smem(), smem()],
        out_specs=vmem(),
        scratch_shapes=[pltpu.SMEM((sources,), jnp.int32), pltpu.SMEM((sources * requests,), jnp.int32)],
        compiler_params=limit(12),
        cost_estimate=cost(2),
        name="place_rows",
    )(ids, decode_rows)

    outs, each = (sources, 1) if relative else (1, sources)
    packed = pl.pallas_call(
        functools.partial(pack_kernel, sizes, relative),
        out_shape=[jax.ShapeDtypeStruct((each, packed_rows, LANES), jnp.bfloat16)] * outs,
        in_specs=[smem(), smem(), vmem(), vmem(), vmem(), anywhere()],
        out_specs=[vmem()] * outs,
        scratch_shapes=[
            pltpu.SMEM((sources * (per_pair + 1),), jnp.int32),
            pltpu.VMEM((2 * per_pair, rows, LANES), jnp.float32),
        ],
        compiler_params=limit(8),
        cost_estimate=cost(6),
        name="pack_queries",
    )(ids, decode_rows, q_nope, q_rope, new_latent, pick)

    def attend(received, base):
        here = sum(part.shape[0] for part in received)
        slots = here * per_pair
        pairs = slots * (512 // BLOCK + 1) + 1
        return pl.pallas_call(
            functools.partial(attend_kernel, sizes, scale, relative, base, len(received)),
            out_shape=jax.ShapeDtypeStruct((slots * steps, heads * value_up.shape[2]), jnp.bfloat16),
            in_specs=[smem(), smem(), smem()] + [vmem()] * (len(received) + 3),
            out_specs=vmem(),
            scratch_shapes=[
                pltpu.SMEM((slots + 1,), jnp.int32),
                pltpu.SMEM((slots + 1,), jnp.int32),
                pltpu.SMEM((sources,), jnp.int32),
                pltpu.SMEM((pairs,), jnp.int32),
                pltpu.SMEM((pairs,), jnp.int32),
                pltpu.VMEM((slots * rows, width), jnp.bfloat16),
                pltpu.VMEM((here * fresh_rows, width), jnp.bfloat16),
                pltpu.VMEM((slots, rows, LATENT), jnp.float32),
                pltpu.VMEM((slots, rows, LANES), jnp.float32),
                pltpu.VMEM((slots, rows, LANES), jnp.float32),
                pltpu.VMEM((slots * rows, LATENT), jnp.bfloat16),
                pltpu.VMEM((2, rows, BLOCK), jnp.float32),
                pltpu.VMEM((2, rows, BLOCK), jnp.float32),
            ],
            compiler_params=limit(14),
            cost_estimate=cost(8),
            name="attend",
        )(ids, decode_rows, lengths, *received, cache, key_up, value_up)

    def order(kernel, in_specs, scratch, arrays):
        return pl.pallas_call(
            kernel,
            out_shape=jax.ShapeDtypeStruct((steps, sources * requests, columns), jnp.bfloat16),
            in_specs=in_specs,
            out_specs=vmem(),
            scratch_shapes=scratch,
            compiler_params=limit(16),
            cost_estimate=cost(2),
            name="order_rows",
        )(*arrays)

    if not relative:
        received = lax.all_to_all(packed[0], "seq", split_axis=0, concat_axis=0, tiled=True)
        every_row = lax.all_gather(attend([received], 0), "seq", axis=0, tiled=True)
        partial_value = jnp.dot(every_row, out_proj, preferred_element_type=jnp.float32).astype(jnp.bfloat16)
        shares = lax.all_to_all(partial_value, "head", split_axis=0, concat_axis=0, tiled=True)
        shares = shares.reshape(head_devices, -1, columns)
        summed = jnp.sum(shares.astype(jnp.float32), axis=0).astype(jnp.bfloat16)
        whole = lax.all_gather(summed, "head", axis=0, tiled=True)
        return order(order_whole_kernel, [vmem()] * 2, [], [pick, whole])

    pieces = 2

    def project(parts, piece):
        part_rows = parts[0].shape[0]
        cols = columns // pieces
        return pl.pallas_call(
            functools.partial(project_kernel, piece * cols),
            out_shape=[jax.ShapeDtypeStruct((2 * part_rows, cols), jnp.bfloat16)] * 2,
            in_specs=[smem()] + [vmem()] * 5,
            out_specs=[vmem()] * 2,
            scratch_shapes=[pltpu.VMEM((4 * part_rows, out_proj.shape[0]), jnp.bfloat16)],
            compiler_params=limit(10),
            cost_estimate=cost(2),
            name="project_out",
        )(ids, *parts, out_proj)

    received = [packed[0]] + [flip(packed[k], "seq", k) for k in range(1, 4)]
    near_rows = attend(received[:2], 0)
    near_across = flip(near_rows, "seq", 2)
    far_rows = attend(received[2:], 2)
    near_across, far_rows = lax.optimization_barrier((near_across, far_rows))
    near = [near_rows, flip(near_rows, "seq", 1), near_across, flip(near_across, "seq", 1)]
    far_across = flip(far_rows, "seq", 2)
    def after(value, *others):
        return lax.optimization_barrier((value,) + others)[0]

    def swap(piece):
        return flip(piece[1], "head", 1)

    first = project(near, 0)
    first_in = swap(first)
    second = project(near, 1)
    second_in = swap(second)
    far = [far_rows, flip(far_rows, "seq", 1), far_across, flip(far_across, "seq", 1)]
    first_pair = add(first[0], first_in)
    first_cross = flip(first_pair, "head", 3)
    second_pair = add(second[0], second_in)
    second_cross = flip(second_pair, "head", 3)
    third = project(far, 0)
    third_in = swap(third)
    fourth = project(far, 1)
    fourth_in = swap(fourth)
    third_pair = add(third[0], third_in)
    third_cross = flip(third_pair, "head", 3)
    fourth_pair = add(fourth[0], fourth_in)
    fourth_cross = flip(fourth_pair, "head", 3)
    first_cross = after(first_cross, third_pair, fourth_pair)
    second_cross = after(second_cross, third_pair, fourth_pair)
    first_sum = add(first_pair, first_cross)
    first_other = flip(first_sum, "head", 1)
    second_sum = add(second_pair, second_cross)
    second_other = flip(second_sum, "head", 1)
    third_sum = add(third_pair, third_cross)
    third_other = flip(third_sum, "head", 1)
    fourth_sum = add(fourth_pair, fourth_cross)
    fourth_other = flip(fourth_sum, "head", 1)
    arrays = [first_sum, first_other, second_sum, second_other, third_sum, third_other, fourth_sum, fourth_other]
    scratch = [pltpu.VMEM((steps * sources * requests, columns), jnp.bfloat16)]
    kernel = functools.partial(order_kernel, 2)
    return order(kernel, [smem()] + [vmem()] * (1 + len(arrays)), scratch, [ids, pick] + arrays)


def solution(mesh):
    return jax.shard_map(
        local,
        mesh=mesh,
        in_specs=(
            P(("groups", "seq"), None),
            P("groups", None),
            P("groups"),
            P(None, ("groups", "seq"), "head", None),
            P(None, ("groups", "seq"), "head", None),
            P(None, ("groups", "seq"), None),
            P("head", None, None),
            P("head", None, None),
            P("head", "seq"),
        ),
        out_specs=P(None, "groups", "seq"),
        check_vma=False,
    )
```

```python
import functools

import jax
import jax.numpy as jnp
from jax import lax
from jax.experimental import pallas as pl
from jax.experimental.pallas import tpu as pltpu
from jax.sharding import PartitionSpec as P

LATENT = 512
BLOCK = 256
LANES = 128
LOG2E = 1.4426950408889634
NEG = -1e30
PLACES = 1024


def own_slots(decode_ref, slot_ref, me, sources, requests, per_pair):
    shift = requests.bit_length() - 1

    def one_source(s, carry):
        count = jnp.int32(0)
        for r in range(requests):
            row = decode_ref[s * requests + r]
            slot_ref[s * (per_pair + 1) + jnp.minimum(count, per_pair)] = row & (requests - 1)
            count = count + jnp.where((row >> shift) == me, 1, 0).astype(jnp.int32)
        return carry

    lax.fori_loop(0, sources, one_source, jnp.int32(0))


def pack_kernel(sizes, relative, ids_ref, decode_ref, nope_ref, rope_ref, fresh_ref, after_ref, *rest):
    sources, per_pair, steps, heads, requests, fresh_rows = sizes
    out_refs, (slots, wide) = rest[:-2], rest[-2:]
    me = ids_ref[0] & (PLACES - 1)
    rows = heads * steps
    half = rows // 2
    rope_base = per_pair * rows
    fresh_base = rope_base + per_pair * half
    own_slots(decode_ref, slots, me, sources, requests, per_pair)

    def one_dest(s, out_ref, e):
        for j in range(per_pair):
            row = slots[s * (per_pair + 1) + j]
            for t in range(steps):
                wide[2 * j, pl.ds(t, heads, stride=steps), :] = nope_ref[t, row].astype(jnp.float32)
                wide[2 * j + 1, pl.ds(t, heads, stride=steps), :] = jnp.concatenate(
                    [rope_ref[t, row].astype(jnp.float32)] * 2, axis=1
                )
        for j in range(per_pair):
            out_ref[e, j * rows : (j + 1) * rows, :] = wide[2 * j].astype(jnp.bfloat16)
            low = lax.broadcasted_iota(jnp.int32, (half, LANES), 1) < LANES // 2
            packed = jnp.where(low, wide[2 * j + 1, 0:half, :], wide[2 * j + 1, half : 2 * half, :])
            out_ref[e, rope_base + j * half : rope_base + (j + 1) * half, :] = packed.astype(jnp.bfloat16)

    if relative:
        dests = [me ^ k for k in range(sources)]
        for k in range(sources):
            one_dest(dests[k], out_refs[k], 0)
    else:
        dests = list(range(sources))

        def step(s, carry):
            one_dest(s, out_refs[0], s)
            return carry

        lax.fori_loop(0, sources, step, jnp.int32(0))
    shape = (sources * fresh_rows, steps * requests)
    row_id = lax.broadcasted_iota(jnp.int32, shape, 0)
    col_id = lax.broadcasted_iota(jnp.int32, shape, 1)
    wanted = jnp.full(shape, -1, jnp.int32)
    for k in range(sources):
        for j in range(per_pair):
            first = k * fresh_rows + j * steps
            here = (row_id >= first) & (row_id < first + steps)
            wanted = jnp.where(here, (row_id - first) * requests + slots[dests[k] * (per_pair + 1) + j], wanted)
    pick = jnp.where(col_id == wanted, 1.0, 0.0).astype(jnp.bfloat16)
    width = fresh_ref.shape[2]
    source_rows = jnp.concatenate([fresh_ref[t] for t in range(steps)], axis=0)
    picked = jnp.dot(pick, source_rows, preferred_element_type=jnp.float32).astype(jnp.bfloat16)
    for k in range(sources):
        for c in range(-(-width // LANES)):
            piece = picked[k * fresh_rows : (k + 1) * fresh_rows, c * LANES : min((c + 1) * LANES, width)]
            if piece.shape[1] < LANES:
                piece = jnp.concatenate([piece] * (LANES // piece.shape[1]), axis=1)
            first = fresh_base + c * fresh_rows
            if relative:
                out_refs[k][0, first : first + fresh_rows, :] = piece
            else:
                out_refs[0][k, first : first + fresh_rows, :] = piece


def attend_kernel(sizes, scale, relative, base, recv_count, ids_ref, decode_ref, length_ref, *rest):
    sources, per_pair, steps, heads, requests, fresh_rows = sizes
    recv_refs = rest[:recv_count]
    (
        cache, key_up, value_up, out_ref,
        slot_offset, slot_length, owner_count, pair_slot, pair_start,
        queries, fresh, acc, run_max, run_sum, latent, even_scores, odd_scores,
    ) = rest[recv_count:]
    owners = [(ref, e) for ref in recv_refs for e in range(ref.shape[0])]
    here = len(owners)
    slots = here * per_pair
    width, tokens = cache.shape
    rows = heads * steps
    half = rows // 2
    rope_base = per_pair * rows
    fresh_base = rope_base + per_pair * half
    group = 16 // steps
    shift = requests.bit_length() - 1
    factor = scale * LOG2E

    for e in range(here):
        ref, at = owners[e]
        for c in range(-(-width // LANES)):
            lanes = min(LANES, width - c * LANES)
            first = fresh_base + c * fresh_rows
            fresh[e * fresh_rows : (e + 1) * fresh_rows, c * LANES : c * LANES + lanes] = ref[
                at, first : first + fresh_rows, 0:lanes
            ]
        for j in range(per_pair):
            slot = e * per_pair + j
            first = rope_base + j * half
            piece = ref[at, first : first + half, :]
            queries[slot * rows : slot * rows + half, LATENT:width] = piece[:, 0 : width - LATENT]
            queries[slot * rows + half : (slot + 1) * rows, LATENT:width] = piece[:, LANES - (width - LATENT) :]

    inner_head = lax.broadcasted_iota(jnp.int32, (slots * 16, LANES), 0) // steps % group
    own_head = [jnp.where(inner_head == u, 1.0, 0.0).astype(jnp.bfloat16) for u in range(group)]
    for i in range(heads // group):
        tall = jnp.concatenate(
            [ref[at, j * rows + i * 16 : j * rows + (i + 1) * 16, :] for ref, at in owners for j in range(per_pair)],
            axis=0,
        )
        left = jnp.concatenate([tall * own_head[u] for u in range(group)], axis=1)
        right = jnp.concatenate([key_up[i * group + u] for u in range(group)], axis=0)
        res = jnp.dot(left, right, preferred_element_type=jnp.float32).astype(jnp.bfloat16)
        for slot in range(slots):
            queries[slot * rows + i * 16 : slot * rows + (i + 1) * 16, 0:LATENT] = res[slot * 16 : (slot + 1) * 16]

    me = ids_ref[0] & (PLACES - 1)
    for o in range(sources):
        owner_count[o] = jnp.int32(0)
    total = jnp.int32(0)
    for r in range(requests):
        owner = decode_ref[me * requests + r] >> shift
        at = owner_count[owner]
        owner_count[owner] = at + 1
        e = (owner ^ me) - base if relative else owner
        slot = jnp.where((e >= 0) & (e < here), e * per_pair + at, slots)
        length = length_ref[me, r]
        slot_offset[slot] = total
        slot_length[slot] = length
        total = total + length
    count = jnp.int32(0)
    for slot in range(slots):
        start = slot_offset[slot] & ~(LANES - 1)
        end = slot_offset[slot] + slot_length[slot]
        for k in range(512 // BLOCK + 1):
            pair_slot[count] = jnp.int32(slot)
            pair_start[count] = start + k * BLOCK
            count = count + jnp.where(start + k * BLOCK < end, 1, 0).astype(jnp.int32)

    fresh_scores = (
        lax.dot_general(queries[...], fresh[...], (((1,), (1,)), ((), ())), preferred_element_type=jnp.float32) * factor
    )
    row_id = lax.broadcasted_iota(jnp.int32, (rows, here * fresh_rows), 0)
    col_id = lax.broadcasted_iota(jnp.int32, (rows, here * fresh_rows), 1)
    behind = row_id & (steps - 1)
    fresh_weights = []
    for slot in range(slots):
        first = (slot // per_pair) * fresh_rows + (slot % per_pair) * steps
        seen = (col_id >= first) & (col_id <= first + behind)
        scores = jnp.where(seen, fresh_scores[slot * rows : (slot + 1) * rows], NEG)
        top = jnp.max(scores, axis=1, keepdims=True)
        weights = jnp.exp2(scores - top)
        run_max[slot] = jnp.broadcast_to(top, (rows, LANES))
        run_sum[slot] = jnp.broadcast_to(jnp.sum(weights, axis=1, keepdims=True), (rows, LANES))
        fresh_weights.append(weights.astype(jnp.bfloat16))
    for slot in range(slots):
        acc[slot] = jnp.dot(fresh_weights[slot], fresh[:, 0:LATENT], preferred_element_type=jnp.float32)

    def make_scores(buffer, g):
        for u in range(2):
            p = jnp.minimum(g * 2 + u, count - 1)
            q = queries[pl.ds(pl.multiple_of(pair_slot[p] * rows, 16), rows), :]
            read = pl.multiple_of(jnp.minimum(pair_start[p], tokens - BLOCK), LANES)
            buffer[u] = jnp.dot(q, cache[:, pl.ds(read, BLOCK)], preferred_element_type=jnp.float32)

    token = lax.broadcasted_iota(jnp.int32, (1, BLOCK), 1)

    def take_scores(buffer, g):
        for u in range(2):
            p = jnp.minimum(g * 2 + u, count - 1)
            slot = pair_slot[p]
            start = pair_start[p]
            read = jnp.minimum(start, tokens - BLOCK)
            low = jnp.maximum(slot_offset[slot], start) - read
            high = jnp.minimum(slot_offset[slot] + slot_length[slot], start + BLOCK) - read
            high = jnp.where(g * 2 + u < count, high, low)
            bias = jnp.where((token >= low) & (token < high), 0.0, NEG)
            scores = buffer[u] * factor + bias
            top = jnp.max(scores, axis=1, keepdims=True)
            weights = jnp.exp2(scores - top)
            part_sum = jnp.broadcast_to(jnp.sum(weights, axis=1, keepdims=True), (rows, LANES))
            part = lax.dot_general(
                weights.astype(jnp.bfloat16),
                cache[0:LATENT, pl.ds(pl.multiple_of(read, LANES), BLOCK)],
                (((1,), (1,)), ((), ())),
                preferred_element_type=jnp.float32,
            )
            part_max = jnp.broadcast_to(top, (rows, LANES))
            old_max = run_max[slot]
            new_max = jnp.maximum(old_max, part_max)
            keep = jnp.exp2(old_max - new_max)
            add = jnp.exp2(part_max - new_max)
            run_max[slot] = new_max
            run_sum[slot] = run_sum[slot] * keep + part_sum * add
            for c in range(LATENT // LANES):
                cols = slice(c * LANES, (c + 1) * LANES)
                acc[slot, :, cols] = acc[slot, :, cols] * keep + part[:, cols] * add

    make_scores(even_scores, 0)

    def four_pairs(i, carry):
        make_scores(odd_scores, 2 * i + 1)
        take_scores(even_scores, 2 * i)
        make_scores(even_scores, 2 * i + 2)
        take_scores(odd_scores, 2 * i + 1)
        return carry

    lax.fori_loop(0, (count + 3) // 4, four_pairs, jnp.int32(0))

    for slot in range(slots):
        inverse = 1.0 / run_sum[slot]
        for c in range(LATENT // LANES):
            cols = slice(c * LANES, (c + 1) * LANES)
            latent[slot * rows : (slot + 1) * rows, cols] = (acc[slot, :, cols] * inverse).astype(jnp.bfloat16)
    vdim = value_up.shape[2]
    for i in range(heads // group):
        left = jnp.concatenate(
            [latent[slot * rows + i * 16 : slot * rows + (i + 1) * 16, :] for slot in range(slots)], axis=0
        )
        right = jnp.concatenate([value_up[i * group + u] for u in range(group)], axis=1)
        res = jnp.dot(left, right, preferred_element_type=jnp.float32)
        for u in range(group):
            own = jnp.concatenate(
                [
                    res[slot * 16 + u * steps : slot * 16 + (u + 1) * steps, u * vdim : (u + 1) * vdim]
                    for slot in range(slots)
                ],
                axis=0,
            )
            head = i * group + u
            out_ref[:, head * vdim : (head + 1) * vdim] = own.astype(jnp.bfloat16)


def place_kernel(sizes, relative, ids_ref, decode_ref, out_ref, owner_count, place):
    sources, per_pair, steps, requests = sizes
    me = ids_ref[0] & (PLACES - 1)
    rows = sources * requests
    shift = requests.bit_length() - 1

    def one_source(s, carry):
        for o in range(sources):
            owner_count[o] = jnp.int32(0)
        for r in range(requests):
            row = decode_ref[s * requests + r]
            owner = row >> shift
            at = owner_count[owner]
            owner_count[owner] = at + 1
            if relative:
                e = owner ^ s
                at_row = (e >> 1) * (2 * sources * per_pair) + (me ^ s) * (2 * per_pair) + (e & 1) * per_pair + at
            else:
                at_row = s * requests + owner * per_pair + at
            place[row] = at_row * steps
        return carry

    lax.fori_loop(0, sources, one_source, jnp.int32(0))
    narrow = (rows, LANES)
    row_id = lax.broadcasted_iota(jnp.int32, narrow, 0)

    def put(b, wanted):
        return jnp.where(row_id == b, place[b], wanted)

    wanted = lax.fori_loop(0, rows, put, jnp.zeros(narrow, jnp.int32), unroll=8)[:, 0:1]
    col_id = lax.broadcasted_iota(jnp.int32, (rows, rows * steps), 1)
    for t in range(steps):
        out_ref[t] = jnp.where(col_id == wanted + t, 1.0, 0.0).astype(jnp.bfloat16)


def keeps_upper(ids_ref):
    z = ids_ref[0] // PLACES
    return (z == 1) | (z == 2)


def order_kernel(halves, ids_ref, pick_ref, *rest):
    pieces, out_ref, x = rest[:-2], rest[-2], rest[-1]
    upper = keeps_upper(ids_ref)
    rows = x.shape[0] // (2 * halves)
    each = len(pieces) // (2 * halves)
    cols = x.shape[1] // each

    def assemble(first, second):
        for h in range(halves):
            for c in range(each):
                at = slice(c * cols, (c + 1) * cols)
                i = 2 * (h * each + c)
                x[2 * h * rows : (2 * h + 1) * rows, at] = pieces[i + first][...]
                x[(2 * h + 1) * rows : (2 * h + 2) * rows, at] = pieces[i + second][...]

    pl.when(upper)(lambda: assemble(1, 0))
    pl.when(jnp.logical_not(upper))(lambda: assemble(0, 1))
    for t in range(pick_ref.shape[0]):
        out_ref[t] = jnp.dot(pick_ref[t], x[...], preferred_element_type=jnp.float32).astype(jnp.bfloat16)


def order_whole_kernel(pick_ref, x_ref, out_ref):
    for t in range(pick_ref.shape[0]):
        out_ref[t] = jnp.dot(pick_ref[t], x_ref[...], preferred_element_type=jnp.float32).astype(jnp.bfloat16)


def project_kernel(first_col, ids_ref, *rest):
    parts, weight, keep, send, x = rest[:4], rest[4], rest[5], rest[6], rest[7]
    rows = parts[0].shape[0]
    upper = keeps_upper(ids_ref)

    def assemble(order):
        for place, q in enumerate(order):
            x[place * rows : (place + 1) * rows, :] = parts[q][...]

    pl.when(upper)(lambda: assemble((2, 3, 0, 1)))
    pl.when(jnp.logical_not(upper))(lambda: assemble((0, 1, 2, 3)))
    cols = keep.shape[1]
    for c in range(0, cols, BLOCK):
        n = min(BLOCK, cols - c)
        tile = jnp.dot(x[...], weight[:, first_col + c : first_col + c + n], preferred_element_type=jnp.float32)
        tile = tile.astype(jnp.bfloat16)
        keep[:, c : c + n] = tile[: 2 * rows]
        send[:, c : c + n] = tile[2 * rows :]


def smem():
    return pl.BlockSpec(memory_space=pltpu.SMEM)


def vmem():
    return pl.BlockSpec(memory_space=pltpu.VMEM)


def anywhere():
    return pl.BlockSpec(memory_space=pl.ANY)


def limit(mib):
    return pltpu.CompilerParams(vmem_limit_bytes=mib * 1024 * 1024)


def cost(microseconds):
    return pl.CostEstimate(
        flops=int(microseconds * 1.0e9), bytes_accessed=int(microseconds * 3.0e6), transcendentals=0
    )


def flip(x, axis, distance):
    size = lax.axis_size(axis)
    return lax.ppermute(x, axis, [(i, i ^ distance) for i in range(size)])


def add(x, y):
    return (x.astype(jnp.float32) + y.astype(jnp.float32)).astype(jnp.bfloat16)


def local(latent_cache, lengths, decode_rows, q_nope, q_rope, new_latent, key_up, value_up, out_proj):
    sources = lax.axis_size("seq")
    head_devices = lax.axis_size("head")
    relative = sources == 4 and head_devices == 4
    requests = lengths.shape[1]
    per_pair = requests // sources
    tokens, width = latent_cache.shape
    steps, _, heads, nope = q_nope.shape
    scale = (nope + q_rope.shape[3]) ** (-0.5)
    fresh_rows = -(-per_pair * steps // 16) * 16
    rows = heads * steps
    columns = out_proj.shape[1]
    packed_rows = per_pair * rows + per_pair * rows // 2 + -(-width // LANES) * fresh_rows
    sizes = (sources, per_pair, steps, heads, requests, fresh_rows)
    ids = (lax.axis_index("seq") + PLACES * lax.axis_index("head")).astype(jnp.int32).reshape(1)
    cache = latent_cache.T

    pick = pl.pallas_call(
        functools.partial(place_kernel, (sources, per_pair, steps, requests), relative),
        out_shape=jax.ShapeDtypeStruct((steps, sources * requests, steps * sources * requests), jnp.bfloat16),
        in_specs=[smem(), smem()],
        out_specs=vmem(),
        scratch_shapes=[pltpu.SMEM((sources,), jnp.int32), pltpu.SMEM((sources * requests,), jnp.int32)],
        compiler_params=limit(12),
        cost_estimate=cost(2),
        name="place_rows",
    )(ids, decode_rows)

    outs, each = (sources, 1) if relative else (1, sources)
    packed = pl.pallas_call(
        functools.partial(pack_kernel, sizes, relative),
        out_shape=[jax.ShapeDtypeStruct((each, packed_rows, LANES), jnp.bfloat16)] * outs,
        in_specs=[smem(), smem(), vmem(), vmem(), vmem(), anywhere()],
        out_specs=[vmem()] * outs,
        scratch_shapes=[
            pltpu.SMEM((sources * (per_pair + 1),), jnp.int32),
            pltpu.VMEM((2 * per_pair, rows, LANES), jnp.float32),
        ],
        compiler_params=limit(8),
        cost_estimate=cost(6),
        name="pack_queries",
    )(ids, decode_rows, q_nope, q_rope, new_latent, pick)

    def attend(received, base):
        here = sum(part.shape[0] for part in received)
        slots = here * per_pair
        pairs = slots * (512 // BLOCK + 1) + 1
        return pl.pallas_call(
            functools.partial(attend_kernel, sizes, scale, relative, base, len(received)),
            out_shape=jax.ShapeDtypeStruct((slots * steps, heads * value_up.shape[2]), jnp.bfloat16),
            in_specs=[smem(), smem(), smem()] + [vmem()] * (len(received) + 3),
            out_specs=vmem(),
            scratch_shapes=[
                pltpu.SMEM((slots + 1,), jnp.int32),
                pltpu.SMEM((slots + 1,), jnp.int32),
                pltpu.SMEM((sources,), jnp.int32),
                pltpu.SMEM((pairs,), jnp.int32),
                pltpu.SMEM((pairs,), jnp.int32),
                pltpu.VMEM((slots * rows, width), jnp.bfloat16),
                pltpu.VMEM((here * fresh_rows, width), jnp.bfloat16),
                pltpu.VMEM((slots, rows, LATENT), jnp.float32),
                pltpu.VMEM((slots, rows, LANES), jnp.float32),
                pltpu.VMEM((slots, rows, LANES), jnp.float32),
                pltpu.VMEM((slots * rows, LATENT), jnp.bfloat16),
                pltpu.VMEM((2, rows, BLOCK), jnp.float32),
                pltpu.VMEM((2, rows, BLOCK), jnp.float32),
            ],
            compiler_params=limit(14),
            cost_estimate=cost(8),
            name="attend",
        )(ids, decode_rows, lengths, *received, cache, key_up, value_up)

    def order(kernel, in_specs, scratch, arrays):
        return pl.pallas_call(
            kernel,
            out_shape=jax.ShapeDtypeStruct((steps, sources * requests, columns), jnp.bfloat16),
            in_specs=in_specs,
            out_specs=vmem(),
            scratch_shapes=scratch,
            compiler_params=limit(16),
            cost_estimate=cost(2),
            name="order_rows",
        )(*arrays)

    if not relative:
        received = lax.all_to_all(packed[0], "seq", split_axis=0, concat_axis=0, tiled=True)
        every_row = lax.all_gather(attend([received], 0), "seq", axis=0, tiled=True)
        partial_value = jnp.dot(every_row, out_proj, preferred_element_type=jnp.float32).astype(jnp.bfloat16)
        shares = lax.all_to_all(partial_value, "head", split_axis=0, concat_axis=0, tiled=True)
        shares = shares.reshape(head_devices, -1, columns)
        summed = jnp.sum(shares.astype(jnp.float32), axis=0).astype(jnp.bfloat16)
        whole = lax.all_gather(summed, "head", axis=0, tiled=True)
        return order(order_whole_kernel, [vmem()] * 2, [], [pick, whole])

    pieces = 2

    def project(parts, piece):
        part_rows = parts[0].shape[0]
        cols = columns // pieces
        return pl.pallas_call(
            functools.partial(project_kernel, piece * cols),
            out_shape=[jax.ShapeDtypeStruct((2 * part_rows, cols), jnp.bfloat16)] * 2,
            in_specs=[smem()] + [vmem()] * 5,
            out_specs=[vmem()] * 2,
            scratch_shapes=[pltpu.VMEM((4 * part_rows, out_proj.shape[0]), jnp.bfloat16)],
            compiler_params=limit(10),
            cost_estimate=cost(2),
            name="project_out",
        )(ids, *parts, out_proj)

    received = [packed[0]] + [flip(packed[k], "seq", k) for k in range(1, 4)]
    near_rows = attend(received[:2], 0)
    near_across = flip(near_rows, "seq", 2)
    far_rows = attend(received[2:], 2)
    near_across, far_rows = lax.optimization_barrier((near_across, far_rows))
    near = [near_rows, flip(near_rows, "seq", 1), near_across, flip(near_across, "seq", 1)]
    far_across = flip(far_rows, "seq", 2)
    def after(value, *others):
        return lax.optimization_barrier((value,) + others)[0]

    def swap(piece):
        return flip(piece[1], "head", 1)

    first = project(near, 0)
    first_in = swap(first)
    second = project(near, 1)
    second_in = swap(second)
    far = [far_rows, flip(far_rows, "seq", 1), far_across, flip(far_across, "seq", 1)]
    first_pair = add(first[0], first_in)
    first_cross = flip(first_pair, "head", 3)
    third = project(far, 0)
    third_in = swap(third)
    fourth = project(far, 1)
    fourth_in = swap(fourth)
    second_in = after(second_in, third[0])
    second_pair = add(second[0], second_in)
    second_cross = flip(second_pair, "head", 3)
    first_cross = after(first_cross, fourth[0])
    first_sum = add(first_pair, first_cross)
    first_other = flip(first_sum, "head", 1)
    third_in = after(third_in, second_pair)
    third_pair = add(third[0], third_in)
    third_cross = flip(third_pair, "head", 3)
    second_cross = after(second_cross, third_pair)
    second_sum = add(second_pair, second_cross)
    second_other = flip(second_sum, "head", 1)
    fourth_in = after(fourth_in, second_sum)
    fourth_pair = add(fourth[0], fourth_in)
    fourth_cross = flip(fourth_pair, "head", 3)
    third_sum = add(third_pair, third_cross)
    third_other = flip(third_sum, "head", 1)
    fourth_sum = add(fourth_pair, fourth_cross)
    fourth_other = flip(fourth_sum, "head", 1)
    arrays = [first_sum, first_other, second_sum, second_other, third_sum, third_other, fourth_sum, fourth_other]
    scratch = [pltpu.VMEM((steps * sources * requests, columns), jnp.bfloat16)]
    kernel = functools.partial(order_kernel, 2)
    return order(kernel, [smem()] + [vmem()] * (1 + len(arrays)), scratch, [ids, pick] + arrays)


def solution(mesh):
    return jax.shard_map(
        local,
        mesh=mesh,
        in_specs=(
            P(("groups", "seq"), None),
            P("groups", None),
            P("groups"),
            P(None, ("groups", "seq"), "head", None),
            P(None, ("groups", "seq"), "head", None),
            P(None, ("groups", "seq"), None),
            P("head", None, None),
            P("head", None, None),
            P("head", "seq"),
        ),
        out_specs=P(None, "groups", "seq"),
        check_vma=False,
    )
```

```python
import functools

import jax
import jax.numpy as jnp
from jax import lax
from jax.experimental import pallas as pl
from jax.experimental.pallas import tpu as pltpu
from jax.sharding import PartitionSpec as P

LATENT = 512
BLOCK = 256
LANES = 128
LOG2E = 1.4426950408889634
NEG = -1e30
PLACES = 1024


def own_slots(decode_ref, slot_ref, me, sources, requests, per_pair):
    shift = requests.bit_length() - 1

    def one_source(s, carry):
        count = jnp.int32(0)
        for r in range(requests):
            row = decode_ref[s * requests + r]
            slot_ref[s * (per_pair + 1) + jnp.minimum(count, per_pair)] = row & (requests - 1)
            count = count + jnp.where((row >> shift) == me, 1, 0).astype(jnp.int32)
        return carry

    lax.fori_loop(0, sources, one_source, jnp.int32(0))


def pack_kernel(sizes, relative, ids_ref, decode_ref, nope_ref, rope_ref, fresh_ref, after_ref, *rest):
    sources, per_pair, steps, heads, requests, fresh_rows = sizes
    out_refs, (slots, wide) = rest[:-2], rest[-2:]
    me = ids_ref[0] & (PLACES - 1)
    rows = heads * steps
    half = rows // 2
    rope_base = per_pair * rows
    fresh_base = rope_base + per_pair * half
    own_slots(decode_ref, slots, me, sources, requests, per_pair)

    def one_dest(s, out_ref, e):
        for j in range(per_pair):
            row = slots[s * (per_pair + 1) + j]
            for t in range(steps):
                wide[2 * j, pl.ds(t, heads, stride=steps), :] = nope_ref[t, row].astype(jnp.float32)
                wide[2 * j + 1, pl.ds(t, heads, stride=steps), :] = jnp.concatenate(
                    [rope_ref[t, row].astype(jnp.float32)] * 2, axis=1
                )
        for j in range(per_pair):
            out_ref[e, j * rows : (j + 1) * rows, :] = wide[2 * j].astype(jnp.bfloat16)
            low = lax.broadcasted_iota(jnp.int32, (half, LANES), 1) < LANES // 2
            packed = jnp.where(low, wide[2 * j + 1, 0:half, :], wide[2 * j + 1, half : 2 * half, :])
            out_ref[e, rope_base + j * half : rope_base + (j + 1) * half, :] = packed.astype(jnp.bfloat16)

    if relative:
        dests = [me ^ k for k in range(sources)]
        for k in range(sources):
            one_dest(dests[k], out_refs[k], 0)
    else:
        dests = list(range(sources))

        def step(s, carry):
            one_dest(s, out_refs[0], s)
            return carry

        lax.fori_loop(0, sources, step, jnp.int32(0))
    shape = (sources * fresh_rows, steps * requests)
    row_id = lax.broadcasted_iota(jnp.int32, shape, 0)
    col_id = lax.broadcasted_iota(jnp.int32, shape, 1)
    wanted = jnp.full(shape, -1, jnp.int32)
    for k in range(sources):
        for j in range(per_pair):
            first = k * fresh_rows + j * steps
            here = (row_id >= first) & (row_id < first + steps)
            wanted = jnp.where(here, (row_id - first) * requests + slots[dests[k] * (per_pair + 1) + j], wanted)
    pick = jnp.where(col_id == wanted, 1.0, 0.0).astype(jnp.bfloat16)
    width = fresh_ref.shape[2]
    source_rows = jnp.concatenate([fresh_ref[t] for t in range(steps)], axis=0)
    picked = jnp.dot(pick, source_rows, preferred_element_type=jnp.float32).astype(jnp.bfloat16)
    for k in range(sources):
        for c in range(-(-width // LANES)):
            piece = picked[k * fresh_rows : (k + 1) * fresh_rows, c * LANES : min((c + 1) * LANES, width)]
            if piece.shape[1] < LANES:
                piece = jnp.concatenate([piece] * (LANES // piece.shape[1]), axis=1)
            first = fresh_base + c * fresh_rows
            if relative:
                out_refs[k][0, first : first + fresh_rows, :] = piece
            else:
                out_refs[0][k, first : first + fresh_rows, :] = piece


def attend_kernel(sizes, scale, relative, base, recv_count, ids_ref, decode_ref, length_ref, *rest):
    sources, per_pair, steps, heads, requests, fresh_rows = sizes
    recv_refs = rest[:recv_count]
    (
        cache, key_up, value_up, out_ref,
        slot_offset, slot_length, owner_count, pair_slot, pair_start,
        queries, fresh, acc, run_max, run_sum, latent, even_scores, odd_scores,
    ) = rest[recv_count:]
    owners = [(ref, e) for ref in recv_refs for e in range(ref.shape[0])]
    here = len(owners)
    slots = here * per_pair
    width, tokens = cache.shape
    rows = heads * steps
    half = rows // 2
    rope_base = per_pair * rows
    fresh_base = rope_base + per_pair * half
    group = 16 // steps
    shift = requests.bit_length() - 1
    factor = scale * LOG2E

    for e in range(here):
        ref, at = owners[e]
        for c in range(-(-width // LANES)):
            lanes = min(LANES, width - c * LANES)
            first = fresh_base + c * fresh_rows
            fresh[e * fresh_rows : (e + 1) * fresh_rows, c * LANES : c * LANES + lanes] = ref[
                at, first : first + fresh_rows, 0:lanes
            ]
        for j in range(per_pair):
            slot = e * per_pair + j
            first = rope_base + j * half
            piece = ref[at, first : first + half, :]
            queries[slot * rows : slot * rows + half, LATENT:width] = piece[:, 0 : width - LATENT]
            queries[slot * rows + half : (slot + 1) * rows, LATENT:width] = piece[:, LANES - (width - LATENT) :]

    inner_head = lax.broadcasted_iota(jnp.int32, (slots * 16, LANES), 0) // steps % group
    own_head = [jnp.where(inner_head == u, 1.0, 0.0).astype(jnp.bfloat16) for u in range(group)]
    for i in range(heads // group):
        tall = jnp.concatenate(
            [ref[at, j * rows + i * 16 : j * rows + (i + 1) * 16, :] for ref, at in owners for j in range(per_pair)],
            axis=0,
        )
        left = jnp.concatenate([tall * own_head[u] for u in range(group)], axis=1)
        right = jnp.concatenate([key_up[i * group + u] for u in range(group)], axis=0)
        res = jnp.dot(left, right, preferred_element_type=jnp.float32).astype(jnp.bfloat16)
        for slot in range(slots):
            queries[slot * rows + i * 16 : slot * rows + (i + 1) * 16, 0:LATENT] = res[slot * 16 : (slot + 1) * 16]

    me = ids_ref[0] & (PLACES - 1)
    for o in range(sources):
        owner_count[o] = jnp.int32(0)
    total = jnp.int32(0)
    for r in range(requests):
        owner = decode_ref[me * requests + r] >> shift
        at = owner_count[owner]
        owner_count[owner] = at + 1
        e = (owner ^ me) - base if relative else owner
        slot = jnp.where((e >= 0) & (e < here), e * per_pair + at, slots)
        length = length_ref[me, r]
        slot_offset[slot] = total
        slot_length[slot] = length
        total = total + length
    count = jnp.int32(0)
    for slot in range(slots):
        start = slot_offset[slot] & ~(LANES - 1)
        end = slot_offset[slot] + slot_length[slot]
        for k in range(512 // BLOCK + 1):
            pair_slot[count] = jnp.int32(slot)
            pair_start[count] = start + k * BLOCK
            count = count + jnp.where(start + k * BLOCK < end, 1, 0).astype(jnp.int32)

    fresh_scores = (
        lax.dot_general(queries[...], fresh[...], (((1,), (1,)), ((), ())), preferred_element_type=jnp.float32) * factor
    )
    row_id = lax.broadcasted_iota(jnp.int32, (rows, here * fresh_rows), 0)
    col_id = lax.broadcasted_iota(jnp.int32, (rows, here * fresh_rows), 1)
    behind = row_id & (steps - 1)
    fresh_weights = []
    for slot in range(slots):
        first = (slot // per_pair) * fresh_rows + (slot % per_pair) * steps
        seen = (col_id >= first) & (col_id <= first + behind)
        scores = jnp.where(seen, fresh_scores[slot * rows : (slot + 1) * rows], NEG)
        top = jnp.max(scores, axis=1, keepdims=True)
        weights = jnp.exp2(scores - top)
        run_max[slot] = jnp.broadcast_to(top, (rows, LANES))
        run_sum[slot] = jnp.broadcast_to(jnp.sum(weights, axis=1, keepdims=True), (rows, LANES))
        fresh_weights.append(weights.astype(jnp.bfloat16))
    for slot in range(slots):
        acc[slot] = jnp.dot(fresh_weights[slot], fresh[:, 0:LATENT], preferred_element_type=jnp.float32)

    def make_scores(buffer, g):
        for u in range(2):
            p = jnp.minimum(g * 2 + u, count - 1)
            q = queries[pl.ds(pl.multiple_of(pair_slot[p] * rows, 16), rows), :]
            read = pl.multiple_of(jnp.minimum(pair_start[p], tokens - BLOCK), LANES)
            buffer[u] = jnp.dot(q, cache[:, pl.ds(read, BLOCK)], preferred_element_type=jnp.float32)

    token = lax.broadcasted_iota(jnp.int32, (1, BLOCK), 1)

    def take_scores(buffer, g):
        for u in range(2):
            p = jnp.minimum(g * 2 + u, count - 1)
            slot = pair_slot[p]
            start = pair_start[p]
            read = jnp.minimum(start, tokens - BLOCK)
            low = jnp.maximum(slot_offset[slot], start) - read
            high = jnp.minimum(slot_offset[slot] + slot_length[slot], start + BLOCK) - read
            high = jnp.where(g * 2 + u < count, high, low)
            bias = jnp.where((token >= low) & (token < high), 0.0, NEG)
            scores = buffer[u] * factor + bias
            top = jnp.max(scores, axis=1, keepdims=True)
            weights = jnp.exp2(scores - top)
            part_sum = jnp.broadcast_to(jnp.sum(weights, axis=1, keepdims=True), (rows, LANES))
            part = lax.dot_general(
                weights.astype(jnp.bfloat16),
                cache[0:LATENT, pl.ds(pl.multiple_of(read, LANES), BLOCK)],
                (((1,), (1,)), ((), ())),
                preferred_element_type=jnp.float32,
            )
            part_max = jnp.broadcast_to(top, (rows, LANES))
            old_max = run_max[slot]
            new_max = jnp.maximum(old_max, part_max)
            keep = jnp.exp2(old_max - new_max)
            add = jnp.exp2(part_max - new_max)
            run_max[slot] = new_max
            run_sum[slot] = run_sum[slot] * keep + part_sum * add
            for c in range(LATENT // LANES):
                cols = slice(c * LANES, (c + 1) * LANES)
                acc[slot, :, cols] = acc[slot, :, cols] * keep + part[:, cols] * add

    make_scores(even_scores, 0)

    def four_pairs(i, carry):
        make_scores(odd_scores, 2 * i + 1)
        take_scores(even_scores, 2 * i)
        make_scores(even_scores, 2 * i + 2)
        take_scores(odd_scores, 2 * i + 1)
        return carry

    lax.fori_loop(0, (count + 3) // 4, four_pairs, jnp.int32(0))

    for slot in range(slots):
        inverse = 1.0 / run_sum[slot]
        for c in range(LATENT // LANES):
            cols = slice(c * LANES, (c + 1) * LANES)
            latent[slot * rows : (slot + 1) * rows, cols] = (acc[slot, :, cols] * inverse).astype(jnp.bfloat16)
    vdim = value_up.shape[2]
    for i in range(heads // group):
        left = jnp.concatenate(
            [latent[slot * rows + i * 16 : slot * rows + (i + 1) * 16, :] for slot in range(slots)], axis=0
        )
        right = jnp.concatenate([value_up[i * group + u] for u in range(group)], axis=1)
        res = jnp.dot(left, right, preferred_element_type=jnp.float32)
        for u in range(group):
            own = jnp.concatenate(
                [
                    res[slot * 16 + u * steps : slot * 16 + (u + 1) * steps, u * vdim : (u + 1) * vdim]
                    for slot in range(slots)
                ],
                axis=0,
            )
            head = i * group + u
            out_ref[:, head * vdim : (head + 1) * vdim] = own.astype(jnp.bfloat16)


def place_kernel(sizes, relative, ids_ref, decode_ref, out_ref, owner_count, place):
    sources, per_pair, steps, requests = sizes
    me = ids_ref[0] & (PLACES - 1)
    rows = sources * requests
    shift = requests.bit_length() - 1

    def one_source(s, carry):
        for o in range(sources):
            owner_count[o] = jnp.int32(0)
        for r in range(requests):
            row = decode_ref[s * requests + r]
            owner = row >> shift
            at = owner_count[owner]
            owner_count[owner] = at + 1
            if relative:
                e = owner ^ s
                at_row = (e >> 1) * (2 * sources * per_pair) + (me ^ s) * (2 * per_pair) + (e & 1) * per_pair + at
            else:
                at_row = s * requests + owner * per_pair + at
            place[row] = at_row * steps
        return carry

    lax.fori_loop(0, sources, one_source, jnp.int32(0))
    narrow = (rows, LANES)
    row_id = lax.broadcasted_iota(jnp.int32, narrow, 0)

    def put(b, wanted):
        return jnp.where(row_id == b, place[b], wanted)

    wanted = lax.fori_loop(0, rows, put, jnp.zeros(narrow, jnp.int32), unroll=8)[:, 0:1]
    col_id = lax.broadcasted_iota(jnp.int32, (rows, rows * steps), 1)
    for t in range(steps):
        out_ref[t] = jnp.where(col_id == wanted + t, 1.0, 0.0).astype(jnp.bfloat16)


def keeps_upper(ids_ref):
    z = ids_ref[0] // PLACES
    return (z == 1) | (z == 2)


def order_kernel(layout, ids_ref, pick_ref, *rest):
    pieces, out_ref, x = rest[:-2], rest[-2], rest[-1]
    upper = keeps_upper(ids_ref)

    def assemble(first, second):
        for i, (row, col) in enumerate(layout):
            rows, cols = pieces[2 * i].shape
            x[row : row + rows, col : col + cols] = pieces[2 * i + first][...]
            x[row + rows : row + 2 * rows, col : col + cols] = pieces[2 * i + second][...]

    pl.when(upper)(lambda: assemble(1, 0))
    pl.when(jnp.logical_not(upper))(lambda: assemble(0, 1))
    steps, rows, _ = pick_ref.shape
    pick = jnp.concatenate([pick_ref[t] for t in range(steps)], axis=0)
    for c in range(0, x.shape[1], BLOCK):
        tile = jnp.dot(pick, x[:, c : c + BLOCK], preferred_element_type=jnp.float32).astype(jnp.bfloat16)
        for t in range(steps):
            out_ref[t, :, c : c + BLOCK] = tile[t * rows : (t + 1) * rows]


def order_whole_kernel(pick_ref, x_ref, out_ref):
    for t in range(pick_ref.shape[0]):
        out_ref[t] = jnp.dot(pick_ref[t], x_ref[...], preferred_element_type=jnp.float32).astype(jnp.bfloat16)


def project_kernel(first_col, ids_ref, *rest):
    parts, (weight, keep, send) = rest[:-3], rest[-3:]
    half = keep.shape[0]
    upper = keeps_upper(ids_ref)
    cols = keep.shape[1]
    x = jnp.concatenate([part[...] for part in parts], axis=0)
    for c in range(0, cols, BLOCK):
        n = min(BLOCK, cols - c)
        tile = jnp.dot(x, weight[:, first_col + c : first_col + c + n], preferred_element_type=jnp.float32)
        keep[:, c : c + n] = jnp.where(upper, tile[half:], tile[:half]).astype(jnp.bfloat16)
        send[:, c : c + n] = jnp.where(upper, tile[:half], tile[half:]).astype(jnp.bfloat16)


def smem():
    return pl.BlockSpec(memory_space=pltpu.SMEM)


def vmem():
    return pl.BlockSpec(memory_space=pltpu.VMEM)


def anywhere():
    return pl.BlockSpec(memory_space=pl.ANY)


def limit(mib):
    return pltpu.CompilerParams(vmem_limit_bytes=mib * 1024 * 1024)


def cost(microseconds):
    return pl.CostEstimate(
        flops=int(microseconds * 1.0e9), bytes_accessed=int(microseconds * 3.0e6), transcendentals=0
    )


def flip(x, axis, distance):
    size = lax.axis_size(axis)
    return lax.ppermute(x, axis, [(i, i ^ distance) for i in range(size)])


def add(x, y):
    return (x.astype(jnp.float32) + y.astype(jnp.float32)).astype(jnp.bfloat16)


def local(latent_cache, lengths, decode_rows, q_nope, q_rope, new_latent, key_up, value_up, out_proj):
    sources = lax.axis_size("seq")
    head_devices = lax.axis_size("head")
    relative = sources == 4 and head_devices == 4
    requests = lengths.shape[1]
    per_pair = requests // sources
    tokens, width = latent_cache.shape
    steps, _, heads, nope = q_nope.shape
    scale = (nope + q_rope.shape[3]) ** (-0.5)
    fresh_rows = -(-per_pair * steps // 16) * 16
    rows = heads * steps
    columns = out_proj.shape[1]
    packed_rows = per_pair * rows + per_pair * rows // 2 + -(-width // LANES) * fresh_rows
    sizes = (sources, per_pair, steps, heads, requests, fresh_rows)
    ids = (lax.axis_index("seq") + PLACES * lax.axis_index("head")).astype(jnp.int32).reshape(1)
    cache = latent_cache.T

    pick = pl.pallas_call(
        functools.partial(place_kernel, (sources, per_pair, steps, requests), relative),
        out_shape=jax.ShapeDtypeStruct((steps, sources * requests, steps * sources * requests), jnp.bfloat16),
        in_specs=[smem(), smem()],
        out_specs=vmem(),
        scratch_shapes=[pltpu.SMEM((sources,), jnp.int32), pltpu.SMEM((sources * requests,), jnp.int32)],
        compiler_params=limit(12),
        cost_estimate=cost(2),
        name="place_rows",
    )(ids, decode_rows)

    outs, each = (sources, 1) if relative else (1, sources)
    packed = pl.pallas_call(
        functools.partial(pack_kernel, sizes, relative),
        out_shape=[jax.ShapeDtypeStruct((each, packed_rows, LANES), jnp.bfloat16)] * outs,
        in_specs=[smem(), smem(), vmem(), vmem(), vmem(), anywhere()],
        out_specs=[vmem()] * outs,
        scratch_shapes=[
            pltpu.SMEM((sources * (per_pair + 1),), jnp.int32),
            pltpu.VMEM((2 * per_pair, rows, LANES), jnp.float32),
        ],
        compiler_params=limit(8),
        cost_estimate=cost(6),
        name="pack_queries",
    )(ids, decode_rows, q_nope, q_rope, new_latent, pick)

    def attend(received, base):
        here = sum(part.shape[0] for part in received)
        slots = here * per_pair
        pairs = slots * (512 // BLOCK + 1) + 1
        return pl.pallas_call(
            functools.partial(attend_kernel, sizes, scale, relative, base, len(received)),
            out_shape=jax.ShapeDtypeStruct((slots * steps, heads * value_up.shape[2]), jnp.bfloat16),
            in_specs=[smem(), smem(), smem()] + [vmem()] * (len(received) + 3),
            out_specs=vmem(),
            scratch_shapes=[
                pltpu.SMEM((slots + 1,), jnp.int32),
                pltpu.SMEM((slots + 1,), jnp.int32),
                pltpu.SMEM((sources,), jnp.int32),
                pltpu.SMEM((pairs,), jnp.int32),
                pltpu.SMEM((pairs,), jnp.int32),
                pltpu.VMEM((slots * rows, width), jnp.bfloat16),
                pltpu.VMEM((here * fresh_rows, width), jnp.bfloat16),
                pltpu.VMEM((slots, rows, LATENT), jnp.float32),
                pltpu.VMEM((slots, rows, LANES), jnp.float32),
                pltpu.VMEM((slots, rows, LANES), jnp.float32),
                pltpu.VMEM((slots * rows, LATENT), jnp.bfloat16),
                pltpu.VMEM((2, rows, BLOCK), jnp.float32),
                pltpu.VMEM((2, rows, BLOCK), jnp.float32),
            ],
            compiler_params=limit(14),
            cost_estimate=cost(8),
            name="attend",
        )(ids, decode_rows, lengths, *received, cache, key_up, value_up)

    def order(kernel, in_specs, scratch, arrays):
        return pl.pallas_call(
            kernel,
            out_shape=jax.ShapeDtypeStruct((steps, sources * requests, columns), jnp.bfloat16),
            in_specs=in_specs,
            out_specs=vmem(),
            scratch_shapes=scratch,
            compiler_params=limit(16),
            cost_estimate=cost(2),
            name="order_rows",
        )(*arrays)

    if not relative:
        received = lax.all_to_all(packed[0], "seq", split_axis=0, concat_axis=0, tiled=True)
        every_row = lax.all_gather(attend([received], 0), "seq", axis=0, tiled=True)
        partial_value = jnp.dot(every_row, out_proj, preferred_element_type=jnp.float32).astype(jnp.bfloat16)
        shares = lax.all_to_all(partial_value, "head", split_axis=0, concat_axis=0, tiled=True)
        shares = shares.reshape(head_devices, -1, columns)
        summed = jnp.sum(shares.astype(jnp.float32), axis=0).astype(jnp.bfloat16)
        whole = lax.all_gather(summed, "head", axis=0, tiled=True)
        return order(order_whole_kernel, [vmem()] * 2, [], [pick, whole])

    def project(parts, first_col, cols):
        rows_here = len(parts) * parts[0].shape[0]
        return pl.pallas_call(
            functools.partial(project_kernel, first_col),
            out_shape=[jax.ShapeDtypeStruct((rows_here // 2, cols), jnp.bfloat16)] * 2,
            in_specs=[smem()] + [vmem()] * (len(parts) + 1),
            out_specs=[vmem()] * 2,
            compiler_params=limit(10),
            cost_estimate=cost(2),
            name="project_out",
        )(ids, *parts, out_proj)

    received = [packed[0]] + [flip(packed[k], "seq", k) for k in range(1, 4)]
    near_rows = attend(received[:2], 0)
    near_across = flip(near_rows, "seq", 2)
    far_rows = attend(received[2:], 2)
    near_across, far_rows = lax.optimization_barrier((near_across, far_rows))
    near = [near_rows, flip(near_rows, "seq", 1), near_across, flip(near_across, "seq", 1)]
    far_across = flip(far_rows, "seq", 2)

    def after(value, *others):
        return lax.optimization_barrier((value,) + others)[0]

    def swap(piece):
        return flip(piece[1], "head", 1)

    far = [far_rows, flip(far_rows, "seq", 1), far_across, flip(far_across, "seq", 1)]
    half = steps * sources * requests // 2

    def cut(parts, first_row, shares):
        groups = columns // LANES
        edges = [LANES * (groups * sum(shares[:i]) // sum(shares)) for i in range(len(shares) + 1)]
        return [(parts, first_row, at, end - at) for at, end in zip(edges, edges[1:])]

    near_pieces, far_pieces = cut(near, 0, (5, 9)), cut(far, half, (6, 5, 3))
    made = []
    for parts, first_row, first_col, cols in near_pieces + far_pieces:
        keep, send = project(parts, first_col, cols)
        made.append((first_row, first_col, keep, swap((keep, send))))
    pairs = [add(keep, incoming) for _, _, keep, incoming in made]
    crossed = [flip(pair, "head", 3) for pair in pairs]
    last_made = made[-1][2]
    arrays = []
    for i, (pair, cross) in enumerate(zip(pairs, crossed)):
        if i < len(near_pieces):
            cross = after(cross, last_made)
        total = add(pair, cross)
        arrays += [total, flip(total, "head", 1)]
    layout = tuple((row, col) for row, col, _, _ in made)
    scratch = [pltpu.VMEM((2 * half, columns), jnp.bfloat16)]
    kernel = functools.partial(order_kernel, layout)
    return order(kernel, [smem()] + [vmem()] * (1 + len(arrays)), scratch, [ids, pick] + arrays)


def solution(mesh):
    return jax.shard_map(
        local,
        mesh=mesh,
        in_specs=(
            P(("groups", "seq"), None),
            P("groups", None),
            P("groups"),
            P(None, ("groups", "seq"), "head", None),
            P(None, ("groups", "seq"), "head", None),
            P(None, ("groups", "seq"), None),
            P("head", None, None),
            P("head", None, None),
            P("head", "seq"),
        ),
        out_specs=P(None, "groups", "seq"),
        check_vma=False,
    )
```

```python
import functools

import jax
import jax.numpy as jnp
from jax import lax
from jax.experimental import pallas as pl
from jax.experimental.pallas import tpu as pltpu
from jax.sharding import PartitionSpec as P

LATENT = 512
BLOCK = 256
LANES = 128
LOG2E = 1.4426950408889634
NEG = -1e30
PLACES = 1024


def own_slots(decode_ref, slot_ref, me, sources, requests, per_pair):
    shift = requests.bit_length() - 1

    def one_source(s, carry):
        count = jnp.int32(0)
        for r in range(requests):
            row = decode_ref[s * requests + r]
            slot_ref[s * (per_pair + 1) + jnp.minimum(count, per_pair)] = row & (requests - 1)
            count = count + jnp.where((row >> shift) == me, 1, 0).astype(jnp.int32)
        return carry

    lax.fori_loop(0, sources, one_source, jnp.int32(0))


def pack_kernel(sizes, relative, ids_ref, decode_ref, nope_ref, rope_ref, fresh_ref, after_ref, *rest):
    sources, per_pair, steps, heads, requests, fresh_rows = sizes
    out_refs, (slots, wide) = rest[:-2], rest[-2:]
    me = ids_ref[0] & (PLACES - 1)
    rows = heads * steps
    half = rows // 2
    rope_base = per_pair * rows
    fresh_base = rope_base + per_pair * half
    own_slots(decode_ref, slots, me, sources, requests, per_pair)

    def one_dest(s, out_ref, e):
        for j in range(per_pair):
            row = slots[s * (per_pair + 1) + j]
            for t in range(steps):
                wide[2 * j, pl.ds(t, heads, stride=steps), :] = nope_ref[t, row].astype(jnp.float32)
                wide[2 * j + 1, pl.ds(t, heads, stride=steps), :] = jnp.concatenate(
                    [rope_ref[t, row].astype(jnp.float32)] * 2, axis=1
                )
        for j in range(per_pair):
            out_ref[e, j * rows : (j + 1) * rows, :] = wide[2 * j].astype(jnp.bfloat16)
            low = lax.broadcasted_iota(jnp.int32, (half, LANES), 1) < LANES // 2
            packed = jnp.where(low, wide[2 * j + 1, 0:half, :], wide[2 * j + 1, half : 2 * half, :])
            out_ref[e, rope_base + j * half : rope_base + (j + 1) * half, :] = packed.astype(jnp.bfloat16)

    if relative:
        dests = [me ^ k for k in range(sources)]
        for k in range(sources):
            one_dest(dests[k], out_refs[k], 0)
    else:
        dests = list(range(sources))

        def step(s, carry):
            one_dest(s, out_refs[0], s)
            return carry

        lax.fori_loop(0, sources, step, jnp.int32(0))
    shape = (sources * fresh_rows, steps * requests)
    row_id = lax.broadcasted_iota(jnp.int32, shape, 0)
    col_id = lax.broadcasted_iota(jnp.int32, shape, 1)
    wanted = jnp.full(shape, -1, jnp.int32)
    for k in range(sources):
        for j in range(per_pair):
            first = k * fresh_rows + j * steps
            here = (row_id >= first) & (row_id < first + steps)
            wanted = jnp.where(here, (row_id - first) * requests + slots[dests[k] * (per_pair + 1) + j], wanted)
    pick = jnp.where(col_id == wanted, 1.0, 0.0).astype(jnp.bfloat16)
    width = fresh_ref.shape[2]
    source_rows = jnp.concatenate([fresh_ref[t] for t in range(steps)], axis=0)
    picked = jnp.dot(pick, source_rows, preferred_element_type=jnp.float32).astype(jnp.bfloat16)
    for k in range(sources):
        for c in range(-(-width // LANES)):
            piece = picked[k * fresh_rows : (k + 1) * fresh_rows, c * LANES : min((c + 1) * LANES, width)]
            if piece.shape[1] < LANES:
                piece = jnp.concatenate([piece] * (LANES // piece.shape[1]), axis=1)
            first = fresh_base + c * fresh_rows
            if relative:
                out_refs[k][0, first : first + fresh_rows, :] = piece
            else:
                out_refs[0][k, first : first + fresh_rows, :] = piece


def attend_kernel(sizes, scale, relative, base, recv_count, ids_ref, decode_ref, length_ref, *rest):
    sources, per_pair, steps, heads, requests, fresh_rows = sizes
    recv_refs = rest[:recv_count]
    (
        cache, key_up, value_up, out_ref,
        slot_offset, slot_length, owner_count, pair_slot, pair_start,
        queries, fresh, acc, run_max, run_sum, latent, even_scores, odd_scores,
    ) = rest[recv_count:]
    owners = [(ref, e) for ref in recv_refs for e in range(ref.shape[0])]
    here = len(owners)
    slots = here * per_pair
    width, tokens = cache.shape
    rows = heads * steps
    half = rows // 2
    rope_base = per_pair * rows
    fresh_base = rope_base + per_pair * half
    group = 16 // steps
    shift = requests.bit_length() - 1
    factor = scale * LOG2E

    for e in range(here):
        ref, at = owners[e]
        for c in range(-(-width // LANES)):
            lanes = min(LANES, width - c * LANES)
            first = fresh_base + c * fresh_rows
            fresh[e * fresh_rows : (e + 1) * fresh_rows, c * LANES : c * LANES + lanes] = ref[
                at, first : first + fresh_rows, 0:lanes
            ]
        for j in range(per_pair):
            slot = e * per_pair + j
            first = rope_base + j * half
            piece = ref[at, first : first + half, :]
            queries[slot * rows : slot * rows + half, LATENT:width] = piece[:, 0 : width - LATENT]
            queries[slot * rows + half : (slot + 1) * rows, LATENT:width] = piece[:, LANES - (width - LATENT) :]

    inner_head = lax.broadcasted_iota(jnp.int32, (slots * 16, LANES), 0) // steps % group
    own_head = [jnp.where(inner_head == u, 1.0, 0.0).astype(jnp.bfloat16) for u in range(group)]
    for i in range(heads // group):
        tall = jnp.concatenate(
            [ref[at, j * rows + i * 16 : j * rows + (i + 1) * 16, :] for ref, at in owners for j in range(per_pair)],
            axis=0,
        )
        left = jnp.concatenate([tall * own_head[u] for u in range(group)], axis=1)
        right = jnp.concatenate([key_up[i * group + u] for u in range(group)], axis=0)
        res = jnp.dot(left, right, preferred_element_type=jnp.float32).astype(jnp.bfloat16)
        for slot in range(slots):
            queries[slot * rows + i * 16 : slot * rows + (i + 1) * 16, 0:LATENT] = res[slot * 16 : (slot + 1) * 16]

    me = ids_ref[0] & (PLACES - 1)
    for o in range(sources):
        owner_count[o] = jnp.int32(0)
    total = jnp.int32(0)
    for r in range(requests):
        owner = decode_ref[me * requests + r] >> shift
        at = owner_count[owner]
        owner_count[owner] = at + 1
        e = (owner ^ me) - base if relative else owner
        slot = jnp.where((e >= 0) & (e < here), e * per_pair + at, slots)
        length = length_ref[me, r]
        slot_offset[slot] = total
        slot_length[slot] = length
        total = total + length
    count = jnp.int32(0)
    for slot in range(slots):
        start = slot_offset[slot] & ~(LANES - 1)
        end = slot_offset[slot] + slot_length[slot]
        for k in range(512 // BLOCK + 1):
            pair_slot[count] = jnp.int32(slot)
            pair_start[count] = start + k * BLOCK
            count = count + jnp.where(start + k * BLOCK < end, 1, 0).astype(jnp.int32)

    fresh_scores = (
        lax.dot_general(queries[...], fresh[...], (((1,), (1,)), ((), ())), preferred_element_type=jnp.float32) * factor
    )
    row_id = lax.broadcasted_iota(jnp.int32, (rows, here * fresh_rows), 0)
    col_id = lax.broadcasted_iota(jnp.int32, (rows, here * fresh_rows), 1)
    behind = row_id & (steps - 1)
    fresh_weights = []
    for slot in range(slots):
        first = (slot // per_pair) * fresh_rows + (slot % per_pair) * steps
        seen = (col_id >= first) & (col_id <= first + behind)
        scores = jnp.where(seen, fresh_scores[slot * rows : (slot + 1) * rows], NEG)
        top = jnp.max(scores, axis=1, keepdims=True)
        weights = jnp.exp2(scores - top)
        run_max[slot] = jnp.broadcast_to(top, (rows, LANES))
        run_sum[slot] = jnp.broadcast_to(jnp.sum(weights, axis=1, keepdims=True), (rows, LANES))
        fresh_weights.append(weights.astype(jnp.bfloat16))
    for slot in range(slots):
        acc[slot] = jnp.dot(fresh_weights[slot], fresh[:, 0:LATENT], preferred_element_type=jnp.float32)

    def make_scores(buffer, g):
        for u in range(2):
            p = jnp.minimum(g * 2 + u, count - 1)
            q = queries[pl.ds(pl.multiple_of(pair_slot[p] * rows, 16), rows), :]
            read = pl.multiple_of(jnp.minimum(pair_start[p], tokens - BLOCK), LANES)
            buffer[u] = jnp.dot(q, cache[:, pl.ds(read, BLOCK)], preferred_element_type=jnp.float32)

    token = lax.broadcasted_iota(jnp.int32, (1, BLOCK), 1)

    def take_scores(buffer, g):
        for u in range(2):
            p = jnp.minimum(g * 2 + u, count - 1)
            slot = pair_slot[p]
            start = pair_start[p]
            read = jnp.minimum(start, tokens - BLOCK)
            low = jnp.maximum(slot_offset[slot], start) - read
            high = jnp.minimum(slot_offset[slot] + slot_length[slot], start + BLOCK) - read
            high = jnp.where(g * 2 + u < count, high, low)
            bias = jnp.where((token >= low) & (token < high), 0.0, NEG)
            scores = buffer[u] * factor + bias
            top = jnp.max(scores, axis=1, keepdims=True)
            weights = jnp.exp2(scores - top)
            part_sum = jnp.broadcast_to(jnp.sum(weights, axis=1, keepdims=True), (rows, LANES))
            part = lax.dot_general(
                weights.astype(jnp.bfloat16),
                cache[0:LATENT, pl.ds(pl.multiple_of(read, LANES), BLOCK)],
                (((1,), (1,)), ((), ())),
                preferred_element_type=jnp.float32,
            )
            part_max = jnp.broadcast_to(top, (rows, LANES))
            old_max = run_max[slot]
            new_max = jnp.maximum(old_max, part_max)
            keep = jnp.exp2(old_max - new_max)
            add = jnp.exp2(part_max - new_max)
            run_max[slot] = new_max
            run_sum[slot] = run_sum[slot] * keep + part_sum * add
            for c in range(LATENT // LANES):
                cols = slice(c * LANES, (c + 1) * LANES)
                acc[slot, :, cols] = acc[slot, :, cols] * keep + part[:, cols] * add

    make_scores(even_scores, 0)

    def four_pairs(i, carry):
        make_scores(odd_scores, 2 * i + 1)
        take_scores(even_scores, 2 * i)
        make_scores(even_scores, 2 * i + 2)
        take_scores(odd_scores, 2 * i + 1)
        return carry

    lax.fori_loop(0, (count + 3) // 4, four_pairs, jnp.int32(0))

    for slot in range(slots):
        inverse = 1.0 / run_sum[slot]
        for c in range(LATENT // LANES):
            cols = slice(c * LANES, (c + 1) * LANES)
            latent[slot * rows : (slot + 1) * rows, cols] = (acc[slot, :, cols] * inverse).astype(jnp.bfloat16)
    vdim = value_up.shape[2]
    for i in range(heads // group):
        left = jnp.concatenate(
            [latent[slot * rows + i * 16 : slot * rows + (i + 1) * 16, :] for slot in range(slots)], axis=0
        )
        right = jnp.concatenate([value_up[i * group + u] for u in range(group)], axis=1)
        res = jnp.dot(left, right, preferred_element_type=jnp.float32)
        for u in range(group):
            own = jnp.concatenate(
                [
                    res[slot * 16 + u * steps : slot * 16 + (u + 1) * steps, u * vdim : (u + 1) * vdim]
                    for slot in range(slots)
                ],
                axis=0,
            )
            head = i * group + u
            out_ref[:, head * vdim : (head + 1) * vdim] = own.astype(jnp.bfloat16)


def place_kernel(sizes, relative, ids_ref, decode_ref, out_ref, owner_count, place):
    sources, per_pair, steps, requests = sizes
    me = ids_ref[0] & (PLACES - 1)
    rows = sources * requests
    shift = requests.bit_length() - 1

    def one_source(s, carry):
        for o in range(sources):
            owner_count[o] = jnp.int32(0)
        for r in range(requests):
            row = decode_ref[s * requests + r]
            owner = row >> shift
            at = owner_count[owner]
            owner_count[owner] = at + 1
            if relative:
                e = owner ^ s
                at_row = (e >> 1) * (2 * sources * per_pair) + (me ^ s) * (2 * per_pair) + (e & 1) * per_pair + at
            else:
                at_row = s * requests + owner * per_pair + at
            place[row] = at_row * steps
        return carry

    lax.fori_loop(0, sources, one_source, jnp.int32(0))
    narrow = (rows, LANES)
    row_id = lax.broadcasted_iota(jnp.int32, narrow, 0)

    def put(b, wanted):
        return jnp.where(row_id == b, place[b], wanted)

    wanted = lax.fori_loop(0, rows, put, jnp.zeros(narrow, jnp.int32), unroll=8)[:, 0:1]
    col_id = lax.broadcasted_iota(jnp.int32, (rows, rows * steps), 1)
    for t in range(steps):
        out_ref[t] = jnp.where(col_id == wanted + t, 1.0, 0.0).astype(jnp.bfloat16)


def keeps_upper(ids_ref):
    return (ids_ref[0] // PLACES) % 2 == 1


def order_kernel(layout, ids_ref, pick_ref, *rest):
    pieces, out_ref, x = rest[:-2], rest[-2], rest[-1]
    upper = keeps_upper(ids_ref)

    def assemble(first, second):
        for i, (row, col) in enumerate(layout):
            rows, cols = pieces[2 * i].shape
            x[row : row + rows, col : col + cols] = pieces[2 * i + first][...]
            x[row + rows : row + 2 * rows, col : col + cols] = pieces[2 * i + second][...]

    pl.when(upper)(lambda: assemble(1, 0))
    pl.when(jnp.logical_not(upper))(lambda: assemble(0, 1))
    steps, rows, _ = pick_ref.shape
    pick = jnp.concatenate([pick_ref[t] for t in range(steps)], axis=0)
    for c in range(0, x.shape[1], BLOCK):
        tile = jnp.dot(pick, x[:, c : c + BLOCK], preferred_element_type=jnp.float32).astype(jnp.bfloat16)
        for t in range(steps):
            out_ref[t, :, c : c + BLOCK] = tile[t * rows : (t + 1) * rows]


def order_whole_kernel(pick_ref, x_ref, out_ref):
    for t in range(pick_ref.shape[0]):
        out_ref[t] = jnp.dot(pick_ref[t], x_ref[...], preferred_element_type=jnp.float32).astype(jnp.bfloat16)


def project_kernel(first_col, ids_ref, *rest):
    parts, (weight, keep, send) = rest[:-3], rest[-3:]
    half = keep.shape[0]
    upper = keeps_upper(ids_ref)
    cols = keep.shape[1]
    x = jnp.concatenate([part[...] for part in parts], axis=0)
    for c in range(0, cols, BLOCK):
        n = min(BLOCK, cols - c)
        tile = jnp.dot(x, weight[:, first_col + c : first_col + c + n], preferred_element_type=jnp.float32)
        keep[:, c : c + n] = jnp.where(upper, tile[half:], tile[:half]).astype(jnp.bfloat16)
        send[:, c : c + n] = jnp.where(upper, tile[:half], tile[half:]).astype(jnp.bfloat16)


def smem():
    return pl.BlockSpec(memory_space=pltpu.SMEM)


def vmem():
    return pl.BlockSpec(memory_space=pltpu.VMEM)


def anywhere():
    return pl.BlockSpec(memory_space=pl.ANY)


def limit(mib):
    return pltpu.CompilerParams(vmem_limit_bytes=mib * 1024 * 1024)


def cost(microseconds):
    return pl.CostEstimate(
        flops=int(microseconds * 1.0e9), bytes_accessed=int(microseconds * 3.0e6), transcendentals=0
    )


def flip(x, axis, distance):
    size = lax.axis_size(axis)
    return lax.ppermute(x, axis, [(i, i ^ distance) for i in range(size)])


def add(x, y):
    return (x.astype(jnp.float32) + y.astype(jnp.float32)).astype(jnp.bfloat16)


def local(latent_cache, lengths, decode_rows, q_nope, q_rope, new_latent, key_up, value_up, out_proj):
    sources = lax.axis_size("seq")
    head_devices = lax.axis_size("head")
    relative = sources == 4 and head_devices == 4
    requests = lengths.shape[1]
    per_pair = requests // sources
    tokens, width = latent_cache.shape
    steps, _, heads, nope = q_nope.shape
    scale = (nope + q_rope.shape[3]) ** (-0.5)
    fresh_rows = -(-per_pair * steps // 16) * 16
    rows = heads * steps
    columns = out_proj.shape[1]
    packed_rows = per_pair * rows + per_pair * rows // 2 + -(-width // LANES) * fresh_rows
    sizes = (sources, per_pair, steps, heads, requests, fresh_rows)
    ids = (lax.axis_index("seq") + PLACES * lax.axis_index("head")).astype(jnp.int32).reshape(1)
    cache = latent_cache.T

    pick = pl.pallas_call(
        functools.partial(place_kernel, (sources, per_pair, steps, requests), relative),
        out_shape=jax.ShapeDtypeStruct((steps, sources * requests, steps * sources * requests), jnp.bfloat16),
        in_specs=[smem(), smem()],
        out_specs=vmem(),
        scratch_shapes=[pltpu.SMEM((sources,), jnp.int32), pltpu.SMEM((sources * requests,), jnp.int32)],
        compiler_params=limit(12),
        cost_estimate=cost(2),
        name="place_rows",
    )(ids, decode_rows)

    outs, each = (sources, 1) if relative else (1, sources)
    packed = pl.pallas_call(
        functools.partial(pack_kernel, sizes, relative),
        out_shape=[jax.ShapeDtypeStruct((each, packed_rows, LANES), jnp.bfloat16)] * outs,
        in_specs=[smem(), smem(), vmem(), vmem(), vmem(), anywhere()],
        out_specs=[vmem()] * outs,
        scratch_shapes=[
            pltpu.SMEM((sources * (per_pair + 1),), jnp.int32),
            pltpu.VMEM((2 * per_pair, rows, LANES), jnp.float32),
        ],
        compiler_params=limit(8),
        cost_estimate=cost(6),
        name="pack_queries",
    )(ids, decode_rows, q_nope, q_rope, new_latent, pick)

    def attend(received, base):
        here = sum(part.shape[0] for part in received)
        slots = here * per_pair
        pairs = slots * (512 // BLOCK + 1) + 1
        return pl.pallas_call(
            functools.partial(attend_kernel, sizes, scale, relative, base, len(received)),
            out_shape=jax.ShapeDtypeStruct((slots * steps, heads * value_up.shape[2]), jnp.bfloat16),
            in_specs=[smem(), smem(), smem()] + [vmem()] * (len(received) + 3),
            out_specs=vmem(),
            scratch_shapes=[
                pltpu.SMEM((slots + 1,), jnp.int32),
                pltpu.SMEM((slots + 1,), jnp.int32),
                pltpu.SMEM((sources,), jnp.int32),
                pltpu.SMEM((pairs,), jnp.int32),
                pltpu.SMEM((pairs,), jnp.int32),
                pltpu.VMEM((slots * rows, width), jnp.bfloat16),
                pltpu.VMEM((here * fresh_rows, width), jnp.bfloat16),
                pltpu.VMEM((slots, rows, LATENT), jnp.float32),
                pltpu.VMEM((slots, rows, LANES), jnp.float32),
                pltpu.VMEM((slots, rows, LANES), jnp.float32),
                pltpu.VMEM((slots * rows, LATENT), jnp.bfloat16),
                pltpu.VMEM((2, rows, BLOCK), jnp.float32),
                pltpu.VMEM((2, rows, BLOCK), jnp.float32),
            ],
            compiler_params=limit(14),
            cost_estimate=cost(8),
            name="attend",
        )(ids, decode_rows, lengths, *received, cache, key_up, value_up)

    def order(kernel, in_specs, scratch, arrays):
        return pl.pallas_call(
            kernel,
            out_shape=jax.ShapeDtypeStruct((steps, sources * requests, columns), jnp.bfloat16),
            in_specs=in_specs,
            out_specs=vmem(),
            scratch_shapes=scratch,
            compiler_params=limit(16),
            cost_estimate=cost(2),
            name="order_rows",
        )(*arrays)

    if not relative:
        received = lax.all_to_all(packed[0], "seq", split_axis=0, concat_axis=0, tiled=True)
        every_row = lax.all_gather(attend([received], 0), "seq", axis=0, tiled=True)
        partial_value = jnp.dot(every_row, out_proj, preferred_element_type=jnp.float32).astype(jnp.bfloat16)
        shares = lax.all_to_all(partial_value, "head", split_axis=0, concat_axis=0, tiled=True)
        shares = shares.reshape(head_devices, -1, columns)
        summed = jnp.sum(shares.astype(jnp.float32), axis=0).astype(jnp.bfloat16)
        whole = lax.all_gather(summed, "head", axis=0, tiled=True)
        return order(order_whole_kernel, [vmem()] * 2, [], [pick, whole])

    def project(parts, first_col, cols):
        rows_here = len(parts) * parts[0].shape[0]
        return pl.pallas_call(
            functools.partial(project_kernel, first_col),
            out_shape=[jax.ShapeDtypeStruct((rows_here // 2, cols), jnp.bfloat16)] * 2,
            in_specs=[smem()] + [vmem()] * (len(parts) + 1),
            out_specs=[vmem()] * 2,
            compiler_params=limit(10),
            cost_estimate=cost(2),
            name="project_out",
        )(ids, *parts, out_proj)

    received = [packed[0]] + [flip(packed[k], "seq", k) for k in range(1, 4)]
    near_rows = attend(received[:2], 0)
    near_across = flip(near_rows, "seq", 2)
    far_rows = attend(received[2:], 2)
    near_across, far_rows = lax.optimization_barrier((near_across, far_rows))
    near = [near_rows, flip(near_rows, "seq", 1), near_across, flip(near_across, "seq", 1)]
    far_across = flip(far_rows, "seq", 2)

    def after(value, *others):
        return lax.optimization_barrier((value,) + others)[0]

    def swap(piece):
        return flip(piece[1], "head", 1)

    half = steps * sources * requests // 2

    def cut(parts, first_row, shares):
        groups = columns // LANES
        edges = [LANES * (groups * sum(shares[:i]) // sum(shares)) for i in range(len(shares) + 1)]
        made = []
        for at, end in zip(edges, edges[1:]):
            keep, send = project(parts, at, end - at)
            made.append((first_row, at, keep, swap((keep, send))))
        return made

    near_made = cut(near, 0, (5, 9))
    pairs = [add(near_made[0][2], near_made[0][3])]
    relayed = far_across
    far = [far_rows, flip(far_rows, "seq", 1), far_across, flip(relayed, "seq", 1)]
    far_made = cut(far, half, (6, 5, 3))
    made = near_made + far_made
    pairs += [add(keep, incoming) for _, _, keep, incoming in made[1:]]
    crossed = [flip(pair, "head", 2) for pair in pairs]
    last_made = made[-1][2]
    arrays = []
    for i, (pair, cross) in enumerate(zip(pairs, crossed)):
        if i < len(near_made):
            cross = after(cross, last_made)
        total = add(pair, cross)
        arrays += [total, flip(total, "head", 1)]
    layout = tuple((row, col) for row, col, _, _ in made)
    scratch = [pltpu.VMEM((2 * half, columns), jnp.bfloat16)]
    kernel = functools.partial(order_kernel, layout)
    return order(kernel, [smem()] + [vmem()] * (1 + len(arrays)), scratch, [ids, pick] + arrays)


def solution(mesh):
    return jax.shard_map(
        local,
        mesh=mesh,
        in_specs=(
            P(("groups", "seq"), None),
            P("groups", None),
            P("groups"),
            P(None, ("groups", "seq"), "head", None),
            P(None, ("groups", "seq"), "head", None),
            P(None, ("groups", "seq"), None),
            P("head", None, None),
            P("head", None, None),
            P("head", "seq"),
        ),
        out_specs=P(None, "groups", "seq"),
        check_vma=False,
    )
```

```python
import functools

import jax
import jax.numpy as jnp
from jax import lax
from jax.experimental import pallas as pl
from jax.experimental.pallas import tpu as pltpu
from jax.sharding import PartitionSpec as P

LATENT = 512
BLOCK = 256
LANES = 128
LOG2E = 1.4426950408889634
NEG = -1e30
PLACES = 1024


def own_slots(decode_ref, slot_ref, me, sources, requests, per_pair):
    shift = requests.bit_length() - 1

    def one_source(s, carry):
        count = jnp.int32(0)
        for r in range(requests):
            row = decode_ref[s * requests + r]
            slot_ref[s * (per_pair + 1) + jnp.minimum(count, per_pair)] = row & (requests - 1)
            count = count + jnp.where((row >> shift) == me, 1, 0).astype(jnp.int32)
        return carry

    lax.fori_loop(0, sources, one_source, jnp.int32(0))


def pack_kernel(sizes, relative, ids_ref, decode_ref, nope_ref, rope_ref, fresh_ref, after_ref, *rest):
    sources, per_pair, steps, heads, requests, fresh_rows = sizes
    out_refs, (slots, wide) = rest[:-2], rest[-2:]
    me = ids_ref[0] & (PLACES - 1)
    rows = heads * steps
    half = rows // 2
    rope_base = per_pair * rows
    fresh_base = rope_base + per_pair * half
    own_slots(decode_ref, slots, me, sources, requests, per_pair)

    def one_dest(s, out_ref, e):
        for j in range(per_pair):
            row = slots[s * (per_pair + 1) + j]
            for t in range(steps):
                wide[2 * j, pl.ds(t, heads, stride=steps), :] = nope_ref[t, row].astype(jnp.float32)
                wide[2 * j + 1, pl.ds(t, heads, stride=steps), :] = jnp.concatenate(
                    [rope_ref[t, row].astype(jnp.float32)] * 2, axis=1
                )
        for j in range(per_pair):
            out_ref[e, j * rows : (j + 1) * rows, :] = wide[2 * j].astype(jnp.bfloat16)
            low = lax.broadcasted_iota(jnp.int32, (half, LANES), 1) < LANES // 2
            packed = jnp.where(low, wide[2 * j + 1, 0:half, :], wide[2 * j + 1, half : 2 * half, :])
            out_ref[e, rope_base + j * half : rope_base + (j + 1) * half, :] = packed.astype(jnp.bfloat16)

    if relative:
        dests = [me ^ k for k in range(sources)]
        for k in range(sources):
            one_dest(dests[k], out_refs[k], 0)
    else:
        dests = list(range(sources))

        def step(s, carry):
            one_dest(s, out_refs[0], s)
            return carry

        lax.fori_loop(0, sources, step, jnp.int32(0))
    shape = (sources * fresh_rows, steps * requests)
    row_id = lax.broadcasted_iota(jnp.int32, shape, 0)
    col_id = lax.broadcasted_iota(jnp.int32, shape, 1)
    wanted = jnp.full(shape, -1, jnp.int32)
    for k in range(sources):
        for j in range(per_pair):
            first = k * fresh_rows + j * steps
            here = (row_id >= first) & (row_id < first + steps)
            wanted = jnp.where(here, (row_id - first) * requests + slots[dests[k] * (per_pair + 1) + j], wanted)
    pick = jnp.where(col_id == wanted, 1.0, 0.0).astype(jnp.bfloat16)
    width = fresh_ref.shape[2]
    source_rows = jnp.concatenate([fresh_ref[t] for t in range(steps)], axis=0)
    picked = jnp.dot(pick, source_rows, preferred_element_type=jnp.float32).astype(jnp.bfloat16)
    for k in range(sources):
        for c in range(-(-width // LANES)):
            piece = picked[k * fresh_rows : (k + 1) * fresh_rows, c * LANES : min((c + 1) * LANES, width)]
            if piece.shape[1] < LANES:
                piece = jnp.concatenate([piece] * (LANES // piece.shape[1]), axis=1)
            first = fresh_base + c * fresh_rows
            if relative:
                out_refs[k][0, first : first + fresh_rows, :] = piece
            else:
                out_refs[0][k, first : first + fresh_rows, :] = piece


def attend_kernel(sizes, scale, relative, base, recv_count, ids_ref, decode_ref, length_ref, *rest):
    sources, per_pair, steps, heads, requests, fresh_rows = sizes
    recv_refs = rest[:recv_count]
    (
        cache, key_up, value_up, out_ref,
        slot_offset, slot_length, owner_count, pair_slot, pair_start,
        queries, fresh, acc, run_max, run_sum, latent, even_scores, odd_scores,
    ) = rest[recv_count:]
    owners = [(ref, e) for ref in recv_refs for e in range(ref.shape[0])]
    here = len(owners)
    slots = here * per_pair
    width, tokens = cache.shape
    rows = heads * steps
    half = rows // 2
    rope_base = per_pair * rows
    fresh_base = rope_base + per_pair * half
    group = 16 // steps
    shift = requests.bit_length() - 1
    factor = scale * LOG2E

    for e in range(here):
        ref, at = owners[e]
        for c in range(-(-width // LANES)):
            lanes = min(LANES, width - c * LANES)
            first = fresh_base + c * fresh_rows
            fresh[e * fresh_rows : (e + 1) * fresh_rows, c * LANES : c * LANES + lanes] = ref[
                at, first : first + fresh_rows, 0:lanes
            ]
        for j in range(per_pair):
            slot = e * per_pair + j
            first = rope_base + j * half
            piece = ref[at, first : first + half, :]
            queries[slot * rows : slot * rows + half, LATENT:width] = piece[:, 0 : width - LATENT]
            queries[slot * rows + half : (slot + 1) * rows, LATENT:width] = piece[:, LANES - (width - LATENT) :]

    inner_head = lax.broadcasted_iota(jnp.int32, (slots * 16, LANES), 0) // steps % group
    own_head = [jnp.where(inner_head == u, 1.0, 0.0).astype(jnp.bfloat16) for u in range(group)]
    for i in range(heads // group):
        tall = jnp.concatenate(
            [ref[at, j * rows + i * 16 : j * rows + (i + 1) * 16, :] for ref, at in owners for j in range(per_pair)],
            axis=0,
        )
        left = jnp.concatenate([tall * own_head[u] for u in range(group)], axis=1)
        right = jnp.concatenate([key_up[i * group + u] for u in range(group)], axis=0)
        res = jnp.dot(left, right, preferred_element_type=jnp.float32).astype(jnp.bfloat16)
        for slot in range(slots):
            queries[slot * rows + i * 16 : slot * rows + (i + 1) * 16, 0:LATENT] = res[slot * 16 : (slot + 1) * 16]

    me = ids_ref[0] & (PLACES - 1)
    for o in range(sources):
        owner_count[o] = jnp.int32(0)
    total = jnp.int32(0)
    for r in range(requests):
        owner = decode_ref[me * requests + r] >> shift
        at = owner_count[owner]
        owner_count[owner] = at + 1
        e = (owner ^ me) - base if relative else owner
        slot = jnp.where((e >= 0) & (e < here), e * per_pair + at, slots)
        length = length_ref[me, r]
        slot_offset[slot] = total
        slot_length[slot] = length
        total = total + length
    count = jnp.int32(0)
    for slot in range(slots):
        start = slot_offset[slot] & ~(LANES - 1)
        end = slot_offset[slot] + slot_length[slot]
        for k in range(512 // BLOCK + 1):
            pair_slot[count] = jnp.int32(slot)
            pair_start[count] = start + k * BLOCK
            count = count + jnp.where(start + k * BLOCK < end, 1, 0).astype(jnp.int32)

    fresh_scores = (
        lax.dot_general(queries[...], fresh[...], (((1,), (1,)), ((), ())), preferred_element_type=jnp.float32) * factor
    )
    row_id = lax.broadcasted_iota(jnp.int32, (rows, here * fresh_rows), 0)
    col_id = lax.broadcasted_iota(jnp.int32, (rows, here * fresh_rows), 1)
    behind = row_id & (steps - 1)
    fresh_weights = []
    for slot in range(slots):
        first = (slot // per_pair) * fresh_rows + (slot % per_pair) * steps
        seen = (col_id >= first) & (col_id <= first + behind)
        scores = jnp.where(seen, fresh_scores[slot * rows : (slot + 1) * rows], NEG)
        top = jnp.max(scores, axis=1, keepdims=True)
        weights = jnp.exp2(scores - top)
        run_max[slot] = jnp.broadcast_to(top, (rows, LANES))
        run_sum[slot] = jnp.broadcast_to(jnp.sum(weights, axis=1, keepdims=True), (rows, LANES))
        fresh_weights.append(weights.astype(jnp.bfloat16))
    for slot in range(slots):
        acc[slot] = jnp.dot(fresh_weights[slot], fresh[:, 0:LATENT], preferred_element_type=jnp.float32)

    def make_scores(buffer, g):
        for u in range(2):
            p = jnp.minimum(g * 2 + u, count - 1)
            q = queries[pl.ds(pl.multiple_of(pair_slot[p] * rows, 16), rows), :]
            read = pl.multiple_of(jnp.minimum(pair_start[p], tokens - BLOCK), LANES)
            buffer[u] = jnp.dot(q, cache[:, pl.ds(read, BLOCK)], preferred_element_type=jnp.float32)

    token = lax.broadcasted_iota(jnp.int32, (1, BLOCK), 1)

    def take_scores(buffer, g):
        for u in range(2):
            p = jnp.minimum(g * 2 + u, count - 1)
            slot = pair_slot[p]
            start = pair_start[p]
            read = jnp.minimum(start, tokens - BLOCK)
            low = jnp.maximum(slot_offset[slot], start) - read
            high = jnp.minimum(slot_offset[slot] + slot_length[slot], start + BLOCK) - read
            high = jnp.where(g * 2 + u < count, high, low)
            bias = jnp.where((token >= low) & (token < high), 0.0, NEG)
            scores = buffer[u] * factor + bias
            top = jnp.max(scores, axis=1, keepdims=True)
            weights = jnp.exp2(scores - top)
            part_sum = jnp.broadcast_to(jnp.sum(weights, axis=1, keepdims=True), (rows, LANES))
            part = lax.dot_general(
                weights.astype(jnp.bfloat16),
                cache[0:LATENT, pl.ds(pl.multiple_of(read, LANES), BLOCK)],
                (((1,), (1,)), ((), ())),
                preferred_element_type=jnp.float32,
            )
            part_max = jnp.broadcast_to(top, (rows, LANES))
            old_max = run_max[slot]
            new_max = jnp.maximum(old_max, part_max)
            keep = jnp.exp2(old_max - new_max)
            add = jnp.exp2(part_max - new_max)
            run_max[slot] = new_max
            run_sum[slot] = run_sum[slot] * keep + part_sum * add
            for c in range(LATENT // LANES):
                cols = slice(c * LANES, (c + 1) * LANES)
                acc[slot, :, cols] = acc[slot, :, cols] * keep + part[:, cols] * add

    make_scores(even_scores, 0)

    def four_pairs(i, carry):
        make_scores(odd_scores, 2 * i + 1)
        take_scores(even_scores, 2 * i)
        make_scores(even_scores, 2 * i + 2)
        take_scores(odd_scores, 2 * i + 1)
        return carry

    fours = count >> 2
    lax.fori_loop(0, fours, four_pairs, jnp.int32(0))

    @pl.when(count > 4 * fours)
    def _():
        take_scores(even_scores, 2 * fours)

    @pl.when(count > 4 * fours + 2)
    def _():
        make_scores(odd_scores, 2 * fours + 1)
        take_scores(odd_scores, 2 * fours + 1)

    for slot in range(slots):
        inverse = 1.0 / run_sum[slot]
        for c in range(LATENT // LANES):
            cols = slice(c * LANES, (c + 1) * LANES)
            latent[slot * rows : (slot + 1) * rows, cols] = (acc[slot, :, cols] * inverse).astype(jnp.bfloat16)
    vdim = value_up.shape[2]
    for i in range(heads // group):
        left = jnp.concatenate(
            [latent[slot * rows + i * 16 : slot * rows + (i + 1) * 16, :] for slot in range(slots)], axis=0
        )
        right = jnp.concatenate([value_up[i * group + u] for u in range(group)], axis=1)
        res = jnp.dot(left, right, preferred_element_type=jnp.float32)
        for u in range(group):
            own = jnp.concatenate(
                [
                    res[slot * 16 + u * steps : slot * 16 + (u + 1) * steps, u * vdim : (u + 1) * vdim]
                    for slot in range(slots)
                ],
                axis=0,
            )
            head = i * group + u
            out_ref[:, head * vdim : (head + 1) * vdim] = own.astype(jnp.bfloat16)


def place_kernel(sizes, relative, ids_ref, decode_ref, out_ref, owner_count, place):
    sources, per_pair, steps, requests = sizes
    me = ids_ref[0] & (PLACES - 1)
    rows = sources * requests
    shift = requests.bit_length() - 1

    def one_source(s, carry):
        for o in range(sources):
            owner_count[o] = jnp.int32(0)
        for r in range(requests):
            row = decode_ref[s * requests + r]
            owner = row >> shift
            at = owner_count[owner]
            owner_count[owner] = at + 1
            if relative:
                e = owner ^ s
                at_row = (e >> 1) * (2 * sources * per_pair) + (me ^ s) * (2 * per_pair) + (e & 1) * per_pair + at
            else:
                at_row = s * requests + owner * per_pair + at
            place[row] = at_row * steps
        return carry

    lax.fori_loop(0, sources, one_source, jnp.int32(0))
    narrow = (rows, LANES)
    row_id = lax.broadcasted_iota(jnp.int32, narrow, 0)

    def put(b, wanted):
        return jnp.where(row_id == b, place[b], wanted)

    wanted = lax.fori_loop(0, rows, put, jnp.zeros(narrow, jnp.int32), unroll=8)[:, 0:1]
    col_id = lax.broadcasted_iota(jnp.int32, (rows, rows * steps), 1)
    for t in range(steps):
        out_ref[t] = jnp.where(col_id == wanted + t, 1.0, 0.0).astype(jnp.bfloat16)


def keeps_upper(ids_ref):
    z = ids_ref[0] // PLACES
    return (z == 1) | (z == 2)


def order_kernel(layout, ids_ref, pick_ref, *rest):
    pieces, out_ref, x = rest[:-2], rest[-2], rest[-1]
    upper = keeps_upper(ids_ref)

    def assemble(first, second):
        for i, (row, col) in enumerate(layout):
            rows, cols = pieces[2 * i].shape
            x[row : row + rows, col : col + cols] = pieces[2 * i + first][...]
            x[row + rows : row + 2 * rows, col : col + cols] = pieces[2 * i + second][...]

    pl.when(upper)(lambda: assemble(1, 0))
    pl.when(jnp.logical_not(upper))(lambda: assemble(0, 1))
    steps, rows, _ = pick_ref.shape
    pick = jnp.concatenate([pick_ref[t] for t in range(steps)], axis=0)
    for c in range(0, x.shape[1], BLOCK):
        tile = jnp.dot(pick, x[:, c : c + BLOCK], preferred_element_type=jnp.float32).astype(jnp.bfloat16)
        for t in range(steps):
            out_ref[t, :, c : c + BLOCK] = tile[t * rows : (t + 1) * rows]


def order_whole_kernel(pick_ref, x_ref, out_ref):
    for t in range(pick_ref.shape[0]):
        out_ref[t] = jnp.dot(pick_ref[t], x_ref[...], preferred_element_type=jnp.float32).astype(jnp.bfloat16)


def project_kernel(first_col, ids_ref, *rest):
    parts, (weight, keep, send) = rest[:-3], rest[-3:]
    half = keep.shape[0]
    upper = keeps_upper(ids_ref)
    cols = keep.shape[1]
    x = jnp.concatenate([part[...] for part in parts], axis=0)
    for c in range(0, cols, BLOCK):
        n = min(BLOCK, cols - c)
        tile = jnp.dot(x, weight[:, first_col + c : first_col + c + n], preferred_element_type=jnp.float32)
        keep[:, c : c + n] = jnp.where(upper, tile[half:], tile[:half]).astype(jnp.bfloat16)
        send[:, c : c + n] = jnp.where(upper, tile[:half], tile[half:]).astype(jnp.bfloat16)


def smem():
    return pl.BlockSpec(memory_space=pltpu.SMEM)


def vmem():
    return pl.BlockSpec(memory_space=pltpu.VMEM)


def anywhere():
    return pl.BlockSpec(memory_space=pl.ANY)


def limit(mib):
    return pltpu.CompilerParams(vmem_limit_bytes=mib * 1024 * 1024)


def cost(microseconds):
    return pl.CostEstimate(
        flops=int(microseconds * 1.0e9), bytes_accessed=int(microseconds * 3.0e6), transcendentals=0
    )


def flip(x, axis, distance):
    size = lax.axis_size(axis)
    return lax.ppermute(x, axis, [(i, i ^ distance) for i in range(size)])


def add(x, y):
    return (x.astype(jnp.float32) + y.astype(jnp.float32)).astype(jnp.bfloat16)


def local(latent_cache, lengths, decode_rows, q_nope, q_rope, new_latent, key_up, value_up, out_proj):
    sources = lax.axis_size("seq")
    head_devices = lax.axis_size("head")
    relative = sources == 4 and head_devices == 4
    requests = lengths.shape[1]
    per_pair = requests // sources
    tokens, width = latent_cache.shape
    steps, _, heads, nope = q_nope.shape
    scale = (nope + q_rope.shape[3]) ** (-0.5)
    fresh_rows = -(-per_pair * steps // 16) * 16
    rows = heads * steps
    columns = out_proj.shape[1]
    packed_rows = per_pair * rows + per_pair * rows // 2 + -(-width // LANES) * fresh_rows
    sizes = (sources, per_pair, steps, heads, requests, fresh_rows)
    ids = (lax.axis_index("seq") + PLACES * lax.axis_index("head")).astype(jnp.int32).reshape(1)
    cache = latent_cache.T

    pick = pl.pallas_call(
        functools.partial(place_kernel, (sources, per_pair, steps, requests), relative),
        out_shape=jax.ShapeDtypeStruct((steps, sources * requests, steps * sources * requests), jnp.bfloat16),
        in_specs=[smem(), smem()],
        out_specs=vmem(),
        scratch_shapes=[pltpu.SMEM((sources,), jnp.int32), pltpu.SMEM((sources * requests,), jnp.int32)],
        compiler_params=limit(12),
        cost_estimate=cost(2),
        name="place_rows",
    )(ids, decode_rows)

    outs, each = (sources, 1) if relative else (1, sources)
    packed = pl.pallas_call(
        functools.partial(pack_kernel, sizes, relative),
        out_shape=[jax.ShapeDtypeStruct((each, packed_rows, LANES), jnp.bfloat16)] * outs,
        in_specs=[smem(), smem(), vmem(), vmem(), vmem(), anywhere()],
        out_specs=[vmem()] * outs,
        scratch_shapes=[
            pltpu.SMEM((sources * (per_pair + 1),), jnp.int32),
            pltpu.VMEM((2 * per_pair, rows, LANES), jnp.float32),
        ],
        compiler_params=limit(8),
        cost_estimate=cost(6),
        name="pack_queries",
    )(ids, decode_rows, q_nope, q_rope, new_latent, pick)

    def attend(received, base):
        here = sum(part.shape[0] for part in received)
        slots = here * per_pair
        pairs = slots * (512 // BLOCK + 1) + 1
        return pl.pallas_call(
            functools.partial(attend_kernel, sizes, scale, relative, base, len(received)),
            out_shape=jax.ShapeDtypeStruct((slots * steps, heads * value_up.shape[2]), jnp.bfloat16),
            in_specs=[smem(), smem(), smem()] + [vmem()] * (len(received) + 3),
            out_specs=vmem(),
            scratch_shapes=[
                pltpu.SMEM((slots + 1,), jnp.int32),
                pltpu.SMEM((slots + 1,), jnp.int32),
                pltpu.SMEM((sources,), jnp.int32),
                pltpu.SMEM((pairs,), jnp.int32),
                pltpu.SMEM((pairs,), jnp.int32),
                pltpu.VMEM((slots * rows, width), jnp.bfloat16),
                pltpu.VMEM((here * fresh_rows, width), jnp.bfloat16),
                pltpu.VMEM((slots, rows, LATENT), jnp.float32),
                pltpu.VMEM((slots, rows, LANES), jnp.float32),
                pltpu.VMEM((slots, rows, LANES), jnp.float32),
                pltpu.VMEM((slots * rows, LATENT), jnp.bfloat16),
                pltpu.VMEM((2, rows, BLOCK), jnp.float32),
                pltpu.VMEM((2, rows, BLOCK), jnp.float32),
            ],
            compiler_params=limit(14),
            cost_estimate=cost(8),
            name="attend",
        )(ids, decode_rows, lengths, *received, cache, key_up, value_up)

    def order(kernel, in_specs, scratch, arrays):
        return pl.pallas_call(
            kernel,
            out_shape=jax.ShapeDtypeStruct((steps, sources * requests, columns), jnp.bfloat16),
            in_specs=in_specs,
            out_specs=vmem(),
            scratch_shapes=scratch,
            compiler_params=limit(16),
            cost_estimate=cost(2),
            name="order_rows",
        )(*arrays)

    if not relative:
        received = lax.all_to_all(packed[0], "seq", split_axis=0, concat_axis=0, tiled=True)
        every_row = lax.all_gather(attend([received], 0), "seq", axis=0, tiled=True)
        partial_value = jnp.dot(every_row, out_proj, preferred_element_type=jnp.float32).astype(jnp.bfloat16)
        shares = lax.all_to_all(partial_value, "head", split_axis=0, concat_axis=0, tiled=True)
        shares = shares.reshape(head_devices, -1, columns)
        summed = jnp.sum(shares.astype(jnp.float32), axis=0).astype(jnp.bfloat16)
        whole = lax.all_gather(summed, "head", axis=0, tiled=True)
        return order(order_whole_kernel, [vmem()] * 2, [], [pick, whole])

    def project(parts, first_col, cols):
        rows_here = len(parts) * parts[0].shape[0]
        return pl.pallas_call(
            functools.partial(project_kernel, first_col),
            out_shape=[jax.ShapeDtypeStruct((rows_here // 2, cols), jnp.bfloat16)] * 2,
            in_specs=[smem()] + [vmem()] * (len(parts) + 1),
            out_specs=[vmem()] * 2,
            compiler_params=limit(10),
            cost_estimate=cost(2),
            name="project_out",
        )(ids, *parts, out_proj)

    received = [packed[0]] + [flip(packed[k], "seq", k) for k in range(1, 4)]
    near_rows = attend(received[:2], 0)
    near_across = flip(near_rows, "seq", 2)
    far_rows = attend(received[2:], 2)
    near_across, far_rows = lax.optimization_barrier((near_across, far_rows))
    near = [near_rows, flip(near_rows, "seq", 1), near_across, flip(near_across, "seq", 1)]
    far_across = flip(far_rows, "seq", 2)

    def after(value, *others):
        return lax.optimization_barrier((value,) + others)[0]

    def swap(piece):
        return flip(piece[1], "head", 1)

    half = steps * sources * requests // 2

    def cut(parts, first_row, shares):
        groups = columns // LANES
        edges = [LANES * (groups * sum(shares[:i]) // sum(shares)) for i in range(len(shares) + 1)]
        made = []
        for at, end in zip(edges, edges[1:]):
            keep, send = project(parts, at, end - at)
            made.append((first_row, at, keep, swap((keep, send))))
        return made

    near_made = cut(near, 0, (5, 9))
    pairs = [add(near_made[0][2], near_made[0][3])]
    far = [far_rows, flip(far_rows, "seq", 1), far_across, flip(far_across, "seq", 1)]
    far_made = cut(far, half, (6, 5, 3))
    made = near_made + far_made
    for i, (_, _, keep, incoming) in enumerate(made[1:], 1):
        pairs.append(add(keep, incoming))
    crossed = [flip(pair, "head", 3) for pair in pairs]
    last_made = made[-1][2]
    arrays = []
    for i, (pair, cross) in enumerate(zip(pairs, crossed)):
        if i < len(near_made):
            cross = after(cross, *(pairs[len(near_made)],))
        total = add(pair, cross)
        arrays += [total, flip(total, "head", 1)]
    layout = tuple((row, col) for row, col, _, _ in made)
    scratch = [pltpu.VMEM((2 * half, columns), jnp.bfloat16)]
    kernel = functools.partial(order_kernel, layout)
    return order(kernel, [smem()] + [vmem()] * (1 + len(arrays)), scratch, [ids, pick] + arrays)


def solution(mesh):
    return jax.shard_map(
        local,
        mesh=mesh,
        in_specs=(
            P(("groups", "seq"), None),
            P("groups", None),
            P("groups"),
            P(None, ("groups", "seq"), "head", None),
            P(None, ("groups", "seq"), "head", None),
            P(None, ("groups", "seq"), None),
            P("head", None, None),
            P("head", None, None),
            P("head", "seq"),
        ),
        out_specs=P(None, "groups", "seq"),
        check_vma=False,
    )
```

```python
import functools

import jax
import jax.numpy as jnp
from jax import lax
from jax.experimental import pallas as pl
from jax.experimental.pallas import tpu as pltpu
from jax.sharding import PartitionSpec as P

LATENT = 512
BLOCK = 256
LANES = 128
LOG2E = 1.4426950408889634
NEG = -1e30
PLACES = 1024


def own_slots(decode_ref, slot_ref, me, sources, requests, per_pair):
    shift = requests.bit_length() - 1

    def one_source(s, carry):
        count = jnp.int32(0)
        for r in range(requests):
            row = decode_ref[s * requests + r]
            slot_ref[s * (per_pair + 1) + jnp.minimum(count, per_pair)] = row & (requests - 1)
            count = count + jnp.where((row >> shift) == me, 1, 0).astype(jnp.int32)
        return carry

    lax.fori_loop(0, sources, one_source, jnp.int32(0))


def pack_kernel(sizes, relative, ids_ref, decode_ref, nope_ref, rope_ref, fresh_ref, after_ref, *rest):
    sources, per_pair, steps, heads, requests, fresh_rows = sizes
    out_refs, (slots, wide) = rest[:-2], rest[-2:]
    me = ids_ref[0] & (PLACES - 1)
    rows = heads * steps
    half = rows // 2
    rope_base = per_pair * rows
    fresh_base = rope_base + per_pair * half
    own_slots(decode_ref, slots, me, sources, requests, per_pair)

    def one_dest(s, out_ref, e):
        for j in range(per_pair):
            row = slots[s * (per_pair + 1) + j]
            for t in range(steps):
                wide[2 * j, pl.ds(t, heads, stride=steps), :] = nope_ref[t, row].astype(jnp.float32)
                wide[2 * j + 1, pl.ds(t, heads, stride=steps), :] = jnp.concatenate(
                    [rope_ref[t, row].astype(jnp.float32)] * 2, axis=1
                )
        for j in range(per_pair):
            out_ref[e, j * rows : (j + 1) * rows, :] = wide[2 * j].astype(jnp.bfloat16)
            low = lax.broadcasted_iota(jnp.int32, (half, LANES), 1) < LANES // 2
            packed = jnp.where(low, wide[2 * j + 1, 0:half, :], wide[2 * j + 1, half : 2 * half, :])
            out_ref[e, rope_base + j * half : rope_base + (j + 1) * half, :] = packed.astype(jnp.bfloat16)

    if relative:
        dests = [me ^ k for k in range(sources)]
        for k in range(sources):
            one_dest(dests[k], out_refs[k], 0)
    else:
        dests = list(range(sources))

        def step(s, carry):
            one_dest(s, out_refs[0], s)
            return carry

        lax.fori_loop(0, sources, step, jnp.int32(0))
    shape = (sources * fresh_rows, steps * requests)
    row_id = lax.broadcasted_iota(jnp.int32, shape, 0)
    col_id = lax.broadcasted_iota(jnp.int32, shape, 1)
    wanted = jnp.full(shape, -1, jnp.int32)
    for k in range(sources):
        for j in range(per_pair):
            first = k * fresh_rows + j * steps
            here = (row_id >= first) & (row_id < first + steps)
            wanted = jnp.where(here, (row_id - first) * requests + slots[dests[k] * (per_pair + 1) + j], wanted)
    pick = jnp.where(col_id == wanted, 1.0, 0.0).astype(jnp.bfloat16)
    width = fresh_ref.shape[2]
    source_rows = jnp.concatenate([fresh_ref[t] for t in range(steps)], axis=0)
    picked = jnp.dot(pick, source_rows, preferred_element_type=jnp.float32).astype(jnp.bfloat16)
    for k in range(sources):
        for c in range(-(-width // LANES)):
            piece = picked[k * fresh_rows : (k + 1) * fresh_rows, c * LANES : min((c + 1) * LANES, width)]
            if piece.shape[1] < LANES:
                piece = jnp.concatenate([piece] * (LANES // piece.shape[1]), axis=1)
            first = fresh_base + c * fresh_rows
            if relative:
                out_refs[k][0, first : first + fresh_rows, :] = piece
            else:
                out_refs[0][k, first : first + fresh_rows, :] = piece


def attend_kernel(sizes, scale, relative, base, recv_count, ids_any, decode_any, length_any, *rest):
    sources, per_pair, steps, heads, requests, fresh_rows = sizes
    recv_refs = rest[:recv_count]
    (
        cache, key_up, value_up, out_ref,
        slot_offset, slot_length, owner_count, pair_slot, pair_start,
        queries, fresh, acc, run_max, run_sum, latent, even_scores, odd_scores,
        ids_ref, decode_ref, length_ref, sems,
    ) = rest[recv_count:]
    tables = [
        pltpu.make_async_copy(ids_any, ids_ref, sems.at[0]),
        pltpu.make_async_copy(decode_any, decode_ref, sems.at[1]),
        pltpu.make_async_copy(length_any, length_ref, sems.at[2]),
    ]
    for table in tables:
        table.start()
    owners = [(ref, e) for ref in recv_refs for e in range(ref.shape[0])]
    here = len(owners)
    slots = here * per_pair
    width, tokens = cache.shape
    rows = heads * steps
    half = rows // 2
    rope_base = per_pair * rows
    fresh_base = rope_base + per_pair * half
    group = 16 // steps
    shift = requests.bit_length() - 1
    factor = scale * LOG2E

    for e in range(here):
        ref, at = owners[e]
        for c in range(-(-width // LANES)):
            lanes = min(LANES, width - c * LANES)
            first = fresh_base + c * fresh_rows
            fresh[e * fresh_rows : (e + 1) * fresh_rows, c * LANES : c * LANES + lanes] = ref[
                at, first : first + fresh_rows, 0:lanes
            ]
        for j in range(per_pair):
            slot = e * per_pair + j
            first = rope_base + j * half
            piece = ref[at, first : first + half, :]
            queries[slot * rows : slot * rows + half, LATENT:width] = piece[:, 0 : width - LATENT]
            queries[slot * rows + half : (slot + 1) * rows, LATENT:width] = piece[:, LANES - (width - LATENT) :]

    inner_head = lax.broadcasted_iota(jnp.int32, (slots * 16, LANES), 0) // steps % group
    own_head = [jnp.where(inner_head == u, 1.0, 0.0).astype(jnp.bfloat16) for u in range(group)]

    def absorb(i):
        tall = jnp.concatenate(
            [ref[at, j * rows + i * 16 : j * rows + (i + 1) * 16, :] for ref, at in owners for j in range(per_pair)],
            axis=0,
        )
        left = jnp.concatenate([tall * own_head[u] for u in range(group)], axis=1)
        right = jnp.concatenate([key_up[i * group + u] for u in range(group)], axis=0)
        res = jnp.dot(left, right, preferred_element_type=jnp.float32).astype(jnp.bfloat16)
        for slot in range(slots):
            queries[slot * rows + i * 16 : slot * rows + (i + 1) * 16, 0:LATENT] = res[slot * 16 : (slot + 1) * 16]

    groups = heads // group
    for i in range(groups // 4):
        absorb(i)
    for table in tables:
        table.wait()

    me = ids_ref[0] & (PLACES - 1)
    for o in range(sources):
        owner_count[o] = jnp.int32(0)
    total = jnp.int32(0)
    for r in range(requests):
        owner = decode_ref[me * requests + r] >> shift
        at = owner_count[owner]
        owner_count[owner] = at + 1
        e = (owner ^ me) - base if relative else owner
        slot = jnp.where((e >= 0) & (e < here), e * per_pair + at, slots)
        length = length_ref[me, r]
        slot_offset[slot] = total
        slot_length[slot] = length
        total = total + length
    count = jnp.int32(0)
    for slot in range(slots):
        start = slot_offset[slot] & ~(LANES - 1)
        end = slot_offset[slot] + slot_length[slot]
        for k in range(512 // BLOCK + 1):
            pair_slot[count] = jnp.int32(slot)
            pair_start[count] = start + k * BLOCK
            count = count + jnp.where(start + k * BLOCK < end, 1, 0).astype(jnp.int32)

    for i in range(groups // 4, groups):
        absorb(i)

    fresh_scores = (
        lax.dot_general(queries[...], fresh[...], (((1,), (1,)), ((), ())), preferred_element_type=jnp.float32) * factor
    )
    row_id = lax.broadcasted_iota(jnp.int32, (rows, here * fresh_rows), 0)
    col_id = lax.broadcasted_iota(jnp.int32, (rows, here * fresh_rows), 1)
    behind = row_id & (steps - 1)
    fresh_weights = []
    for slot in range(slots):
        first = (slot // per_pair) * fresh_rows + (slot % per_pair) * steps
        seen = (col_id >= first) & (col_id <= first + behind)
        scores = jnp.where(seen, fresh_scores[slot * rows : (slot + 1) * rows], NEG)
        top = jnp.max(scores, axis=1, keepdims=True)
        weights = jnp.exp2(scores - top)
        run_max[slot] = jnp.broadcast_to(top, (rows, LANES))
        run_sum[slot] = jnp.broadcast_to(jnp.sum(weights, axis=1, keepdims=True), (rows, LANES))
        fresh_weights.append(weights.astype(jnp.bfloat16))
    for slot in range(slots):
        acc[slot] = jnp.dot(fresh_weights[slot], fresh[:, 0:LATENT], preferred_element_type=jnp.float32)

    def make_scores(buffer, g):
        for u in range(2):
            p = jnp.minimum(g * 2 + u, count - 1)
            q = queries[pl.ds(pl.multiple_of(pair_slot[p] * rows, 16), rows), :]
            read = pl.multiple_of(jnp.minimum(pair_start[p], tokens - BLOCK), LANES)
            buffer[u] = jnp.dot(q, cache[:, pl.ds(read, BLOCK)], preferred_element_type=jnp.float32)

    token = lax.broadcasted_iota(jnp.int32, (1, BLOCK), 1)

    def take_scores(buffer, g):
        for u in range(2):
            p = jnp.minimum(g * 2 + u, count - 1)
            slot = pair_slot[p]
            start = pair_start[p]
            read = jnp.minimum(start, tokens - BLOCK)
            low = jnp.maximum(slot_offset[slot], start) - read
            high = jnp.minimum(slot_offset[slot] + slot_length[slot], start + BLOCK) - read
            high = jnp.where(g * 2 + u < count, high, low)
            bias = jnp.where((token >= low) & (token < high), 0.0, NEG)
            scores = buffer[u] * factor + bias
            top = jnp.max(scores, axis=1, keepdims=True)
            weights = jnp.exp2(scores - top)
            part_sum = jnp.broadcast_to(jnp.sum(weights, axis=1, keepdims=True), (rows, LANES))
            part = lax.dot_general(
                weights.astype(jnp.bfloat16),
                cache[0:LATENT, pl.ds(pl.multiple_of(read, LANES), BLOCK)],
                (((1,), (1,)), ((), ())),
                preferred_element_type=jnp.float32,
            )
            part_max = jnp.broadcast_to(top, (rows, LANES))
            old_max = run_max[slot]
            new_max = jnp.maximum(old_max, part_max)
            keep = jnp.exp2(old_max - new_max)
            add = jnp.exp2(part_max - new_max)
            run_max[slot] = new_max
            run_sum[slot] = run_sum[slot] * keep + part_sum * add
            for c in range(LATENT // LANES):
                cols = slice(c * LANES, (c + 1) * LANES)
                acc[slot, :, cols] = acc[slot, :, cols] * keep + part[:, cols] * add

    make_scores(even_scores, 0)

    def four_pairs(i, carry):
        make_scores(odd_scores, 2 * i + 1)
        take_scores(even_scores, 2 * i)
        make_scores(even_scores, 2 * i + 2)
        take_scores(odd_scores, 2 * i + 1)
        return carry

    fours = count >> 2
    lax.fori_loop(0, fours, four_pairs, jnp.int32(0))

    @pl.when(count > 4 * fours)
    def _():
        take_scores(even_scores, 2 * fours)

    @pl.when(count > 4 * fours + 2)
    def _():
        make_scores(odd_scores, 2 * fours + 1)
        take_scores(odd_scores, 2 * fours + 1)

    for slot in range(slots):
        inverse = 1.0 / run_sum[slot]
        for c in range(LATENT // LANES):
            cols = slice(c * LANES, (c + 1) * LANES)
            latent[slot * rows : (slot + 1) * rows, cols] = (acc[slot, :, cols] * inverse).astype(jnp.bfloat16)
    vdim = value_up.shape[2]
    for i in range(heads // group):
        left = jnp.concatenate(
            [latent[slot * rows + i * 16 : slot * rows + (i + 1) * 16, :] for slot in range(slots)], axis=0
        )
        right = jnp.concatenate([value_up[i * group + u] for u in range(group)], axis=1)
        res = jnp.dot(left, right, preferred_element_type=jnp.float32)
        for u in range(group):
            own = jnp.concatenate(
                [
                    res[slot * 16 + u * steps : slot * 16 + (u + 1) * steps, u * vdim : (u + 1) * vdim]
                    for slot in range(slots)
                ],
                axis=0,
            )
            head = i * group + u
            out_ref[:, head * vdim : (head + 1) * vdim] = own.astype(jnp.bfloat16)


def place_kernel(sizes, relative, ids_ref, decode_ref, out_ref, owner_count, place):
    sources, per_pair, steps, requests = sizes
    me = ids_ref[0] & (PLACES - 1)
    rows = sources * requests
    shift = requests.bit_length() - 1

    def one_source(s, carry):
        for o in range(sources):
            owner_count[o] = jnp.int32(0)
        for r in range(requests):
            row = decode_ref[s * requests + r]
            owner = row >> shift
            at = owner_count[owner]
            owner_count[owner] = at + 1
            if relative:
                e = owner ^ s
                at_row = (e >> 1) * (2 * sources * per_pair) + (me ^ s) * (2 * per_pair) + (e & 1) * per_pair + at
            else:
                at_row = s * requests + owner * per_pair + at
            place[row] = at_row * steps
        return carry

    lax.fori_loop(0, sources, one_source, jnp.int32(0))
    narrow = (rows, LANES)
    row_id = lax.broadcasted_iota(jnp.int32, narrow, 0)

    def put(b, wanted):
        return jnp.where(row_id == b, place[b], wanted)

    wanted = lax.fori_loop(0, rows, put, jnp.zeros(narrow, jnp.int32), unroll=8)[:, 0:1]
    col_id = lax.broadcasted_iota(jnp.int32, (rows, rows * steps), 1)
    for t in range(steps):
        out_ref[t] = jnp.where(col_id == wanted + t, 1.0, 0.0).astype(jnp.bfloat16)


def keeps_upper(ids_ref):
    z = ids_ref[0] // PLACES
    return (z == 1) | (z == 2)


def order_kernel(layout, ids_ref, pick_ref, *rest):
    pieces, out_ref, x = rest[:-2], rest[-2], rest[-1]
    upper = keeps_upper(ids_ref)

    def assemble(first, second):
        for i, (row, col) in enumerate(layout):
            rows, cols = pieces[2 * i].shape
            x[row : row + rows, col : col + cols] = pieces[2 * i + first][...]
            x[row + rows : row + 2 * rows, col : col + cols] = pieces[2 * i + second][...]

    pl.when(upper)(lambda: assemble(1, 0))
    pl.when(jnp.logical_not(upper))(lambda: assemble(0, 1))
    steps, rows, _ = pick_ref.shape
    pick = jnp.concatenate([pick_ref[t] for t in range(steps)], axis=0)
    for c in range(0, x.shape[1], BLOCK):
        tile = jnp.dot(pick, x[:, c : c + BLOCK], preferred_element_type=jnp.float32).astype(jnp.bfloat16)
        for t in range(steps):
            out_ref[t, :, c : c + BLOCK] = tile[t * rows : (t + 1) * rows]


def order_whole_kernel(pick_ref, x_ref, out_ref):
    for t in range(pick_ref.shape[0]):
        out_ref[t] = jnp.dot(pick_ref[t], x_ref[...], preferred_element_type=jnp.float32).astype(jnp.bfloat16)


def project_kernel(first_col, ids_ref, *rest):
    parts, (weight, keep, send) = rest[:-3], rest[-3:]
    half = keep.shape[0]
    upper = keeps_upper(ids_ref)
    cols = keep.shape[1]
    x = jnp.concatenate([part[...] for part in parts], axis=0)
    for c in range(0, cols, BLOCK):
        n = min(BLOCK, cols - c)
        tile = jnp.dot(x, weight[:, first_col + c : first_col + c + n], preferred_element_type=jnp.float32)
        keep[:, c : c + n] = jnp.where(upper, tile[half:], tile[:half]).astype(jnp.bfloat16)
        send[:, c : c + n] = jnp.where(upper, tile[:half], tile[half:]).astype(jnp.bfloat16)


def smem():
    return pl.BlockSpec(memory_space=pltpu.SMEM)


def vmem():
    return pl.BlockSpec(memory_space=pltpu.VMEM)


def anywhere():
    return pl.BlockSpec(memory_space=pl.ANY)


def limit(mib):
    return pltpu.CompilerParams(vmem_limit_bytes=mib * 1024 * 1024)


def cost(microseconds):
    return pl.CostEstimate(
        flops=int(microseconds * 1.0e9), bytes_accessed=int(microseconds * 3.0e6), transcendentals=0
    )


def flip(x, axis, distance):
    size = lax.axis_size(axis)
    return lax.ppermute(x, axis, [(i, i ^ distance) for i in range(size)])


def add(x, y):
    return (x.astype(jnp.float32) + y.astype(jnp.float32)).astype(jnp.bfloat16)


def local(latent_cache, lengths, decode_rows, q_nope, q_rope, new_latent, key_up, value_up, out_proj):
    sources = lax.axis_size("seq")
    head_devices = lax.axis_size("head")
    relative = sources == 4 and head_devices == 4
    requests = lengths.shape[1]
    per_pair = requests // sources
    tokens, width = latent_cache.shape
    steps, _, heads, nope = q_nope.shape
    scale = (nope + q_rope.shape[3]) ** (-0.5)
    fresh_rows = -(-per_pair * steps // 16) * 16
    rows = heads * steps
    columns = out_proj.shape[1]
    packed_rows = per_pair * rows + per_pair * rows // 2 + -(-width // LANES) * fresh_rows
    sizes = (sources, per_pair, steps, heads, requests, fresh_rows)
    ids = (lax.axis_index("seq") + PLACES * lax.axis_index("head")).astype(jnp.int32).reshape(1)
    cache = latent_cache.T

    pick = pl.pallas_call(
        functools.partial(place_kernel, (sources, per_pair, steps, requests), relative),
        out_shape=jax.ShapeDtypeStruct((steps, sources * requests, steps * sources * requests), jnp.bfloat16),
        in_specs=[smem(), smem()],
        out_specs=vmem(),
        scratch_shapes=[pltpu.SMEM((sources,), jnp.int32), pltpu.SMEM((sources * requests,), jnp.int32)],
        compiler_params=limit(12),
        cost_estimate=cost(2),
        name="place_rows",
    )(ids, decode_rows)

    outs, each = (sources, 1) if relative else (1, sources)
    packed = pl.pallas_call(
        functools.partial(pack_kernel, sizes, relative),
        out_shape=[jax.ShapeDtypeStruct((each, packed_rows, LANES), jnp.bfloat16)] * outs,
        in_specs=[smem(), smem(), vmem(), vmem(), vmem(), anywhere()],
        out_specs=[vmem()] * outs,
        scratch_shapes=[
            pltpu.SMEM((sources * (per_pair + 1),), jnp.int32),
            pltpu.VMEM((2 * per_pair, rows, LANES), jnp.float32),
        ],
        compiler_params=limit(8),
        cost_estimate=cost(2),
        name="pack_queries",
    )(ids, decode_rows, q_nope, q_rope, new_latent, pick)

    def attend(received, base):
        here = sum(part.shape[0] for part in received)
        slots = here * per_pair
        pairs = slots * (512 // BLOCK + 1) + 1
        return pl.pallas_call(
            functools.partial(attend_kernel, sizes, scale, relative, base, len(received)),
            out_shape=jax.ShapeDtypeStruct((slots * steps, heads * value_up.shape[2]), jnp.bfloat16),
            in_specs=[anywhere()] * 3 + [vmem()] * (len(received) + 3),
            out_specs=vmem(),
            scratch_shapes=[
                pltpu.SMEM((slots + 1,), jnp.int32),
                pltpu.SMEM((slots + 1,), jnp.int32),
                pltpu.SMEM((sources,), jnp.int32),
                pltpu.SMEM((pairs,), jnp.int32),
                pltpu.SMEM((pairs,), jnp.int32),
                pltpu.VMEM((slots * rows, width), jnp.bfloat16),
                pltpu.VMEM((here * fresh_rows, width), jnp.bfloat16),
                pltpu.VMEM((slots, rows, LATENT), jnp.float32),
                pltpu.VMEM((slots, rows, LANES), jnp.float32),
                pltpu.VMEM((slots, rows, LANES), jnp.float32),
                pltpu.VMEM((slots * rows, LATENT), jnp.bfloat16),
                pltpu.VMEM((2, rows, BLOCK), jnp.float32),
                pltpu.VMEM((2, rows, BLOCK), jnp.float32),
                pltpu.SMEM(ids.shape, jnp.int32),
                pltpu.SMEM(decode_rows.shape, jnp.int32),
                pltpu.SMEM(lengths.shape, jnp.int32),
                pltpu.SemaphoreType.DMA((3,)),
            ],
            compiler_params=limit(14),
            cost_estimate=cost(8),
            name="attend",
        )(ids, decode_rows, lengths, *received, cache, key_up, value_up)

    def order(kernel, in_specs, scratch, arrays):
        return pl.pallas_call(
            kernel,
            out_shape=jax.ShapeDtypeStruct((steps, sources * requests, columns), jnp.bfloat16),
            in_specs=in_specs,
            out_specs=vmem(),
            scratch_shapes=scratch,
            compiler_params=limit(16),
            cost_estimate=cost(2),
            name="order_rows",
        )(*arrays)

    if not relative:
        received = lax.all_to_all(packed[0], "seq", split_axis=0, concat_axis=0, tiled=True)
        every_row = lax.all_gather(attend([received], 0), "seq", axis=0, tiled=True)
        partial_value = jnp.dot(every_row, out_proj, preferred_element_type=jnp.float32).astype(jnp.bfloat16)
        shares = lax.all_to_all(partial_value, "head", split_axis=0, concat_axis=0, tiled=True)
        shares = shares.reshape(head_devices, -1, columns)
        summed = jnp.sum(shares.astype(jnp.float32), axis=0).astype(jnp.bfloat16)
        whole = lax.all_gather(summed, "head", axis=0, tiled=True)
        return order(order_whole_kernel, [vmem()] * 2, [], [pick, whole])

    def project(parts, first_col, cols):
        rows_here = len(parts) * parts[0].shape[0]
        return pl.pallas_call(
            functools.partial(project_kernel, first_col),
            out_shape=[jax.ShapeDtypeStruct((rows_here // 2, cols), jnp.bfloat16)] * 2,
            in_specs=[smem()] + [vmem()] * (len(parts) + 1),
            out_specs=[vmem()] * 2,
            compiler_params=limit(10),
            cost_estimate=cost(2),
            name="project_out",
        )(ids, *parts, out_proj)

    received = [packed[0]] + [flip(packed[k], "seq", k) for k in range(1, 4)]
    near_rows = attend(received[:2], 0)
    near_across = flip(near_rows, "seq", 2)
    far_rows = attend(received[2:], 2)
    near_across, far_rows = lax.optimization_barrier((near_across, far_rows))
    near = [near_rows, flip(near_rows, "seq", 1), near_across, flip(near_across, "seq", 1)]
    far_across = flip(far_rows, "seq", 2)

    def after(value, *others):
        return lax.optimization_barrier((value,) + others)[0]

    def swap(piece):
        return flip(piece[1], "head", 1)

    half = steps * sources * requests // 2

    def cut(parts, first_row, shares):
        groups = columns // LANES
        edges = [LANES * (groups * sum(shares[:i]) // sum(shares)) for i in range(len(shares) + 1)]
        made = []
        for at, end in zip(edges, edges[1:]):
            keep, send = project(parts, at, end - at)
            made.append((first_row, at, keep, swap((keep, send))))
        return made

    near_made = cut(near, 0, (5, 9))
    pairs = [add(near_made[0][2], near_made[0][3])]
    far = [far_rows, flip(far_rows, "seq", 1), far_across, flip(far_across, "seq", 1)]
    far_made = cut(far, half, (6, 5, 3))
    made = near_made + far_made
    for i, (_, _, keep, incoming) in enumerate(made[1:], 1):
        pairs.append(add(keep, incoming))
    crossed = [flip(pair, "head", 3) for pair in pairs]
    last_made = made[-1][2]
    arrays = []
    for i, (pair, cross) in enumerate(zip(pairs, crossed)):
        if i < len(near_made):
            cross = after(cross, *(pairs[len(near_made)],))
        total = add(pair, cross)
        arrays += [total, flip(total, "head", 1)]
    layout = tuple((row, col) for row, col, _, _ in made)
    scratch = [pltpu.VMEM((2 * half, columns), jnp.bfloat16)]
    kernel = functools.partial(order_kernel, layout)
    return order(kernel, [smem()] + [vmem()] * (1 + len(arrays)), scratch, [ids, pick] + arrays)


def solution(mesh):
    return jax.shard_map(
        local,
        mesh=mesh,
        in_specs=(
            P(("groups", "seq"), None),
            P("groups", None),
            P("groups"),
            P(None, ("groups", "seq"), "head", None),
            P(None, ("groups", "seq"), "head", None),
            P(None, ("groups", "seq"), None),
            P("head", None, None),
            P("head", None, None),
            P("head", "seq"),
        ),
        out_specs=P(None, "groups", "seq"),
        check_vma=False,
    )
```

```python
import functools

import jax
import jax.numpy as jnp
from jax import lax
from jax.experimental import pallas as pl
from jax.experimental.pallas import tpu as pltpu
from jax.sharding import PartitionSpec as P

LATENT = 512
BLOCK = 256
LANES = 128
LOG2E = 1.4426950408889634
NEG = -1e30
PLACES = 1024


def own_slots(decode_ref, slot_ref, me, sources, requests, per_pair):
    shift = requests.bit_length() - 1

    def one_source(s, carry):
        count = jnp.int32(0)
        for r in range(requests):
            row = decode_ref[s * requests + r]
            slot_ref[s * (per_pair + 1) + jnp.minimum(count, per_pair)] = row & (requests - 1)
            count = count + jnp.where((row >> shift) == me, 1, 0).astype(jnp.int32)
        return carry

    lax.fori_loop(0, sources, one_source, jnp.int32(0))


def pack_kernel(sizes, relative, ids_ref, decode_ref, nope_ref, rope_ref, fresh_ref, after_ref, *rest):
    sources, per_pair, steps, heads, requests, fresh_rows = sizes
    out_refs, (slots, wide) = rest[:-2], rest[-2:]
    me = ids_ref[0] & (PLACES - 1)
    rows = heads * steps
    half = rows // 2
    rope_base = per_pair * rows
    fresh_base = rope_base + per_pair * half
    own_slots(decode_ref, slots, me, sources, requests, per_pair)

    def one_dest(s, out_ref, e):
        for j in range(per_pair):
            row = slots[s * (per_pair + 1) + j]
            for t in range(steps):
                wide[2 * j, pl.ds(t, heads, stride=steps), :] = nope_ref[t, row].astype(jnp.float32)
                wide[2 * j + 1, pl.ds(t, heads, stride=steps), :] = jnp.concatenate(
                    [rope_ref[t, row].astype(jnp.float32)] * 2, axis=1
                )
        for j in range(per_pair):
            out_ref[e, j * rows : (j + 1) * rows, :] = wide[2 * j].astype(jnp.bfloat16)
            low = lax.broadcasted_iota(jnp.int32, (half, LANES), 1) < LANES // 2
            packed = jnp.where(low, wide[2 * j + 1, 0:half, :], wide[2 * j + 1, half : 2 * half, :])
            out_ref[e, rope_base + j * half : rope_base + (j + 1) * half, :] = packed.astype(jnp.bfloat16)

    if relative:
        dests = [me ^ k for k in range(sources)]
        for k in range(sources):
            one_dest(dests[k], out_refs[k], 0)
    else:
        dests = list(range(sources))

        def step(s, carry):
            one_dest(s, out_refs[0], s)
            return carry

        lax.fori_loop(0, sources, step, jnp.int32(0))
    shape = (sources * fresh_rows, steps * requests)
    row_id = lax.broadcasted_iota(jnp.int32, shape, 0)
    col_id = lax.broadcasted_iota(jnp.int32, shape, 1)
    wanted = jnp.full(shape, -1, jnp.int32)
    for k in range(sources):
        for j in range(per_pair):
            first = k * fresh_rows + j * steps
            here = (row_id >= first) & (row_id < first + steps)
            wanted = jnp.where(here, (row_id - first) * requests + slots[dests[k] * (per_pair + 1) + j], wanted)
    pick = jnp.where(col_id == wanted, 1.0, 0.0).astype(jnp.bfloat16)
    width = fresh_ref.shape[2]
    source_rows = jnp.concatenate([fresh_ref[t] for t in range(steps)], axis=0)
    picked = jnp.dot(pick, source_rows, preferred_element_type=jnp.float32).astype(jnp.bfloat16)
    for k in range(sources):
        for c in range(-(-width // LANES)):
            piece = picked[k * fresh_rows : (k + 1) * fresh_rows, c * LANES : min((c + 1) * LANES, width)]
            if piece.shape[1] < LANES:
                piece = jnp.concatenate([piece] * (LANES // piece.shape[1]), axis=1)
            first = fresh_base + c * fresh_rows
            if relative:
                out_refs[k][0, first : first + fresh_rows, :] = piece
            else:
                out_refs[0][k, first : first + fresh_rows, :] = piece


def attend_kernel(sizes, scale, relative, base, recv_count, ids_any, decode_any, length_any, *rest):
    sources, per_pair, steps, heads, requests, fresh_rows = sizes
    recv_refs = rest[:recv_count]
    (
        cache, key_up, value_up, out_ref,
        slot_offset, slot_length, owner_count, pair_slot, pair_start,
        queries, fresh, acc, run_max, run_sum, latent, even_scores, odd_scores,
        ids_ref, decode_ref, length_ref, sems,
    ) = rest[recv_count:]
    tables = [
        pltpu.make_async_copy(ids_any, ids_ref, sems.at[0]),
        pltpu.make_async_copy(decode_any, decode_ref, sems.at[1]),
        pltpu.make_async_copy(length_any, length_ref, sems.at[2]),
    ]
    for table in tables:
        table.start()
    owners = [(ref, e) for ref in recv_refs for e in range(ref.shape[0])]
    here = len(owners)
    slots = here * per_pair
    width, tokens = cache.shape
    rows = heads * steps
    half = rows // 2
    rope_base = per_pair * rows
    fresh_base = rope_base + per_pair * half
    group = 16 // steps
    shift = requests.bit_length() - 1
    factor = scale * LOG2E

    for e in range(here):
        ref, at = owners[e]
        for c in range(-(-width // LANES)):
            lanes = min(LANES, width - c * LANES)
            first = fresh_base + c * fresh_rows
            fresh[e * fresh_rows : (e + 1) * fresh_rows, c * LANES : c * LANES + lanes] = ref[
                at, first : first + fresh_rows, 0:lanes
            ]
        for j in range(per_pair):
            slot = e * per_pair + j
            first = rope_base + j * half
            piece = ref[at, first : first + half, :]
            queries[slot * rows : slot * rows + half, LATENT:width] = piece[:, 0 : width - LATENT]
            queries[slot * rows + half : (slot + 1) * rows, LATENT:width] = piece[:, LANES - (width - LATENT) :]

    inner_head = lax.broadcasted_iota(jnp.int32, (slots * 16, LANES), 0) // steps % group
    own_head = [jnp.where(inner_head == u, 1.0, 0.0).astype(jnp.bfloat16) for u in range(group)]

    def absorb(i):
        tall = jnp.concatenate(
            [ref[at, j * rows + i * 16 : j * rows + (i + 1) * 16, :] for ref, at in owners for j in range(per_pair)],
            axis=0,
        )
        left = jnp.concatenate([tall * own_head[u] for u in range(group)], axis=1)
        right = jnp.concatenate([key_up[i * group + u] for u in range(group)], axis=0)
        res = jnp.dot(left, right, preferred_element_type=jnp.float32).astype(jnp.bfloat16)
        for slot in range(slots):
            queries[slot * rows + i * 16 : slot * rows + (i + 1) * 16, 0:LATENT] = res[slot * 16 : (slot + 1) * 16]

    groups = heads // group
    for i in range(groups // 4):
        absorb(i)
    for table in tables:
        table.wait()

    me = ids_ref[0] & (PLACES - 1)
    for o in range(sources):
        owner_count[o] = jnp.int32(0)
    total = jnp.int32(0)
    for r in range(requests):
        owner = decode_ref[me * requests + r] >> shift
        at = owner_count[owner]
        owner_count[owner] = at + 1
        e = (owner ^ me) - base if relative else owner
        slot = jnp.where((e >= 0) & (e < here), e * per_pair + at, slots)
        length = length_ref[me, r]
        slot_offset[slot] = total
        slot_length[slot] = length
        total = total + length
    count = jnp.int32(0)
    for slot in range(slots):
        start = slot_offset[slot] & ~(LANES - 1)
        end = slot_offset[slot] + slot_length[slot]
        for k in range(512 // BLOCK + 1):
            pair_slot[count] = jnp.int32(slot)
            pair_start[count] = start + k * BLOCK
            count = count + jnp.where(start + k * BLOCK < end, 1, 0).astype(jnp.int32)

    for i in range(groups // 4, groups):
        absorb(i)

    fresh_scores = (
        lax.dot_general(queries[...], fresh[...], (((1,), (1,)), ((), ())), preferred_element_type=jnp.float32) * factor
    )
    row_id = lax.broadcasted_iota(jnp.int32, (rows, here * fresh_rows), 0)
    col_id = lax.broadcasted_iota(jnp.int32, (rows, here * fresh_rows), 1)
    behind = row_id & (steps - 1)
    fresh_weights = []
    for slot in range(slots):
        first = (slot // per_pair) * fresh_rows + (slot % per_pair) * steps
        seen = (col_id >= first) & (col_id <= first + behind)
        scores = jnp.where(seen, fresh_scores[slot * rows : (slot + 1) * rows], NEG)
        top = jnp.max(scores, axis=1, keepdims=True)
        weights = jnp.exp2(scores - top)
        run_max[slot] = jnp.broadcast_to(top, (rows, LANES))
        run_sum[slot] = jnp.broadcast_to(jnp.sum(weights, axis=1, keepdims=True), (rows, LANES))
        fresh_weights.append(weights.astype(jnp.bfloat16))
    for slot in range(slots):
        acc[slot] = jnp.dot(fresh_weights[slot], fresh[:, 0:LATENT], preferred_element_type=jnp.float32)

    def make_scores(buffer, g):
        for u in range(2):
            p = jnp.minimum(g * 2 + u, count - 1)
            q = queries[pl.ds(pl.multiple_of(pair_slot[p] * rows, 16), rows), :]
            read = pl.multiple_of(jnp.minimum(pair_start[p], tokens - BLOCK), LANES)
            buffer[u] = jnp.dot(q, cache[:, pl.ds(read, BLOCK)], preferred_element_type=jnp.float32)

    token = lax.broadcasted_iota(jnp.int32, (1, BLOCK), 1)

    def take_scores(buffer, g):
        for u in range(2):
            p = jnp.minimum(g * 2 + u, count - 1)
            slot = pair_slot[p]
            start = pair_start[p]
            read = jnp.minimum(start, tokens - BLOCK)
            low = jnp.maximum(slot_offset[slot], start) - read
            high = jnp.minimum(slot_offset[slot] + slot_length[slot], start + BLOCK) - read
            high = jnp.where(g * 2 + u < count, high, low)
            bias = jnp.where((token >= low) & (token < high), 0.0, NEG)
            scores = buffer[u] * factor + bias
            top = jnp.max(scores, axis=1, keepdims=True)
            weights = jnp.exp2(scores - top)
            part_sum = jnp.broadcast_to(jnp.sum(weights, axis=1, keepdims=True), (rows, LANES))
            part = lax.dot_general(
                weights.astype(jnp.bfloat16),
                cache[0:LATENT, pl.ds(pl.multiple_of(read, LANES), BLOCK)],
                (((1,), (1,)), ((), ())),
                preferred_element_type=jnp.float32,
            )
            part_max = jnp.broadcast_to(top, (rows, LANES))
            old_max = run_max[slot]
            new_max = jnp.maximum(old_max, part_max)
            keep = jnp.exp2(old_max - new_max)
            add = jnp.exp2(part_max - new_max)
            run_max[slot] = new_max
            run_sum[slot] = run_sum[slot] * keep + part_sum * add
            for c in range(LATENT // LANES):
                cols = slice(c * LANES, (c + 1) * LANES)
                acc[slot, :, cols] = acc[slot, :, cols] * keep + part[:, cols] * add

    make_scores(even_scores, 0)

    def four_pairs(i, carry):
        make_scores(odd_scores, 2 * i + 1)
        take_scores(even_scores, 2 * i)
        make_scores(even_scores, 2 * i + 2)
        take_scores(odd_scores, 2 * i + 1)
        return carry

    fours = count >> 2
    lax.fori_loop(0, fours, four_pairs, jnp.int32(0))

    @pl.when(count > 4 * fours)
    def _():
        take_scores(even_scores, 2 * fours)

    @pl.when(count > 4 * fours + 2)
    def _():
        make_scores(odd_scores, 2 * fours + 1)
        take_scores(odd_scores, 2 * fours + 1)

    for slot in range(slots):
        inverse = 1.0 / run_sum[slot]
        for c in range(LATENT // LANES):
            cols = slice(c * LANES, (c + 1) * LANES)
            latent[slot * rows : (slot + 1) * rows, cols] = (acc[slot, :, cols] * inverse).astype(jnp.bfloat16)
    vdim = value_up.shape[2]
    for i in range(heads // group):
        left = jnp.concatenate(
            [latent[slot * rows + i * 16 : slot * rows + (i + 1) * 16, :] for slot in range(slots)], axis=0
        )
        right = jnp.concatenate([value_up[i * group + u] for u in range(group)], axis=1)
        res = jnp.dot(left, right, preferred_element_type=jnp.float32)
        for u in range(group):
            own = jnp.concatenate(
                [
                    res[slot * 16 + u * steps : slot * 16 + (u + 1) * steps, u * vdim : (u + 1) * vdim]
                    for slot in range(slots)
                ],
                axis=0,
            )
            head = i * group + u
            out_ref[:, head * vdim : (head + 1) * vdim] = own.astype(jnp.bfloat16)


def place_kernel(sizes, relative, ids_ref, decode_ref, out_ref, owner_count, place):
    sources, per_pair, steps, requests = sizes
    me = ids_ref[0] & (PLACES - 1)
    rows = sources * requests
    shift = requests.bit_length() - 1

    def one_source(s, carry):
        for o in range(sources):
            owner_count[o] = jnp.int32(0)
        for r in range(requests):
            row = decode_ref[s * requests + r]
            owner = row >> shift
            at = owner_count[owner]
            owner_count[owner] = at + 1
            if relative:
                e = owner ^ s
                at_row = (e >> 1) * (2 * sources * per_pair) + (me ^ s) * (2 * per_pair) + (e & 1) * per_pair + at
            else:
                at_row = s * requests + owner * per_pair + at
            place[row] = at_row * steps
        return carry

    lax.fori_loop(0, sources, one_source, jnp.int32(0))
    narrow = (rows, LANES)
    row_id = lax.broadcasted_iota(jnp.int32, narrow, 0)

    def put(b, wanted):
        return jnp.where(row_id == b, place[b], wanted)

    wanted = lax.fori_loop(0, rows, put, jnp.zeros(narrow, jnp.int32), unroll=8)[:, 0:1]
    col_id = lax.broadcasted_iota(jnp.int32, (rows, rows * steps), 1)
    for t in range(steps):
        out_ref[t] = jnp.where(col_id == wanted + t, 1.0, 0.0).astype(jnp.bfloat16)


def keeps_upper(ids_ref):
    z = ids_ref[0] // PLACES
    return (z == 1) | (z == 2)


def order_kernel(layout, ids_ref, pick_ref, *rest):
    pieces, out_ref, x = rest[:-2], rest[-2], rest[-1]
    upper = keeps_upper(ids_ref)

    def assemble(first, second):
        for i, (row, col) in enumerate(layout):
            rows, cols = pieces[2 * i].shape
            x[row : row + rows, col : col + cols] = pieces[2 * i + first][...]
            x[row + rows : row + 2 * rows, col : col + cols] = pieces[2 * i + second][...]

    pl.when(upper)(lambda: assemble(1, 0))
    pl.when(jnp.logical_not(upper))(lambda: assemble(0, 1))
    steps, rows, _ = pick_ref.shape
    pick = jnp.concatenate([pick_ref[t] for t in range(steps)], axis=0)
    for c in range(0, x.shape[1], BLOCK):
        tile = jnp.dot(pick, x[:, c : c + BLOCK], preferred_element_type=jnp.float32).astype(jnp.bfloat16)
        for t in range(steps):
            out_ref[t, :, c : c + BLOCK] = tile[t * rows : (t + 1) * rows]


def order_whole_kernel(pick_ref, x_ref, out_ref):
    for t in range(pick_ref.shape[0]):
        out_ref[t] = jnp.dot(pick_ref[t], x_ref[...], preferred_element_type=jnp.float32).astype(jnp.bfloat16)


def project_kernel(first_col, ids_ref, *rest):
    parts, (weight, keep, send) = rest[:-3], rest[-3:]
    half = keep.shape[0]
    upper = keeps_upper(ids_ref)
    cols = keep.shape[1]
    x = jnp.concatenate([part[...] for part in parts], axis=0)
    for c in range(0, cols, BLOCK):
        n = min(BLOCK, cols - c)
        tile = jnp.dot(x, weight[:, first_col + c : first_col + c + n], preferred_element_type=jnp.float32)
        keep[:, c : c + n] = jnp.where(upper, tile[half:], tile[:half]).astype(jnp.bfloat16)
        send[:, c : c + n] = jnp.where(upper, tile[:half], tile[half:]).astype(jnp.bfloat16)


def smem():
    return pl.BlockSpec(memory_space=pltpu.SMEM)


def vmem():
    return pl.BlockSpec(memory_space=pltpu.VMEM)


def anywhere():
    return pl.BlockSpec(memory_space=pl.ANY)


def limit(mib):
    return pltpu.CompilerParams(vmem_limit_bytes=mib * 1024 * 1024)


def cost(microseconds):
    return pl.CostEstimate(
        flops=int(microseconds * 1.0e9), bytes_accessed=int(microseconds * 3.0e6), transcendentals=0
    )


def flip(x, axis, distance):
    size = lax.axis_size(axis)
    return lax.ppermute(x, axis, [(i, i ^ distance) for i in range(size)])


def add(x, y):
    return (x.astype(jnp.float32) + y.astype(jnp.float32)).astype(jnp.bfloat16)


def local(latent_cache, lengths, decode_rows, q_nope, q_rope, new_latent, key_up, value_up, out_proj):
    sources = lax.axis_size("seq")
    head_devices = lax.axis_size("head")
    relative = sources == 4 and head_devices == 4
    requests = lengths.shape[1]
    per_pair = requests // sources
    tokens, width = latent_cache.shape
    steps, _, heads, nope = q_nope.shape
    scale = (nope + q_rope.shape[3]) ** (-0.5)
    fresh_rows = -(-per_pair * steps // 16) * 16
    rows = heads * steps
    columns = out_proj.shape[1]
    packed_rows = per_pair * rows + per_pair * rows // 2 + -(-width // LANES) * fresh_rows
    sizes = (sources, per_pair, steps, heads, requests, fresh_rows)
    ids = (lax.axis_index("seq") + PLACES * lax.axis_index("head")).astype(jnp.int32).reshape(1)
    cache = latent_cache.T

    pick = pl.pallas_call(
        functools.partial(place_kernel, (sources, per_pair, steps, requests), relative),
        out_shape=jax.ShapeDtypeStruct((steps, sources * requests, steps * sources * requests), jnp.bfloat16),
        in_specs=[smem(), smem()],
        out_specs=vmem(),
        scratch_shapes=[pltpu.SMEM((sources,), jnp.int32), pltpu.SMEM((sources * requests,), jnp.int32)],
        compiler_params=limit(12),
        cost_estimate=cost(2),
        name="place_rows",
    )(ids, decode_rows)

    outs, each = (sources, 1) if relative else (1, sources)
    packed = pl.pallas_call(
        functools.partial(pack_kernel, sizes, relative),
        out_shape=[jax.ShapeDtypeStruct((each, packed_rows, LANES), jnp.bfloat16)] * outs,
        in_specs=[smem(), smem(), vmem(), vmem(), vmem(), anywhere()],
        out_specs=[vmem()] * outs,
        scratch_shapes=[
            pltpu.SMEM((sources * (per_pair + 1),), jnp.int32),
            pltpu.VMEM((2 * per_pair, rows, LANES), jnp.float32),
        ],
        compiler_params=limit(8),
        cost_estimate=cost(2),
        name="pack_queries",
    )(ids, decode_rows, q_nope, q_rope, new_latent, pick)

    def attend(received, base):
        here = sum(part.shape[0] for part in received)
        slots = here * per_pair
        pairs = slots * (512 // BLOCK + 1) + 1
        return pl.pallas_call(
            functools.partial(attend_kernel, sizes, scale, relative, base, len(received)),
            out_shape=jax.ShapeDtypeStruct((slots * steps, heads * value_up.shape[2]), jnp.bfloat16),
            in_specs=[anywhere()] * 3 + [vmem()] * (len(received) + 3),
            out_specs=vmem(),
            scratch_shapes=[
                pltpu.SMEM((slots + 1,), jnp.int32),
                pltpu.SMEM((slots + 1,), jnp.int32),
                pltpu.SMEM((sources,), jnp.int32),
                pltpu.SMEM((pairs,), jnp.int32),
                pltpu.SMEM((pairs,), jnp.int32),
                pltpu.VMEM((slots * rows, width), jnp.bfloat16),
                pltpu.VMEM((here * fresh_rows, width), jnp.bfloat16),
                pltpu.VMEM((slots, rows, LATENT), jnp.float32),
                pltpu.VMEM((slots, rows, LANES), jnp.float32),
                pltpu.VMEM((slots, rows, LANES), jnp.float32),
                pltpu.VMEM((slots * rows, LATENT), jnp.bfloat16),
                pltpu.VMEM((2, rows, BLOCK), jnp.float32),
                pltpu.VMEM((2, rows, BLOCK), jnp.float32),
                pltpu.SMEM(ids.shape, jnp.int32),
                pltpu.SMEM(decode_rows.shape, jnp.int32),
                pltpu.SMEM(lengths.shape, jnp.int32),
                pltpu.SemaphoreType.DMA((3,)),
            ],
            compiler_params=limit(14),
            cost_estimate=cost(8),
            name="attend",
        )(ids, decode_rows, lengths, *received, cache, key_up, value_up)

    def order(kernel, in_specs, scratch, arrays):
        return pl.pallas_call(
            kernel,
            out_shape=jax.ShapeDtypeStruct((steps, sources * requests, columns), jnp.bfloat16),
            in_specs=in_specs,
            out_specs=vmem(),
            scratch_shapes=scratch,
            compiler_params=limit(16),
            cost_estimate=cost(2),
            name="order_rows",
        )(*arrays)

    if not relative:
        received = lax.all_to_all(packed[0], "seq", split_axis=0, concat_axis=0, tiled=True)
        every_row = lax.all_gather(attend([received], 0), "seq", axis=0, tiled=True)
        partial_value = jnp.dot(every_row, out_proj, preferred_element_type=jnp.float32).astype(jnp.bfloat16)
        shares = lax.all_to_all(partial_value, "head", split_axis=0, concat_axis=0, tiled=True)
        shares = shares.reshape(head_devices, -1, columns)
        summed = jnp.sum(shares.astype(jnp.float32), axis=0).astype(jnp.bfloat16)
        whole = lax.all_gather(summed, "head", axis=0, tiled=True)
        return order(order_whole_kernel, [vmem()] * 2, [], [pick, whole])

    def project(parts, first_col, cols):
        rows_here = len(parts) * parts[0].shape[0]
        return pl.pallas_call(
            functools.partial(project_kernel, first_col),
            out_shape=[jax.ShapeDtypeStruct((rows_here // 2, cols), jnp.bfloat16)] * 2,
            in_specs=[smem()] + [vmem()] * (len(parts) + 1),
            out_specs=[vmem()] * 2,
            compiler_params=limit(10),
            cost_estimate=cost(2),
            name="project_out",
        )(ids, *parts, out_proj)

    received = [packed[0]] + [flip(packed[k], "seq", k) for k in range(1, 4)]
    near_rows = attend(received[:2], 0)
    near_across = flip(near_rows, "seq", 2)
    far_rows = attend(received[2:], 2)
    near_across, far_rows = lax.optimization_barrier((near_across, far_rows))
    near = [near_rows, flip(near_rows, "seq", 1), near_across, flip(near_across, "seq", 1)]
    far_across = flip(far_rows, "seq", 2)

    def after(value, *others):
        return lax.optimization_barrier((value,) + others)[0]

    def swap(piece):
        return flip(piece[1], "head", 1)

    half = steps * sources * requests // 2

    def cut(parts, first_row, shares):
        groups = columns // LANES
        edges = [LANES * (groups * sum(shares[:i]) // sum(shares)) for i in range(len(shares) + 1)]
        made = []
        for at, end in zip(edges, edges[1:]):
            keep, send = project(parts, at, end - at)
            made.append((first_row, at, keep, swap((keep, send))))
        return made

    near_made = cut(near, 0, (1, 1))
    pairs = [add(near_made[0][2], near_made[0][3])]
    relayed = after(far_across, near_made[1][2])
    far = [far_rows, flip(far_rows, "seq", 1), far_across, flip(relayed, "seq", 1)]
    far_made = cut(far, half, (1, 1))
    made = near_made + far_made
    for i, (_, _, keep, incoming) in enumerate(made[1:], 1):
        if i == 1: incoming = after(incoming, made[2][2])
        pairs.append(add(keep, incoming))
    crossed = [flip(pair, "head", 3) for pair in pairs]
    last_made = made[-1][2]
    arrays = []
    for i, (pair, cross) in enumerate(zip(pairs, crossed)):
        if i < len(near_made):
            cross = after(cross, *(pairs[len(near_made)],))
        total = add(pair, cross)
        arrays += [total, flip(total, "head", 1)]
    layout = tuple((row, col) for row, col, _, _ in made)
    scratch = [pltpu.VMEM((2 * half, columns), jnp.bfloat16)]
    kernel = functools.partial(order_kernel, layout)
    return order(kernel, [smem()] + [vmem()] * (1 + len(arrays)), scratch, [ids, pick] + arrays)


def solution(mesh):
    return jax.shard_map(
        local,
        mesh=mesh,
        in_specs=(
            P(("groups", "seq"), None),
            P("groups", None),
            P("groups"),
            P(None, ("groups", "seq"), "head", None),
            P(None, ("groups", "seq"), "head", None),
            P(None, ("groups", "seq"), None),
            P("head", None, None),
            P("head", None, None),
            P("head", "seq"),
        ),
        out_specs=P(None, "groups", "seq"),
        check_vma=False,
    )
```

```python
import functools

import jax
import jax.numpy as jnp
from jax import lax
from jax.experimental import pallas as pl
from jax.experimental.pallas import tpu as pltpu
from jax.sharding import PartitionSpec as P

LATENT = 512
BLOCK = 256
LANES = 128
LOG2E = 1.4426950408889634
NEG = -1e30
PLACES = 1024


def own_slots(decode_ref, slot_ref, me, sources, requests, per_pair):
    shift = requests.bit_length() - 1

    def one_source(s, carry):
        count = jnp.int32(0)
        for r in range(requests):
            row = decode_ref[s * requests + r]
            slot_ref[s * (per_pair + 1) + jnp.minimum(count, per_pair)] = row & (requests - 1)
            count = count + jnp.where((row >> shift) == me, 1, 0).astype(jnp.int32)
        return carry

    lax.fori_loop(0, sources, one_source, jnp.int32(0))


def mark_kernel(ids_ref, out_ref):
    out_ref[...] = jnp.full(out_ref.shape, ids_ref[0], jnp.int32)


def pack_kernel(sizes, relative, ids_ref, decode_ref, nope_ref, rope_ref, fresh_ref, after_ref, *rest):
    sources, per_pair, steps, heads, requests, fresh_rows = sizes
    out_refs, (slots, wide) = rest[:-2], rest[-2:]
    me = ids_ref[0] & (PLACES - 1)
    rows = heads * steps
    half = rows // 2
    rope_base = per_pair * rows
    fresh_base = rope_base + per_pair * half
    own_slots(decode_ref, slots, me, sources, requests, per_pair)

    def one_dest(s, out_ref, e):
        for j in range(per_pair):
            row = slots[s * (per_pair + 1) + j]
            for t in range(steps):
                wide[2 * j, pl.ds(t, heads, stride=steps), :] = nope_ref[t, row].astype(jnp.float32)
                wide[2 * j + 1, pl.ds(t, heads, stride=steps), :] = jnp.concatenate(
                    [rope_ref[t, row].astype(jnp.float32)] * 2, axis=1
                )
        for j in range(per_pair):
            out_ref[e, j * rows : (j + 1) * rows, :] = wide[2 * j].astype(jnp.bfloat16)
            low = lax.broadcasted_iota(jnp.int32, (half, LANES), 1) < LANES // 2
            packed = jnp.where(low, wide[2 * j + 1, 0:half, :], wide[2 * j + 1, half : 2 * half, :])
            out_ref[e, rope_base + j * half : rope_base + (j + 1) * half, :] = packed.astype(jnp.bfloat16)

    if relative:
        dests = [me ^ k for k in range(sources)]
        for k in range(sources):
            one_dest(dests[k], out_refs[k], 0)
    else:
        dests = list(range(sources))

        def step(s, carry):
            one_dest(s, out_refs[0], s)
            return carry

        lax.fori_loop(0, sources, step, jnp.int32(0))
    shape = (sources * fresh_rows, steps * requests)
    row_id = lax.broadcasted_iota(jnp.int32, shape, 0)
    col_id = lax.broadcasted_iota(jnp.int32, shape, 1)
    wanted = jnp.full(shape, -1, jnp.int32)
    for k in range(sources):
        for j in range(per_pair):
            first = k * fresh_rows + j * steps
            here = (row_id >= first) & (row_id < first + steps)
            wanted = jnp.where(here, (row_id - first) * requests + slots[dests[k] * (per_pair + 1) + j], wanted)
    pick = jnp.where(col_id == wanted, 1.0, 0.0).astype(jnp.bfloat16)
    width = fresh_ref.shape[2]
    source_rows = jnp.concatenate([fresh_ref[t] for t in range(steps)], axis=0)
    picked = jnp.dot(pick, source_rows, preferred_element_type=jnp.float32).astype(jnp.bfloat16)
    for k in range(sources):
        for c in range(-(-width // LANES)):
            piece = picked[k * fresh_rows : (k + 1) * fresh_rows, c * LANES : min((c + 1) * LANES, width)]
            if piece.shape[1] < LANES:
                piece = jnp.concatenate([piece] * (LANES // piece.shape[1]), axis=1)
            first = fresh_base + c * fresh_rows
            if relative:
                out_refs[k][0, first : first + fresh_rows, :] = piece
            else:
                out_refs[0][k, first : first + fresh_rows, :] = piece


def attend_kernel(sizes, scale, relative, base, recv_count, ids_any, decode_any, length_any, *rest):
    sources, per_pair, steps, heads, requests, fresh_rows = sizes
    recv_refs = rest[:recv_count]
    (
        cache, key_up, value_up, out_ref,
        slot_offset, slot_length, owner_count, pair_slot, pair_start,
        queries, fresh, acc, run_max, run_sum, latent, even_scores, odd_scores,
        ids_ref, decode_ref, length_ref, sems,
    ) = rest[recv_count:]
    tables = [
        pltpu.make_async_copy(ids_any, ids_ref, sems.at[0]),
        pltpu.make_async_copy(decode_any, decode_ref, sems.at[1]),
        pltpu.make_async_copy(length_any, length_ref, sems.at[2]),
    ]
    for table in tables:
        table.start()
    owners = [(ref, e) for ref in recv_refs for e in range(ref.shape[0])]
    here = len(owners)
    slots = here * per_pair
    width, tokens = cache.shape
    rows = heads * steps
    half = rows // 2
    rope_base = per_pair * rows
    fresh_base = rope_base + per_pair * half
    group = 16 // steps
    shift = requests.bit_length() - 1
    factor = scale * LOG2E

    for e in range(here):
        ref, at = owners[e]
        for c in range(-(-width // LANES)):
            lanes = min(LANES, width - c * LANES)
            first = fresh_base + c * fresh_rows
            fresh[e * fresh_rows : (e + 1) * fresh_rows, c * LANES : c * LANES + lanes] = ref[
                at, first : first + fresh_rows, 0:lanes
            ]
        for j in range(per_pair):
            slot = e * per_pair + j
            first = rope_base + j * half
            piece = ref[at, first : first + half, :]
            queries[slot * rows : slot * rows + half, LATENT:width] = piece[:, 0 : width - LATENT]
            queries[slot * rows + half : (slot + 1) * rows, LATENT:width] = piece[:, LANES - (width - LATENT) :]

    inner_head = lax.broadcasted_iota(jnp.int32, (slots * 16, LANES), 0) // steps % group
    own_head = [jnp.where(inner_head == u, 1.0, 0.0).astype(jnp.bfloat16) for u in range(group)]

    def absorb(i):
        tall = jnp.concatenate(
            [ref[at, j * rows + i * 16 : j * rows + (i + 1) * 16, :] for ref, at in owners for j in range(per_pair)],
            axis=0,
        )
        left = jnp.concatenate([tall * own_head[u] for u in range(group)], axis=1)
        right = jnp.concatenate([key_up[i * group + u] for u in range(group)], axis=0)
        res = jnp.dot(left, right, preferred_element_type=jnp.float32).astype(jnp.bfloat16)
        for slot in range(slots):
            queries[slot * rows + i * 16 : slot * rows + (i + 1) * 16, 0:LATENT] = res[slot * 16 : (slot + 1) * 16]

    groups = heads // group
    for i in range(groups // 4):
        absorb(i)
    for table in tables:
        table.wait()

    me = ids_ref[0] & (PLACES - 1)
    for o in range(sources):
        owner_count[o] = jnp.int32(0)
    total = jnp.int32(0)
    for r in range(requests):
        owner = decode_ref[me * requests + r] >> shift
        at = owner_count[owner]
        owner_count[owner] = at + 1
        e = (owner ^ me) - base if relative else owner
        slot = jnp.where((e >= 0) & (e < here), e * per_pair + at, slots)
        length = length_ref[me, r]
        slot_offset[slot] = total
        slot_length[slot] = length
        total = total + length
    count = jnp.int32(0)
    for slot in range(slots):
        start = slot_offset[slot] & ~(LANES - 1)
        end = slot_offset[slot] + slot_length[slot]
        for k in range(512 // BLOCK + 1):
            pair_slot[count] = jnp.int32(slot)
            pair_start[count] = start + k * BLOCK
            count = count + jnp.where(start + k * BLOCK < end, 1, 0).astype(jnp.int32)

    for i in range(groups // 4, groups):
        absorb(i)

    fresh_scores = (
        lax.dot_general(queries[...], fresh[...], (((1,), (1,)), ((), ())), preferred_element_type=jnp.float32) * factor
    )
    row_id = lax.broadcasted_iota(jnp.int32, (rows, here * fresh_rows), 0)
    col_id = lax.broadcasted_iota(jnp.int32, (rows, here * fresh_rows), 1)
    behind = row_id & (steps - 1)
    fresh_weights = []
    for slot in range(slots):
        first = (slot // per_pair) * fresh_rows + (slot % per_pair) * steps
        seen = (col_id >= first) & (col_id <= first + behind)
        scores = jnp.where(seen, fresh_scores[slot * rows : (slot + 1) * rows], NEG)
        top = jnp.max(scores, axis=1, keepdims=True)
        weights = jnp.exp2(scores - top)
        run_max[slot] = jnp.broadcast_to(top, (rows, LANES))
        run_sum[slot] = jnp.broadcast_to(jnp.sum(weights, axis=1, keepdims=True), (rows, LANES))
        fresh_weights.append(weights.astype(jnp.bfloat16))
    for slot in range(slots):
        acc[slot] = jnp.dot(fresh_weights[slot], fresh[:, 0:LATENT], preferred_element_type=jnp.float32)

    def make_scores(buffer, g):
        for u in range(2):
            p = jnp.minimum(g * 2 + u, count - 1)
            q = queries[pl.ds(pl.multiple_of(pair_slot[p] * rows, 16), rows), :]
            read = pl.multiple_of(jnp.minimum(pair_start[p], tokens - BLOCK), LANES)
            buffer[u] = jnp.dot(q, cache[:, pl.ds(read, BLOCK)], preferred_element_type=jnp.float32)

    token = lax.broadcasted_iota(jnp.int32, (1, BLOCK), 1)

    def take_scores(buffer, g):
        for u in range(2):
            p = jnp.minimum(g * 2 + u, count - 1)
            slot = pair_slot[p]
            start = pair_start[p]
            read = jnp.minimum(start, tokens - BLOCK)
            low = jnp.maximum(slot_offset[slot], start) - read
            high = jnp.minimum(slot_offset[slot] + slot_length[slot], start + BLOCK) - read
            high = jnp.where(g * 2 + u < count, high, low)
            bias = jnp.where((token >= low) & (token < high), 0.0, NEG)
            scores = buffer[u] * factor + bias
            top = jnp.max(scores, axis=1, keepdims=True)
            weights = jnp.exp2(scores - top)
            part_sum = jnp.broadcast_to(jnp.sum(weights, axis=1, keepdims=True), (rows, LANES))
            part = lax.dot_general(
                weights.astype(jnp.bfloat16),
                cache[0:LATENT, pl.ds(pl.multiple_of(read, LANES), BLOCK)],
                (((1,), (1,)), ((), ())),
                preferred_element_type=jnp.float32,
            )
            part_max = jnp.broadcast_to(top, (rows, LANES))
            old_max = run_max[slot]
            new_max = jnp.maximum(old_max, part_max)
            keep = jnp.exp2(old_max - new_max)
            add = jnp.exp2(part_max - new_max)
            run_max[slot] = new_max
            run_sum[slot] = run_sum[slot] * keep + part_sum * add
            for c in range(LATENT // LANES):
                cols = slice(c * LANES, (c + 1) * LANES)
                acc[slot, :, cols] = acc[slot, :, cols] * keep + part[:, cols] * add

    make_scores(even_scores, 0)

    def four_pairs(i, carry):
        make_scores(odd_scores, 2 * i + 1)
        take_scores(even_scores, 2 * i)
        make_scores(even_scores, 2 * i + 2)
        take_scores(odd_scores, 2 * i + 1)
        return carry

    fours = count >> 2
    lax.fori_loop(0, fours, four_pairs, jnp.int32(0))

    @pl.when(count > 4 * fours)
    def _():
        take_scores(even_scores, 2 * fours)

    @pl.when(count > 4 * fours + 2)
    def _():
        make_scores(odd_scores, 2 * fours + 1)
        take_scores(odd_scores, 2 * fours + 1)

    for slot in range(slots):
        inverse = 1.0 / run_sum[slot]
        for c in range(LATENT // LANES):
            cols = slice(c * LANES, (c + 1) * LANES)
            latent[slot * rows : (slot + 1) * rows, cols] = (acc[slot, :, cols] * inverse).astype(jnp.bfloat16)
    vdim = value_up.shape[2]
    for i in range(heads // group):
        left = jnp.concatenate(
            [latent[slot * rows + i * 16 : slot * rows + (i + 1) * 16, :] for slot in range(slots)], axis=0
        )
        right = jnp.concatenate([value_up[i * group + u] for u in range(group)], axis=1)
        res = jnp.dot(left, right, preferred_element_type=jnp.float32)
        for u in range(group):
            own = jnp.concatenate(
                [
                    res[slot * 16 + u * steps : slot * 16 + (u + 1) * steps, u * vdim : (u + 1) * vdim]
                    for slot in range(slots)
                ],
                axis=0,
            )
            head = i * group + u
            out_ref[:, head * vdim : (head + 1) * vdim] = own.astype(jnp.bfloat16)


def place_kernel(sizes, relative, ids_ref, decode_ref, out_ref, owner_count, place):
    sources, per_pair, steps, requests = sizes
    me = ids_ref[0] & (PLACES - 1)
    rows = sources * requests
    shift = requests.bit_length() - 1

    def one_source(s, carry):
        for o in range(sources):
            owner_count[o] = jnp.int32(0)
        for r in range(requests):
            row = decode_ref[s * requests + r]
            owner = row >> shift
            at = owner_count[owner]
            owner_count[owner] = at + 1
            if relative:
                e = owner ^ s
                at_row = (e >> 1) * (2 * sources * per_pair) + (me ^ s) * (2 * per_pair) + (e & 1) * per_pair + at
            else:
                at_row = s * requests + owner * per_pair + at
            place[row] = at_row * steps
        return carry

    lax.fori_loop(0, sources, one_source, jnp.int32(0))
    narrow = (rows, LANES)
    row_id = lax.broadcasted_iota(jnp.int32, narrow, 0)

    def put(b, wanted):
        return jnp.where(row_id == b, place[b], wanted)

    wanted = lax.fori_loop(0, rows, put, jnp.zeros(narrow, jnp.int32), unroll=8)[:, 0:1]
    col_id = lax.broadcasted_iota(jnp.int32, (rows, rows * steps), 1)
    for t in range(steps):
        out_ref[t] = jnp.where(col_id == wanted + t, 1.0, 0.0).astype(jnp.bfloat16)


def keeps_upper(ids_ref):
    z = ids_ref[0] // PLACES
    return (z == 1) | (z == 2)


def order_kernel(layout, ids_ref, pick_ref, *rest):
    pieces, out_ref, x = rest[:-2], rest[-2], rest[-1]
    upper = keeps_upper(ids_ref)

    def assemble(first, second):
        for i, (row, col) in enumerate(layout):
            rows, cols = pieces[2 * i].shape
            x[row : row + rows, col : col + cols] = pieces[2 * i + first][...]
            x[row + rows : row + 2 * rows, col : col + cols] = pieces[2 * i + second][...]

    pl.when(upper)(lambda: assemble(1, 0))
    pl.when(jnp.logical_not(upper))(lambda: assemble(0, 1))
    steps, rows, _ = pick_ref.shape
    pick = jnp.concatenate([pick_ref[t] for t in range(steps)], axis=0)
    for c in range(0, x.shape[1], BLOCK):
        tile = jnp.dot(pick, x[:, c : c + BLOCK], preferred_element_type=jnp.float32).astype(jnp.bfloat16)
        for t in range(steps):
            out_ref[t, :, c : c + BLOCK] = tile[t * rows : (t + 1) * rows]


def order_whole_kernel(pick_ref, x_ref, out_ref):
    for t in range(pick_ref.shape[0]):
        out_ref[t] = jnp.dot(pick_ref[t], x_ref[...], preferred_element_type=jnp.float32).astype(jnp.bfloat16)


def project_kernel(first_col, ids_ref, *rest):
    parts, (weight, keep, send) = rest[:-3], rest[-3:]
    half = keep.shape[0]
    upper = keeps_upper(ids_ref)
    cols = keep.shape[1]
    x = jnp.concatenate([part[...] for part in parts], axis=0)
    for c in range(0, cols, BLOCK):
        n = min(BLOCK, cols - c)
        tile = jnp.dot(x, weight[:, first_col + c : first_col + c + n], preferred_element_type=jnp.float32)
        keep[:, c : c + n] = jnp.where(upper, tile[half:], tile[:half]).astype(jnp.bfloat16)
        send[:, c : c + n] = jnp.where(upper, tile[:half], tile[half:]).astype(jnp.bfloat16)


def smem():
    return pl.BlockSpec(memory_space=pltpu.SMEM)


def vmem():
    return pl.BlockSpec(memory_space=pltpu.VMEM)


def anywhere():
    return pl.BlockSpec(memory_space=pl.ANY)


def limit(mib):
    return pltpu.CompilerParams(vmem_limit_bytes=mib * 1024 * 1024)


def cost(microseconds):
    return pl.CostEstimate(
        flops=int(microseconds * 1.0e9), bytes_accessed=int(microseconds * 3.0e6), transcendentals=0
    )


def flip(x, axis, distance):
    size = lax.axis_size(axis)
    return lax.ppermute(x, axis, [(i, i ^ distance) for i in range(size)])


def add(x, y):
    return (x.astype(jnp.float32) + y.astype(jnp.float32)).astype(jnp.bfloat16)


def local(latent_cache, lengths, decode_rows, q_nope, q_rope, new_latent, key_up, value_up, out_proj):
    sources = lax.axis_size("seq")
    head_devices = lax.axis_size("head")
    relative = sources == 4 and head_devices == 4
    requests = lengths.shape[1]
    per_pair = requests // sources
    tokens, width = latent_cache.shape
    steps, _, heads, nope = q_nope.shape
    scale = (nope + q_rope.shape[3]) ** (-0.5)
    fresh_rows = -(-per_pair * steps // 16) * 16
    rows = heads * steps
    columns = out_proj.shape[1]
    packed_rows = per_pair * rows + per_pair * rows // 2 + -(-width // LANES) * fresh_rows
    sizes = (sources, per_pair, steps, heads, requests, fresh_rows)
    ids = (lax.axis_index("seq") + PLACES * lax.axis_index("head")).astype(jnp.int32).reshape(1)
    cache = latent_cache.T

    pick = pl.pallas_call(
        functools.partial(place_kernel, (sources, per_pair, steps, requests), relative),
        out_shape=jax.ShapeDtypeStruct((steps, sources * requests, steps * sources * requests), jnp.bfloat16),
        in_specs=[smem(), smem()],
        out_specs=vmem(),
        scratch_shapes=[pltpu.SMEM((sources,), jnp.int32), pltpu.SMEM((sources * requests,), jnp.int32)],
        compiler_params=limit(12),
        cost_estimate=cost(2),
        name="place_rows",
    )(ids, decode_rows)

    mark = pl.pallas_call(
        mark_kernel,
        out_shape=jax.ShapeDtypeStruct((8, LANES), jnp.int32),
        in_specs=[smem()],
        out_specs=vmem(),
        compiler_params=limit(4),
        cost_estimate=cost(2),
        name="mark_start",
    )(ids)

    outs, each = (sources, 1) if relative else (1, sources)
    packed = pl.pallas_call(
        functools.partial(pack_kernel, sizes, relative),
        out_shape=[jax.ShapeDtypeStruct((each, packed_rows, LANES), jnp.bfloat16)] * outs,
        in_specs=[smem(), smem(), vmem(), vmem(), vmem(), anywhere()],
        out_specs=[vmem()] * outs,
        scratch_shapes=[
            pltpu.SMEM((sources * (per_pair + 1),), jnp.int32),
            pltpu.VMEM((2 * per_pair, rows, LANES), jnp.float32),
        ],
        compiler_params=limit(8),
        cost_estimate=cost(2),
        name="pack_queries",
    )(ids, decode_rows, q_nope, q_rope, new_latent, mark)

    def attend(received, base):
        here = sum(part.shape[0] for part in received)
        slots = here * per_pair
        pairs = slots * (512 // BLOCK + 1) + 1
        return pl.pallas_call(
            functools.partial(attend_kernel, sizes, scale, relative, base, len(received)),
            out_shape=jax.ShapeDtypeStruct((slots * steps, heads * value_up.shape[2]), jnp.bfloat16),
            in_specs=[anywhere()] * 3 + [vmem()] * (len(received) + 3),
            out_specs=vmem(),
            scratch_shapes=[
                pltpu.SMEM((slots + 1,), jnp.int32),
                pltpu.SMEM((slots + 1,), jnp.int32),
                pltpu.SMEM((sources,), jnp.int32),
                pltpu.SMEM((pairs,), jnp.int32),
                pltpu.SMEM((pairs,), jnp.int32),
                pltpu.VMEM((slots * rows, width), jnp.bfloat16),
                pltpu.VMEM((here * fresh_rows, width), jnp.bfloat16),
                pltpu.VMEM((slots, rows, LATENT), jnp.float32),
                pltpu.VMEM((slots, rows, LANES), jnp.float32),
                pltpu.VMEM((slots, rows, LANES), jnp.float32),
                pltpu.VMEM((slots * rows, LATENT), jnp.bfloat16),
                pltpu.VMEM((2, rows, BLOCK), jnp.float32),
                pltpu.VMEM((2, rows, BLOCK), jnp.float32),
                pltpu.SMEM(ids.shape, jnp.int32),
                pltpu.SMEM(decode_rows.shape, jnp.int32),
                pltpu.SMEM(lengths.shape, jnp.int32),
                pltpu.SemaphoreType.DMA((3,)),
            ],
            compiler_params=limit(14),
            cost_estimate=cost(8),
            name="attend",
        )(ids, decode_rows, lengths, *received, cache, key_up, value_up)

    def order(kernel, in_specs, scratch, arrays):
        return pl.pallas_call(
            kernel,
            out_shape=jax.ShapeDtypeStruct((steps, sources * requests, columns), jnp.bfloat16),
            in_specs=in_specs,
            out_specs=vmem(),
            scratch_shapes=scratch,
            compiler_params=limit(16),
            cost_estimate=cost(2),
            name="order_rows",
        )(*arrays)

    if not relative:
        received = lax.all_to_all(packed[0], "seq", split_axis=0, concat_axis=0, tiled=True)
        every_row = lax.all_gather(attend([received], 0), "seq", axis=0, tiled=True)
        partial_value = jnp.dot(every_row, out_proj, preferred_element_type=jnp.float32).astype(jnp.bfloat16)
        shares = lax.all_to_all(partial_value, "head", split_axis=0, concat_axis=0, tiled=True)
        shares = shares.reshape(head_devices, -1, columns)
        summed = jnp.sum(shares.astype(jnp.float32), axis=0).astype(jnp.bfloat16)
        whole = lax.all_gather(summed, "head", axis=0, tiled=True)
        return order(order_whole_kernel, [vmem()] * 2, [], [pick, whole])

    def project(parts, first_col, cols):
        rows_here = len(parts) * parts[0].shape[0]
        return pl.pallas_call(
            functools.partial(project_kernel, first_col),
            out_shape=[jax.ShapeDtypeStruct((rows_here // 2, cols), jnp.bfloat16)] * 2,
            in_specs=[smem()] + [vmem()] * (len(parts) + 1),
            out_specs=[vmem()] * 2,
            compiler_params=limit(10),
            cost_estimate=cost(2),
            name="project_out",
        )(ids, *parts, out_proj)

    received = [packed[0]] + [flip(packed[k], "seq", k) for k in range(1, 4)]
    near_rows = attend(received[:2], 0)
    near_across = flip(near_rows, "seq", 2)
    far_rows = attend(received[2:], 2)
    near_across, far_rows = lax.optimization_barrier((near_across, far_rows))
    near = [near_rows, flip(near_rows, "seq", 1), near_across, flip(near_across, "seq", 1)]
    far_across = flip(far_rows, "seq", 2)

    def after(value, *others):
        return lax.optimization_barrier((value,) + others)[0]

    def swap(piece):
        return flip(piece[1], "head", 1)

    half = steps * sources * requests // 2

    def cut(parts, first_row, shares):
        groups = columns // LANES
        edges = [LANES * (groups * sum(shares[:i]) // sum(shares)) for i in range(len(shares) + 1)]
        made = []
        for at, end in zip(edges, edges[1:]):
            keep, send = project(parts, at, end - at)
            made.append((first_row, at, keep, swap((keep, send))))
        return made

    near_made = cut(near, 0, (5, 9))
    pairs = [add(near_made[0][2], near_made[0][3])]
    far = [far_rows, flip(far_rows, "seq", 1), far_across, flip(far_across, "seq", 1)]
    far_made = cut(far, half, (6, 5, 3))
    made = near_made + far_made
    for i, (_, _, keep, incoming) in enumerate(made[1:], 1):
        pairs.append(add(keep, incoming))
    crossed = [flip(pair, "head", 3) for pair in pairs]
    last_made = made[-1][2]
    arrays = []
    for i, (pair, cross) in enumerate(zip(pairs, crossed)):
        if i < len(near_made):
            cross = after(cross, *(last_made,))
        total = add(pair, cross)
        arrays += [total, flip(total, "head", 1)]
    layout = tuple((row, col) for row, col, _, _ in made)
    scratch = [pltpu.VMEM((2 * half, columns), jnp.bfloat16)]
    kernel = functools.partial(order_kernel, layout)
    return order(kernel, [smem()] + [vmem()] * (1 + len(arrays)), scratch, [ids, pick] + arrays)


def solution(mesh):
    return jax.shard_map(
        local,
        mesh=mesh,
        in_specs=(
            P(("groups", "seq"), None),
            P("groups", None),
            P("groups"),
            P(None, ("groups", "seq"), "head", None),
            P(None, ("groups", "seq"), "head", None),
            P(None, ("groups", "seq"), None),
            P("head", None, None),
            P("head", None, None),
            P("head", "seq"),
        ),
        out_specs=P(None, "groups", "seq"),
        check_vma=False,
    )
```

```python
import functools

import jax
import jax.numpy as jnp
from jax import lax
from jax.experimental import pallas as pl
from jax.experimental.pallas import tpu as pltpu
from jax.sharding import PartitionSpec as P

LATENT = 512
BLOCK = 256
LANES = 128
LOG2E = 1.4426950408889634
NEG = -1e30
PLACES = 1024


def own_slots(decode_ref, slot_ref, me, sources, requests, per_pair):
    shift = requests.bit_length() - 1

    def one_source(s, carry):
        count = jnp.int32(0)
        for r in range(requests):
            row = decode_ref[s * requests + r]
            slot_ref[s * (per_pair + 1) + jnp.minimum(count, per_pair)] = row & (requests - 1)
            count = count + jnp.where((row >> shift) == me, 1, 0).astype(jnp.int32)
        return carry

    lax.fori_loop(0, sources, one_source, jnp.int32(0))


def mark_kernel(ids_ref, out_ref):
    out_ref[...] = jnp.full(out_ref.shape, ids_ref[0], jnp.int32)


def pack_kernel(sizes, relative, ids_ref, decode_ref, nope_ref, rope_ref, fresh_ref, after_ref, *rest):
    sources, per_pair, steps, heads, requests, fresh_rows = sizes
    out_refs, (slots, wide) = rest[:-2], rest[-2:]
    me = ids_ref[0] & (PLACES - 1)
    rows = heads * steps
    half = rows // 2
    rope_base = per_pair * rows
    fresh_base = rope_base + per_pair * half
    own_slots(decode_ref, slots, me, sources, requests, per_pair)

    def one_dest(s, out_ref, e):
        for j in range(per_pair):
            row = slots[s * (per_pair + 1) + j]
            for t in range(steps):
                wide[2 * j, pl.ds(t, heads, stride=steps), :] = nope_ref[t, row].astype(jnp.float32)
                wide[2 * j + 1, pl.ds(t, heads, stride=steps), :] = jnp.concatenate(
                    [rope_ref[t, row].astype(jnp.float32)] * 2, axis=1
                )
        for j in range(per_pair):
            out_ref[e, j * rows : (j + 1) * rows, :] = wide[2 * j].astype(jnp.bfloat16)
            low = lax.broadcasted_iota(jnp.int32, (half, LANES), 1) < LANES // 2
            packed = jnp.where(low, wide[2 * j + 1, 0:half, :], wide[2 * j + 1, half : 2 * half, :])
            out_ref[e, rope_base + j * half : rope_base + (j + 1) * half, :] = packed.astype(jnp.bfloat16)

    if relative:
        dests = [me ^ k for k in range(sources)]
        for k in range(sources):
            one_dest(dests[k], out_refs[k], 0)
    else:
        dests = list(range(sources))

        def step(s, carry):
            one_dest(s, out_refs[0], s)
            return carry

        lax.fori_loop(0, sources, step, jnp.int32(0))
    shape = (sources * fresh_rows, steps * requests)
    row_id = lax.broadcasted_iota(jnp.int32, shape, 0)
    col_id = lax.broadcasted_iota(jnp.int32, shape, 1)
    wanted = jnp.full(shape, -1, jnp.int32)
    for k in range(sources):
        for j in range(per_pair):
            first = k * fresh_rows + j * steps
            here = (row_id >= first) & (row_id < first + steps)
            wanted = jnp.where(here, (row_id - first) * requests + slots[dests[k] * (per_pair + 1) + j], wanted)
    pick = jnp.where(col_id == wanted, 1.0, 0.0).astype(jnp.bfloat16)
    width = fresh_ref.shape[2]
    source_rows = jnp.concatenate([fresh_ref[t] for t in range(steps)], axis=0)
    picked = jnp.dot(pick, source_rows, preferred_element_type=jnp.float32).astype(jnp.bfloat16)
    for k in range(sources):
        for c in range(-(-width // LANES)):
            piece = picked[k * fresh_rows : (k + 1) * fresh_rows, c * LANES : min((c + 1) * LANES, width)]
            if piece.shape[1] < LANES:
                piece = jnp.concatenate([piece] * (LANES // piece.shape[1]), axis=1)
            first = fresh_base + c * fresh_rows
            if relative:
                out_refs[k][0, first : first + fresh_rows, :] = piece
            else:
                out_refs[0][k, first : first + fresh_rows, :] = piece


def attend_kernel(sizes, scale, relative, base, recv_count, ids_any, decode_any, length_any, *rest):
    sources, per_pair, steps, heads, requests, fresh_rows = sizes
    recv_refs = rest[:recv_count]
    (
        cache, key_up, value_up, out_ref,
        slot_offset, slot_length, owner_count, pair_slot, pair_start,
        queries, fresh, acc, run_max, run_sum, latent, even_scores, odd_scores,
        ids_ref, decode_ref, length_ref, sems,
    ) = rest[recv_count:]
    tables = [
        pltpu.make_async_copy(ids_any, ids_ref, sems.at[0]),
        pltpu.make_async_copy(decode_any, decode_ref, sems.at[1]),
        pltpu.make_async_copy(length_any, length_ref, sems.at[2]),
    ]
    for table in tables:
        table.start()
    owners = [(ref, e) for ref in recv_refs for e in range(ref.shape[0])]
    here = len(owners)
    slots = here * per_pair
    width, tokens = cache.shape
    rows = heads * steps
    half = rows // 2
    rope_base = per_pair * rows
    fresh_base = rope_base + per_pair * half
    group = 16 // steps
    shift = requests.bit_length() - 1
    factor = scale * LOG2E

    for e in range(here):
        ref, at = owners[e]
        for c in range(-(-width // LANES)):
            lanes = min(LANES, width - c * LANES)
            first = fresh_base + c * fresh_rows
            fresh[e * fresh_rows : (e + 1) * fresh_rows, c * LANES : c * LANES + lanes] = ref[
                at, first : first + fresh_rows, 0:lanes
            ]
        for j in range(per_pair):
            slot = e * per_pair + j
            first = rope_base + j * half
            piece = ref[at, first : first + half, :]
            queries[slot * rows : slot * rows + half, LATENT:width] = piece[:, 0 : width - LATENT]
            queries[slot * rows + half : (slot + 1) * rows, LATENT:width] = piece[:, LANES - (width - LATENT) :]

    inner_head = lax.broadcasted_iota(jnp.int32, (slots * 16, LANES), 0) // steps % group
    own_head = [jnp.where(inner_head == u, 1.0, 0.0).astype(jnp.bfloat16) for u in range(group)]

    def absorb(i):
        tall = jnp.concatenate(
            [ref[at, j * rows + i * 16 : j * rows + (i + 1) * 16, :] for ref, at in owners for j in range(per_pair)],
            axis=0,
        )
        left = jnp.concatenate([tall * own_head[u] for u in range(group)], axis=1)
        right = jnp.concatenate([key_up[i * group + u] for u in range(group)], axis=0)
        res = jnp.dot(left, right, preferred_element_type=jnp.float32).astype(jnp.bfloat16)
        for slot in range(slots):
            queries[slot * rows + i * 16 : slot * rows + (i + 1) * 16, 0:LATENT] = res[slot * 16 : (slot + 1) * 16]

    groups = heads // group
    for i in range(groups // 4):
        absorb(i)
    for table in tables:
        table.wait()

    me = ids_ref[0] & (PLACES - 1)
    for o in range(sources):
        owner_count[o] = jnp.int32(0)
    total = jnp.int32(0)
    for r in range(requests):
        owner = decode_ref[me * requests + r] >> shift
        at = owner_count[owner]
        owner_count[owner] = at + 1
        e = (owner ^ me) - base if relative else owner
        slot = jnp.where((e >= 0) & (e < here), e * per_pair + at, slots)
        length = length_ref[me, r]
        slot_offset[slot] = total
        slot_length[slot] = length
        total = total + length
    count = jnp.int32(0)
    for slot in range(slots):
        start = slot_offset[slot] & ~(LANES - 1)
        end = slot_offset[slot] + slot_length[slot]
        for k in range(512 // BLOCK + 1):
            pair_slot[count] = jnp.int32(slot)
            pair_start[count] = start + k * BLOCK
            count = count + jnp.where(start + k * BLOCK < end, 1, 0).astype(jnp.int32)

    for i in range(groups // 4, groups):
        absorb(i)

    fresh_scores = (
        lax.dot_general(queries[...], fresh[...], (((1,), (1,)), ((), ())), preferred_element_type=jnp.float32) * factor
    )
    row_id = lax.broadcasted_iota(jnp.int32, (rows, here * fresh_rows), 0)
    col_id = lax.broadcasted_iota(jnp.int32, (rows, here * fresh_rows), 1)
    behind = row_id & (steps - 1)
    fresh_weights = []
    for slot in range(slots):
        first = (slot // per_pair) * fresh_rows + (slot % per_pair) * steps
        seen = (col_id >= first) & (col_id <= first + behind)
        scores = jnp.where(seen, fresh_scores[slot * rows : (slot + 1) * rows], NEG)
        top = jnp.max(scores, axis=1, keepdims=True)
        weights = jnp.exp2(scores - top)
        run_max[slot] = jnp.broadcast_to(top, (rows, LANES))
        run_sum[slot] = jnp.broadcast_to(jnp.sum(weights, axis=1, keepdims=True), (rows, LANES))
        fresh_weights.append(weights.astype(jnp.bfloat16))
    for slot in range(slots):
        acc[slot] = jnp.dot(fresh_weights[slot], fresh[:, 0:LATENT], preferred_element_type=jnp.float32)

    def make_scores(buffer, g):
        for u in range(2):
            p = jnp.minimum(g * 2 + u, count - 1)
            q = queries[pl.ds(pl.multiple_of(pair_slot[p] * rows, 16), rows), :]
            read = pl.multiple_of(jnp.minimum(pair_start[p], tokens - BLOCK), LANES)
            buffer[u] = jnp.dot(q, cache[:, pl.ds(read, BLOCK)], preferred_element_type=jnp.float32)

    token = lax.broadcasted_iota(jnp.int32, (1, BLOCK), 1)

    def take_scores(buffer, g):
        for u in range(2):
            p = jnp.minimum(g * 2 + u, count - 1)
            slot = pair_slot[p]
            start = pair_start[p]
            read = jnp.minimum(start, tokens - BLOCK)
            low = jnp.maximum(slot_offset[slot], start) - read
            high = jnp.minimum(slot_offset[slot] + slot_length[slot], start + BLOCK) - read
            high = jnp.where(g * 2 + u < count, high, low)
            bias = jnp.where((token >= low) & (token < high), 0.0, NEG)
            scores = buffer[u] * factor + bias
            top = jnp.max(scores, axis=1, keepdims=True)
            weights = jnp.exp2(scores - top)
            part_sum = jnp.broadcast_to(jnp.sum(weights, axis=1, keepdims=True), (rows, LANES))
            part = lax.dot_general(
                weights.astype(jnp.bfloat16),
                cache[0:LATENT, pl.ds(pl.multiple_of(read, LANES), BLOCK)],
                (((1,), (1,)), ((), ())),
                preferred_element_type=jnp.float32,
            )
            part_max = jnp.broadcast_to(top, (rows, LANES))
            old_max = run_max[slot]
            new_max = jnp.maximum(old_max, part_max)
            keep = jnp.exp2(old_max - new_max)
            add = jnp.exp2(part_max - new_max)
            run_max[slot] = new_max
            run_sum[slot] = run_sum[slot] * keep + part_sum * add
            for c in range(LATENT // LANES):
                cols = slice(c * LANES, (c + 1) * LANES)
                acc[slot, :, cols] = acc[slot, :, cols] * keep + part[:, cols] * add

    make_scores(even_scores, 0)

    def four_pairs(i, carry):
        make_scores(odd_scores, 2 * i + 1)
        take_scores(even_scores, 2 * i)
        make_scores(even_scores, 2 * i + 2)
        take_scores(odd_scores, 2 * i + 1)
        return carry

    fours = count >> 2
    lax.fori_loop(0, fours, four_pairs, jnp.int32(0))

    @pl.when(count > 4 * fours)
    def _():
        take_scores(even_scores, 2 * fours)

    @pl.when(count > 4 * fours + 2)
    def _():
        make_scores(odd_scores, 2 * fours + 1)
        take_scores(odd_scores, 2 * fours + 1)

    for slot in range(slots):
        inverse = 1.0 / run_sum[slot]
        for c in range(LATENT // LANES):
            cols = slice(c * LANES, (c + 1) * LANES)
            latent[slot * rows : (slot + 1) * rows, cols] = (acc[slot, :, cols] * inverse).astype(jnp.bfloat16)
    vdim = value_up.shape[2]
    for i in range(heads // group):
        left = jnp.concatenate(
            [latent[slot * rows + i * 16 : slot * rows + (i + 1) * 16, :] for slot in range(slots)], axis=0
        )
        right = jnp.concatenate([value_up[i * group + u] for u in range(group)], axis=1)
        res = jnp.dot(left, right, preferred_element_type=jnp.float32)
        for u in range(group):
            own = jnp.concatenate(
                [
                    res[slot * 16 + u * steps : slot * 16 + (u + 1) * steps, u * vdim : (u + 1) * vdim]
                    for slot in range(slots)
                ],
                axis=0,
            )
            head = i * group + u
            out_ref[:, head * vdim : (head + 1) * vdim] = own.astype(jnp.bfloat16)


def place_kernel(sizes, relative, ids_ref, decode_ref, out_ref, owner_count, place):
    sources, per_pair, steps, requests = sizes
    me = ids_ref[0] & (PLACES - 1)
    rows = sources * requests
    shift = requests.bit_length() - 1

    def one_source(s, carry):
        for o in range(sources):
            owner_count[o] = jnp.int32(0)
        for r in range(requests):
            row = decode_ref[s * requests + r]
            owner = row >> shift
            at = owner_count[owner]
            owner_count[owner] = at + 1
            if relative:
                e = owner ^ s
                at_row = (e >> 1) * (2 * sources * per_pair) + (me ^ s) * (2 * per_pair) + (e & 1) * per_pair + at
            else:
                at_row = s * requests + owner * per_pair + at
            place[row] = at_row * steps
        return carry

    lax.fori_loop(0, sources, one_source, jnp.int32(0))
    narrow = (rows, LANES)
    row_id = lax.broadcasted_iota(jnp.int32, narrow, 0)

    def put(b, wanted):
        return jnp.where(row_id == b, place[b], wanted)

    wanted = lax.fori_loop(0, rows, put, jnp.zeros(narrow, jnp.int32), unroll=8)[:, 0:1]
    col_id = lax.broadcasted_iota(jnp.int32, (rows, rows * steps), 1)
    for t in range(steps):
        out_ref[t] = jnp.where(col_id == wanted + t, 1.0, 0.0).astype(jnp.bfloat16)


def keeps_upper(ids_ref):
    z = ids_ref[0] // PLACES
    return (z == 1) | (z == 2)


def order_kernel(layout, ids_ref, pick_ref, *rest):
    pieces, out_ref, x = rest[:-2], rest[-2], rest[-1]
    upper = keeps_upper(ids_ref)

    def assemble(first, second):
        for i, (row, col) in enumerate(layout):
            rows, cols = pieces[2 * i].shape
            x[row : row + rows, col : col + cols] = pieces[2 * i + first][...]
            x[row + rows : row + 2 * rows, col : col + cols] = pieces[2 * i + second][...]

    pl.when(upper)(lambda: assemble(1, 0))
    pl.when(jnp.logical_not(upper))(lambda: assemble(0, 1))
    steps, rows, _ = pick_ref.shape
    pick = jnp.concatenate([pick_ref[t] for t in range(steps)], axis=0)
    for c in range(0, x.shape[1], BLOCK):
        tile = jnp.dot(pick, x[:, c : c + BLOCK], preferred_element_type=jnp.float32).astype(jnp.bfloat16)
        for t in range(steps):
            out_ref[t, :, c : c + BLOCK] = tile[t * rows : (t + 1) * rows]


def order_whole_kernel(pick_ref, x_ref, out_ref):
    for t in range(pick_ref.shape[0]):
        out_ref[t] = jnp.dot(pick_ref[t], x_ref[...], preferred_element_type=jnp.float32).astype(jnp.bfloat16)


def project_kernel(first_col, ids_ref, *rest):
    parts, (weight, keep, send) = rest[:-3], rest[-3:]
    half = keep.shape[0]
    upper = keeps_upper(ids_ref)
    cols = keep.shape[1]
    x = jnp.concatenate([part[...] for part in parts], axis=0)
    for c in range(0, cols, BLOCK):
        n = min(BLOCK, cols - c)
        tile = jnp.dot(x, weight[:, first_col + c : first_col + c + n], preferred_element_type=jnp.float32)
        keep[:, c : c + n] = jnp.where(upper, tile[half:], tile[:half]).astype(jnp.bfloat16)
        send[:, c : c + n] = jnp.where(upper, tile[:half], tile[half:]).astype(jnp.bfloat16)


def smem():
    return pl.BlockSpec(memory_space=pltpu.SMEM)


def vmem():
    return pl.BlockSpec(memory_space=pltpu.VMEM)


def anywhere():
    return pl.BlockSpec(memory_space=pl.ANY)


def limit(mib):
    return pltpu.CompilerParams(vmem_limit_bytes=mib * 1024 * 1024)


def cost(microseconds):
    return pl.CostEstimate(
        flops=int(microseconds * 1.0e9), bytes_accessed=int(microseconds * 3.0e6), transcendentals=0
    )


def flip(x, axis, distance):
    size = lax.axis_size(axis)
    return lax.ppermute(x, axis, [(i, i ^ distance) for i in range(size)])


def add(x, y):
    return (x.astype(jnp.float32) + y.astype(jnp.float32)).astype(jnp.bfloat16)


def local(latent_cache, lengths, decode_rows, q_nope, q_rope, new_latent, key_up, value_up, out_proj):
    sources = lax.axis_size("seq")
    head_devices = lax.axis_size("head")
    relative = sources == 4 and head_devices == 4
    requests = lengths.shape[1]
    per_pair = requests // sources
    tokens, width = latent_cache.shape
    steps, _, heads, nope = q_nope.shape
    scale = (nope + q_rope.shape[3]) ** (-0.5)
    fresh_rows = -(-per_pair * steps // 16) * 16
    rows = heads * steps
    columns = out_proj.shape[1]
    packed_rows = per_pair * rows + per_pair * rows // 2 + -(-width // LANES) * fresh_rows
    sizes = (sources, per_pair, steps, heads, requests, fresh_rows)
    ids = (lax.axis_index("seq") + PLACES * lax.axis_index("head")).astype(jnp.int32).reshape(1)
    cache = latent_cache.T

    pick = pl.pallas_call(
        functools.partial(place_kernel, (sources, per_pair, steps, requests), relative),
        out_shape=jax.ShapeDtypeStruct((steps, sources * requests, steps * sources * requests), jnp.bfloat16),
        in_specs=[smem(), smem()],
        out_specs=vmem(),
        scratch_shapes=[pltpu.SMEM((sources,), jnp.int32), pltpu.SMEM((sources * requests,), jnp.int32)],
        compiler_params=limit(12),
        cost_estimate=cost(0.1),
        name="place_rows",
    )(ids, decode_rows)

    mark = pl.pallas_call(
        mark_kernel,
        out_shape=jax.ShapeDtypeStruct((8, LANES), jnp.int32),
        in_specs=[smem()],
        out_specs=vmem(),
        compiler_params=limit(4),
        cost_estimate=cost(2),
        name="mark_start",
    )(ids)

    outs, each = (sources, 1) if relative else (1, sources)
    packed = pl.pallas_call(
        functools.partial(pack_kernel, sizes, relative),
        out_shape=[jax.ShapeDtypeStruct((each, packed_rows, LANES), jnp.bfloat16)] * outs,
        in_specs=[smem(), smem(), vmem(), vmem(), vmem(), anywhere()],
        out_specs=[vmem()] * outs,
        scratch_shapes=[
            pltpu.SMEM((sources * (per_pair + 1),), jnp.int32),
            pltpu.VMEM((2 * per_pair, rows, LANES), jnp.float32),
        ],
        compiler_params=limit(8),
        cost_estimate=cost(2),
        name="pack_queries",
    )(ids, decode_rows, q_nope, q_rope, new_latent, mark)

    def attend(received, base):
        here = sum(part.shape[0] for part in received)
        slots = here * per_pair
        pairs = slots * (512 // BLOCK + 1) + 1
        return pl.pallas_call(
            functools.partial(attend_kernel, sizes, scale, relative, base, len(received)),
            out_shape=jax.ShapeDtypeStruct((slots * steps, heads * value_up.shape[2]), jnp.bfloat16),
            in_specs=[anywhere()] * 3 + [vmem()] * (len(received) + 3),
            out_specs=vmem(),
            scratch_shapes=[
                pltpu.SMEM((slots + 1,), jnp.int32),
                pltpu.SMEM((slots + 1,), jnp.int32),
                pltpu.SMEM((sources,), jnp.int32),
                pltpu.SMEM((pairs,), jnp.int32),
                pltpu.SMEM((pairs,), jnp.int32),
                pltpu.VMEM((slots * rows, width), jnp.bfloat16),
                pltpu.VMEM((here * fresh_rows, width), jnp.bfloat16),
                pltpu.VMEM((slots, rows, LATENT), jnp.float32),
                pltpu.VMEM((slots, rows, LANES), jnp.float32),
                pltpu.VMEM((slots, rows, LANES), jnp.float32),
                pltpu.VMEM((slots * rows, LATENT), jnp.bfloat16),
                pltpu.VMEM((2, rows, BLOCK), jnp.float32),
                pltpu.VMEM((2, rows, BLOCK), jnp.float32),
                pltpu.SMEM(ids.shape, jnp.int32),
                pltpu.SMEM(decode_rows.shape, jnp.int32),
                pltpu.SMEM(lengths.shape, jnp.int32),
                pltpu.SemaphoreType.DMA((3,)),
            ],
            compiler_params=limit(14),
            cost_estimate=cost(8),
            name="attend",
        )(ids, decode_rows, lengths, *received, cache, key_up, value_up)

    def order(kernel, in_specs, scratch, arrays):
        return pl.pallas_call(
            kernel,
            out_shape=jax.ShapeDtypeStruct((steps, sources * requests, columns), jnp.bfloat16),
            in_specs=in_specs,
            out_specs=vmem(),
            scratch_shapes=scratch,
            compiler_params=limit(16),
            cost_estimate=cost(2),
            name="order_rows",
        )(*arrays)

    if not relative:
        received = lax.all_to_all(packed[0], "seq", split_axis=0, concat_axis=0, tiled=True)
        every_row = lax.all_gather(attend([received], 0), "seq", axis=0, tiled=True)
        partial_value = jnp.dot(every_row, out_proj, preferred_element_type=jnp.float32).astype(jnp.bfloat16)
        shares = lax.all_to_all(partial_value, "head", split_axis=0, concat_axis=0, tiled=True)
        shares = shares.reshape(head_devices, -1, columns)
        summed = jnp.sum(shares.astype(jnp.float32), axis=0).astype(jnp.bfloat16)
        whole = lax.all_gather(summed, "head", axis=0, tiled=True)
        return order(order_whole_kernel, [vmem()] * 2, [], [pick, whole])

    def project(parts, first_col, cols):
        rows_here = len(parts) * parts[0].shape[0]
        return pl.pallas_call(
            functools.partial(project_kernel, first_col),
            out_shape=[jax.ShapeDtypeStruct((rows_here // 2, cols), jnp.bfloat16)] * 2,
            in_specs=[smem()] + [vmem()] * (len(parts) + 1),
            out_specs=[vmem()] * 2,
            compiler_params=limit(10),
            cost_estimate=cost(2),
            name="project_out",
        )(ids, *parts, out_proj)

    received = [packed[0]] + [flip(packed[k], "seq", k) for k in range(1, 4)]
    near_rows = attend(received[:2], 0)
    near_across = flip(near_rows, "seq", 2)
    far_rows = attend(received[2:], 2)
    near_across, far_rows = lax.optimization_barrier((near_across, far_rows))
    near = [near_rows, flip(near_rows, "seq", 1), near_across, flip(near_across, "seq", 1)]
    far_across = flip(far_rows, "seq", 2)

    def after(value, *others):
        return lax.optimization_barrier((value,) + others)[0]

    def swap(piece):
        return flip(piece[1], "head", 1)

    half = steps * sources * requests // 2

    def cut(parts, first_row, shares):
        groups = columns // LANES
        edges = [LANES * (groups * sum(shares[:i]) // sum(shares)) for i in range(len(shares) + 1)]
        made = []
        for at, end in zip(edges, edges[1:]):
            keep, send = project(parts, at, end - at)
            made.append((first_row, at, keep, swap((keep, send))))
        return made

    near_made = cut(near, 0, (5, 9))
    pairs = [add(near_made[0][2], near_made[0][3])]
    far = [far_rows, flip(far_rows, "seq", 1), far_across, flip(far_across, "seq", 1)]
    far_made = cut(far, half, (6, 5, 3))
    made = near_made + far_made
    for i, (_, _, keep, incoming) in enumerate(made[1:], 1):
        pairs.append(add(keep, incoming))
    crossed = [flip(pair, "head", 3) for pair in pairs]
    last_made = made[-1][2]
    arrays = []
    for i, (pair, cross) in enumerate(zip(pairs, crossed)):
        if i < len(near_made):
            cross = after(cross, *(last_made,))
        total = add(pair, cross)
        arrays += [total, flip(total, "head", 1)]
    layout = tuple((row, col) for row, col, _, _ in made)
    scratch = [pltpu.VMEM((2 * half, columns), jnp.bfloat16)]
    kernel = functools.partial(order_kernel, layout)
    return order(kernel, [smem()] + [vmem()] * (1 + len(arrays)), scratch, [ids, pick] + arrays)


def solution(mesh):
    return jax.shard_map(
        local,
        mesh=mesh,
        in_specs=(
            P(("groups", "seq"), None),
            P("groups", None),
            P("groups"),
            P(None, ("groups", "seq"), "head", None),
            P(None, ("groups", "seq"), "head", None),
            P(None, ("groups", "seq"), None),
            P("head", None, None),
            P("head", None, None),
            P("head", "seq"),
        ),
        out_specs=P(None, "groups", "seq"),
        check_vma=False,
    )
```

```python
import functools

import jax
import jax.numpy as jnp
from jax import lax
from jax.experimental import pallas as pl
from jax.experimental.pallas import tpu as pltpu
from jax.sharding import PartitionSpec as P

LATENT = 512
BLOCK = 256
LANES = 128
LOG2E = 1.4426950408889634
NEG = -1e30
PLACES = 1024


def own_slots(decode_ref, slot_ref, me, sources, requests, per_pair):
    shift = requests.bit_length() - 1

    def one_source(s, carry):
        count = jnp.int32(0)
        for r in range(requests):
            row = decode_ref[s * requests + r]
            slot_ref[s * (per_pair + 1) + jnp.minimum(count, per_pair)] = row & (requests - 1)
            count = count + jnp.where((row >> shift) == me, 1, 0).astype(jnp.int32)
        return carry

    lax.fori_loop(0, sources, one_source, jnp.int32(0))


def mark_kernel(ids_ref, out_ref):
    out_ref[...] = jnp.full(out_ref.shape, ids_ref[0], jnp.int32)


def pack_kernel(sizes, relative, ids_ref, decode_ref, nope_ref, rope_ref, fresh_ref, after_ref, *rest):
    sources, per_pair, steps, heads, requests, fresh_rows = sizes
    out_refs, (slots, wide) = rest[:-2], rest[-2:]
    me = ids_ref[0] & (PLACES - 1)
    rows = heads * steps
    half = rows // 2
    rope_base = per_pair * rows
    fresh_base = rope_base + per_pair * half
    own_slots(decode_ref, slots, me, sources, requests, per_pair)

    def one_dest(s, out_ref, e):
        for j in range(per_pair):
            row = slots[s * (per_pair + 1) + j]
            for t in range(steps):
                wide[2 * j, pl.ds(t, heads, stride=steps), :] = nope_ref[t, row].astype(jnp.float32)
                wide[2 * j + 1, pl.ds(t, heads, stride=steps), :] = jnp.concatenate(
                    [rope_ref[t, row].astype(jnp.float32)] * 2, axis=1
                )
        for j in range(per_pair):
            out_ref[e, j * rows : (j + 1) * rows, :] = wide[2 * j].astype(jnp.bfloat16)
            low = lax.broadcasted_iota(jnp.int32, (half, LANES), 1) < LANES // 2
            packed = jnp.where(low, wide[2 * j + 1, 0:half, :], wide[2 * j + 1, half : 2 * half, :])
            out_ref[e, rope_base + j * half : rope_base + (j + 1) * half, :] = packed.astype(jnp.bfloat16)

    if relative:
        dests = [me ^ k for k in range(sources)]
        for k in range(sources):
            one_dest(dests[k], out_refs[k], 0)
    else:
        dests = list(range(sources))

        def step(s, carry):
            one_dest(s, out_refs[0], s)
            return carry

        lax.fori_loop(0, sources, step, jnp.int32(0))
    shape = (sources * fresh_rows, steps * requests)
    row_id = lax.broadcasted_iota(jnp.int32, shape, 0)
    col_id = lax.broadcasted_iota(jnp.int32, shape, 1)
    wanted = jnp.full(shape, -1, jnp.int32)
    for k in range(sources):
        for j in range(per_pair):
            first = k * fresh_rows + j * steps
            here = (row_id >= first) & (row_id < first + steps)
            wanted = jnp.where(here, (row_id - first) * requests + slots[dests[k] * (per_pair + 1) + j], wanted)
    pick = jnp.where(col_id == wanted, 1.0, 0.0).astype(jnp.bfloat16)
    width = fresh_ref.shape[2]
    source_rows = jnp.concatenate([fresh_ref[t] for t in range(steps)], axis=0)
    picked = jnp.dot(pick, source_rows, preferred_element_type=jnp.float32).astype(jnp.bfloat16)
    for k in range(sources):
        for c in range(-(-width // LANES)):
            piece = picked[k * fresh_rows : (k + 1) * fresh_rows, c * LANES : min((c + 1) * LANES, width)]
            if piece.shape[1] < LANES:
                piece = jnp.concatenate([piece] * (LANES // piece.shape[1]), axis=1)
            first = fresh_base + c * fresh_rows
            if relative:
                out_refs[k][0, first : first + fresh_rows, :] = piece
            else:
                out_refs[0][k, first : first + fresh_rows, :] = piece


def attend_kernel(sizes, scale, relative, base, recv_count, ids_any, decode_any, length_any, *rest):
    sources, per_pair, steps, heads, requests, fresh_rows = sizes
    recv_refs = rest[:recv_count]
    (
        cache, key_up, value_up, out_ref,
        slot_offset, slot_length, owner_count, pair_slot, pair_start,
        queries, fresh, acc, run_max, run_sum, latent, even_scores, odd_scores,
        ids_ref, decode_ref, length_ref, sems,
    ) = rest[recv_count:]
    tables = [
        pltpu.make_async_copy(ids_any, ids_ref, sems.at[0]),
        pltpu.make_async_copy(decode_any, decode_ref, sems.at[1]),
        pltpu.make_async_copy(length_any, length_ref, sems.at[2]),
    ]
    for table in tables:
        table.start()
    owners = [(ref, e) for ref in recv_refs for e in range(ref.shape[0])]
    here = len(owners)
    slots = here * per_pair
    width, tokens = cache.shape
    rows = heads * steps
    half = rows // 2
    rope_base = per_pair * rows
    fresh_base = rope_base + per_pair * half
    group = 16 // steps
    shift = requests.bit_length() - 1
    factor = scale * LOG2E

    for e in range(here):
        ref, at = owners[e]
        for c in range(-(-width // LANES)):
            lanes = min(LANES, width - c * LANES)
            first = fresh_base + c * fresh_rows
            fresh[e * fresh_rows : (e + 1) * fresh_rows, c * LANES : c * LANES + lanes] = ref[
                at, first : first + fresh_rows, 0:lanes
            ]
        for j in range(per_pair):
            slot = e * per_pair + j
            first = rope_base + j * half
            piece = ref[at, first : first + half, :]
            queries[slot * rows : slot * rows + half, LATENT:width] = piece[:, 0 : width - LATENT]
            queries[slot * rows + half : (slot + 1) * rows, LATENT:width] = piece[:, LANES - (width - LATENT) :]

    inner_head = lax.broadcasted_iota(jnp.int32, (slots * 16, LANES), 0) // steps % group
    own_head = [jnp.where(inner_head == u, 1.0, 0.0).astype(jnp.bfloat16) for u in range(group)]

    def absorb(i):
        tall = jnp.concatenate(
            [ref[at, j * rows + i * 16 : j * rows + (i + 1) * 16, :] for ref, at in owners for j in range(per_pair)],
            axis=0,
        )
        left = jnp.concatenate([tall * own_head[u] for u in range(group)], axis=1)
        right = jnp.concatenate([key_up[i * group + u] for u in range(group)], axis=0)
        res = jnp.dot(left, right, preferred_element_type=jnp.float32).astype(jnp.bfloat16)
        for slot in range(slots):
            queries[slot * rows + i * 16 : slot * rows + (i + 1) * 16, 0:LATENT] = res[slot * 16 : (slot + 1) * 16]

    groups = heads // group
    for i in range(groups // 4):
        absorb(i)
    for table in tables:
        table.wait()

    me = ids_ref[0] & (PLACES - 1)
    for o in range(sources):
        owner_count[o] = jnp.int32(0)
    total = jnp.int32(0)
    for r in range(requests):
        owner = decode_ref[me * requests + r] >> shift
        at = owner_count[owner]
        owner_count[owner] = at + 1
        e = (owner ^ me) - base if relative else owner
        slot = jnp.where((e >= 0) & (e < here), e * per_pair + at, slots)
        length = length_ref[me, r]
        slot_offset[slot] = total
        slot_length[slot] = length
        total = total + length
    count = jnp.int32(0)
    for slot in range(slots):
        start = slot_offset[slot] & ~(LANES - 1)
        end = slot_offset[slot] + slot_length[slot]
        for k in range(512 // BLOCK + 1):
            pair_slot[count] = jnp.int32(slot)
            pair_start[count] = start + k * BLOCK
            count = count + jnp.where(start + k * BLOCK < end, 1, 0).astype(jnp.int32)

    for i in range(groups // 4, groups):
        absorb(i)

    fresh_scores = (
        lax.dot_general(queries[...], fresh[...], (((1,), (1,)), ((), ())), preferred_element_type=jnp.float32) * factor
    )
    row_id = lax.broadcasted_iota(jnp.int32, (rows, here * fresh_rows), 0)
    col_id = lax.broadcasted_iota(jnp.int32, (rows, here * fresh_rows), 1)
    behind = row_id & (steps - 1)
    fresh_weights = []
    for slot in range(slots):
        first = (slot // per_pair) * fresh_rows + (slot % per_pair) * steps
        seen = (col_id >= first) & (col_id <= first + behind)
        scores = jnp.where(seen, fresh_scores[slot * rows : (slot + 1) * rows], NEG)
        top = jnp.max(scores, axis=1, keepdims=True)
        weights = jnp.exp2(scores - top)
        run_max[slot] = jnp.broadcast_to(top, (rows, LANES))
        run_sum[slot] = jnp.broadcast_to(jnp.sum(weights, axis=1, keepdims=True), (rows, LANES))
        fresh_weights.append(weights.astype(jnp.bfloat16))
    for slot in range(slots):
        acc[slot] = jnp.dot(fresh_weights[slot], fresh[:, 0:LATENT], preferred_element_type=jnp.float32)

    def make_scores(buffer, g):
        for u in range(2):
            p = jnp.minimum(g * 2 + u, count - 1)
            q = queries[pl.ds(pl.multiple_of(pair_slot[p] * rows, 16), rows), :]
            read = pl.multiple_of(jnp.minimum(pair_start[p], tokens - BLOCK), LANES)
            buffer[u] = jnp.dot(q, cache[:, pl.ds(read, BLOCK)], preferred_element_type=jnp.float32)

    token = lax.broadcasted_iota(jnp.int32, (1, BLOCK), 1)

    def take_scores(buffer, g):
        for u in range(2):
            p = jnp.minimum(g * 2 + u, count - 1)
            slot = pair_slot[p]
            start = pair_start[p]
            read = jnp.minimum(start, tokens - BLOCK)
            low = jnp.maximum(slot_offset[slot], start) - read
            high = jnp.minimum(slot_offset[slot] + slot_length[slot], start + BLOCK) - read
            high = jnp.where(g * 2 + u < count, high, low)
            bias = jnp.where((token >= low) & (token < high), 0.0, NEG)
            scores = buffer[u] * factor + bias
            top = jnp.max(scores, axis=1, keepdims=True)
            weights = jnp.exp2(scores - top)
            part_sum = jnp.broadcast_to(jnp.sum(weights, axis=1, keepdims=True), (rows, LANES))
            part = lax.dot_general(
                weights.astype(jnp.bfloat16),
                cache[0:LATENT, pl.ds(pl.multiple_of(read, LANES), BLOCK)],
                (((1,), (1,)), ((), ())),
                preferred_element_type=jnp.float32,
            )
            part_max = jnp.broadcast_to(top, (rows, LANES))
            old_max = run_max[slot]
            new_max = jnp.maximum(old_max, part_max)
            keep = jnp.exp2(old_max - new_max)
            add = jnp.exp2(part_max - new_max)
            run_max[slot] = new_max
            run_sum[slot] = run_sum[slot] * keep + part_sum * add
            for c in range(LATENT // LANES):
                cols = slice(c * LANES, (c + 1) * LANES)
                acc[slot, :, cols] = acc[slot, :, cols] * keep + part[:, cols] * add

    make_scores(even_scores, 0)

    def four_pairs(i, carry):
        make_scores(odd_scores, 2 * i + 1)
        take_scores(even_scores, 2 * i)
        make_scores(even_scores, 2 * i + 2)
        take_scores(odd_scores, 2 * i + 1)
        return carry

    fours = count >> 2
    lax.fori_loop(0, fours, four_pairs, jnp.int32(0))

    @pl.when(count > 4 * fours)
    def _():
        take_scores(even_scores, 2 * fours)

    @pl.when(count > 4 * fours + 2)
    def _():
        make_scores(odd_scores, 2 * fours + 1)
        take_scores(odd_scores, 2 * fours + 1)

    for slot in range(slots):
        inverse = 1.0 / run_sum[slot]
        for c in range(LATENT // LANES):
            cols = slice(c * LANES, (c + 1) * LANES)
            latent[slot * rows : (slot + 1) * rows, cols] = (acc[slot, :, cols] * inverse).astype(jnp.bfloat16)
    vdim = value_up.shape[2]
    for i in range(heads // group):
        left = jnp.concatenate(
            [latent[slot * rows + i * 16 : slot * rows + (i + 1) * 16, :] for slot in range(slots)], axis=0
        )
        right = jnp.concatenate([value_up[i * group + u] for u in range(group)], axis=1)
        res = jnp.dot(left, right, preferred_element_type=jnp.float32)
        for u in range(group):
            own = jnp.concatenate(
                [
                    res[slot * 16 + u * steps : slot * 16 + (u + 1) * steps, u * vdim : (u + 1) * vdim]
                    for slot in range(slots)
                ],
                axis=0,
            )
            head = i * group + u
            out_ref[:, head * vdim : (head + 1) * vdim] = own.astype(jnp.bfloat16)


def place_kernel(sizes, relative, ids_ref, decode_ref, out_ref, owner_count, place):
    sources, per_pair, steps, requests = sizes
    me = ids_ref[0] & (PLACES - 1)
    rows = sources * requests
    shift = requests.bit_length() - 1

    def one_source(s, carry):
        for o in range(sources):
            owner_count[o] = jnp.int32(0)
        for r in range(requests):
            row = decode_ref[s * requests + r]
            owner = row >> shift
            at = owner_count[owner]
            owner_count[owner] = at + 1
            if relative:
                e = owner ^ s
                at_row = (e >> 1) * (2 * sources * per_pair) + (me ^ s) * (2 * per_pair) + (e & 1) * per_pair + at
            else:
                at_row = s * requests + owner * per_pair + at
            place[row] = at_row * steps
        return carry

    lax.fori_loop(0, sources, one_source, jnp.int32(0))
    narrow = (rows, LANES)
    row_id = lax.broadcasted_iota(jnp.int32, narrow, 0)

    def put(b, wanted):
        return jnp.where(row_id == b, place[b], wanted)

    wanted = lax.fori_loop(0, rows, put, jnp.zeros(narrow, jnp.int32), unroll=8)[:, 0:1]
    col_id = lax.broadcasted_iota(jnp.int32, (rows, rows * steps), 1)
    for t in range(steps):
        out_ref[t] = jnp.where(col_id == wanted + t, 1.0, 0.0).astype(jnp.bfloat16)


def keeps_upper(ids_ref):
    z = ids_ref[0] // PLACES
    return (z == 1) | (z == 2)


def order_kernel(layout, ids_ref, pick_ref, *rest):
    pieces, out_ref, x = rest[:-2], rest[-2], rest[-1]
    upper = keeps_upper(ids_ref)

    def assemble(first, second):
        for i, (row, col) in enumerate(layout):
            rows, cols = pieces[2 * i].shape
            x[row : row + rows, col : col + cols] = pieces[2 * i + first][...]
            x[row + rows : row + 2 * rows, col : col + cols] = pieces[2 * i + second][...]

    pl.when(upper)(lambda: assemble(1, 0))
    pl.when(jnp.logical_not(upper))(lambda: assemble(0, 1))
    steps, rows, _ = pick_ref.shape
    pick = jnp.concatenate([pick_ref[t] for t in range(steps)], axis=0)
    for c in range(0, x.shape[1], BLOCK):
        tile = jnp.dot(pick, x[:, c : c + BLOCK], preferred_element_type=jnp.float32).astype(jnp.bfloat16)
        for t in range(steps):
            out_ref[t, :, c : c + BLOCK] = tile[t * rows : (t + 1) * rows]


def order_whole_kernel(pick_ref, x_ref, out_ref):
    for t in range(pick_ref.shape[0]):
        out_ref[t] = jnp.dot(pick_ref[t], x_ref[...], preferred_element_type=jnp.float32).astype(jnp.bfloat16)


def project_kernel(first_col, ids_ref, *rest):
    parts, (weight, keep, send) = rest[:-3], rest[-3:]
    half = keep.shape[0]
    upper = keeps_upper(ids_ref)
    cols = keep.shape[1]
    x = jnp.concatenate([part[...] for part in parts], axis=0)
    for c in range(0, cols, BLOCK):
        n = min(BLOCK, cols - c)
        tile = jnp.dot(x, weight[:, first_col + c : first_col + c + n], preferred_element_type=jnp.float32)
        keep[:, c : c + n] = jnp.where(upper, tile[half:], tile[:half]).astype(jnp.bfloat16)
        send[:, c : c + n] = jnp.where(upper, tile[:half], tile[half:]).astype(jnp.bfloat16)


def smem():
    return pl.BlockSpec(memory_space=pltpu.SMEM)


def vmem():
    return pl.BlockSpec(memory_space=pltpu.VMEM)


def anywhere():
    return pl.BlockSpec(memory_space=pl.ANY)


def limit(mib):
    return pltpu.CompilerParams(vmem_limit_bytes=mib * 1024 * 1024)


def cost(microseconds):
    return pl.CostEstimate(
        flops=int(microseconds * 1.0e9), bytes_accessed=int(microseconds * 3.0e6), transcendentals=0
    )


def flip(x, axis, distance):
    size = lax.axis_size(axis)
    return lax.ppermute(x, axis, [(i, i ^ distance) for i in range(size)])


def add(x, y):
    return (x.astype(jnp.float32) + y.astype(jnp.float32)).astype(jnp.bfloat16)


def local(latent_cache, lengths, decode_rows, q_nope, q_rope, new_latent, key_up, value_up, out_proj):
    sources = lax.axis_size("seq")
    head_devices = lax.axis_size("head")
    relative = sources == 4 and head_devices == 4
    requests = lengths.shape[1]
    per_pair = requests // sources
    tokens, width = latent_cache.shape
    steps, _, heads, nope = q_nope.shape
    scale = (nope + q_rope.shape[3]) ** (-0.5)
    fresh_rows = -(-per_pair * steps // 16) * 16
    rows = heads * steps
    columns = out_proj.shape[1]
    packed_rows = per_pair * rows + per_pair * rows // 2 + -(-width // LANES) * fresh_rows
    sizes = (sources, per_pair, steps, heads, requests, fresh_rows)
    ids = (lax.axis_index("seq") + PLACES * lax.axis_index("head")).astype(jnp.int32).reshape(1)
    cache = latent_cache.T

    pick = pl.pallas_call(
        functools.partial(place_kernel, (sources, per_pair, steps, requests), relative),
        out_shape=jax.ShapeDtypeStruct((steps, sources * requests, steps * sources * requests), jnp.bfloat16),
        in_specs=[smem(), smem()],
        out_specs=vmem(),
        scratch_shapes=[pltpu.SMEM((sources,), jnp.int32), pltpu.SMEM((sources * requests,), jnp.int32)],
        compiler_params=limit(12),
        cost_estimate=cost(0.1),
        name="place_rows",
    )(ids, decode_rows)

    mark = pl.pallas_call(
        mark_kernel,
        out_shape=jax.ShapeDtypeStruct((8, LANES), jnp.int32),
        in_specs=[smem()],
        out_specs=vmem(),
        compiler_params=limit(4),
        cost_estimate=cost(2),
        name="mark_start",
    )(ids)

    outs, each = (sources, 1) if relative else (1, sources)
    packed = pl.pallas_call(
        functools.partial(pack_kernel, sizes, relative),
        out_shape=[jax.ShapeDtypeStruct((each, packed_rows, LANES), jnp.bfloat16)] * outs,
        in_specs=[smem(), smem(), vmem(), vmem(), vmem(), anywhere()],
        out_specs=[vmem()] * outs,
        scratch_shapes=[
            pltpu.SMEM((sources * (per_pair + 1),), jnp.int32),
            pltpu.VMEM((2 * per_pair, rows, LANES), jnp.float32),
        ],
        compiler_params=limit(8),
        cost_estimate=cost(2),
        name="pack_queries",
    )(ids, decode_rows, q_nope, q_rope, new_latent, mark)

    def attend(received, base):
        here = sum(part.shape[0] for part in received)
        slots = here * per_pair
        pairs = slots * (512 // BLOCK + 1) + 1
        return pl.pallas_call(
            functools.partial(attend_kernel, sizes, scale, relative, base, len(received)),
            out_shape=jax.ShapeDtypeStruct((slots * steps, heads * value_up.shape[2]), jnp.bfloat16),
            in_specs=[anywhere()] * 3 + [vmem()] * (len(received) + 3),
            out_specs=vmem(),
            scratch_shapes=[
                pltpu.SMEM((slots + 1,), jnp.int32),
                pltpu.SMEM((slots + 1,), jnp.int32),
                pltpu.SMEM((sources,), jnp.int32),
                pltpu.SMEM((pairs,), jnp.int32),
                pltpu.SMEM((pairs,), jnp.int32),
                pltpu.VMEM((slots * rows, width), jnp.bfloat16),
                pltpu.VMEM((here * fresh_rows, width), jnp.bfloat16),
                pltpu.VMEM((slots, rows, LATENT), jnp.float32),
                pltpu.VMEM((slots, rows, LANES), jnp.float32),
                pltpu.VMEM((slots, rows, LANES), jnp.float32),
                pltpu.VMEM((slots * rows, LATENT), jnp.bfloat16),
                pltpu.VMEM((2, rows, BLOCK), jnp.float32),
                pltpu.VMEM((2, rows, BLOCK), jnp.float32),
                pltpu.SMEM(ids.shape, jnp.int32),
                pltpu.SMEM(decode_rows.shape, jnp.int32),
                pltpu.SMEM(lengths.shape, jnp.int32),
                pltpu.SemaphoreType.DMA((3,)),
            ],
            compiler_params=limit(14),
            cost_estimate=cost(8),
            name="attend",
        )(ids, decode_rows, lengths, *received, cache, key_up, value_up)

    def order(kernel, in_specs, scratch, arrays):
        return pl.pallas_call(
            kernel,
            out_shape=jax.ShapeDtypeStruct((steps, sources * requests, columns), jnp.bfloat16),
            in_specs=in_specs,
            out_specs=vmem(),
            scratch_shapes=scratch,
            compiler_params=limit(16),
            cost_estimate=cost(2),
            name="order_rows",
        )(*arrays)

    if not relative:
        received = lax.all_to_all(packed[0], "seq", split_axis=0, concat_axis=0, tiled=True)
        every_row = lax.all_gather(attend([received], 0), "seq", axis=0, tiled=True)
        partial_value = jnp.dot(every_row, out_proj, preferred_element_type=jnp.float32).astype(jnp.bfloat16)
        shares = lax.all_to_all(partial_value, "head", split_axis=0, concat_axis=0, tiled=True)
        shares = shares.reshape(head_devices, -1, columns)
        summed = jnp.sum(shares.astype(jnp.float32), axis=0).astype(jnp.bfloat16)
        whole = lax.all_gather(summed, "head", axis=0, tiled=True)
        return order(order_whole_kernel, [vmem()] * 2, [], [pick, whole])

    def project(parts, first_col, cols):
        rows_here = len(parts) * parts[0].shape[0]
        return pl.pallas_call(
            functools.partial(project_kernel, first_col),
            out_shape=[jax.ShapeDtypeStruct((rows_here // 2, cols), jnp.bfloat16)] * 2,
            in_specs=[smem()] + [vmem()] * (len(parts) + 1),
            out_specs=[vmem()] * 2,
            compiler_params=limit(10),
            cost_estimate=cost(2),
            name="project_out",
        )(ids, *parts, out_proj)

    received = [packed[0]] + [flip(packed[k], "seq", k) for k in range(1, 4)]
    near_rows = attend(received[:2], 0)
    near_across = flip(near_rows, "seq", 2)
    far_rows = attend(received[2:], 2)
    near_across, far_rows = lax.optimization_barrier((near_across, far_rows))
    near = [near_rows, flip(near_rows, "seq", 1), near_across, flip(near_across, "seq", 1)]
    far_across = flip(far_rows, "seq", 2)

    def after(value, *others):
        return lax.optimization_barrier((value,) + others)[0]

    def swap(piece):
        return flip(piece[1], "head", 1)

    half = steps * sources * requests // 2

    def cut(parts, first_row, shares):
        groups = columns // LANES
        edges = [LANES * (groups * sum(shares[:i]) // sum(shares)) for i in range(len(shares) + 1)]
        made = []
        for at, end in zip(edges, edges[1:]):
            keep, send = project(parts, at, end - at)
            made.append((first_row, at, keep, swap((keep, send))))
        return made

    near_made = cut(near, 0, (5, 9))
    pairs = [add(near_made[0][2], near_made[0][3])]
    relayed = after(far_across, pairs[0])
    far = [far_rows, flip(far_rows, "seq", 1), far_across, flip(relayed, "seq", 1)]
    far_made = cut(far, half, (6, 5, 3))
    made = near_made + far_made
    for i, (_, _, keep, incoming) in enumerate(made[1:], 1):
        pairs.append(add(keep, incoming))
    crossed = [flip(pair, "head", 3) for pair in pairs]
    last_made = made[-1][2]
    arrays = []
    for i, (pair, cross) in enumerate(zip(pairs, crossed)):
        if i < len(near_made):
            cross = after(cross, *(pairs[len(near_made)],))
        total = add(pair, cross)
        arrays += [total, flip(total, "head", 1)]
    layout = tuple((row, col) for row, col, _, _ in made)
    scratch = [pltpu.VMEM((2 * half, columns), jnp.bfloat16)]
    kernel = functools.partial(order_kernel, layout)
    return order(kernel, [smem()] + [vmem()] * (1 + len(arrays)), scratch, [ids, pick] + arrays)


def solution(mesh):
    return jax.shard_map(
        local,
        mesh=mesh,
        in_specs=(
            P(("groups", "seq"), None),
            P("groups", None),
            P("groups"),
            P(None, ("groups", "seq"), "head", None),
            P(None, ("groups", "seq"), "head", None),
            P(None, ("groups", "seq"), None),
            P("head", None, None),
            P("head", None, None),
            P("head", "seq"),
        ),
        out_specs=P(None, "groups", "seq"),
        check_vma=False,
    )
```

```python
import functools

import jax
import jax.numpy as jnp
from jax import lax
from jax.experimental import pallas as pl
from jax.experimental.pallas import tpu as pltpu
from jax.sharding import PartitionSpec as P

LATENT = 512
BLOCK = 256
LANES = 128
LOG2E = 1.4426950408889634
NEG = -1e30
PLACES = 1024


def own_slots(decode_ref, slot_ref, me, sources, requests, per_pair):
    shift = requests.bit_length() - 1

    def one_source(s, carry):
        count = jnp.int32(0)
        for r in range(requests):
            row = decode_ref[s * requests + r]
            slot_ref[s * (per_pair + 1) + jnp.minimum(count, per_pair)] = row & (requests - 1)
            count = count + jnp.where((row >> shift) == me, 1, 0).astype(jnp.int32)
        return carry

    lax.fori_loop(0, sources, one_source, jnp.int32(0))


def mark_kernel(ids_ref, out_ref):
    out_ref[...] = jnp.full(out_ref.shape, ids_ref[0], jnp.int32)


def pack_kernel(sizes, relative, ids_ref, decode_ref, nope_ref, rope_ref, fresh_ref, after_ref, *rest):
    sources, per_pair, steps, heads, requests, fresh_rows = sizes
    out_refs, (slots, wide) = rest[:-2], rest[-2:]
    me = ids_ref[0] & (PLACES - 1)
    rows = heads * steps
    half = rows // 2
    rope_base = per_pair * rows
    fresh_base = rope_base + per_pair * half
    own_slots(decode_ref, slots, me, sources, requests, per_pair)

    def one_dest(s, out_ref, e):
        for j in range(per_pair):
            row = slots[s * (per_pair + 1) + j]
            for t in range(steps):
                wide[2 * j, pl.ds(t, heads, stride=steps), :] = nope_ref[t, row].astype(jnp.float32)
                wide[2 * j + 1, pl.ds(t, heads, stride=steps), :] = jnp.concatenate(
                    [rope_ref[t, row].astype(jnp.float32)] * 2, axis=1
                )
        for j in range(per_pair):
            out_ref[e, j * rows : (j + 1) * rows, :] = wide[2 * j].astype(jnp.bfloat16)
            low = lax.broadcasted_iota(jnp.int32, (half, LANES), 1) < LANES // 2
            packed = jnp.where(low, wide[2 * j + 1, 0:half, :], wide[2 * j + 1, half : 2 * half, :])
            out_ref[e, rope_base + j * half : rope_base + (j + 1) * half, :] = packed.astype(jnp.bfloat16)

    if relative:
        dests = [me ^ k for k in range(sources)]
        for k in range(sources):
            one_dest(dests[k], out_refs[k], 0)
    else:
        dests = list(range(sources))

        def step(s, carry):
            one_dest(s, out_refs[0], s)
            return carry

        lax.fori_loop(0, sources, step, jnp.int32(0))
    shape = (sources * fresh_rows, steps * requests)
    row_id = lax.broadcasted_iota(jnp.int32, shape, 0)
    col_id = lax.broadcasted_iota(jnp.int32, shape, 1)
    wanted = jnp.full(shape, -1, jnp.int32)
    for k in range(sources):
        for j in range(per_pair):
            first = k * fresh_rows + j * steps
            here = (row_id >= first) & (row_id < first + steps)
            wanted = jnp.where(here, (row_id - first) * requests + slots[dests[k] * (per_pair + 1) + j], wanted)
    pick = jnp.where(col_id == wanted, 1.0, 0.0).astype(jnp.bfloat16)
    width = fresh_ref.shape[2]
    source_rows = jnp.concatenate([fresh_ref[t] for t in range(steps)], axis=0)
    picked = jnp.dot(pick, source_rows, preferred_element_type=jnp.float32).astype(jnp.bfloat16)
    for k in range(sources):
        for c in range(-(-width // LANES)):
            piece = picked[k * fresh_rows : (k + 1) * fresh_rows, c * LANES : min((c + 1) * LANES, width)]
            if piece.shape[1] < LANES:
                piece = jnp.concatenate([piece] * (LANES // piece.shape[1]), axis=1)
            first = fresh_base + c * fresh_rows
            if relative:
                out_refs[k][0, first : first + fresh_rows, :] = piece
            else:
                out_refs[0][k, first : first + fresh_rows, :] = piece


def attend_kernel(sizes, scale, relative, base, recv_count, ids_any, decode_any, length_any, *rest):
    sources, per_pair, steps, heads, requests, fresh_rows = sizes
    recv_refs = rest[:recv_count]
    (
        cache, key_up, value_up, out_ref,
        slot_offset, slot_length, owner_count, pair_slot, pair_start,
        queries, fresh, acc, run_max, run_sum, latent, even_scores, odd_scores,
        ids_ref, decode_ref, length_ref, sems,
    ) = rest[recv_count:]
    tables = [
        pltpu.make_async_copy(ids_any, ids_ref, sems.at[0]),
        pltpu.make_async_copy(decode_any, decode_ref, sems.at[1]),
        pltpu.make_async_copy(length_any, length_ref, sems.at[2]),
    ]
    for table in tables:
        table.start()
    owners = [(ref, e) for ref in recv_refs for e in range(ref.shape[0])]
    here = len(owners)
    slots = here * per_pair
    width, tokens = cache.shape
    rows = heads * steps
    half = rows // 2
    rope_base = per_pair * rows
    fresh_base = rope_base + per_pair * half
    group = 16 // steps
    shift = requests.bit_length() - 1
    factor = scale * LOG2E

    for e in range(here):
        ref, at = owners[e]
        for c in range(-(-width // LANES)):
            lanes = min(LANES, width - c * LANES)
            first = fresh_base + c * fresh_rows
            fresh[e * fresh_rows : (e + 1) * fresh_rows, c * LANES : c * LANES + lanes] = ref[
                at, first : first + fresh_rows, 0:lanes
            ]
        for j in range(per_pair):
            slot = e * per_pair + j
            first = rope_base + j * half
            piece = ref[at, first : first + half, :]
            queries[slot * rows : slot * rows + half, LATENT:width] = piece[:, 0 : width - LATENT]
            queries[slot * rows + half : (slot + 1) * rows, LATENT:width] = piece[:, LANES - (width - LATENT) :]

    inner_head = lax.broadcasted_iota(jnp.int32, (slots * 16, LANES), 0) // steps % group
    own_head = [jnp.where(inner_head == u, 1.0, 0.0).astype(jnp.bfloat16) for u in range(group)]

    def absorb(i):
        tall = jnp.concatenate(
            [ref[at, j * rows + i * 16 : j * rows + (i + 1) * 16, :] for ref, at in owners for j in range(per_pair)],
            axis=0,
        )
        left = jnp.concatenate([tall * own_head[u] for u in range(group)], axis=1)
        right = jnp.concatenate([key_up[i * group + u] for u in range(group)], axis=0)
        res = jnp.dot(left, right, preferred_element_type=jnp.float32).astype(jnp.bfloat16)
        for slot in range(slots):
            queries[slot * rows + i * 16 : slot * rows + (i + 1) * 16, 0:LATENT] = res[slot * 16 : (slot + 1) * 16]

    groups = heads // group
    for i in range(groups // 4):
        absorb(i)
    for table in tables:
        table.wait()

    me = ids_ref[0] & (PLACES - 1)
    for o in range(sources):
        owner_count[o] = jnp.int32(0)
    total = jnp.int32(0)
    for r in range(requests):
        owner = decode_ref[me * requests + r] >> shift
        at = owner_count[owner]
        owner_count[owner] = at + 1
        e = (owner ^ me) - base if relative else owner
        slot = jnp.where((e >= 0) & (e < here), e * per_pair + at, slots)
        length = length_ref[me, r]
        slot_offset[slot] = total
        slot_length[slot] = length
        total = total + length
    count = jnp.int32(0)
    for slot in range(slots):
        start = slot_offset[slot] & ~(LANES - 1)
        end = slot_offset[slot] + slot_length[slot]
        for k in range(512 // BLOCK + 1):
            pair_slot[count] = jnp.int32(slot)
            pair_start[count] = start + k * BLOCK
            count = count + jnp.where(start + k * BLOCK < end, 1, 0).astype(jnp.int32)

    for i in range(groups // 4, groups):
        absorb(i)

    fresh_scores = (
        lax.dot_general(queries[...], fresh[...], (((1,), (1,)), ((), ())), preferred_element_type=jnp.float32) * factor
    )
    row_id = lax.broadcasted_iota(jnp.int32, (rows, here * fresh_rows), 0)
    col_id = lax.broadcasted_iota(jnp.int32, (rows, here * fresh_rows), 1)
    behind = row_id & (steps - 1)
    fresh_weights = []
    for slot in range(slots):
        first = (slot // per_pair) * fresh_rows + (slot % per_pair) * steps
        seen = (col_id >= first) & (col_id <= first + behind)
        scores = jnp.where(seen, fresh_scores[slot * rows : (slot + 1) * rows], NEG)
        top = jnp.max(scores, axis=1, keepdims=True)
        weights = jnp.exp2(scores - top)
        run_max[slot] = jnp.broadcast_to(top, (rows, LANES))
        run_sum[slot] = jnp.broadcast_to(jnp.sum(weights, axis=1, keepdims=True), (rows, LANES))
        fresh_weights.append(weights.astype(jnp.bfloat16))
    for slot in range(slots):
        acc[slot] = jnp.dot(fresh_weights[slot], fresh[:, 0:LATENT], preferred_element_type=jnp.float32)

    def make_scores(buffer, g):
        for u in range(2):
            p = jnp.minimum(g * 2 + u, count - 1)
            q = queries[pl.ds(pl.multiple_of(pair_slot[p] * rows, 16), rows), :]
            read = pl.multiple_of(jnp.minimum(pair_start[p], tokens - BLOCK), LANES)
            buffer[u] = jnp.dot(q, cache[:, pl.ds(read, BLOCK)], preferred_element_type=jnp.float32)

    token = lax.broadcasted_iota(jnp.int32, (1, BLOCK), 1)

    def take_scores(buffer, g):
        for u in range(2):
            p = jnp.minimum(g * 2 + u, count - 1)
            slot = pair_slot[p]
            start = pair_start[p]
            read = jnp.minimum(start, tokens - BLOCK)
            low = jnp.maximum(slot_offset[slot], start) - read
            high = jnp.minimum(slot_offset[slot] + slot_length[slot], start + BLOCK) - read
            high = jnp.where(g * 2 + u < count, high, low)
            bias = jnp.where((token >= low) & (token < high), 0.0, NEG)
            scores = buffer[u] * factor + bias
            top = jnp.max(scores, axis=1, keepdims=True)
            weights = jnp.exp2(scores - top)
            part_sum = jnp.broadcast_to(jnp.sum(weights, axis=1, keepdims=True), (rows, LANES))
            part = lax.dot_general(
                weights.astype(jnp.bfloat16),
                cache[0:LATENT, pl.ds(pl.multiple_of(read, LANES), BLOCK)],
                (((1,), (1,)), ((), ())),
                preferred_element_type=jnp.float32,
            )
            part_max = jnp.broadcast_to(top, (rows, LANES))
            old_max = run_max[slot]
            new_max = jnp.maximum(old_max, part_max)
            keep = jnp.exp2(old_max - new_max)
            add = jnp.exp2(part_max - new_max)
            run_max[slot] = new_max
            run_sum[slot] = run_sum[slot] * keep + part_sum * add
            for c in range(LATENT // LANES):
                cols = slice(c * LANES, (c + 1) * LANES)
                acc[slot, :, cols] = acc[slot, :, cols] * keep + part[:, cols] * add

    make_scores(even_scores, 0)

    def four_pairs(i, carry):
        make_scores(odd_scores, 2 * i + 1)
        take_scores(even_scores, 2 * i)
        make_scores(even_scores, 2 * i + 2)
        take_scores(odd_scores, 2 * i + 1)
        return carry

    fours = count >> 2
    lax.fori_loop(0, fours, four_pairs, jnp.int32(0))

    @pl.when(count > 4 * fours)
    def _():
        take_scores(even_scores, 2 * fours)

    @pl.when(count > 4 * fours + 2)
    def _():
        make_scores(odd_scores, 2 * fours + 1)
        take_scores(odd_scores, 2 * fours + 1)

    for slot in range(slots):
        inverse = 1.0 / run_sum[slot]
        for c in range(LATENT // LANES):
            cols = slice(c * LANES, (c + 1) * LANES)
            latent[slot * rows : (slot + 1) * rows, cols] = (acc[slot, :, cols] * inverse).astype(jnp.bfloat16)
    vdim = value_up.shape[2]
    for i in range(heads // group):
        left = jnp.concatenate(
            [latent[slot * rows + i * 16 : slot * rows + (i + 1) * 16, :] for slot in range(slots)], axis=0
        )
        right = jnp.concatenate([value_up[i * group + u] for u in range(group)], axis=1)
        res = jnp.dot(left, right, preferred_element_type=jnp.float32)
        for u in range(group):
            own = jnp.concatenate(
                [
                    res[slot * 16 + u * steps : slot * 16 + (u + 1) * steps, u * vdim : (u + 1) * vdim]
                    for slot in range(slots)
                ],
                axis=0,
            )
            head = i * group + u
            out_ref[:, head * vdim : (head + 1) * vdim] = own.astype(jnp.bfloat16)


def place_kernel(sizes, relative, ids_ref, decode_ref, out_ref, owner_count, place):
    sources, per_pair, steps, requests = sizes
    me = ids_ref[0] & (PLACES - 1)
    rows = sources * requests
    shift = requests.bit_length() - 1

    def one_source(s, carry):
        for o in range(sources):
            owner_count[o] = jnp.int32(0)
        for r in range(requests):
            row = decode_ref[s * requests + r]
            owner = row >> shift
            at = owner_count[owner]
            owner_count[owner] = at + 1
            if relative:
                e = owner ^ s
                at_row = (e >> 1) * (2 * sources * per_pair) + (me ^ s) * (2 * per_pair) + (e & 1) * per_pair + at
            else:
                at_row = s * requests + owner * per_pair + at
            place[row] = at_row * steps
        return carry

    lax.fori_loop(0, sources, one_source, jnp.int32(0))
    narrow = (rows, LANES)
    row_id = lax.broadcasted_iota(jnp.int32, narrow, 0)

    def put(b, wanted):
        return jnp.where(row_id == b, place[b], wanted)

    wanted = lax.fori_loop(0, rows, put, jnp.zeros(narrow, jnp.int32), unroll=8)[:, 0:1]
    col_id = lax.broadcasted_iota(jnp.int32, (rows, rows * steps), 1)
    for t in range(steps):
        out_ref[t] = jnp.where(col_id == wanted + t, 1.0, 0.0).astype(jnp.bfloat16)


def keeps_upper(ids_ref):
    z = ids_ref[0] // PLACES
    return (z == 1) | (z == 2)


def order_kernel(layout, ids_ref, pick_ref, *rest):
    pieces, out_ref, x = rest[:-2], rest[-2], rest[-1]
    upper = keeps_upper(ids_ref)

    def assemble(first, second):
        for i, (row, col) in enumerate(layout):
            rows, cols = pieces[2 * i].shape
            x[row : row + rows, col : col + cols] = pieces[2 * i + first][...]
            x[row + rows : row + 2 * rows, col : col + cols] = pieces[2 * i + second][...]

    pl.when(upper)(lambda: assemble(1, 0))
    pl.when(jnp.logical_not(upper))(lambda: assemble(0, 1))
    steps, rows, _ = pick_ref.shape
    pick = jnp.concatenate([pick_ref[t] for t in range(steps)], axis=0)
    for c in range(0, x.shape[1], BLOCK):
        tile = jnp.dot(pick, x[:, c : c + BLOCK], preferred_element_type=jnp.float32).astype(jnp.bfloat16)
        for t in range(steps):
            out_ref[t, :, c : c + BLOCK] = tile[t * rows : (t + 1) * rows]


def order_whole_kernel(pick_ref, x_ref, out_ref):
    for t in range(pick_ref.shape[0]):
        out_ref[t] = jnp.dot(pick_ref[t], x_ref[...], preferred_element_type=jnp.float32).astype(jnp.bfloat16)


def project_kernel(first_col, ids_ref, *rest):
    parts, (weight, keep, send) = rest[:-3], rest[-3:]
    half = keep.shape[0]
    upper = keeps_upper(ids_ref)
    cols = keep.shape[1]
    x = jnp.concatenate([part[...] for part in parts], axis=0)
    for c in range(0, cols, BLOCK):
        n = min(BLOCK, cols - c)
        tile = jnp.dot(x, weight[:, first_col + c : first_col + c + n], preferred_element_type=jnp.float32)
        keep[:, c : c + n] = jnp.where(upper, tile[half:], tile[:half]).astype(jnp.bfloat16)
        send[:, c : c + n] = jnp.where(upper, tile[:half], tile[half:]).astype(jnp.bfloat16)


def smem():
    return pl.BlockSpec(memory_space=pltpu.SMEM)


def vmem():
    return pl.BlockSpec(memory_space=pltpu.VMEM)


def anywhere():
    return pl.BlockSpec(memory_space=pl.ANY)


def limit(mib):
    return pltpu.CompilerParams(vmem_limit_bytes=mib * 1024 * 1024)


def cost(microseconds):
    return pl.CostEstimate(
        flops=int(microseconds * 1.0e9), bytes_accessed=int(microseconds * 3.0e6), transcendentals=0
    )


def flip(x, axis, distance):
    size = lax.axis_size(axis)
    return lax.ppermute(x, axis, [(i, i ^ distance) for i in range(size)])


def add(x, y):
    return (x.astype(jnp.float32) + y.astype(jnp.float32)).astype(jnp.bfloat16)


def local(latent_cache, lengths, decode_rows, q_nope, q_rope, new_latent, key_up, value_up, out_proj):
    sources = lax.axis_size("seq")
    head_devices = lax.axis_size("head")
    relative = sources == 4 and head_devices == 4
    requests = lengths.shape[1]
    per_pair = requests // sources
    tokens, width = latent_cache.shape
    steps, _, heads, nope = q_nope.shape
    scale = (nope + q_rope.shape[3]) ** (-0.5)
    fresh_rows = -(-per_pair * steps // 16) * 16
    rows = heads * steps
    columns = out_proj.shape[1]
    packed_rows = per_pair * rows + per_pair * rows // 2 + -(-width // LANES) * fresh_rows
    sizes = (sources, per_pair, steps, heads, requests, fresh_rows)
    ids = (lax.axis_index("seq") + PLACES * lax.axis_index("head")).astype(jnp.int32).reshape(1)
    cache = latent_cache.T

    pick = pl.pallas_call(
        functools.partial(place_kernel, (sources, per_pair, steps, requests), relative),
        out_shape=jax.ShapeDtypeStruct((steps, sources * requests, steps * sources * requests), jnp.bfloat16),
        in_specs=[smem(), smem()],
        out_specs=vmem(),
        scratch_shapes=[pltpu.SMEM((sources,), jnp.int32), pltpu.SMEM((sources * requests,), jnp.int32)],
        compiler_params=limit(12),
        cost_estimate=cost(0.1),
        name="place_rows",
    )(ids, decode_rows)

    mark = pl.pallas_call(
        mark_kernel,
        out_shape=jax.ShapeDtypeStruct((8, LANES), jnp.int32),
        in_specs=[smem()],
        out_specs=vmem(),
        compiler_params=limit(4),
        cost_estimate=cost(2),
        name="mark_start",
    )(ids)

    outs, each = (sources, 1) if relative else (1, sources)
    packed = pl.pallas_call(
        functools.partial(pack_kernel, sizes, relative),
        out_shape=[jax.ShapeDtypeStruct((each, packed_rows, LANES), jnp.bfloat16)] * outs,
        in_specs=[smem(), smem(), vmem(), vmem(), vmem(), anywhere()],
        out_specs=[vmem()] * outs,
        scratch_shapes=[
            pltpu.SMEM((sources * (per_pair + 1),), jnp.int32),
            pltpu.VMEM((2 * per_pair, rows, LANES), jnp.float32),
        ],
        compiler_params=limit(8),
        cost_estimate=cost(2),
        name="pack_queries",
    )(ids, decode_rows, q_nope, q_rope, new_latent, mark)

    def attend(received, base):
        here = sum(part.shape[0] for part in received)
        slots = here * per_pair
        pairs = slots * (512 // BLOCK + 1) + 1
        return pl.pallas_call(
            functools.partial(attend_kernel, sizes, scale, relative, base, len(received)),
            out_shape=jax.ShapeDtypeStruct((slots * steps, heads * value_up.shape[2]), jnp.bfloat16),
            in_specs=[anywhere()] * 3 + [vmem()] * (len(received) + 3),
            out_specs=vmem(),
            scratch_shapes=[
                pltpu.SMEM((slots + 1,), jnp.int32),
                pltpu.SMEM((slots + 1,), jnp.int32),
                pltpu.SMEM((sources,), jnp.int32),
                pltpu.SMEM((pairs,), jnp.int32),
                pltpu.SMEM((pairs,), jnp.int32),
                pltpu.VMEM((slots * rows, width), jnp.bfloat16),
                pltpu.VMEM((here * fresh_rows, width), jnp.bfloat16),
                pltpu.VMEM((slots, rows, LATENT), jnp.float32),
                pltpu.VMEM((slots, rows, LANES), jnp.float32),
                pltpu.VMEM((slots, rows, LANES), jnp.float32),
                pltpu.VMEM((slots * rows, LATENT), jnp.bfloat16),
                pltpu.VMEM((2, rows, BLOCK), jnp.float32),
                pltpu.VMEM((2, rows, BLOCK), jnp.float32),
                pltpu.SMEM(ids.shape, jnp.int32),
                pltpu.SMEM(decode_rows.shape, jnp.int32),
                pltpu.SMEM(lengths.shape, jnp.int32),
                pltpu.SemaphoreType.DMA((3,)),
            ],
            compiler_params=limit(14),
            cost_estimate=cost(8),
            name="attend",
        )(ids, decode_rows, lengths, *received, cache, key_up, value_up)

    def order(kernel, in_specs, scratch, arrays):
        return pl.pallas_call(
            kernel,
            out_shape=jax.ShapeDtypeStruct((steps, sources * requests, columns), jnp.bfloat16),
            in_specs=in_specs,
            out_specs=vmem(),
            scratch_shapes=scratch,
            compiler_params=limit(16),
            cost_estimate=cost(2),
            name="order_rows",
        )(*arrays)

    if not relative:
        received = lax.all_to_all(packed[0], "seq", split_axis=0, concat_axis=0, tiled=True)
        every_row = lax.all_gather(attend([received], 0), "seq", axis=0, tiled=True)
        partial_value = jnp.dot(every_row, out_proj, preferred_element_type=jnp.float32).astype(jnp.bfloat16)
        shares = lax.all_to_all(partial_value, "head", split_axis=0, concat_axis=0, tiled=True)
        shares = shares.reshape(head_devices, -1, columns)
        summed = jnp.sum(shares.astype(jnp.float32), axis=0).astype(jnp.bfloat16)
        whole = lax.all_gather(summed, "head", axis=0, tiled=True)
        return order(order_whole_kernel, [vmem()] * 2, [], [pick, whole])

    def project(parts, first_col, cols):
        rows_here = len(parts) * parts[0].shape[0]
        return pl.pallas_call(
            functools.partial(project_kernel, first_col),
            out_shape=[jax.ShapeDtypeStruct((rows_here // 2, cols), jnp.bfloat16)] * 2,
            in_specs=[smem()] + [vmem()] * (len(parts) + 1),
            out_specs=[vmem()] * 2,
            compiler_params=limit(10),
            cost_estimate=cost(2),
            name="project_out",
        )(ids, *parts, out_proj)

    received = [packed[0]] + [flip(packed[k], "seq", k) for k in range(1, 4)]
    near_rows = attend(received[:2], 0)
    near_across = flip(near_rows, "seq", 2)
    far_rows = attend(received[2:], 2)
    near_across, far_rows = lax.optimization_barrier((near_across, far_rows))
    near = [near_rows, flip(near_rows, "seq", 1), near_across, flip(near_across, "seq", 1)]
    far_across = flip(far_rows, "seq", 2)

    def after(value, *others):
        return lax.optimization_barrier((value,) + others)[0]

    def swap(piece):
        return flip(piece[1], "head", 1)

    half = steps * sources * requests // 2

    def cut(parts, first_row, shares):
        groups = columns // LANES
        edges = [LANES * (groups * sum(shares[:i]) // sum(shares)) for i in range(len(shares) + 1)]
        made = []
        for at, end in zip(edges, edges[1:]):
            keep, send = project(parts, at, end - at)
            made.append((first_row, at, keep, swap((keep, send))))
        return made

    near_made = cut(near, 0, (1, 1))
    pairs = [add(near_made[0][2], near_made[0][3])]
    far = [far_rows, flip(far_rows, "seq", 1), far_across, flip(far_across, "seq", 1)]
    far_made = cut(far, half, (1, 1))
    made = near_made + far_made
    for i, (_, _, keep, incoming) in enumerate(made[1:], 1):
        pairs.append(add(keep, incoming))
    crossed = [flip(pair, "head", 3) for pair in pairs]
    last_made = made[-1][2]
    arrays = []
    for i, (pair, cross) in enumerate(zip(pairs, crossed)):
        if i < len(near_made):
            cross = after(cross, *(last_made,))
        total = add(pair, cross)
        arrays += [total, flip(total, "head", 1)]
    layout = tuple((row, col) for row, col, _, _ in made)
    scratch = [pltpu.VMEM((2 * half, columns), jnp.bfloat16)]
    kernel = functools.partial(order_kernel, layout)
    return order(kernel, [smem()] + [vmem()] * (1 + len(arrays)), scratch, [ids, pick] + arrays)


def solution(mesh):
    return jax.shard_map(
        local,
        mesh=mesh,
        in_specs=(
            P(("groups", "seq"), None),
            P("groups", None),
            P("groups"),
            P(None, ("groups", "seq"), "head", None),
            P(None, ("groups", "seq"), "head", None),
            P(None, ("groups", "seq"), None),
            P("head", None, None),
            P("head", None, None),
            P("head", "seq"),
        ),
        out_specs=P(None, "groups", "seq"),
        check_vma=False,
    )
```

```python
import functools

import jax
import jax.numpy as jnp
from jax import lax
from jax.experimental import pallas as pl
from jax.experimental.pallas import tpu as pltpu
from jax.sharding import PartitionSpec as P

LATENT = 512
BLOCK = 256
LANES = 128
LOG2E = 1.4426950408889634
NEG = -1e30
PLACES = 1024


def own_slots(decode_ref, slot_ref, me, sources, requests, per_pair):
    shift = requests.bit_length() - 1

    def one_source(s, carry):
        count = jnp.int32(0)
        for r in range(requests):
            row = decode_ref[s * requests + r]
            slot_ref[s * (per_pair + 1) + jnp.minimum(count, per_pair)] = row & (requests - 1)
            count = count + jnp.where((row >> shift) == me, 1, 0).astype(jnp.int32)
        return carry

    lax.fori_loop(0, sources, one_source, jnp.int32(0))


def mark_kernel(ids_ref, out_ref):
    out_ref[...] = jnp.full(out_ref.shape, ids_ref[0], jnp.int32)


def pack_kernel(sizes, relative, ids_ref, decode_ref, nope_ref, rope_ref, fresh_ref, after_ref, *rest):
    sources, per_pair, steps, heads, requests, fresh_rows = sizes
    out_refs, (slots, wide) = rest[:-2], rest[-2:]
    me = ids_ref[0] & (PLACES - 1)
    rows = heads * steps
    half = rows // 2
    rope_base = per_pair * rows
    fresh_base = rope_base + per_pair * half
    own_slots(decode_ref, slots, me, sources, requests, per_pair)

    def one_dest(s, out_ref, e):
        for j in range(per_pair):
            row = slots[s * (per_pair + 1) + j]
            for t in range(steps):
                wide[2 * j, pl.ds(t, heads, stride=steps), :] = nope_ref[t, row].astype(jnp.float32)
                wide[2 * j + 1, pl.ds(t, heads, stride=steps), :] = jnp.concatenate(
                    [rope_ref[t, row].astype(jnp.float32)] * 2, axis=1
                )
        for j in range(per_pair):
            out_ref[e, j * rows : (j + 1) * rows, :] = wide[2 * j].astype(jnp.bfloat16)
            low = lax.broadcasted_iota(jnp.int32, (half, LANES), 1) < LANES // 2
            packed = jnp.where(low, wide[2 * j + 1, 0:half, :], wide[2 * j + 1, half : 2 * half, :])
            out_ref[e, rope_base + j * half : rope_base + (j + 1) * half, :] = packed.astype(jnp.bfloat16)

    if relative:
        dests = [me ^ k for k in range(sources)]
        for k in range(sources):
            one_dest(dests[k], out_refs[k], 0)
    else:
        dests = list(range(sources))

        def step(s, carry):
            one_dest(s, out_refs[0], s)
            return carry

        lax.fori_loop(0, sources, step, jnp.int32(0))
    shape = (sources * fresh_rows, steps * requests)
    row_id = lax.broadcasted_iota(jnp.int32, shape, 0)
    col_id = lax.broadcasted_iota(jnp.int32, shape, 1)
    wanted = jnp.full(shape, -1, jnp.int32)
    for k in range(sources):
        for j in range(per_pair):
            first = k * fresh_rows + j * steps
            here = (row_id >= first) & (row_id < first + steps)
            wanted = jnp.where(here, (row_id - first) * requests + slots[dests[k] * (per_pair + 1) + j], wanted)
    pick = jnp.where(col_id == wanted, 1.0, 0.0).astype(jnp.bfloat16)
    width = fresh_ref.shape[2]
    source_rows = jnp.concatenate([fresh_ref[t] for t in range(steps)], axis=0)
    picked = jnp.dot(pick, source_rows, preferred_element_type=jnp.float32).astype(jnp.bfloat16)
    for k in range(sources):
        for c in range(-(-width // LANES)):
            piece = picked[k * fresh_rows : (k + 1) * fresh_rows, c * LANES : min((c + 1) * LANES, width)]
            if piece.shape[1] < LANES:
                piece = jnp.concatenate([piece] * (LANES // piece.shape[1]), axis=1)
            first = fresh_base + c * fresh_rows
            if relative:
                out_refs[k][0, first : first + fresh_rows, :] = piece
            else:
                out_refs[0][k, first : first + fresh_rows, :] = piece


def attend_kernel(sizes, scale, relative, base, recv_count, ids_any, decode_any, length_any, *rest):
    sources, per_pair, steps, heads, requests, fresh_rows = sizes
    recv_refs = rest[:recv_count]
    (
        cache, key_up, value_up, out_ref,
        slot_offset, slot_length, owner_count, pair_slot, pair_start,
        queries, fresh, acc, run_max, run_sum, latent, even_scores, odd_scores,
        ids_ref, decode_ref, length_ref, sems,
    ) = rest[recv_count:]
    tables = [
        pltpu.make_async_copy(ids_any, ids_ref, sems.at[0]),
        pltpu.make_async_copy(decode_any, decode_ref, sems.at[1]),
        pltpu.make_async_copy(length_any, length_ref, sems.at[2]),
    ]
    for table in tables:
        table.start()
    owners = [(ref, e) for ref in recv_refs for e in range(ref.shape[0])]
    here = len(owners)
    slots = here * per_pair
    width, tokens = cache.shape
    rows = heads * steps
    half = rows // 2
    rope_base = per_pair * rows
    fresh_base = rope_base + per_pair * half
    group = 16 // steps
    shift = requests.bit_length() - 1
    factor = scale * LOG2E

    for e in range(here):
        ref, at = owners[e]
        for c in range(-(-width // LANES)):
            lanes = min(LANES, width - c * LANES)
            first = fresh_base + c * fresh_rows
            fresh[e * fresh_rows : (e + 1) * fresh_rows, c * LANES : c * LANES + lanes] = ref[
                at, first : first + fresh_rows, 0:lanes
            ]
        for j in range(per_pair):
            slot = e * per_pair + j
            first = rope_base + j * half
            piece = ref[at, first : first + half, :]
            queries[slot * rows : slot * rows + half, LATENT:width] = piece[:, 0 : width - LATENT]
            queries[slot * rows + half : (slot + 1) * rows, LATENT:width] = piece[:, LANES - (width - LATENT) :]

    inner_head = lax.broadcasted_iota(jnp.int32, (slots * 16, LANES), 0) // steps % group
    own_head = [jnp.where(inner_head == u, 1.0, 0.0).astype(jnp.bfloat16) for u in range(group)]

    def absorb(i):
        tall = jnp.concatenate(
            [ref[at, j * rows + i * 16 : j * rows + (i + 1) * 16, :] for ref, at in owners for j in range(per_pair)],
            axis=0,
        )
        left = jnp.concatenate([tall * own_head[u] for u in range(group)], axis=1)
        right = jnp.concatenate([key_up[i * group + u] for u in range(group)], axis=0)
        res = jnp.dot(left, right, preferred_element_type=jnp.float32).astype(jnp.bfloat16)
        for slot in range(slots):
            queries[slot * rows + i * 16 : slot * rows + (i + 1) * 16, 0:LATENT] = res[slot * 16 : (slot + 1) * 16]

    groups = heads // group
    for i in range(groups // 4):
        absorb(i)
    for table in tables:
        table.wait()

    me = ids_ref[0] & (PLACES - 1)
    for o in range(sources):
        owner_count[o] = jnp.int32(0)
    total = jnp.int32(0)
    for r in range(requests):
        owner = decode_ref[me * requests + r] >> shift
        at = owner_count[owner]
        owner_count[owner] = at + 1
        e = (owner ^ me) - base if relative else owner
        slot = jnp.where((e >= 0) & (e < here), e * per_pair + at, slots)
        length = length_ref[me, r]
        slot_offset[slot] = total
        slot_length[slot] = length
        total = total + length
    count = jnp.int32(0)
    for slot in range(slots):
        start = slot_offset[slot] & ~(LANES - 1)
        end = slot_offset[slot] + slot_length[slot]
        for k in range(512 // BLOCK + 1):
            pair_slot[count] = jnp.int32(slot)
            pair_start[count] = start + k * BLOCK
            count = count + jnp.where(start + k * BLOCK < end, 1, 0).astype(jnp.int32)

    for i in range(groups // 4, groups):
        absorb(i)

    fresh_scores = (
        lax.dot_general(queries[...], fresh[...], (((1,), (1,)), ((), ())), preferred_element_type=jnp.float32) * factor
    )
    row_id = lax.broadcasted_iota(jnp.int32, (rows, here * fresh_rows), 0)
    col_id = lax.broadcasted_iota(jnp.int32, (rows, here * fresh_rows), 1)
    behind = row_id & (steps - 1)
    fresh_weights = []
    for slot in range(slots):
        first = (slot // per_pair) * fresh_rows + (slot % per_pair) * steps
        seen = (col_id >= first) & (col_id <= first + behind)
        scores = jnp.where(seen, fresh_scores[slot * rows : (slot + 1) * rows], NEG)
        top = jnp.max(scores, axis=1, keepdims=True)
        weights = jnp.exp2(scores - top)
        run_max[slot] = jnp.broadcast_to(top, (rows, LANES))
        run_sum[slot] = jnp.broadcast_to(jnp.sum(weights, axis=1, keepdims=True), (rows, LANES))
        fresh_weights.append(weights.astype(jnp.bfloat16))
    for slot in range(slots):
        acc[slot] = jnp.dot(fresh_weights[slot], fresh[:, 0:LATENT], preferred_element_type=jnp.float32)

    def make_scores(buffer, g):
        for u in range(2):
            p = jnp.minimum(g * 2 + u, count - 1)
            q = queries[pl.ds(pl.multiple_of(pair_slot[p] * rows, 16), rows), :]
            read = pl.multiple_of(jnp.minimum(pair_start[p], tokens - BLOCK), LANES)
            buffer[u] = jnp.dot(q, cache[:, pl.ds(read, BLOCK)], preferred_element_type=jnp.float32)

    token = lax.broadcasted_iota(jnp.int32, (1, BLOCK), 1)

    def take_scores(buffer, g):
        for u in range(2):
            p = jnp.minimum(g * 2 + u, count - 1)
            slot = pair_slot[p]
            start = pair_start[p]
            read = jnp.minimum(start, tokens - BLOCK)
            low = jnp.maximum(slot_offset[slot], start) - read
            high = jnp.minimum(slot_offset[slot] + slot_length[slot], start + BLOCK) - read
            high = jnp.where(g * 2 + u < count, high, low)
            bias = jnp.where((token >= low) & (token < high), 0.0, NEG)
            scores = buffer[u] * factor + bias
            top = jnp.max(scores, axis=1, keepdims=True)
            weights = jnp.exp2(scores - top)
            part_sum = jnp.broadcast_to(jnp.sum(weights, axis=1, keepdims=True), (rows, LANES))
            part = lax.dot_general(
                weights.astype(jnp.bfloat16),
                cache[0:LATENT, pl.ds(pl.multiple_of(read, LANES), BLOCK)],
                (((1,), (1,)), ((), ())),
                preferred_element_type=jnp.float32,
            )
            part_max = jnp.broadcast_to(top, (rows, LANES))
            old_max = run_max[slot]
            new_max = jnp.maximum(old_max, part_max)
            keep = jnp.exp2(old_max - new_max)
            add = jnp.exp2(part_max - new_max)
            run_max[slot] = new_max
            run_sum[slot] = run_sum[slot] * keep + part_sum * add
            for c in range(LATENT // LANES):
                cols = slice(c * LANES, (c + 1) * LANES)
                acc[slot, :, cols] = acc[slot, :, cols] * keep + part[:, cols] * add

    make_scores(even_scores, 0)

    def four_pairs(i, carry):
        make_scores(odd_scores, 2 * i + 1)
        take_scores(even_scores, 2 * i)
        make_scores(even_scores, 2 * i + 2)
        take_scores(odd_scores, 2 * i + 1)
        return carry

    fours = count >> 2
    lax.fori_loop(0, fours, four_pairs, jnp.int32(0))

    @pl.when(count > 4 * fours)
    def _():
        take_scores(even_scores, 2 * fours)

    @pl.when(count > 4 * fours + 2)
    def _():
        make_scores(odd_scores, 2 * fours + 1)
        take_scores(odd_scores, 2 * fours + 1)

    for slot in range(slots):
        inverse = 1.0 / run_sum[slot]
        for c in range(LATENT // LANES):
            cols = slice(c * LANES, (c + 1) * LANES)
            latent[slot * rows : (slot + 1) * rows, cols] = (acc[slot, :, cols] * inverse).astype(jnp.bfloat16)
    vdim = value_up.shape[2]
    for i in range(heads // group):
        left = jnp.concatenate(
            [latent[slot * rows + i * 16 : slot * rows + (i + 1) * 16, :] for slot in range(slots)], axis=0
        )
        right = jnp.concatenate([value_up[i * group + u] for u in range(group)], axis=1)
        res = jnp.dot(left, right, preferred_element_type=jnp.float32)
        for u in range(group):
            own = jnp.concatenate(
                [
                    res[slot * 16 + u * steps : slot * 16 + (u + 1) * steps, u * vdim : (u + 1) * vdim]
                    for slot in range(slots)
                ],
                axis=0,
            )
            head = i * group + u
            out_ref[:, head * vdim : (head + 1) * vdim] = own.astype(jnp.bfloat16)


def place_kernel(sizes, relative, ids_ref, decode_ref, out_ref, owner_count, place):
    sources, per_pair, steps, requests = sizes
    me = ids_ref[0] & (PLACES - 1)
    rows = sources * requests
    shift = requests.bit_length() - 1

    def one_source(s, carry):
        for o in range(sources):
            owner_count[o] = jnp.int32(0)
        for r in range(requests):
            row = decode_ref[s * requests + r]
            owner = row >> shift
            at = owner_count[owner]
            owner_count[owner] = at + 1
            if relative:
                e = owner ^ s
                at_row = (e >> 1) * (2 * sources * per_pair) + (me ^ s) * (2 * per_pair) + (e & 1) * per_pair + at
            else:
                at_row = s * requests + owner * per_pair + at
            place[row] = at_row * steps
        return carry

    lax.fori_loop(0, sources, one_source, jnp.int32(0))
    narrow = (rows, LANES)
    row_id = lax.broadcasted_iota(jnp.int32, narrow, 0)

    def put(b, wanted):
        return jnp.where(row_id == b, place[b], wanted)

    wanted = lax.fori_loop(0, rows, put, jnp.zeros(narrow, jnp.int32), unroll=8)[:, 0:1]
    col_id = lax.broadcasted_iota(jnp.int32, (rows, rows * steps), 1)
    for t in range(steps):
        out_ref[t] = jnp.where(col_id == wanted + t, 1.0, 0.0).astype(jnp.bfloat16)


def keeps_upper(ids_ref):
    z = ids_ref[0] // PLACES
    return (z == 1) | (z == 2)


def order_kernel(layout, ids_ref, pick_ref, *rest):
    pieces, out_ref, x = rest[:-2], rest[-2], rest[-1]
    upper = keeps_upper(ids_ref)

    def assemble(first, second):
        for i, (row, col) in enumerate(layout):
            rows, cols = pieces[2 * i].shape
            x[row : row + rows, col : col + cols] = pieces[2 * i + first][...]
            x[row + rows : row + 2 * rows, col : col + cols] = pieces[2 * i + second][...]

    pl.when(upper)(lambda: assemble(1, 0))
    pl.when(jnp.logical_not(upper))(lambda: assemble(0, 1))
    steps, rows, _ = pick_ref.shape
    pick = jnp.concatenate([pick_ref[t] for t in range(steps)], axis=0)
    for c in range(0, x.shape[1], BLOCK):
        tile = jnp.dot(pick, x[:, c : c + BLOCK], preferred_element_type=jnp.float32).astype(jnp.bfloat16)
        for t in range(steps):
            out_ref[t, :, c : c + BLOCK] = tile[t * rows : (t + 1) * rows]


def order_whole_kernel(pick_ref, x_ref, out_ref):
    for t in range(pick_ref.shape[0]):
        out_ref[t] = jnp.dot(pick_ref[t], x_ref[...], preferred_element_type=jnp.float32).astype(jnp.bfloat16)


def project_kernel(first_col, ids_ref, *rest):
    parts, (weight, keep, send) = rest[:-3], rest[-3:]
    half = keep.shape[0]
    upper = keeps_upper(ids_ref)
    cols = keep.shape[1]
    x = jnp.concatenate([part[...] for part in parts], axis=0)
    for c in range(0, cols, BLOCK):
        n = min(BLOCK, cols - c)
        tile = jnp.dot(x, weight[:, first_col + c : first_col + c + n], preferred_element_type=jnp.float32)
        keep[:, c : c + n] = jnp.where(upper, tile[half:], tile[:half]).astype(jnp.bfloat16)
        send[:, c : c + n] = jnp.where(upper, tile[:half], tile[half:]).astype(jnp.bfloat16)


def smem():
    return pl.BlockSpec(memory_space=pltpu.SMEM)


def vmem():
    return pl.BlockSpec(memory_space=pltpu.VMEM)


def anywhere():
    return pl.BlockSpec(memory_space=pl.ANY)


def limit(mib):
    return pltpu.CompilerParams(vmem_limit_bytes=mib * 1024 * 1024)


def cost(microseconds):
    return pl.CostEstimate(
        flops=int(microseconds * 1.0e9), bytes_accessed=int(microseconds * 3.0e6), transcendentals=0
    )


def flip(x, axis, distance):
    size = lax.axis_size(axis)
    return lax.ppermute(x, axis, [(i, i ^ distance) for i in range(size)])


def add(x, y):
    return (x.astype(jnp.float32) + y.astype(jnp.float32)).astype(jnp.bfloat16)


def local(latent_cache, lengths, decode_rows, q_nope, q_rope, new_latent, key_up, value_up, out_proj):
    sources = lax.axis_size("seq")
    head_devices = lax.axis_size("head")
    relative = sources == 4 and head_devices == 4
    requests = lengths.shape[1]
    per_pair = requests // sources
    tokens, width = latent_cache.shape
    steps, _, heads, nope = q_nope.shape
    scale = (nope + q_rope.shape[3]) ** (-0.5)
    fresh_rows = -(-per_pair * steps // 16) * 16
    rows = heads * steps
    columns = out_proj.shape[1]
    packed_rows = per_pair * rows + per_pair * rows // 2 + -(-width // LANES) * fresh_rows
    sizes = (sources, per_pair, steps, heads, requests, fresh_rows)
    ids = (lax.axis_index("seq") + PLACES * lax.axis_index("head")).astype(jnp.int32).reshape(1)
    cache = latent_cache.T

    pick = pl.pallas_call(
        functools.partial(place_kernel, (sources, per_pair, steps, requests), relative),
        out_shape=jax.ShapeDtypeStruct((steps, sources * requests, steps * sources * requests), jnp.bfloat16),
        in_specs=[smem(), smem()],
        out_specs=vmem(),
        scratch_shapes=[pltpu.SMEM((sources,), jnp.int32), pltpu.SMEM((sources * requests,), jnp.int32)],
        compiler_params=limit(12),
        cost_estimate=cost(0.1),
        name="place_rows",
    )(ids, decode_rows)

    mark = pl.pallas_call(
        mark_kernel,
        out_shape=jax.ShapeDtypeStruct((8, LANES), jnp.int32),
        in_specs=[smem()],
        out_specs=vmem(),
        compiler_params=limit(4),
        cost_estimate=cost(2),
        name="mark_start",
    )(ids)

    outs, each = (sources, 1) if relative else (1, sources)
    packed = pl.pallas_call(
        functools.partial(pack_kernel, sizes, relative),
        out_shape=[jax.ShapeDtypeStruct((each, packed_rows, LANES), jnp.bfloat16)] * outs,
        in_specs=[smem(), smem(), vmem(), vmem(), vmem(), anywhere()],
        out_specs=[vmem()] * outs,
        scratch_shapes=[
            pltpu.SMEM((sources * (per_pair + 1),), jnp.int32),
            pltpu.VMEM((2 * per_pair, rows, LANES), jnp.float32),
        ],
        compiler_params=limit(8),
        cost_estimate=cost(2),
        name="pack_queries",
    )(ids, decode_rows, q_nope, q_rope, new_latent, mark)

    def attend(received, base):
        here = sum(part.shape[0] for part in received)
        slots = here * per_pair
        pairs = slots * (512 // BLOCK + 1) + 1
        return pl.pallas_call(
            functools.partial(attend_kernel, sizes, scale, relative, base, len(received)),
            out_shape=jax.ShapeDtypeStruct((slots * steps, heads * value_up.shape[2]), jnp.bfloat16),
            in_specs=[anywhere()] * 3 + [vmem()] * (len(received) + 3),
            out_specs=vmem(),
            scratch_shapes=[
                pltpu.SMEM((slots + 1,), jnp.int32),
                pltpu.SMEM((slots + 1,), jnp.int32),
                pltpu.SMEM((sources,), jnp.int32),
                pltpu.SMEM((pairs,), jnp.int32),
                pltpu.SMEM((pairs,), jnp.int32),
                pltpu.VMEM((slots * rows, width), jnp.bfloat16),
                pltpu.VMEM((here * fresh_rows, width), jnp.bfloat16),
                pltpu.VMEM((slots, rows, LATENT), jnp.float32),
                pltpu.VMEM((slots, rows, LANES), jnp.float32),
                pltpu.VMEM((slots, rows, LANES), jnp.float32),
                pltpu.VMEM((slots * rows, LATENT), jnp.bfloat16),
                pltpu.VMEM((2, rows, BLOCK), jnp.float32),
                pltpu.VMEM((2, rows, BLOCK), jnp.float32),
                pltpu.SMEM(ids.shape, jnp.int32),
                pltpu.SMEM(decode_rows.shape, jnp.int32),
                pltpu.SMEM(lengths.shape, jnp.int32),
                pltpu.SemaphoreType.DMA((3,)),
            ],
            compiler_params=limit(14),
            cost_estimate=cost(8),
            name="attend",
        )(ids, decode_rows, lengths, *received, cache, key_up, value_up)

    def order(kernel, in_specs, scratch, arrays):
        return pl.pallas_call(
            kernel,
            out_shape=jax.ShapeDtypeStruct((steps, sources * requests, columns), jnp.bfloat16),
            in_specs=in_specs,
            out_specs=vmem(),
            scratch_shapes=scratch,
            compiler_params=limit(16),
            cost_estimate=cost(2),
            name="order_rows",
        )(*arrays)

    if not relative:
        received = lax.all_to_all(packed[0], "seq", split_axis=0, concat_axis=0, tiled=True)
        every_row = lax.all_gather(attend([received], 0), "seq", axis=0, tiled=True)
        partial_value = jnp.dot(every_row, out_proj, preferred_element_type=jnp.float32).astype(jnp.bfloat16)
        shares = lax.all_to_all(partial_value, "head", split_axis=0, concat_axis=0, tiled=True)
        shares = shares.reshape(head_devices, -1, columns)
        summed = jnp.sum(shares.astype(jnp.float32), axis=0).astype(jnp.bfloat16)
        whole = lax.all_gather(summed, "head", axis=0, tiled=True)
        return order(order_whole_kernel, [vmem()] * 2, [], [pick, whole])

    def project(parts, first_col, cols):
        rows_here = len(parts) * parts[0].shape[0]
        return pl.pallas_call(
            functools.partial(project_kernel, first_col),
            out_shape=[jax.ShapeDtypeStruct((rows_here // 2, cols), jnp.bfloat16)] * 2,
            in_specs=[smem()] + [vmem()] * (len(parts) + 1),
            out_specs=[vmem()] * 2,
            compiler_params=limit(10),
            cost_estimate=cost(2),
            name="project_out",
        )(ids, *parts, out_proj)

    received = [packed[0]] + [flip(packed[k], "seq", k) for k in range(1, 4)]
    near_rows = attend(received[:2], 0)
    near_across = flip(near_rows, "seq", 2)
    far_rows = attend(received[2:], 2)
    near_across, far_rows = lax.optimization_barrier((near_across, far_rows))
    near = [near_rows, flip(near_rows, "seq", 1), near_across, flip(near_across, "seq", 1)]
    far_across = flip(far_rows, "seq", 2)

    def after(value, *others):
        return lax.optimization_barrier((value,) + others)[0]

    def swap(piece):
        return flip(piece[1], "head", 1)

    half = steps * sources * requests // 2

    def cut(parts, first_row, shares):
        groups = columns // LANES
        edges = [LANES * (groups * sum(shares[:i]) // sum(shares)) for i in range(len(shares) + 1)]
        made = []
        for at, end in zip(edges, edges[1:]):
            keep, send = project(parts, at, end - at)
            made.append((first_row, at, keep, swap((keep, send))))
        return made

    near_made = cut(near, 0, (1, 1))
    pairs = [add(near_made[0][2], near_made[0][3])]
    far = [far_rows, flip(far_rows, "seq", 1), far_across, flip(far_across, "seq", 1)]
    far_made = cut(far, half, (1, 1))
    made = near_made + far_made
    for i, (_, _, keep, incoming) in enumerate(made[1:], 1):
        pairs.append(add(keep, incoming))
    crossed = [flip(pair, "head", 3) for pair in pairs]
    last_made = made[-1][2]
    near_total = jnp.concatenate(
        [add(pair, after(cross, last_made)) for pair, cross in zip(pairs[: len(near_made)], crossed)], axis=1
    )
    arrays = [near_total, flip(near_total, "head", 1)]
    for pair, cross in list(zip(pairs, crossed))[len(near_made) :]:
        total = add(pair, cross)
        arrays += [total, flip(total, "head", 1)]
    layout = ((0, 0),) + tuple((row, col) for row, col, _, _ in far_made)
    scratch = [pltpu.VMEM((2 * half, columns), jnp.bfloat16)]
    kernel = functools.partial(order_kernel, layout)
    return order(kernel, [smem()] + [vmem()] * (1 + len(arrays)), scratch, [ids, pick] + arrays)


def solution(mesh):
    return jax.shard_map(
        local,
        mesh=mesh,
        in_specs=(
            P(("groups", "seq"), None),
            P("groups", None),
            P("groups"),
            P(None, ("groups", "seq"), "head", None),
            P(None, ("groups", "seq"), "head", None),
            P(None, ("groups", "seq"), None),
            P("head", None, None),
            P("head", None, None),
            P("head", "seq"),
        ),
        out_specs=P(None, "groups", "seq"),
        check_vma=False,
    )
```

```python
import functools

import jax
import jax.numpy as jnp
from jax import lax
from jax.experimental import pallas as pl
from jax.experimental.pallas import tpu as pltpu
from jax.sharding import PartitionSpec as P

LATENT = 512
BLOCK = 256
LANES = 128
LOG2E = 1.4426950408889634
NEG = -1e30
PLACES = 1024


def own_slots(decode_ref, slot_ref, me, sources, requests, per_pair):
    shift = requests.bit_length() - 1

    def one_source(s, carry):
        count = jnp.int32(0)
        for r in range(requests):
            row = decode_ref[s * requests + r]
            slot_ref[s * (per_pair + 1) + jnp.minimum(count, per_pair)] = row & (requests - 1)
            count = count + jnp.where((row >> shift) == me, 1, 0).astype(jnp.int32)
        return carry

    lax.fori_loop(0, sources, one_source, jnp.int32(0))


def mark_kernel(ids_ref, out_ref):
    out_ref[...] = jnp.full(out_ref.shape, ids_ref[0], jnp.int32)


def pack_kernel(sizes, relative, ids_ref, decode_ref, nope_ref, rope_ref, fresh_ref, after_ref, *rest):
    sources, per_pair, steps, heads, requests, fresh_rows = sizes
    out_refs, (slots, wide) = rest[:-2], rest[-2:]
    me = ids_ref[0] & (PLACES - 1)
    rows = heads * steps
    half = rows // 2
    rope_base = per_pair * rows
    fresh_base = rope_base + per_pair * half
    own_slots(decode_ref, slots, me, sources, requests, per_pair)

    def one_dest(s, out_ref, e):
        for j in range(per_pair):
            row = slots[s * (per_pair + 1) + j]
            for t in range(steps):
                wide[2 * j, pl.ds(t, heads, stride=steps), :] = nope_ref[t, row].astype(jnp.float32)
                wide[2 * j + 1, pl.ds(t, heads, stride=steps), :] = jnp.concatenate(
                    [rope_ref[t, row].astype(jnp.float32)] * 2, axis=1
                )
        for j in range(per_pair):
            out_ref[e, j * rows : (j + 1) * rows, :] = wide[2 * j].astype(jnp.bfloat16)
            low = lax.broadcasted_iota(jnp.int32, (half, LANES), 1) < LANES // 2
            packed = jnp.where(low, wide[2 * j + 1, 0:half, :], wide[2 * j + 1, half : 2 * half, :])
            out_ref[e, rope_base + j * half : rope_base + (j + 1) * half, :] = packed.astype(jnp.bfloat16)

    if relative:
        dests = [me ^ k for k in range(sources)]
        for k in range(sources):
            one_dest(dests[k], out_refs[k], 0)
    else:
        dests = list(range(sources))

        def step(s, carry):
            one_dest(s, out_refs[0], s)
            return carry

        lax.fori_loop(0, sources, step, jnp.int32(0))
    shape = (sources * fresh_rows, steps * requests)
    row_id = lax.broadcasted_iota(jnp.int32, shape, 0)
    col_id = lax.broadcasted_iota(jnp.int32, shape, 1)
    wanted = jnp.full(shape, -1, jnp.int32)
    for k in range(sources):
        for j in range(per_pair):
            first = k * fresh_rows + j * steps
            here = (row_id >= first) & (row_id < first + steps)
            wanted = jnp.where(here, (row_id - first) * requests + slots[dests[k] * (per_pair + 1) + j], wanted)
    pick = jnp.where(col_id == wanted, 1.0, 0.0).astype(jnp.bfloat16)
    width = fresh_ref.shape[2]
    source_rows = jnp.concatenate([fresh_ref[t] for t in range(steps)], axis=0)
    picked = jnp.dot(pick, source_rows, preferred_element_type=jnp.float32).astype(jnp.bfloat16)
    for k in range(sources):
        for c in range(-(-width // LANES)):
            piece = picked[k * fresh_rows : (k + 1) * fresh_rows, c * LANES : min((c + 1) * LANES, width)]
            if piece.shape[1] < LANES:
                piece = jnp.concatenate([piece] * (LANES // piece.shape[1]), axis=1)
            first = fresh_base + c * fresh_rows
            if relative:
                out_refs[k][0, first : first + fresh_rows, :] = piece
            else:
                out_refs[0][k, first : first + fresh_rows, :] = piece


def attend_kernel(sizes, scale, relative, base, recv_count, ids_any, decode_any, length_any, *rest):
    sources, per_pair, steps, heads, requests, fresh_rows = sizes
    recv_refs = rest[:recv_count]
    (
        cache, key_up, value_up, out_ref,
        slot_offset, slot_length, owner_count, pair_slot, pair_start,
        queries, fresh, acc, run_max, run_sum, latent, even_scores, odd_scores,
        ids_ref, decode_ref, length_ref, sems,
    ) = rest[recv_count:]
    tables = [
        pltpu.make_async_copy(ids_any, ids_ref, sems.at[0]),
        pltpu.make_async_copy(decode_any, decode_ref, sems.at[1]),
        pltpu.make_async_copy(length_any, length_ref, sems.at[2]),
    ]
    for table in tables:
        table.start()
    owners = [(ref, e) for ref in recv_refs for e in range(ref.shape[0])]
    here = len(owners)
    slots = here * per_pair
    width, tokens = cache.shape
    rows = heads * steps
    half = rows // 2
    rope_base = per_pair * rows
    fresh_base = rope_base + per_pair * half
    group = 16 // steps
    shift = requests.bit_length() - 1
    factor = scale * LOG2E

    for e in range(here):
        ref, at = owners[e]
        for c in range(-(-width // LANES)):
            lanes = min(LANES, width - c * LANES)
            first = fresh_base + c * fresh_rows
            fresh[e * fresh_rows : (e + 1) * fresh_rows, c * LANES : c * LANES + lanes] = ref[
                at, first : first + fresh_rows, 0:lanes
            ]
        for j in range(per_pair):
            slot = e * per_pair + j
            first = rope_base + j * half
            piece = ref[at, first : first + half, :]
            queries[slot * rows : slot * rows + half, LATENT:width] = piece[:, 0 : width - LATENT]
            queries[slot * rows + half : (slot + 1) * rows, LATENT:width] = piece[:, LANES - (width - LATENT) :]

    inner_head = lax.broadcasted_iota(jnp.int32, (slots * 16, LANES), 0) // steps % group
    own_head = [jnp.where(inner_head == u, 1.0, 0.0).astype(jnp.bfloat16) for u in range(group)]

    def absorb(i):
        tall = jnp.concatenate(
            [ref[at, j * rows + i * 16 : j * rows + (i + 1) * 16, :] for ref, at in owners for j in range(per_pair)],
            axis=0,
        )
        left = jnp.concatenate([tall * own_head[u] for u in range(group)], axis=1)
        right = jnp.concatenate([key_up[i * group + u] for u in range(group)], axis=0)
        res = jnp.dot(left, right, preferred_element_type=jnp.float32).astype(jnp.bfloat16)
        for slot in range(slots):
            queries[slot * rows + i * 16 : slot * rows + (i + 1) * 16, 0:LATENT] = res[slot * 16 : (slot + 1) * 16]

    groups = heads // group
    for i in range(groups // 4):
        absorb(i)
    for table in tables:
        table.wait()

    me = ids_ref[0] & (PLACES - 1)
    for o in range(sources):
        owner_count[o] = jnp.int32(0)
    total = jnp.int32(0)
    for r in range(requests):
        owner = decode_ref[me * requests + r] >> shift
        at = owner_count[owner]
        owner_count[owner] = at + 1
        e = (owner ^ me) - base if relative else owner
        slot = jnp.where((e >= 0) & (e < here), e * per_pair + at, slots)
        length = length_ref[me, r]
        slot_offset[slot] = total
        slot_length[slot] = length
        total = total + length
    count = jnp.int32(0)
    for slot in range(slots):
        start = slot_offset[slot] & ~(LANES - 1)
        end = slot_offset[slot] + slot_length[slot]
        for k in range(512 // BLOCK + 1):
            pair_slot[count] = jnp.int32(slot)
            pair_start[count] = start + k * BLOCK
            count = count + jnp.where(start + k * BLOCK < end, 1, 0).astype(jnp.int32)

    for i in range(groups // 4, groups):
        absorb(i)

    fresh_scores = (
        lax.dot_general(queries[...], fresh[...], (((1,), (1,)), ((), ())), preferred_element_type=jnp.float32) * factor
    )
    row_id = lax.broadcasted_iota(jnp.int32, (rows, here * fresh_rows), 0)
    col_id = lax.broadcasted_iota(jnp.int32, (rows, here * fresh_rows), 1)
    behind = row_id & (steps - 1)
    fresh_weights = []
    for slot in range(slots):
        first = (slot // per_pair) * fresh_rows + (slot % per_pair) * steps
        seen = (col_id >= first) & (col_id <= first + behind)
        scores = jnp.where(seen, fresh_scores[slot * rows : (slot + 1) * rows], NEG)
        top = jnp.max(scores, axis=1, keepdims=True)
        weights = jnp.exp2(scores - top)
        run_max[slot] = jnp.broadcast_to(top, (rows, LANES))
        run_sum[slot] = jnp.broadcast_to(jnp.sum(weights, axis=1, keepdims=True), (rows, LANES))
        fresh_weights.append(weights.astype(jnp.bfloat16))
    for slot in range(slots):
        acc[slot] = jnp.dot(fresh_weights[slot], fresh[:, 0:LATENT], preferred_element_type=jnp.float32)

    def make_scores(buffer, g):
        for u in range(2):
            p = jnp.minimum(g * 2 + u, count - 1)
            q = queries[pl.ds(pl.multiple_of(pair_slot[p] * rows, 16), rows), :]
            read = pl.multiple_of(jnp.minimum(pair_start[p], tokens - BLOCK), LANES)
            buffer[u] = jnp.dot(q, cache[:, pl.ds(read, BLOCK)], preferred_element_type=jnp.float32)

    token = lax.broadcasted_iota(jnp.int32, (1, BLOCK), 1)

    def take_scores(buffer, g):
        for u in range(2):
            p = jnp.minimum(g * 2 + u, count - 1)
            slot = pair_slot[p]
            start = pair_start[p]
            read = jnp.minimum(start, tokens - BLOCK)
            low = jnp.maximum(slot_offset[slot], start) - read
            high = jnp.minimum(slot_offset[slot] + slot_length[slot], start + BLOCK) - read
            high = jnp.where(g * 2 + u < count, high, low)
            bias = jnp.where((token >= low) & (token < high), 0.0, NEG)
            scores = buffer[u] * factor + bias
            top = jnp.max(scores, axis=1, keepdims=True)
            weights = jnp.exp2(scores - top)
            part_sum = jnp.broadcast_to(jnp.sum(weights, axis=1, keepdims=True), (rows, LANES))
            part = lax.dot_general(
                weights.astype(jnp.bfloat16),
                cache[0:LATENT, pl.ds(pl.multiple_of(read, LANES), BLOCK)],
                (((1,), (1,)), ((), ())),
                preferred_element_type=jnp.float32,
            )
            part_max = jnp.broadcast_to(top, (rows, LANES))
            old_max = run_max[slot]
            new_max = jnp.maximum(old_max, part_max)
            keep = jnp.exp2(old_max - new_max)
            add = jnp.exp2(part_max - new_max)
            run_max[slot] = new_max
            run_sum[slot] = run_sum[slot] * keep + part_sum * add
            for c in range(LATENT // LANES):
                cols = slice(c * LANES, (c + 1) * LANES)
                acc[slot, :, cols] = acc[slot, :, cols] * keep + part[:, cols] * add

    make_scores(even_scores, 0)

    def four_pairs(i, carry):
        make_scores(odd_scores, 2 * i + 1)
        take_scores(even_scores, 2 * i)
        make_scores(even_scores, 2 * i + 2)
        take_scores(odd_scores, 2 * i + 1)
        return carry

    fours = count >> 2
    lax.fori_loop(0, fours, four_pairs, jnp.int32(0))

    @pl.when(count > 4 * fours)
    def _():
        take_scores(even_scores, 2 * fours)

    @pl.when(count > 4 * fours + 2)
    def _():
        make_scores(odd_scores, 2 * fours + 1)
        take_scores(odd_scores, 2 * fours + 1)

    for slot in range(slots):
        inverse = 1.0 / run_sum[slot]
        for c in range(LATENT // LANES):
            cols = slice(c * LANES, (c + 1) * LANES)
            latent[slot * rows : (slot + 1) * rows, cols] = (acc[slot, :, cols] * inverse).astype(jnp.bfloat16)
    vdim = value_up.shape[2]
    for i in range(heads // group):
        left = jnp.concatenate(
            [latent[slot * rows + i * 16 : slot * rows + (i + 1) * 16, :] for slot in range(slots)], axis=0
        )
        right = jnp.concatenate([value_up[i * group + u] for u in range(group)], axis=1)
        res = jnp.dot(left, right, preferred_element_type=jnp.float32)
        for u in range(group):
            own = jnp.concatenate(
                [
                    res[slot * 16 + u * steps : slot * 16 + (u + 1) * steps, u * vdim : (u + 1) * vdim]
                    for slot in range(slots)
                ],
                axis=0,
            )
            head = i * group + u
            out_ref[:, head * vdim : (head + 1) * vdim] = own.astype(jnp.bfloat16)


def place_kernel(sizes, relative, ids_ref, decode_ref, out_ref, owner_count, place):
    sources, per_pair, steps, requests = sizes
    me = ids_ref[0] & (PLACES - 1)
    rows = sources * requests
    shift = requests.bit_length() - 1

    def one_source(s, carry):
        for o in range(sources):
            owner_count[o] = jnp.int32(0)
        for r in range(requests):
            row = decode_ref[s * requests + r]
            owner = row >> shift
            at = owner_count[owner]
            owner_count[owner] = at + 1
            if relative:
                e = owner ^ s
                at_row = (e >> 1) * (2 * sources * per_pair) + (me ^ s) * (2 * per_pair) + (e & 1) * per_pair + at
            else:
                at_row = s * requests + owner * per_pair + at
            place[row] = at_row * steps
        return carry

    lax.fori_loop(0, sources, one_source, jnp.int32(0))
    narrow = (rows, LANES)
    row_id = lax.broadcasted_iota(jnp.int32, narrow, 0)

    def put(b, wanted):
        return jnp.where(row_id == b, place[b], wanted)

    wanted = lax.fori_loop(0, rows, put, jnp.zeros(narrow, jnp.int32), unroll=8)[:, 0:1]
    col_id = lax.broadcasted_iota(jnp.int32, (rows, rows * steps), 1)
    for t in range(steps):
        out_ref[t] = jnp.where(col_id == wanted + t, 1.0, 0.0).astype(jnp.bfloat16)


def keeps_upper(ids_ref):
    z = ids_ref[0] // PLACES
    return (z == 1) | (z == 2)


def order_kernel(layout, ids_ref, pick_ref, *rest):
    pieces, out_ref, x = rest[:-2], rest[-2], rest[-1]
    upper = keeps_upper(ids_ref)

    def assemble(first, second):
        for i, (row, col) in enumerate(layout):
            rows, cols = pieces[2 * i].shape
            x[row : row + rows, col : col + cols] = pieces[2 * i + first][...]
            x[row + rows : row + 2 * rows, col : col + cols] = pieces[2 * i + second][...]

    pl.when(upper)(lambda: assemble(1, 0))
    pl.when(jnp.logical_not(upper))(lambda: assemble(0, 1))
    steps, rows, _ = pick_ref.shape
    pick = jnp.concatenate([pick_ref[t] for t in range(steps)], axis=0)
    for c in range(0, x.shape[1], BLOCK):
        tile = jnp.dot(pick, x[:, c : c + BLOCK], preferred_element_type=jnp.float32).astype(jnp.bfloat16)
        for t in range(steps):
            out_ref[t, :, c : c + BLOCK] = tile[t * rows : (t + 1) * rows]


def order_whole_kernel(pick_ref, x_ref, out_ref):
    for t in range(pick_ref.shape[0]):
        out_ref[t] = jnp.dot(pick_ref[t], x_ref[...], preferred_element_type=jnp.float32).astype(jnp.bfloat16)


def project_kernel(first_col, ids_ref, *rest):
    parts, (weight, keep, send) = rest[:-3], rest[-3:]
    half = keep.shape[0]
    upper = keeps_upper(ids_ref)
    cols = keep.shape[1]
    x = jnp.concatenate([part[...] for part in parts], axis=0)
    for c in range(0, cols, BLOCK):
        n = min(BLOCK, cols - c)
        tile = jnp.dot(x, weight[:, first_col + c : first_col + c + n], preferred_element_type=jnp.float32)
        keep[:, c : c + n] = jnp.where(upper, tile[half:], tile[:half]).astype(jnp.bfloat16)
        send[:, c : c + n] = jnp.where(upper, tile[:half], tile[half:]).astype(jnp.bfloat16)


def smem():
    return pl.BlockSpec(memory_space=pltpu.SMEM)


def vmem():
    return pl.BlockSpec(memory_space=pltpu.VMEM)


def anywhere():
    return pl.BlockSpec(memory_space=pl.ANY)


def limit(mib):
    return pltpu.CompilerParams(vmem_limit_bytes=mib * 1024 * 1024)


def cost(microseconds):
    return pl.CostEstimate(
        flops=int(microseconds * 1.0e9), bytes_accessed=int(microseconds * 3.0e6), transcendentals=0
    )


def flip(x, axis, distance):
    size = lax.axis_size(axis)
    return lax.ppermute(x, axis, [(i, i ^ distance) for i in range(size)])


def add(x, y):
    return (x.astype(jnp.float32) + y.astype(jnp.float32)).astype(jnp.bfloat16)


def local(latent_cache, lengths, decode_rows, q_nope, q_rope, new_latent, key_up, value_up, out_proj):
    sources = lax.axis_size("seq")
    head_devices = lax.axis_size("head")
    relative = sources == 4 and head_devices == 4
    requests = lengths.shape[1]
    per_pair = requests // sources
    tokens, width = latent_cache.shape
    steps, _, heads, nope = q_nope.shape
    scale = (nope + q_rope.shape[3]) ** (-0.5)
    fresh_rows = -(-per_pair * steps // 16) * 16
    rows = heads * steps
    columns = out_proj.shape[1]
    packed_rows = per_pair * rows + per_pair * rows // 2 + -(-width // LANES) * fresh_rows
    sizes = (sources, per_pair, steps, heads, requests, fresh_rows)
    ids = (lax.axis_index("seq") + PLACES * lax.axis_index("head")).astype(jnp.int32).reshape(1)
    cache = latent_cache.T

    pick = pl.pallas_call(
        functools.partial(place_kernel, (sources, per_pair, steps, requests), relative),
        out_shape=jax.ShapeDtypeStruct((steps, sources * requests, steps * sources * requests), jnp.bfloat16),
        in_specs=[smem(), smem()],
        out_specs=vmem(),
        scratch_shapes=[pltpu.SMEM((sources,), jnp.int32), pltpu.SMEM((sources * requests,), jnp.int32)],
        compiler_params=limit(12),
        cost_estimate=cost(0.1),
        name="place_rows",
    )(ids, decode_rows)

    mark = pl.pallas_call(
        mark_kernel,
        out_shape=jax.ShapeDtypeStruct((8, LANES), jnp.int32),
        in_specs=[smem()],
        out_specs=vmem(),
        compiler_params=limit(4),
        cost_estimate=cost(2),
        name="mark_start",
    )(ids)

    outs, each = (sources, 1) if relative else (1, sources)
    packed = pl.pallas_call(
        functools.partial(pack_kernel, sizes, relative),
        out_shape=[jax.ShapeDtypeStruct((each, packed_rows, LANES), jnp.bfloat16)] * outs,
        in_specs=[smem(), smem(), vmem(), vmem(), vmem(), anywhere()],
        out_specs=[vmem()] * outs,
        scratch_shapes=[
            pltpu.SMEM((sources * (per_pair + 1),), jnp.int32),
            pltpu.VMEM((2 * per_pair, rows, LANES), jnp.float32),
        ],
        compiler_params=limit(8),
        cost_estimate=cost(2),
        name="pack_queries",
    )(ids, decode_rows, q_nope, q_rope, new_latent, mark)

    def attend(received, base):
        here = sum(part.shape[0] for part in received)
        slots = here * per_pair
        pairs = slots * (512 // BLOCK + 1) + 1
        return pl.pallas_call(
            functools.partial(attend_kernel, sizes, scale, relative, base, len(received)),
            out_shape=jax.ShapeDtypeStruct((slots * steps, heads * value_up.shape[2]), jnp.bfloat16),
            in_specs=[anywhere()] * 3 + [vmem()] * (len(received) + 3),
            out_specs=vmem(),
            scratch_shapes=[
                pltpu.SMEM((slots + 1,), jnp.int32),
                pltpu.SMEM((slots + 1,), jnp.int32),
                pltpu.SMEM((sources,), jnp.int32),
                pltpu.SMEM((pairs,), jnp.int32),
                pltpu.SMEM((pairs,), jnp.int32),
                pltpu.VMEM((slots * rows, width), jnp.bfloat16),
                pltpu.VMEM((here * fresh_rows, width), jnp.bfloat16),
                pltpu.VMEM((slots, rows, LATENT), jnp.float32),
                pltpu.VMEM((slots, rows, LANES), jnp.float32),
                pltpu.VMEM((slots, rows, LANES), jnp.float32),
                pltpu.VMEM((slots * rows, LATENT), jnp.bfloat16),
                pltpu.VMEM((2, rows, BLOCK), jnp.float32),
                pltpu.VMEM((2, rows, BLOCK), jnp.float32),
                pltpu.SMEM(ids.shape, jnp.int32),
                pltpu.SMEM(decode_rows.shape, jnp.int32),
                pltpu.SMEM(lengths.shape, jnp.int32),
                pltpu.SemaphoreType.DMA((3,)),
            ],
            compiler_params=limit(14),
            cost_estimate=cost(8),
            name="attend",
        )(ids, decode_rows, lengths, *received, cache, key_up, value_up)

    def order(kernel, in_specs, scratch, arrays):
        return pl.pallas_call(
            kernel,
            out_shape=jax.ShapeDtypeStruct((steps, sources * requests, columns), jnp.bfloat16),
            in_specs=in_specs,
            out_specs=vmem(),
            scratch_shapes=scratch,
            compiler_params=limit(16),
            cost_estimate=cost(2),
            name="order_rows",
        )(*arrays)

    if not relative:
        received = lax.all_to_all(packed[0], "seq", split_axis=0, concat_axis=0, tiled=True)
        every_row = lax.all_gather(attend([received], 0), "seq", axis=0, tiled=True)
        partial_value = jnp.dot(every_row, out_proj, preferred_element_type=jnp.float32).astype(jnp.bfloat16)
        shares = lax.all_to_all(partial_value, "head", split_axis=0, concat_axis=0, tiled=True)
        shares = shares.reshape(head_devices, -1, columns)
        summed = jnp.sum(shares.astype(jnp.float32), axis=0).astype(jnp.bfloat16)
        whole = lax.all_gather(summed, "head", axis=0, tiled=True)
        return order(order_whole_kernel, [vmem()] * 2, [], [pick, whole])

    def project(parts, first_col, cols):
        rows_here = len(parts) * parts[0].shape[0]
        return pl.pallas_call(
            functools.partial(project_kernel, first_col),
            out_shape=[jax.ShapeDtypeStruct((rows_here // 2, cols), jnp.bfloat16)] * 2,
            in_specs=[smem()] + [vmem()] * (len(parts) + 1),
            out_specs=[vmem()] * 2,
            compiler_params=limit(10),
            cost_estimate=cost(2),
            name="project_out",
        )(ids, *parts, out_proj)

    received = [packed[0]] + [flip(packed[k], "seq", k) for k in range(1, 4)]
    near_rows = attend(received[:2], 0)
    near_across = flip(near_rows, "seq", 2)
    far_rows = attend(received[2:], 2)
    near_across, far_rows = lax.optimization_barrier((near_across, far_rows))
    near = [near_rows, flip(near_rows, "seq", 1), near_across, flip(near_across, "seq", 1)]
    far_across = flip(far_rows, "seq", 2)

    def after(value, *others):
        return lax.optimization_barrier((value,) + others)[0]

    def swap(piece):
        return flip(piece[1], "head", 1)

    half = steps * sources * requests // 2

    def cut(parts, first_row, shares):
        groups = columns // LANES
        edges = [LANES * (groups * sum(shares[:i]) // sum(shares)) for i in range(len(shares) + 1)]
        made = []
        for at, end in zip(edges, edges[1:]):
            keep, send = project(parts, at, end - at)
            made.append((first_row, at, keep, swap((keep, send))))
        return made

    near_made = cut(near, 0, (1, 1))
    pairs = [add(near_made[0][2], near_made[0][3])]
    relayed = after(far_across, near_made[1][2])
    far = [far_rows, flip(far_rows, "seq", 1), far_across, flip(relayed, "seq", 1)]
    far_made = cut(far, half, (1, 1))
    made = near_made + far_made
    for i, (_, _, keep, incoming) in enumerate(made[1:], 1):
        if i == 1: incoming = after(incoming, made[2][2])
        pairs.append(add(keep, incoming))
    crossed = [flip(pair, "head", 3) for pair in pairs]
    last_made = made[-1][2]
    arrays = []
    for i, (pair, cross) in enumerate(zip(pairs, crossed)):
        if i < len(near_made):
            cross = after(cross, *(pairs[len(near_made)],))
        total = add(pair, cross)
        arrays += [total, flip(total, "head", 1)]
    layout = tuple((row, col) for row, col, _, _ in made)
    scratch = [pltpu.VMEM((2 * half, columns), jnp.bfloat16)]
    kernel = functools.partial(order_kernel, layout)
    return order(kernel, [smem()] + [vmem()] * (1 + len(arrays)), scratch, [ids, pick] + arrays)


def solution(mesh):
    return jax.shard_map(
        local,
        mesh=mesh,
        in_specs=(
            P(("groups", "seq"), None),
            P("groups", None),
            P("groups"),
            P(None, ("groups", "seq"), "head", None),
            P(None, ("groups", "seq"), "head", None),
            P(None, ("groups", "seq"), None),
            P("head", None, None),
            P("head", None, None),
            P("head", "seq"),
        ),
        out_specs=P(None, "groups", "seq"),
        check_vma=False,
    )
```
